32 devices in a mesh: dp: 4 (over x, core), seq: 8 (over z, y).
Axes of the slice: x: 2, y: 2, z: 4, core: 2. Of those that a mesh axis runs over, the one named last changes fastest.
Arguments:
- tokens: bfloat16 [8, 2048, 768], P('dp', 'seq'), may hold values from -6 to 6
- cotangent: bfloat16 [8, 2048, 768], P('dp', 'seq'), may hold values from -6 to 6
- lengths: int32 [8], P('dp'), may hold values from 1024 to 2048, as said below
- w_mx: bfloat16 [768, 3200], P(('dp', 'seq')), may hold values from -0.21875 to 0.21875
- w_value: bfloat16 [768, 1536], P(('dp', 'seq')), may hold values from -0.21875 to 0.21875
- w_out: bfloat16 [1536, 768], P(('dp', 'seq')), may hold values from -0.4375 to 0.4375
- w_up: bfloat16 [768, 1536], P(('dp', 'seq')), may hold values from -0.21875 to 0.21875
- w_down: bfloat16 [1536, 768], P(('dp', 'seq')), may hold values from -0.15625 to 0.15625
- ema_rate: bfloat16 [768, 16], P(('dp', 'seq'))
- ema_in: bfloat16 [768, 16], P(('dp', 'seq')), may hold values from -4 to 4
- ema_out: bfloat16 [768, 16], P(('dp', 'seq')), may hold values from -1.5 to 1.5
- gains: bfloat16 [768, 3], P(('dp', 'seq')), may hold values from 0.5 to 1.5
- qk_affine: bfloat16 [3, 128], replicated, may hold values from -6 to 6
Outputs:
- result: bfloat16 [8, 2048, 768], P('dp', 'seq')
- grad_tokens: float32 [8, 2048, 768], P('dp', 'seq')
- grad_w_mx: float32 [768, 3200], P(('dp', 'seq'))
- grad_w_value: float32 [768, 1536], P(('dp', 'seq'))
- grad_w_out: float32 [1536, 768], P(('dp', 'seq'))
- grad_w_up: float32 [768, 1536], P(('dp', 'seq'))
- grad_w_down: float32 [1536, 768], P(('dp', 'seq'))
- grad_ema_rate: float32 [768, 16], P(('dp', 'seq'))
- grad_ema_in: float32 [768, 16], P(('dp', 'seq'))
- grad_ema_out: float32 [768, 16], P(('dp', 'seq'))
- grad_gains: float32 [768, 3], P(('dp', 'seq'))
- grad_qk_affine: float32 [3, 128], replicated
- rms_values: float32 [3], replicated
The draws below stay inside these ranges and needn't reach their ends.
Inputs may be any that keep to these rules, and one draw needn't show every extreme that they name: `lengths`: in each aligned pair of rows 2i, 2i + 1 one row, which one is drawn, has length 2048.
All inputs are finite; a program needn't handle non-finite values.
Results may differ from the reference program's by a relative error of at most 0.0169.
The reference program's roundings to bfloat16 on the way count: a program that leaves them out, or rounds other values in their place, can miss the bound.
Values may be sent and summed in bfloat16 or wider, within the bound.
A program may use at most 320 MiB of HBM per device.

```python
import jax
import jax.numpy as jnp
from jax import lax

D = 768
Z = 128
V = 1536
NDIM = 16
FF = 1536
SPAN = 128
SEQ_LEN = 2048
BATCH = 8


def draw_lengths(key, part):
    key = jax.random.fold_in(key, 11)
    pick_key, length_key = jax.random.split(key)
    which = jax.random.randint(pick_key, (BATCH // 2,), 0, 2)
    shorter = jax.random.randint(length_key, (BATCH // 2,), SEQ_LEN // 2, SEQ_LEN + 1)
    first = jnp.where(which == 0, SEQ_LEN, shorter)
    second = jnp.where(which == 0, shorter, SEQ_LEN)
    return jnp.stack([first, second], axis=1).reshape(BATCH).astype(jnp.int32)


def draw_ema_rate(key, part):
    key = jax.random.fold_in(key, 5)
    pick_key, fast_key, slow_key = jax.random.split(key, 3)
    percent = 50
    fast_pick = jax.random.randint(pick_key, (D, NDIM), 0, 100) < percent
    fast_rate = jnp.exp(jax.random.uniform(fast_key, (D, NDIM), jnp.float32, jnp.log(1.0 / 50.0), jnp.log(1.0 / 30.0)))
    slow_rate = jnp.exp(jax.random.uniform(slow_key, (D, NDIM), jnp.float32, jnp.log(0.2 / SEQ_LEN), jnp.log(2.0 / SEQ_LEN)))
    return jnp.where(fast_pick, fast_rate, slow_rate).astype(jnp.bfloat16)


def level_of(stream_key, extent, cuts, smallest, high):
    def one(position, parts):
        draws = jax.random.uniform(jax.random.fold_in(jax.random.fold_in(stream_key, 6), position), (parts,), jnp.float32, smallest / len(cuts), high / len(cuts))
        return jnp.repeat(jnp.exp(draws), extent[position] // parts).reshape((-1,) + (1,) * (len(extent) - position - 1))

    level = one(*cuts[0])
    for cut in cuts[1:]:
        level = level * one(*cut)
    return level


def gaussian(key, extent, scale, most, pieces=(), kind=jnp.bfloat16):
    values = jax.random.normal(key, extent, jnp.float32) * scale
    if len(pieces) > 0:
        values = level_of(key, extent, pieces, -0.22, 0.18) * values
    return jnp.clip(values, min=-most, max=most).astype(kind)


def setup_inputs(seed: int = 0) -> dict:
    seeds = jax.random.split(jax.random.key(seed), 14)
    return {
        "tokens": gaussian(seeds[0], (BATCH, SEQ_LEN, D), 1.0, 6.0, ((0, 4), (1, 8))),
        "cotangent": gaussian(seeds[1], (BATCH, SEQ_LEN, D), 1.0, 6.0, ((0, 4), (1, 8))),
        "lengths": draw_lengths(jax.random.fold_in(seeds[13], 71), 0),
        "w_mx": gaussian(seeds[3], (D, 2 * D + Z + V), D ** -0.5, 0.21875, ((0, 32),)),
        "w_value": gaussian(seeds[4], (D, V), D ** -0.5, 0.21875, ((0, 32),)),
        "w_out": gaussian(seeds[5], (V, D), (V // 8) ** -0.5, 0.4375, ((0, 32),)),
        "w_up": gaussian(seeds[6], (D, FF), D ** -0.5, 0.21875, ((0, 32),)),
        "w_down": gaussian(seeds[7], (FF, D), FF ** -0.5, 0.15625, ((0, 32),)),
        "ema_rate": draw_ema_rate(jax.random.fold_in(seeds[13], 71), 0),
        "ema_in": gaussian(seeds[9], (D, NDIM), 1.0, 4.0, ((0, 32),)),
        "ema_out": gaussian(seeds[10], (D, NDIM), NDIM ** -0.5, 1.5, ((0, 32),)),
        "gains": jnp.clip(1.0 + 0.1 * jax.random.normal(seeds[11], (D, 3), jnp.float32), 0.5, 1.5).astype(jnp.bfloat16),
        "qk_affine": gaussian(seeds[12], (3, Z), 1.5, 6.0),
    }


@jax.custom_vjp
def reduced_precision(v):
    return lax.optimization_barrier(v.astype(jnp.bfloat16)).astype(jnp.float32)

@jax.custom_vjp
def reduced_backward(v):
    return v

def low_keep(v):
    return (reduced_precision(v), None)

def low_pass(kept, grad):
    return (grad,)

def back_keep(v):
    return (v, None)

def back_low(kept, grad):
    return (reduced_precision(grad),)
reduced_precision.defvjp(low_keep, low_pass)
reduced_backward.defvjp(back_keep, back_low)
EPSILON = 1e-06
TOP_PRECISION = lax.Precision.HIGHEST

def matmul(left, right):
    return jnp.dot(left, right, precision=TOP_PRECISION, preferred_element_type=jnp.float32)

def rms_norm(values, gain):
    return values * lax.rsqrt(lax.optimization_barrier(jnp.mean(values * values, axis=-1, keepdims=True)) + EPSILON) * gain

def damped_ema(input_signal, rate, beta, eta):
    decay = jnp.exp(-rate)
    scale_in = jnp.sqrt(-jnp.expm1(-2.0 * rate)) * beta

    def one_step(carried, token_row):
        carried = decay * carried + scale_in * token_row[:, None]
        return (carried, lax.optimization_barrier(jnp.sum(eta * carried, axis=1)))

    def one_block(carried, block_rows):
        return lax.scan(one_step, carried, block_rows)
    blocks = input_signal.reshape(-1, SPAN, input_signal.shape[1])
    initial = jnp.zeros(rate.shape, jnp.float32)
    _, smooth = lax.scan(jax.checkpoint(one_block), initial, blocks)
    return smooth.reshape(input_signal.shape)

def span_attention(query, key_rows, value_rows):
    blocks_count = query.shape[0] // SPAN
    query_blocks = query.reshape(blocks_count, SPAN, Z)
    key_blocks = key_rows.reshape(blocks_count, SPAN, Z)
    value_tiles = value_rows.reshape(blocks_count, SPAN, V)
    scores = reduced_backward(jnp.einsum('nqz,nkz->nqk', query_blocks, key_blocks, precision=TOP_PRECISION) * Z ** (-0.5))
    causal = jnp.arange(SPAN)[:, None] >= jnp.arange(SPAN)[None, :]
    attention_weights = jax.nn.softmax(jnp.where(causal, scores, -1e+30), axis=-1)
    attended_output = reduced_backward(jnp.einsum('abu,auf->abf', reduced_precision(attention_weights), value_tiles, precision=TOP_PRECISION))
    return attended_output.reshape(-1, V)

def layer(params, inputs):
    w_mx, w_value, w_out, w_up, w_down, ema_rate, ema_in, ema_out, gains, qk_affine = params
    normed = rms_norm(inputs, gains[:, 0])
    values = jax.nn.silu(reduced_backward(matmul(reduced_precision(normed), w_value)))
    smooth = damped_ema(normed, ema_rate, ema_in, ema_out)
    shifted = jax.nn.silu(smooth + gains[:, 2] * normed)
    mixed = reduced_backward(matmul(reduced_precision(shifted), w_mx))
    update = jax.nn.sigmoid(mixed[:, :D])
    shared = jax.nn.silu(mixed[:, D:D + Z])
    reset = jax.nn.silu(mixed[:, D + Z:D + Z + V])
    direct = mixed[:, D + Z + V:]
    query = reduced_precision(shared * qk_affine[0] + qk_affine[1])
    key_rows = reduced_precision(shared * qk_affine[2])
    attended_output = span_attention(query, key_rows, reduced_precision(values))
    candidate = jax.nn.silu(direct + reduced_backward(matmul(reduced_precision(reset * attended_output), w_out)))
    attn_branch = update * (candidate - inputs)
    middle = inputs + attn_branch
    normed2 = rms_norm(middle, gains[:, 1])
    hidden = reduced_precision(jax.nn.silu(reduced_backward(matmul(reduced_precision(normed2), w_up))))
    ffn_branch = reduced_backward(matmul(hidden, w_down))
    return (middle + ffn_branch, attn_branch, ffn_branch)

def reference(tokens, cotangent, lengths, w_mx, w_value, w_out, w_up, w_down, ema_rate, ema_in, ema_out, gains, qk_affine):
    params = tuple((item.astype(jnp.float32) for item in (w_mx, w_value, w_out, w_up, w_down, ema_rate, ema_in, ema_out, gains, qk_affine)))
    positions = jnp.arange(SEQ_LEN, dtype=jnp.int32)

    def per_row(totals, row_items):
        token_row, grad_row, row_length = row_items
        valid_rows = (positions < row_length).astype(jnp.float32)[:, None]
        outputs, pull = jax.vjp(layer, params, token_row.astype(jnp.float32))
        output, attn_branch, ffn_branch = outputs
        zeros_like = jnp.zeros_like(output)
        grad_params, grad_inputs = pull((grad_row.astype(jnp.float32) * valid_rows, zeros_like, zeros_like))
        squares = jnp.stack([jnp.sum(valid_rows * output * output), jnp.sum(valid_rows * attn_branch * attn_branch), jnp.sum(valid_rows * ffn_branch * ffn_branch)])
        totals = (jax.tree.map(jnp.add, totals[0], grad_params), totals[1] + squares)
        return (totals, (output.astype(jnp.bfloat16), grad_inputs))
    initial = (jax.tree.map(jnp.zeros_like, params), jnp.zeros((3,), jnp.float32))
    totals, (result, grad_tokens) = lax.scan(per_row, initial, (tokens, cotangent, lengths))
    grads, squares = totals
    counted = jnp.sum(lengths).astype(jnp.float32)
    rms_values = jnp.sqrt(squares / (counted * D))
    return (result, grad_tokens, grads[0], grads[1], grads[2], grads[3], grads[4], grads[5], grads[6], grads[7], grads[8], grads[9], rms_values)
```

```python
import functools

import jax
import jax.numpy as jnp
from jax import lax
from jax.experimental import pallas as pl
from jax.experimental.pallas import tpu as pltpu
from jax.sharding import PartitionSpec as P

MESH = pl.DeviceIdType.MESH
bf16, f32 = jnp.bfloat16, jnp.float32
D = 768
Z = 128
V = 1536
SPAN = 128
SEQ_DEV = 256


EPSILON = 1e-06
TOP_PRECISION = lax.Precision.HIGHEST


def prefix(value, axis, join, neutral):
    count, mine = (lax.axis_size(axis), lax.axis_index(axis))
    pieces = jax.tree.map(lambda part: lax.all_gather(part, axis), value)
    so_far = jax.tree.map(
        lambda part, zero: jnp.full_like(part, 0) + jnp.asarray(zero, part.dtype), value, neutral
    )

    def lap(position, so_far):
        longer = join(so_far, jax.tree.map(lambda part: part[position], pieces))
        return jax.tree.map(lambda new, old: jnp.where(position < mine, new, old), longer, so_far)

    return lax.fori_loop(0, count - 1, lap, so_far)


def prefix_2(value, axis, combine, identity):
    length, here = (lax.axis_size(axis), lax.axis_index(axis))
    everything = jax.tree.map(
        lambda part, kind: lax.all_gather(part.astype(kind), axis),
        value,
        jax.tree.map(lambda a: jnp.bfloat16 if a.dtype == jnp.float32 else a.dtype, value),
    )
    start = jax.tree.map(
        lambda part, zero: jnp.broadcast_to(jnp.asarray(zero, part.dtype), part.shape),
        value,
        identity,
    )

    def lap(k, before):
        at = length - 1 - k
        reached = at > here
        new = combine(
            before, jax.tree.map(lambda part, own: part[at].astype(own.dtype), everything, value)
        )
        return jax.tree.map(lambda a, b: jnp.where(reached, a, b), new, before)

    return lax.fori_loop(0, length, lap, start)


def silu_slope(values):
    sigmoid = jax.nn.sigmoid(values)
    return sigmoid * (1.0 + values * (1.0 - sigmoid))


def chain_combine(earlier, later):
    return (earlier[0] * later[0], later[0] * earlier[1] + later[1])


def ema_local(rate, beta, eta, input_signal):
    rows_here, length, channels = input_signal.shape
    block_len = min(64, length)
    blocks_count = length // block_len
    lag_values = jnp.arange(block_len, dtype=jnp.float32)
    powers = jnp.exp(-lag_values[:, None, None] * rate[None])
    scale_in = jnp.sqrt(-jnp.expm1(-2.0 * rate)) * beta
    kernel = jnp.sum(powers * (eta * scale_in)[None], axis=2)
    step_ids = jnp.arange(block_len)
    lag_index = jnp.clip(step_ids[:, None] - step_ids[None, :], 0, block_len - 1)
    toeplitz = jnp.where(
        (step_ids[:, None] >= step_ids[None, :])[:, :, None], kernel[lag_index], 0.0
    )
    leading = jnp.exp(-(lag_values[:, None, None] + 1.0) * rate[None]) * eta[None]
    trailing = powers[::-1] * scale_in[None]
    block_decay = jnp.exp(-block_len * rate)
    blocks = jnp.swapaxes(input_signal.reshape(rows_here, blocks_count, block_len, channels), 0, 1)

    def advance(carried, segment):
        smooth = jnp.einsum("tsd,bsd->btd", toeplitz, segment, precision=TOP_PRECISION)
        smooth = smooth + jnp.einsum("tdh,bdh->btd", leading, carried, precision=TOP_PRECISION)
        carried = block_decay * carried + jnp.einsum(
            "sdh,bsd->bdh", trailing, segment, precision=TOP_PRECISION
        )
        return (carried, smooth)

    initial = jnp.zeros((rows_here, channels, rate.shape[1]), jnp.float32)
    final_state, smooth = lax.scan(advance, initial, blocks)
    return (jnp.swapaxes(smooth, 0, 1).reshape(rows_here, length, channels), final_state)


def ema_carry(rate, eta, incoming):
    block_len = min(64, SEQ_DEV)
    blocks_count = SEQ_DEV // block_len
    lag_values = jnp.arange(block_len, dtype=jnp.float32)
    leading = jnp.exp(-(lag_values[:, None, None] + 1.0) * rate[None]) * eta[None]
    block_decay = jnp.exp(-block_len * rate)

    def advance(carried, unused):
        return (
            block_decay * carried,
            jnp.einsum("tdh,bdh->btd", leading, carried, precision=TOP_PRECISION),
        )

    _, smooth = lax.scan(advance, incoming, None, length=blocks_count)
    return jnp.swapaxes(smooth, 0, 1).reshape(incoming.shape[0], SEQ_DEV, incoming.shape[1])


def per_device(
    tokens,
    cotangent,
    lengths,
    w_mx,
    w_value,
    w_out,
    w_up,
    w_down,
    ema_rate,
    ema_in,
    ema_out,
    gains,
    qk_affine,
):
    gathered = (
        lax.all_gather(w_mx, ("dp", "seq"), axis=0, tiled=True),
        lax.all_gather(w_value, ("dp", "seq"), axis=0, tiled=True),
        lax.all_gather(w_out, ("dp", "seq"), axis=0, tiled=True),
        lax.all_gather(w_up, ("dp", "seq"), axis=0, tiled=True),
        lax.all_gather(w_down, ("dp", "seq"), axis=0, tiled=True),
        lax.all_gather(ema_rate, ("dp", "seq"), axis=0, tiled=True),
        lax.all_gather(ema_in, ("dp", "seq"), axis=0, tiled=True),
        lax.all_gather(ema_out, ("dp", "seq"), axis=0, tiled=True),
        lax.all_gather(gains, ("dp", "seq"), axis=0, tiled=True),
    )
    mx_full, value_full, out_full, up_full, down_full, rate_low, beta_low, eta_low, gain_low = (
        gathered
    )
    rate = rate_low.astype(jnp.float32)
    beta = beta_low.astype(jnp.float32)
    eta = eta_low.astype(jnp.float32)
    gain_all = gain_low.astype(jnp.float32)
    gain_first = gain_all[:, 0]
    gain_second = gain_all[:, 1]
    omega_gain = gain_all[:, 2]
    affine = qk_affine.astype(jnp.float32)
    rows_here = tokens.shape[0]
    spans_dev = SEQ_DEV // SPAN
    score_scale = Z ** (-0.5)
    inputs = tokens.astype(jnp.float32)
    seq_pos = lax.axis_index("seq") * SEQ_DEV + jnp.arange(SEQ_DEV, dtype=jnp.int32)
    valid_rows = (seq_pos[None, :] < lengths[:, None]).astype(jnp.float32)[:, :, None]
    inverse1 = lax.rsqrt(jnp.mean(inputs * inputs, axis=-1, keepdims=True) + EPSILON)
    unit1 = inputs * inverse1
    normed = unit1 * gain_first
    normed_low = normed.astype(jnp.bfloat16)
    value_pre = jnp.einsum(
        "bsd,dv->bsv", normed_low, value_full, preferred_element_type=jnp.float32
    )
    value_low = jax.nn.silu(value_pre).astype(jnp.bfloat16)
    (smooth_local, end_local), pull_local = jax.vjp(ema_local, rate, beta, eta, normed)
    growth = jnp.exp(-SEQ_DEV * rate)
    start_state = prefix(
        (growth, end_local),
        "seq",
        chain_combine,
        (jnp.ones_like(growth), jnp.zeros_like(end_local)),
    )[1]
    smooth_carry, pull_carry = jax.vjp(ema_carry, rate, eta, start_state)
    blend = smooth_local + smooth_carry + omega_gain * normed
    shifted_low = jax.nn.silu(blend).astype(jnp.bfloat16)
    mixed = jnp.einsum("bsd,dk->bsk", shifted_low, mx_full, preferred_element_type=jnp.float32)
    update = jax.nn.sigmoid(mixed[..., :D])
    shared_pre = mixed[..., D : D + Z]
    shared = jax.nn.silu(shared_pre)
    reset_pre = mixed[..., D + Z : D + Z + V]
    reset = jax.nn.silu(reset_pre)
    direct = mixed[..., D + Z + V :]
    query_low = (
        (shared * affine[0] + affine[1]).astype(jnp.bfloat16).reshape(rows_here, spans_dev, SPAN, Z)
    )
    key_low = (shared * affine[2]).astype(jnp.bfloat16).reshape(rows_here, spans_dev, SPAN, Z)
    value_tiles = value_low.reshape(rows_here, spans_dev, SPAN, V)
    scores = (
        jnp.einsum("bnqz,bnkz->bnqk", query_low, key_low, preferred_element_type=jnp.float32)
        * score_scale
    )
    causal = jnp.arange(SPAN)[:, None] >= jnp.arange(SPAN)[None, :]
    masked = jnp.where(causal, scores, -1e30)
    peak = jnp.max(masked, axis=-1, keepdims=True)
    expo = jnp.exp(masked - peak)
    attention_weights = expo / jnp.sum(expo, axis=-1, keepdims=True)
    probs_low = attention_weights.astype(jnp.bfloat16)
    attended_output = jnp.einsum(
        "bnqk,bnkv->bnqv", probs_low, value_tiles, preferred_element_type=jnp.float32
    ).reshape(rows_here, SEQ_DEV, V)
    gated_low = (reset * attended_output).astype(jnp.bfloat16)
    cand_pre = direct + jnp.einsum(
        "bsv,vd->bsd", gated_low, out_full, preferred_element_type=jnp.float32
    )
    candidate = jax.nn.silu(cand_pre)
    attn_branch = update * (candidate - inputs)
    middle = inputs + attn_branch
    inverse2 = lax.rsqrt(jnp.mean(middle * middle, axis=-1, keepdims=True) + EPSILON)
    unit2 = middle * inverse2
    normed2_low = (unit2 * gain_second).astype(jnp.bfloat16)
    up_pre = jnp.einsum("bsd,df->bsf", normed2_low, up_full, preferred_element_type=jnp.float32)
    hidden_low = jax.nn.silu(up_pre).astype(jnp.bfloat16)
    ffn_branch = jnp.einsum(
        "bsf,fd->bsd", hidden_low, down_full, preferred_element_type=jnp.float32
    )
    output = middle + ffn_branch
    again = (
        lax.all_gather(w_mx, ("dp", "seq"), axis=0, tiled=True),
        lax.all_gather(w_value, ("dp", "seq"), axis=0, tiled=True),
        lax.all_gather(w_out, ("dp", "seq"), axis=0, tiled=True),
        lax.all_gather(w_up, ("dp", "seq"), axis=0, tiled=True),
        lax.all_gather(w_down, ("dp", "seq"), axis=0, tiled=True),
    )
    mixer_backward, value_back, out_back, up_back, down_back = again
    grad_out = cotangent.astype(jnp.float32) * valid_rows
    grad_out_low = grad_out.astype(jnp.bfloat16)
    grad_down = jnp.einsum(
        "bsf,bsd->fd", hidden_low, grad_out_low, preferred_element_type=jnp.float32
    )
    grad_hidden = jnp.einsum(
        "bsd,fd->bsf", grad_out_low, down_back, preferred_element_type=jnp.float32
    )
    grad_up_low = (grad_hidden * silu_slope(up_pre)).astype(jnp.bfloat16)
    grad_up = jnp.einsum(
        "bsd,bsf->df", normed2_low, grad_up_low, preferred_element_type=jnp.float32
    )
    grad_normed2 = jnp.einsum(
        "bsf,df->bsd", grad_up_low, up_back, preferred_element_type=jnp.float32
    )
    grad_gain_second = jnp.sum(grad_normed2 * unit2, axis=(0, 1))
    scaled2 = grad_normed2 * gain_second
    grad_middle = grad_out + inverse2 * (
        scaled2 - unit2 * jnp.mean(scaled2 * unit2, axis=-1, keepdims=True)
    )
    grad_update = grad_middle * (candidate - inputs)
    grad_cand_pre = grad_middle * update * silu_slope(cand_pre)
    grad_cand_low = grad_cand_pre.astype(jnp.bfloat16)
    grad_out_proj = jnp.einsum(
        "bsv,bsd->vd", gated_low, grad_cand_low, preferred_element_type=jnp.float32
    )
    grad_gated = jnp.einsum(
        "bsd,vd->bsv", grad_cand_low, out_back, preferred_element_type=jnp.float32
    )
    grad_reset = grad_gated * attended_output
    grad_attended_low = (
        (grad_gated * reset).astype(jnp.bfloat16).reshape(rows_here, spans_dev, SPAN, V)
    )
    grad_probs = jnp.einsum(
        "bnqv,bnkv->bnqk", grad_attended_low, value_tiles, preferred_element_type=jnp.float32
    )
    grad_values = jnp.einsum(
        "bnqk,bnqv->bnkv", probs_low, grad_attended_low, preferred_element_type=jnp.float32
    ).reshape(rows_here, SEQ_DEV, V)
    grad_scores_low = (
        attention_weights
        * (grad_probs - jnp.sum(grad_probs * attention_weights, axis=-1, keepdims=True))
    ).astype(jnp.bfloat16)
    grad_query = (
        jnp.einsum("bnqk,bnkz->bnqz", grad_scores_low, key_low, preferred_element_type=jnp.float32)
        * score_scale
    ).reshape(rows_here, SEQ_DEV, Z)
    grad_key = (
        jnp.einsum(
            "bnqk,bnqz->bnkz", grad_scores_low, query_low, preferred_element_type=jnp.float32
        )
        * score_scale
    ).reshape(rows_here, SEQ_DEV, Z)
    grad_affine = jnp.stack(
        [
            jnp.sum(grad_query * shared, axis=(0, 1)),
            jnp.sum(grad_query, axis=(0, 1)),
            jnp.sum(grad_key * shared, axis=(0, 1)),
        ]
    )
    grad_shared = grad_query * affine[0] + grad_key * affine[2]
    grad_mixed_low = jnp.concatenate(
        [
            grad_update * update * (1.0 - update),
            grad_shared * silu_slope(shared_pre),
            grad_reset * silu_slope(reset_pre),
            grad_cand_pre,
        ],
        axis=-1,
    ).astype(jnp.bfloat16)
    grad_mx = jnp.einsum(
        "bsd,bsk->dk", shifted_low, grad_mixed_low, preferred_element_type=jnp.float32
    )
    grad_shifted = jnp.einsum(
        "bsk,dk->bsd", grad_mixed_low, mixer_backward, preferred_element_type=jnp.float32
    )
    grad_blend = grad_shifted * silu_slope(blend)
    grad_omega = jnp.sum(grad_blend * normed, axis=(0, 1))
    grad_value_low = (grad_values * silu_slope(value_pre)).astype(jnp.bfloat16)
    grad_value_proj = jnp.einsum(
        "bsd,bsv->dv", normed_low, grad_value_low, preferred_element_type=jnp.float32
    )
    grad_normed = grad_blend * omega_gain + jnp.einsum(
        "bsv,dv->bsd", grad_value_low, value_back, preferred_element_type=jnp.float32
    )
    rate_from_carry, eta_from_carry, direct_adjoint = pull_carry(grad_blend)
    later_adjoint = prefix_2(
        (growth, direct_adjoint),
        "seq",
        chain_combine,
        (jnp.ones_like(growth), jnp.zeros_like(direct_adjoint)),
    )[1]
    rate_from_local, grad_beta, eta_from_local, normed_from_ema = pull_local(
        (grad_blend, later_adjoint)
    )
    rate_from_growth = jnp.sum(later_adjoint * start_state, axis=0) * (-SEQ_DEV * growth)
    grad_rate = rate_from_carry + rate_from_local + rate_from_growth
    grad_eta = eta_from_carry + eta_from_local
    grad_normed = grad_normed + normed_from_ema
    grad_gain_first = jnp.sum(grad_normed * unit1, axis=(0, 1))
    scaled1 = grad_normed * gain_first
    grad_tokens = grad_middle * (1.0 - update) + inverse1 * (
        scaled1 - unit1 * jnp.mean(scaled1 * unit1, axis=-1, keepdims=True)
    )
    grad_gains = jnp.stack([grad_gain_first, grad_gain_second, grad_omega], axis=1)
    shards = (
        lax.psum_scatter(grad_mx, ("dp", "seq"), scatter_dimension=0, tiled=True),
        lax.psum_scatter(grad_value_proj, ("dp", "seq"), scatter_dimension=0, tiled=True),
        lax.psum_scatter(grad_out_proj, ("dp", "seq"), scatter_dimension=0, tiled=True),
        lax.psum_scatter(grad_up, ("dp", "seq"), scatter_dimension=0, tiled=True),
        lax.psum_scatter(grad_down, ("dp", "seq"), scatter_dimension=0, tiled=True),
        lax.psum_scatter(grad_rate, ("dp", "seq"), scatter_dimension=0, tiled=True),
        lax.psum_scatter(grad_beta, ("dp", "seq"), scatter_dimension=0, tiled=True),
        lax.psum_scatter(grad_eta, ("dp", "seq"), scatter_dimension=0, tiled=True),
        lax.psum_scatter(grad_gains, ("dp", "seq"), scatter_dimension=0, tiled=True),
    )
    squares = jnp.stack(
        [
            jnp.sum(valid_rows * output * output),
            jnp.sum(valid_rows * attn_branch * attn_branch),
            jnp.sum(valid_rows * ffn_branch * ffn_branch),
            jnp.sum(valid_rows),
        ]
    )
    affine_total, square_total = lax.psum((grad_affine, squares), ("dp", "seq"))
    rms_values = jnp.sqrt(square_total[:3] / (square_total[3] * D))
    return (
        output.astype(jnp.bfloat16),
        grad_tokens,
        shards[0],
        shards[1],
        shards[2],
        shards[3],
        shards[4],
        shards[5],
        shards[6],
        shards[7],
        shards[8],
        affine_total,
        rms_values,
    )


HA, HB = 3200, 768
RA, RB = 48, 96

CHUNKS = [(0, 0, 640, "xy"), (0, 640, 640, "yx"), (0, 1280, 640, "xy"), (0, 1920, 640, "yx"), (0, 2560, 640, "xy"), (1, 0, 384, "yx"), (1, 384, 384, "xy")]

class Pos:
    def __init__(s):
        s.dp, s.sq = lax.axis_index("dp"), lax.axis_index("seq")
        s.x, s.c, s.z, s.y = s.dp // 2, s.dp % 2, s.sq // 2, s.sq % 2
        s.sib = (s.dp + 1 - 2 * s.c, s.sq)
        s.xn = (s.dp + 2 - 4 * s.x, s.sq)
        s.yn = (s.dp, s.sq + 1 - 2 * s.y)
        s.up = (s.dp, jnp.minimum(s.sq + 2, s.sq + 2 * (3 - s.z)))
        s.dn = (s.dp, jnp.maximum(s.sq - 2, s.y))
        s.dpx = s.dp + 2 - 4 * s.x

def rcopy(src, dst, ss, rs, dev):
    return pltpu.make_async_remote_copy(src_ref=src, dst_ref=dst, send_sem=ss, recv_sem=rs, device_id=dev, device_id_type=MESH)

def barrier(pos):
    bar = pltpu.get_barrier_semaphore()
    sig = lambda d: pl.semaphore_signal(bar, inc=1, device_id=d, device_id_type=MESH)
    sig(pos.sib); sig(pos.xn); sig(pos.yn)
    @pl.when(pos.z < 3)
    def _(): sig(pos.up)
    @pl.when(pos.z > 0)
    def _(): sig(pos.dn)
    pl.semaphore_wait(bar, 3 + jnp.minimum(pos.z, 1) + jnp.minimum(3 - pos.z, 1))

def at(ref, rows, nrows, half, w, off, width):
    r = pl.ds(pl.multiple_of(rows, 48), nrows)
    c = pl.ds(pl.multiple_of(half * w + off, 128), width)
    return ref.at[r, c]

class Gather:
    def __init__(s, pos, bufs, ss, rs):
        s.p, s.bufs, s.ss, s.rs = pos, bufs, ss, rs
    def geom(s, i):
        b, off, width, order = CHUNKS[i]
        return s.bufs[b], (RA, RB)[b], (HA, HB)[b], off, width, order
    def unit(s, i, dp, z, half, n=1):
        ref, R, W, off, width, _ = s.geom(i)
        return at(ref, (dp * 4 + z) * R, n * R, half, W, off, width)
    def cp(s, i, k, ref, dev):
        return rcopy(ref, ref, s.ss.at[i, k], s.rs.at[i, k], dev)
    def z0(s, i):
        p = s.p
        u = s.unit(i, p.dp, p.z, p.y)
        @pl.when(p.z < 3)
        def _(): rcopy(u, u, s.ss.at[i, 0], s.rs.at[i, p.z], p.up).start()
        @pl.when(p.z > 0)
        def _(): rcopy(u, u, s.ss.at[i, 1], s.rs.at[i, p.z], p.dn).start()
    def zrecv(s, i, zz):
        u = s.unit(i, s.p.dp, zz, s.p.y)
        rcopy(u, u, s.ss.at[i, 0], s.rs.at[i, zz], s.p.up).wait_recv()
        return u
    def zhop(s, i, h):
        p = s.p
        @pl.when(p.z >= h)
        def _():
            u = s.zrecv(i, p.z - h)
            @pl.when(p.z < 3)
            def _(): rcopy(u, u, s.ss.at[i, 1 + h], s.rs.at[i, p.z - h], p.up).start()
        @pl.when(p.z + h <= 3)
        def _():
            u = s.zrecv(i, p.z + h)
            @pl.when(p.z > 0)
            def _(): rcopy(u, u, s.ss.at[i, 10 + h], s.rs.at[i, p.z + h], p.dn).start()
    def s1(s, i):
        p = s.p; order = CHUNKS[i][3]
        u = s.unit(i, p.dp, 0, p.y, 4)
        s.cp(i, 4, u, p.xn if order == "xy" else p.yn).start()
        s.cp(i, 7, u, p.sib).start()
    def s1_in(s, i):
        p = s.p; order = CHUNKS[i][3]
        return s.unit(i, p.dpx, 0, p.y, 4) if order == "xy" else s.unit(i, p.dp, 0, 1 - p.y, 4)
    def s2(s, i):
        p = s.p; order = CHUNKS[i][3]
        r = s.s1_in(i)
        s.cp(i, 4, r, p.xn).wait_recv()
        nxt = p.yn if order == "xy" else p.xn
        u = s.unit(i, p.dp, 0, p.y, 4)
        s.cp(i, 5, u, nxt).start()
        s.cp(i, 6, r, nxt).start()
        s.cp(i, 8, r, p.sib).start()
    def s2_in(s, i):
        p = s.p; order = CHUNKS[i][3]
        if order == "xy":
            return s.unit(i, p.dp, 0, 1 - p.y, 4), s.unit(i, p.dpx, 0, 1 - p.y, 4)
        return s.unit(i, p.dpx, 0, p.y, 4), s.unit(i, p.dpx, 0, 1 - p.y, 4)
    def s3(s, i):
        p = s.p
        for k, r in enumerate(s.s2_in(i)):
            s.cp(i, 5 + k, r, p.sib).wait_recv()
            s.cp(i, 9 + k, r, p.sib).start()
    def s4(s, i):
        p = s.p
        u = s.unit(i, p.dp, 0, p.y, 4)
        for k in (7, 8, 9, 10):
            s.cp(i, k, u, p.sib).wait_recv()
    def drain(s, i):
        p = s.p
        u1 = s.unit(i, p.dp, 0, p.y)
        u = s.unit(i, p.dp, 0, p.y, 4)
        for k in (4, 5, 6, 7, 8, 9, 10):
            s.cp(i, k, u, p.sib).wait_send()
        w = lambda k: rcopy(u1, u1, s.ss.at[i, k], s.rs.at[i, 0], p.sib).wait_send()
        @pl.when(p.z < 3)
        def _(): w(0)
        @pl.when(p.z > 0)
        def _(): w(1)
        for h in (1, 2):
            @pl.when((p.z >= h) & (p.z < 3))
            def _(): w(1 + h)
            @pl.when((p.z + h <= 3) & (p.z > 0))
            def _(): w(10 + h)

def first_exchange(pos, wa_ref, wb_ref, WA, WB, land, ss, rs):
    p = pos
    ca = rcopy(wa_ref.at[:, pl.ds(pl.multiple_of((1 - p.y) * HA, 128), HA)], land, ss.at[0], rs.at[0], p.yn)
    ca.start()
    mine = (p.dp * 4 + p.z) * RB + p.y * 48
    other = (p.dp * 4 + p.z) * RB + (1 - p.y) * 48
    cb = rcopy(wb_ref.at[:, pl.ds(pl.multiple_of((1 - p.y) * HB, 128), HB)], at(WB, mine, 48, 1 - p.y, HB, 0, HB), ss.at[1], rs.at[1], p.yn)
    cb.start()
    at_own = at(WB, mine, 48, p.y, HB, 0, HB)
    loc = pltpu.make_async_copy(wb_ref.at[:, pl.ds(pl.multiple_of(p.y * HB, 128), HB)], at_own, ss.at[2])
    loc.start()
    ca.wait()
    own = wa_ref[:, pl.ds(pl.multiple_of(p.y * HA, 128), HA)].astype(jnp.float32)
    got = land[...].astype(jnp.float32)
    f = (p.y == 0)
    lo = jnp.where(f, own, got); hi = jnp.where(f, got, own)
    WA[pl.ds(pl.multiple_of((p.dp * 4 + p.z) * RA, 16), RA), pl.ds(pl.multiple_of(p.y * HA, 128), HA)] = jnp.concatenate([lo, hi], axis=0).astype(jnp.bfloat16)
    cb.wait(); loc.wait()

def ag_kernel(wa_ref, wb_ref, oa_ref, ob_ref, WA, WB, land, s0, r0, ss, rs, osem):
    pos = Pos()
    barrier(pos)
    first_exchange(pos, wa_ref, wb_ref, WA, WB, land, s0, r0)
    g = Gather(pos, (WA, WB), ss, rs)
    n = len(CHUNKS)
    for i in range(n): g.z0(i)
    for t in range(n + 3):
        if 0 <= t - 3 < n: g.s3(t - 3)
        if 0 <= t - 2 < n: g.s2(t - 2)
        if t < n:
            g.zhop(t, 1)
            g.zhop(t, 2)
            g.zhop(t, 3)
            g.s1(t)
    for i in range(n): g.s4(i)
    for i in range(n): g.drain(i)
    a = pltpu.make_async_copy(WA, oa_ref, osem.at[0]); b = pltpu.make_async_copy(WB, ob_ref, osem.at[1])
    a.start(); b.start(); a.wait(); b.wait()

def gather_call(wa, wb):
    n = len(CHUNKS)
    return pl.pallas_call(
        ag_kernel,
        out_shape=(jax.ShapeDtypeStruct((768, 2 * HA), jnp.bfloat16), jax.ShapeDtypeStruct((1536, 2 * HB), jnp.bfloat16)),
        in_specs=[pl.BlockSpec(memory_space=pltpu.VMEM)] * 2,
        out_specs=[pl.BlockSpec(memory_space=pl.ANY)] * 2,
        scratch_shapes=[pltpu.VMEM((768, 2 * HA), jnp.bfloat16), pltpu.VMEM((1536, 2 * HB), jnp.bfloat16), pltpu.VMEM((24, HA), jnp.bfloat16),
            pltpu.SemaphoreType.DMA((3,)), pltpu.SemaphoreType.DMA((3,)), pltpu.SemaphoreType.DMA((n, 13)), pltpu.SemaphoreType.DMA((n, 13)), pltpu.SemaphoreType.DMA((2,))],
        compiler_params=pltpu.CompilerParams(collective_id=0, has_side_effects=True, vmem_limit_bytes=60 * 2**20),
    )(wa, wb)


class Scatter:
    NS = 14
    def __init__(s, pos, P, L1, L2, L3, L4, F, G, out, ss, rs):
        s.p, s.P, s.L1, s.L2, s.L3, s.L4, s.F, s.G, s.out, s.ss, s.rs = pos, P, L1, L2, L3, L4, F, G, out, ss, rs
    def geom(s, i):
        b, off, w, order = CHUNKS[i]
        return b, (RA, RB)[b], (HA, HB)[b], off, w, order
    def rows(s, i, xx, c, z=0):
        R = (RA, RB)[CHUNKS[i][0]]
        return pl.multiple_of(((xx * 2 + c) * 4 + z) * R, 48)
    def cols(s, i, yy):
        b, R, W, off, w, _ = s.geom(i)
        return pl.ds(pl.multiple_of(yy * W + off, 128), w)
    def piece(s, i, xx, c, yy, z=0, n=4):
        b, R, W, off, w, _ = s.geom(i)
        return s.P[b].at[pl.ds(s.rows(i, xx, c, z), n * R), s.cols(i, yy)]
    def cp(s, i, k, src, dst, dev):
        return rcopy(src, dst, s.ss.at[i, k], s.rs.at[i, k], dev)
    def add(s, dst, src, nrows):
        def body(r, _):
            rr = pl.ds(pl.multiple_of(r * 48, 48), 48)
            dst[rr, :] = (dst[rr, :].astype(f32) + src[rr, :].astype(f32)).astype(bf16)
            return 0
        lax.fori_loop(0, nrows // 48, body, 0)
    def l1(s, i, xx, yy):
        b, R, W, off, w, _ = s.geom(i)
        return s.L1[b].at[xx, :, s.cols(i, yy)]
    def st0(s, i):
        p = s.p
        for k, (xx, yy) in enumerate(((0, 0), (0, 1), (1, 0), (1, 1))):
            s.cp(i, k, s.piece(i, xx, 1 - p.c, yy), s.l1(i, xx, yy), p.sib).start()
    def a0(s, i):
        b, R, W, off, w, _ = s.geom(i)
        for k, (xx, yy) in enumerate(((0, 0), (0, 1), (1, 0), (1, 1))):
            l = s.l1(i, xx, yy)
            s.cp(i, k, l, l, s.p.sib).wait_recv()
            s.add(s.piece(i, xx, s.p.c, yy), l, 4 * R)
    def l2(s, i, k):
        b, R, W, off, w, _ = s.geom(i)
        return s.L2[b].at[k, :, pl.ds(off, w)]
    def l3(s, i):
        b, R, W, off, w, _ = s.geom(i)
        return s.L3[b].at[:, pl.ds(off, w)]
    def st1(s, i):
        p, order = s.p, s.geom(i)[5]
        for k in (0, 1):
            src = s.piece(i, k, p.c, 1 - p.y) if order == "xy" else s.piece(i, 1 - p.x, p.c, k)
            s.cp(i, 4 + k, src, s.l2(i, k), p.yn if order == "xy" else p.xn).start()
    def a1(s, i):
        p = s.p; b, R, W, off, w, order = s.geom(i)
        for k in (0, 1):
            l = s.l2(i, k)
            s.cp(i, 4 + k, l, l, p.xn).wait_recv()
            s.add(s.piece(i, k, p.c, p.y) if order == "xy" else s.piece(i, p.x, p.c, k), l, 4 * R)
    def st2(s, i):
        p, order = s.p, s.geom(i)[5]
        src = s.piece(i, 1 - p.x, p.c, p.y) if order == "xy" else s.piece(i, p.x, p.c, 1 - p.y)
        s.cp(i, 6, src, s.l3(i), p.xn if order == "xy" else p.yn).start()
    def a2(s, i):
        p = s.p; b, R, W, off, w, order = s.geom(i)
        l = s.l3(i)
        s.cp(i, 6, l, l, p.xn).wait_recv()
        s.add(s.piece(i, p.x, p.c, p.y), l, 4 * R)
    def l4(s, i, d, t):
        b, R, W, off, w, _ = s.geom(i)
        return s.L4[b].at[d, t, :, pl.ds(off, w)]
    def own(s, i, t):
        p = s.p
        return s.piece(i, p.x, p.c, p.y, t, 1)
    def zsem(s, d, t):
        return 6 + t if d == 0 else 10 + t
    def zflow(s, i, d, z):
        p = s.p; R = s.geom(i)[1]
        first = z == (0, 3)[d]
        mine = () if first else (z,)
        on = tuple(range(3, z, -1)) if d == 0 else tuple(range(0, z))
        for t in on:
            l = s.l4(i, d, t)
            if not first:
                s.cp(i, s.zsem(d, t), l, l, p.sib).wait_recv()
                s.add(l, s.own(i, t), R)
            s.cp(i, s.zsem(d, t), s.own(i, t) if first else l, l, p.up if d == 0 else p.dn).start()
        for t in mine:
            l = s.l4(i, d, t)
            s.cp(i, s.zsem(d, t), l, l, p.sib).wait_recv()
    def zstep(s, i, h):
        p = s.p
        for z, d in ((h, 0), (3 - h, 1)):
            @pl.when(p.z == z)
            def _(): s.zflow(i, d, z)
    def fin(s, i):
        p = s.p; b, R, W, off, w, _ = s.geom(i)
        u = s.own(i, p.z)
        hu, hd = (p.z > 0), (p.z < 3)
        lu, ld = s.l4(i, 0, p.z), s.l4(i, 1, p.z)
        F, G, out = s.F[b], s.G[b], s.out[b]
        h = R // 2
        for z in range(4):
            @pl.when(p.z == z)
            def _():
                t = u[...].astype(f32)
                if z > 0: t = t + lu[...].astype(f32)
                if z < 3: t = t + ld[...].astype(f32)
                F[:, pl.ds(off, w)] = t
        src = F.at[pl.ds(pl.multiple_of((1 - p.y) * h, 8), h), pl.ds(off, w)]
        s.cp(i, 13, src, G.at[:, pl.ds(off, w)], p.yn).start()
        out[:, s.cols(i, p.y)] = F[pl.ds(pl.multiple_of(p.y * h, 8), h), pl.ds(off, w)]
    def last(s, i):
        p = s.p; b, R, W, off, w, _ = s.geom(i)
        l = s.G[b].at[:, pl.ds(off, w)]
        s.cp(i, 13, l, l, p.yn).wait_recv()
        s.out[b][:, s.cols(i, 1 - p.y)] = l[...]
    def drain(s, i):
        p = s.p; b, R, W, off, w, _ = s.geom(i)
        for k, ref in [(k, s.l1(i, 0, 0)) for k in range(4)] + [(4, s.l2(i, 0)), (5, s.l2(i, 1)), (6, s.l3(i)), (13, s.G[b].at[:, pl.ds(off, w)])]:
            s.cp(i, k, ref, ref, p.sib).wait_send()
        for d in (0, 1):
            for t in ((1, 2, 3), (0, 1, 2))[d]:
                l = s.l4(i, d, t)
                @pl.when((p.z < t) if d == 0 else (p.z > t))
                def _(): s.cp(i, s.zsem(d, t), l, l, p.sib).wait_send()

def rs_schedule(g, n, before=lambda i: None):
    for t in range(n + 9):
        if t < n: before(t); g.st0(t)
        if 0 <= t - 1 < n: g.a0(t - 1); g.st1(t - 1)
        if 0 <= t - 2 < n: g.a1(t - 2); g.st2(t - 2)
        if 0 <= t - 3 < n: g.a2(t - 3); g.zstep(t - 3, 0)
        for h in (1, 2, 3):
            if 0 <= t - 3 - h < n: g.zstep(t - 3 - h, h)
        if 0 <= t - 6 < n: g.fin(t - 6)
        if 0 <= t - 7 < n: g.last(t - 7)
    for i in range(n): g.drain(i)

def rs_kernel(pa_ref, pb_ref, oa, ob, PA, PB, L1A, L1B, L2A, L2B, L3A, L3B, L4A, L4B, FA, FB, GA, GB, ss, rs, ls):
    pos = Pos(); barrier(pos)
    n = len(CHUNKS)
    a = pltpu.make_async_copy(pa_ref, PA, ls.at[0]); b = pltpu.make_async_copy(pb_ref, PB, ls.at[1])
    a.start(); b.start(); a.wait(); b.wait()
    g = Scatter(pos, (PA, PB), (L1A, L1B), (L2A, L2B), (L3A, L3B), (L4A, L4B), (FA, FB), (GA, GB), (oa, ob), ss, rs)
    rs_schedule(g, n)

def rs_scratch():
    n = len(CHUNKS)
    V = pltpu.VMEM
    return [V((768, 2 * HA), bf16), V((1536, 2 * HB), bf16), V((2, 192, 2 * HA), bf16), V((2, 384, 2 * HB), bf16),
        V((2, 192, HA), bf16), V((2, 384, HB), bf16), V((192, HA), bf16), V((384, HB), bf16),
        V((2, 4, 48, HA), bf16), V((2, 4, 96, HB), bf16), V((48, HA), f32), V((96, HB), f32), V((24, HA), f32), V((48, HB), f32),
        pltpu.SemaphoreType.DMA((n, Scatter.NS)), pltpu.SemaphoreType.DMA((n, Scatter.NS)), pltpu.SemaphoreType.DMA((2,))]

def scatter_call(pa, pb):
    return pl.pallas_call(rs_kernel,
        out_shape=(jax.ShapeDtypeStruct((24, 2 * HA), f32), jax.ShapeDtypeStruct((48, 2 * HB), f32)),
        in_specs=[pl.BlockSpec(memory_space=pl.ANY)] * 2,
        out_specs=[pl.BlockSpec(memory_space=pltpu.VMEM)] * 2,
        scratch_shapes=rs_scratch(),
        compiler_params=pltpu.CompilerParams(collective_id=1, has_side_effects=True, vmem_limit_bytes=60 * 2**20))(pa, pb)

NK = 32
NB = 2

def lanes(j): return pl.ds(pl.multiple_of(j * 128, 128), 128)
def rows_(i): return pl.ds(pl.multiple_of(i * 8, 8), 8)
def tree(xs):
    xs = list(xs)
    while len(xs) > 1:
        xs = [xs[i] + xs[i + 1] if i + 1 < len(xs) else xs[i] for i in range(0, len(xs), 2)]
    return xs[0]

def fwd_states(U, rate, S, END, j, unroll=2):
    ln = lanes(j)
    r = rate[0:16, ln]
    w = [jnp.exp(r * (s - 7.0)) for s in range(8)]
    q8 = jnp.exp(r * -8.0)
    def body(k, st):
        new = []
        for b in range(NB):
            S[b * NK + k, :, ln] = st[b]
            parts = [w[s] * U[b * NK + k, pl.ds(s, 1), ln] for s in range(8)]
            new.append(q8 * st[b] + tree(parts))
        return tuple(new)
    st = lax.fori_loop(0, NK, body, tuple(jnp.zeros((16, 128), f32) for _ in range(NB)), unroll=unroll)
    for b in range(NB): END[b, :, ln] = st[b]

def conv_tables(rate, ec, j):
    ln = lanes(j)
    it = lax.broadcasted_iota(jnp.int32, (8, 128), 0).astype(f32)
    E, K = [], []
    for h in range(16):
        rb = jnp.broadcast_to(rate[pl.ds(h, 1), ln], (8, 128)); eb = jnp.broadcast_to(ec[pl.ds(h, 1), ln], (8, 128))
        K.append(jnp.exp(-it * rb) * eb)
        E.append(jnp.exp(-(it + 1.0) * rb) * eb)
    return E, tree(K)

def fwd_smooth(U, S, S0, rate, ec, omega, BL, KS, j, unroll=1):
    ln = lanes(j)
    r = rate[0:16, ln]
    q8 = jnp.exp(r * -8.0)
    E, K = conv_tables(rate, ec, j)
    KS[...] = K
    ii = lax.broadcasted_iota(jnp.int32, (8, 128), 0)
    KM = [jnp.where(ii >= l, jnp.broadcast_to(KS[pl.ds(l, 1), :], (8, 128)), 0.0) for l in range(8)]
    om = jnp.broadcast_to(omega[:, ln], (8, 128))
    KM[0] = KM[0] + om
    def body(k, gs):
        new = []
        for b in range(NB):
            i = b * NK + k
            S[i, :, ln] = S[i, :, ln] + gs[b]
            u = U[i, :, ln]
            parts = [KM[0] * u] + [KM[l] * pltpu.roll(u, l, 0) for l in range(1, 8)]
            parts += [E[h] * S[i, pl.ds(h, 1), ln] for h in range(16)]
            BL[i, :, ln] = tree(parts)
            new.append(q8 * gs[b])
        return tuple(new)
    lax.fori_loop(0, NK, body, tuple(S0[b, :, ln] for b in range(NB)), unroll=unroll)

def bwd_states(Gr, U, S, rate, A, DIR, G1, H, CS, j, unroll=1):
    ln = lanes(j)
    r = rate[0:16, ln]
    w = [jnp.exp(r * -float(s)) for s in range(8)]
    q8 = jnp.exp(r * -8.0)
    def body(kk, c):
        k = NK - 1 - kk
        st, g1, h1, C = c
        new, C = [], list(C)
        for b in range(NB):
            i = b * NK + k
            A[i, :, ln] = st[b]
            p = [w[s] * Gr[i, pl.ds(s, 1), ln] for s in range(8)]
            Bg = tree(p)
            B1 = tree([p[s] if s == 1 else p[s] * float(s) for s in range(1, 8)])
            Sk = S[i, :, ln]
            g1 = g1 + Sk * Bg
            h1 = h1 + Sk * B1
            new.append(q8 * st[b] + Bg)
            u, g = U[i, :, ln], Gr[i, :, ln]
            C = [C[l] + g * (pltpu.roll(u, l, 0) if l else u) for l in range(8)]
        return tuple(new), g1, h1, tuple(C)
    z = jnp.zeros((16, 128), f32)
    st, g1, h1, C = lax.fori_loop(0, NK, body, (tuple(z for _ in range(NB)), z, z, tuple(jnp.zeros((8, 128), f32) for _ in range(8))), unroll=unroll)
    for b in range(NB): DIR[b, :, ln] = st[b]
    ii = lax.broadcasted_iota(jnp.int32, (8, 128), 0)
    g1, h1 = g1 * w[1], h1 * w[1]
    for l in range(8):
        cl = jnp.sum(jnp.where(ii >= l, C[l], 0.0), axis=0, keepdims=True)
        t = w[l] * cl
        g1 = g1 + t
        if l: h1 = h1 + t * float(l)
    G1[:, ln] = g1
    H[:, ln] = h1

def bwd_grad(Gr, U, S, A, A0, rate, ec, H, DU, KS, AT, j, unroll=1):
    ln = lanes(j)
    r = rate[0:16, ln]
    q8 = jnp.exp(r * -8.0)
    c8 = 8.0 * jnp.exp(r * -9.0)
    wu = [jnp.exp(r * (s - 8.0)) * (8.0 - s) for s in range(8)]
    it = lax.broadcasted_iota(jnp.int32, (8, 128), 0).astype(f32)
    E, K = [], []
    for h in range(16):
        rb = jnp.broadcast_to(rate[pl.ds(h, 1), ln], (8, 128)); eb = jnp.broadcast_to(ec[pl.ds(h, 1), ln], (8, 128))
        K.append(jnp.exp(-it * rb) * eb)
        E.append(jnp.exp((it - 8.0) * rb) * eb)
    KS[...] = tree(K)
    ii = lax.broadcasted_iota(jnp.int32, (8, 128), 0)
    KM = [jnp.where(ii < 8 - l, jnp.broadcast_to(KS[pl.ds(l, 1), :], (8, 128)), 0.0) for l in range(8)]
    def body(kk, c):
        k = NK - 1 - kk
        gs, h1 = c
        new = []
        for b in range(NB):
            i = b * NK + k
            Ak = A[i, :, ln] + gs[b]
            AT[b] = Ak
            Bu = tree([wu[s] * U[i, pl.ds(s, 1), ln] for s in range(8)])
            h1 = h1 + Ak * (Bu + c8 * S[i, :, ln])
            g = Gr[i, :, ln]
            parts = [KM[0] * g] + [KM[l] * pltpu.roll(g, 8 - l, 0) for l in range(1, 8)]
            parts += [E[h] * AT[b, pl.ds(h, 1), :] for h in range(16)]
            DU[i, :, ln] = tree(parts)
            new.append(q8 * gs[b])
        return tuple(new), h1
    gs, h1 = lax.fori_loop(0, NK, body, (tuple(A0[b, :, ln] for b in range(NB)), H[:, ln]), unroll=unroll)
    H[:, ln] = h1

def six(f):
    def body(j, _):
        f(j); return 0
    lax.fori_loop(0, 6, body, 0)

vm = lambda s, t=f32: pltpu.VMEM(s, t)
SH = jax.ShapeDtypeStruct
CP = pltpu.CompilerParams(vmem_limit_bytes=56 * 2**20)

def ema1(U, rate, unroll=2):
    def k(U, rate, S, END): six(lambda j: fwd_states(U, rate, S, END, j, unroll))
    return pl.pallas_call(k, out_shape=(SH((64, 16, 768), f32), SH((2, 16, 768), f32)), compiler_params=CP)(U, rate)
def ema2(U, S, S0, rate, ec, omega, unroll=1):
    def k(U, Sin, S0, rate, ec, omega, S, BL, KS):
        S[...] = Sin[...]
        six(lambda j: fwd_smooth(U, S, S0, rate, ec, omega, BL, KS, j, unroll))
    return pl.pallas_call(k, out_shape=(SH((64, 16, 768), f32), SH((64, 8, 768), f32)), scratch_shapes=[vm((8, 128))], compiler_params=CP)(U, S, S0, rate, ec, omega)
def emab1(Gr, U, S, rate, unroll=1):
    def k(Gr, U, S, rate, A, DIR, G1, H, CS): six(lambda j: bwd_states(Gr, U, S, rate, A, DIR, G1, H, CS, j, unroll))
    return pl.pallas_call(k, out_shape=(SH((64, 16, 768), f32), SH((2, 16, 768), f32), SH((16, 768), f32), SH((16, 768), f32)), scratch_shapes=[vm((8, 128))], compiler_params=CP)(Gr, U, S, rate)
def emab2(Gr, U, S, A, A0, rate, ec, H, unroll=1):
    def k(Gr, U, S, A, A0, rate, ec, Hin, H, DU, KS, AT):
        H[...] = Hin[...]
        six(lambda j: bwd_grad(Gr, U, S, A, A0, rate, ec, H, DU, KS, AT, j, unroll))
    return pl.pallas_call(k, out_shape=(SH((16, 768), f32), SH((64, 8, 768), f32)), scratch_shapes=[vm((8, 128)), vm((2, 16, 128))], compiler_params=CP)(Gr, U, S, A, A0, rate, ec, H)

def scan_kernel(way, e_ref, rate_ref, z_ref, W, L, ss, rs):
    sq, dp = lax.axis_index("seq"), lax.axis_index("dp")
    bar = pltpu.get_barrier_semaphore()
    n = 8
    has = lambda d: (sq + d < n) if d > 0 else (sq + d >= 0)
    to = lambda d: (dp, jnp.clip(sq + d, 0, n - 1))
    for s in (1, 2, 4):
        for d in (s, -s):
            @pl.when(has(d))
            def _(): pl.semaphore_signal(bar, inc=1, device_id=to(d), device_id_type=MESH)
    pl.semaphore_wait(bar, sum(jnp.clip(sq - s + 1, 0, 1) + jnp.clip(n - s - sq, 0, 1) for s in (1, 2, 4)))
    W[0] = e_ref[...]
    z_ref[...] = jnp.zeros_like(z_ref)
    g = jnp.exp(rate_ref[...] * -256.0)
    g2 = g * g
    grow, keep = (g, g2, g2 * g2), (jnp.ones_like(g), g, g2 * g)
    for k, s in enumerate((1, 2, 4)):
        cp = rcopy(W.at[k], L.at[k], ss.at[k], rs.at[k], to(way * s))
        @pl.when(has(way * s))
        def _(): cp.start()
        if k < 2: W[k + 1] = W[k]
        @pl.when(has(-way * s))
        def _():
            cp.wait_recv()
            z_ref[...] = z_ref[...] + keep[k][None] * L[k]
            if k < 2: W[k + 1] = W[k + 1] + grow[k][None] * L[k]
    for k, s in enumerate((1, 2, 4)):
        @pl.when(has(way * s))
        def _(): rcopy(W.at[k], L.at[k], ss.at[k], rs.at[k], to(way * s)).wait_send()
def scan_call(e, rate, way, cid):
    return pl.pallas_call(functools.partial(scan_kernel, way),
        out_shape=jax.ShapeDtypeStruct(e.shape, f32),
        scratch_shapes=[pltpu.VMEM((3,) + e.shape, f32), pltpu.VMEM((3,) + e.shape, f32), pltpu.SemaphoreType.DMA((3,)), pltpu.SemaphoreType.DMA((3,))],
        compiler_params=pltpu.CompilerParams(collective_id=cid, has_side_effects=True, vmem_limit_bytes=40 * 2**20))(e, rate)


def per_device_tuned(tokens, cotangent, lengths, w_mx, w_value, w_out, w_up, w_down, ema_rate, ema_in, ema_out, gains, qk_affine):
    wa = jnp.pad(jnp.concatenate([w_mx, w_value, w_up], axis=1), ((0, 0), (0, 128)))
    wb = jnp.concatenate([w_out, w_down], axis=1)
    rate_own, in_own, out_own = (t.astype(f32) for t in (ema_rate, ema_in, ema_out))
    scale_own = jnp.sqrt(-jnp.expm1(-2.0 * rate_own))
    mine = jnp.pad(jnp.concatenate([rate_own, out_own * scale_own * in_own, gains.astype(f32)], axis=1), ((0, 0), (0, 93)))
    small = lax.all_gather(mine, ("dp", "seq"), axis=0, tiled=True).T
    full_a, full_b = gather_call(wa, wb)
    rate, coef = small[:16], small[16:32]
    gain_first, gain_second, omega_gain = small[32], small[33], small[34]
    mx_full, value_full, up_full = full_a[:, :3200], full_a[:, 3200:4736], full_a[:, 4736:6272]
    out_full, down_full = full_b[:, :768], full_b[:, 768:]
    affine = qk_affine.astype(f32)
    rows_here = tokens.shape[0]
    spans_dev = SEQ_DEV // SPAN
    score_scale = Z ** (-0.5)
    inputs = tokens.astype(f32)
    seq_pos = lax.axis_index("seq") * SEQ_DEV + jnp.arange(SEQ_DEV, dtype=jnp.int32)
    valid_rows = (seq_pos[None, :] < lengths[:, None]).astype(f32)[:, :, None]
    inverse1 = lax.rsqrt(jnp.mean(inputs * inputs, axis=-1, keepdims=True) + EPSILON)
    unit1 = inputs * inverse1
    normed = unit1 * gain_first
    normed_low = normed.astype(bf16)
    u3 = normed.reshape(64, 8, D)
    states, ends = ema1(u3, rate, 4)
    start_state = scan_call(ends, rate, 1, 2)
    states, blend3 = ema2(u3, states, start_state, rate, coef, omega_gain[None], 2)
    blend = blend3.reshape(normed.shape)
    value_pre = jnp.einsum("bsd,dv->bsv", normed_low, value_full, preferred_element_type=f32)
    value_low = jax.nn.silu(value_pre).astype(bf16)
    shifted_low = jax.nn.silu(blend).astype(jnp.bfloat16)
    mixed = jnp.einsum("bsd,dk->bsk", shifted_low, mx_full, preferred_element_type=jnp.float32)
    update = jax.nn.sigmoid(mixed[..., :D])
    shared_pre = mixed[..., D : D + Z]
    shared = jax.nn.silu(shared_pre)
    reset_pre = mixed[..., D + Z : D + Z + V]
    reset = jax.nn.silu(reset_pre)
    direct = mixed[..., D + Z + V :]
    query_low = (
        (shared * affine[0] + affine[1]).astype(jnp.bfloat16).reshape(rows_here, spans_dev, SPAN, Z)
    )
    key_low = (shared * affine[2]).astype(jnp.bfloat16).reshape(rows_here, spans_dev, SPAN, Z)
    value_tiles = value_low.reshape(rows_here, spans_dev, SPAN, V)
    scores = (
        jnp.einsum("bnqz,bnkz->bnqk", query_low, key_low, preferred_element_type=jnp.float32)
        * score_scale
    )
    causal = jnp.arange(SPAN)[:, None] >= jnp.arange(SPAN)[None, :]
    masked = jnp.where(causal, scores, -1e30)
    peak = jnp.max(masked, axis=-1, keepdims=True)
    expo = jnp.exp(masked - peak)
    attention_weights = expo / jnp.sum(expo, axis=-1, keepdims=True)
    probs_low = attention_weights.astype(jnp.bfloat16)
    attended_output = jnp.einsum(
        "bnqk,bnkv->bnqv", probs_low, value_tiles, preferred_element_type=jnp.float32
    ).reshape(rows_here, SEQ_DEV, V)
    gated_low = (reset * attended_output).astype(jnp.bfloat16)
    cand_pre = direct + jnp.einsum(
        "bsv,vd->bsd", gated_low, out_full, preferred_element_type=jnp.float32
    )
    candidate = jax.nn.silu(cand_pre)
    attn_branch = update * (candidate - inputs)
    middle = inputs + attn_branch
    inverse2 = lax.rsqrt(jnp.mean(middle * middle, axis=-1, keepdims=True) + EPSILON)
    unit2 = middle * inverse2
    normed2_low = (unit2 * gain_second).astype(jnp.bfloat16)
    up_pre = jnp.einsum("bsd,df->bsf", normed2_low, up_full, preferred_element_type=jnp.float32)
    hidden_low = jax.nn.silu(up_pre).astype(jnp.bfloat16)
    ffn_branch = jnp.einsum(
        "bsf,fd->bsd", hidden_low, down_full, preferred_element_type=jnp.float32
    )
    output = middle + ffn_branch
    mixer_backward, value_back, out_back, up_back, down_back = mx_full, value_full, out_full, up_full, down_full
    grad_out = cotangent.astype(jnp.float32) * valid_rows
    grad_out_low = grad_out.astype(jnp.bfloat16)
    grad_down = jnp.einsum(
        "bsf,bsd->fd", hidden_low, grad_out_low, preferred_element_type=jnp.float32
    )
    grad_hidden = jnp.einsum(
        "bsd,fd->bsf", grad_out_low, down_back, preferred_element_type=jnp.float32
    )
    grad_up_low = (grad_hidden * silu_slope(up_pre)).astype(jnp.bfloat16)
    grad_up = jnp.einsum(
        "bsd,bsf->df", normed2_low, grad_up_low, preferred_element_type=jnp.float32
    )
    grad_normed2 = jnp.einsum(
        "bsf,df->bsd", grad_up_low, up_back, preferred_element_type=jnp.float32
    )
    grad_gain_second = jnp.sum(grad_normed2 * unit2, axis=(0, 1))
    scaled2 = grad_normed2 * gain_second
    grad_middle = grad_out + inverse2 * (
        scaled2 - unit2 * jnp.mean(scaled2 * unit2, axis=-1, keepdims=True)
    )
    grad_update = grad_middle * (candidate - inputs)
    grad_cand_pre = grad_middle * update * silu_slope(cand_pre)
    grad_cand_low = grad_cand_pre.astype(jnp.bfloat16)
    grad_out_proj = jnp.einsum(
        "bsv,bsd->vd", gated_low, grad_cand_low, preferred_element_type=jnp.float32
    )
    grad_gated = jnp.einsum(
        "bsd,vd->bsv", grad_cand_low, out_back, preferred_element_type=jnp.float32
    )
    grad_reset = grad_gated * attended_output
    grad_attended_low = (
        (grad_gated * reset).astype(jnp.bfloat16).reshape(rows_here, spans_dev, SPAN, V)
    )
    grad_probs = jnp.einsum(
        "bnqv,bnkv->bnqk", grad_attended_low, value_tiles, preferred_element_type=jnp.float32
    )
    grad_values = jnp.einsum(
        "bnqk,bnqv->bnkv", probs_low, grad_attended_low, preferred_element_type=jnp.float32
    ).reshape(rows_here, SEQ_DEV, V)
    grad_scores_low = (
        attention_weights
        * (grad_probs - jnp.sum(grad_probs * attention_weights, axis=-1, keepdims=True))
    ).astype(jnp.bfloat16)
    grad_query = (
        jnp.einsum("bnqk,bnkz->bnqz", grad_scores_low, key_low, preferred_element_type=jnp.float32)
        * score_scale
    ).reshape(rows_here, SEQ_DEV, Z)
    grad_key = (
        jnp.einsum(
            "bnqk,bnqz->bnkz", grad_scores_low, query_low, preferred_element_type=jnp.float32
        )
        * score_scale
    ).reshape(rows_here, SEQ_DEV, Z)
    grad_affine = jnp.stack(
        [
            jnp.sum(grad_query * shared, axis=(0, 1)),
            jnp.sum(grad_query, axis=(0, 1)),
            jnp.sum(grad_key * shared, axis=(0, 1)),
        ]
    )
    grad_shared = grad_query * affine[0] + grad_key * affine[2]
    grad_mixed_low = jnp.concatenate(
        [
            grad_update * update * (1.0 - update),
            grad_shared * silu_slope(shared_pre),
            grad_reset * silu_slope(reset_pre),
            grad_cand_pre,
        ],
        axis=-1,
    ).astype(jnp.bfloat16)
    grad_mx = jnp.einsum(
        "bsd,bsk->dk", shifted_low, grad_mixed_low, preferred_element_type=jnp.float32
    )
    grad_shifted = jnp.einsum(
        "bsk,dk->bsd", grad_mixed_low, mixer_backward, preferred_element_type=jnp.float32
    )
    grad_blend = grad_shifted * silu_slope(blend)
    grad_omega = jnp.sum(grad_blend * normed, axis=(0, 1))
    grad_value_low = (grad_values * silu_slope(value_pre)).astype(jnp.bfloat16)
    grad_value_proj = jnp.einsum(
        "bsd,bsv->dv", normed_low, grad_value_low, preferred_element_type=jnp.float32
    )
    grad_normed = grad_blend * omega_gain + jnp.einsum(
        "bsv,dv->bsd", grad_value_low, value_back, preferred_element_type=jnp.float32
    )
    g3 = grad_blend.reshape(64, 8, D)
    adj, direct, g1, h1 = emab1(g3, u3, states, rate, 2)
    later = scan_call(direct, rate, -1, 3)
    h1, du3 = emab2(g3, u3, states, adj, later, rate, coef, h1, 2)
    grad_normed = grad_normed + du3.reshape(normed.shape)
    grad_gain_first = jnp.sum(grad_normed * unit1, axis=(0, 1))
    scaled1 = grad_normed * gain_first
    grad_tokens = grad_middle * (1.0 - update) + inverse1 * (
        scaled1 - unit1 * jnp.mean(scaled1 * unit1, axis=-1, keepdims=True)
    )
    pa = jnp.pad(jnp.concatenate([grad_mx, grad_value_proj, grad_up], axis=1).astype(bf16), ((0, 0), (0, 128)))
    pb = jnp.concatenate([grad_out_proj, grad_down], axis=1).astype(bf16)
    oa, ob = scatter_call(pa, pb)
    tiny = jnp.concatenate([g1.T, h1.T, jnp.stack([grad_gain_first, grad_gain_second, grad_omega], axis=1)], axis=1)
    tiny = lax.psum_scatter(jnp.pad(tiny, ((0, 0), (0, 93))), ("dp", "seq"), scatter_dimension=0, tiled=True)
    g1, h1 = tiny[:, :16], tiny[:, 16:32]
    grad_ema_out = in_own * scale_own * g1
    grad_ema_in = out_own * scale_own * g1
    grad_ema_rate = out_own * in_own * (jnp.exp(-2.0 * rate_own) / scale_own * g1 - scale_own * h1)
    squares = jnp.stack([
        jnp.sum(valid_rows * output * output),
        jnp.sum(valid_rows * attn_branch * attn_branch),
        jnp.sum(valid_rows * ffn_branch * ffn_branch),
        jnp.sum(valid_rows),
    ])
    affine_total, square_total = lax.psum((grad_affine, squares), ("dp", "seq"))
    rms_values = jnp.sqrt(square_total[:3] / (square_total[3] * D))
    return (output.astype(bf16), grad_tokens, oa[:, :3200], oa[:, 3200:4736], ob[:, :768], oa[:, 4736:6272], ob[:, 768:],
        grad_ema_rate, grad_ema_in, grad_ema_out, tiny[:, 32:35], affine_total, rms_values)


def solution(mesh):
    placed = (
        P("dp", "seq", None),
        P("dp", "seq", None),
        P("dp"),
        P(("dp", "seq"), None),
        P(("dp", "seq"), None),
        P(("dp", "seq"), None),
        P(("dp", "seq"), None),
        P(("dp", "seq"), None),
        P(("dp", "seq"), None),
        P(("dp", "seq"), None),
        P(("dp", "seq"), None),
        P(("dp", "seq"), None),
        P(),
    )
    step = per_device_tuned if dict(mesh.shape) == {"dp": 4, "seq": 8} else per_device
    return jax.shard_map(
        step,
        mesh=mesh,
        in_specs=placed,
        out_specs=(
            P("dp", "seq", None),
            P("dp", "seq", None),
            P(("dp", "seq"), None),
            P(("dp", "seq"), None),
            P(("dp", "seq"), None),
            P(("dp", "seq"), None),
            P(("dp", "seq"), None),
            P(("dp", "seq"), None),
            P(("dp", "seq"), None),
            P(("dp", "seq"), None),
            P(("dp", "seq"), None),
            P(),
            P(),
        ),
        check_vma=False,
    )
```

```python
import functools

import jax
import jax.numpy as jnp
from jax import lax
from jax.experimental import pallas as pl
from jax.experimental.pallas import tpu as pltpu
from jax.sharding import PartitionSpec as P

MESH = pl.DeviceIdType.MESH
bf16, f32 = jnp.bfloat16, jnp.float32
D = 768
Z = 128
V = 1536
SPAN = 128
SEQ_DEV = 256


EPSILON = 1e-06
TOP_PRECISION = lax.Precision.HIGHEST


def prefix(value, axis, join, neutral):
    count, mine = (lax.axis_size(axis), lax.axis_index(axis))
    pieces = jax.tree.map(lambda part: lax.all_gather(part, axis), value)
    so_far = jax.tree.map(
        lambda part, zero: jnp.full_like(part, 0) + jnp.asarray(zero, part.dtype), value, neutral
    )

    def lap(position, so_far):
        longer = join(so_far, jax.tree.map(lambda part: part[position], pieces))
        return jax.tree.map(lambda new, old: jnp.where(position < mine, new, old), longer, so_far)

    return lax.fori_loop(0, count - 1, lap, so_far)


def prefix_2(value, axis, combine, identity):
    length, here = (lax.axis_size(axis), lax.axis_index(axis))
    everything = jax.tree.map(
        lambda part, kind: lax.all_gather(part.astype(kind), axis),
        value,
        jax.tree.map(lambda a: jnp.bfloat16 if a.dtype == jnp.float32 else a.dtype, value),
    )
    start = jax.tree.map(
        lambda part, zero: jnp.broadcast_to(jnp.asarray(zero, part.dtype), part.shape),
        value,
        identity,
    )

    def lap(k, before):
        at = length - 1 - k
        reached = at > here
        new = combine(
            before, jax.tree.map(lambda part, own: part[at].astype(own.dtype), everything, value)
        )
        return jax.tree.map(lambda a, b: jnp.where(reached, a, b), new, before)

    return lax.fori_loop(0, length, lap, start)


def silu_slope(values):
    sigmoid = jax.nn.sigmoid(values)
    return sigmoid * (1.0 + values * (1.0 - sigmoid))


def chain_combine(earlier, later):
    return (earlier[0] * later[0], later[0] * earlier[1] + later[1])


def ema_local(rate, beta, eta, input_signal):
    rows_here, length, channels = input_signal.shape
    block_len = min(64, length)
    blocks_count = length // block_len
    lag_values = jnp.arange(block_len, dtype=jnp.float32)
    powers = jnp.exp(-lag_values[:, None, None] * rate[None])
    scale_in = jnp.sqrt(-jnp.expm1(-2.0 * rate)) * beta
    kernel = jnp.sum(powers * (eta * scale_in)[None], axis=2)
    step_ids = jnp.arange(block_len)
    lag_index = jnp.clip(step_ids[:, None] - step_ids[None, :], 0, block_len - 1)
    toeplitz = jnp.where(
        (step_ids[:, None] >= step_ids[None, :])[:, :, None], kernel[lag_index], 0.0
    )
    leading = jnp.exp(-(lag_values[:, None, None] + 1.0) * rate[None]) * eta[None]
    trailing = powers[::-1] * scale_in[None]
    block_decay = jnp.exp(-block_len * rate)
    blocks = jnp.swapaxes(input_signal.reshape(rows_here, blocks_count, block_len, channels), 0, 1)

    def advance(carried, segment):
        smooth = jnp.einsum("tsd,bsd->btd", toeplitz, segment, precision=TOP_PRECISION)
        smooth = smooth + jnp.einsum("tdh,bdh->btd", leading, carried, precision=TOP_PRECISION)
        carried = block_decay * carried + jnp.einsum(
            "sdh,bsd->bdh", trailing, segment, precision=TOP_PRECISION
        )
        return (carried, smooth)

    initial = jnp.zeros((rows_here, channels, rate.shape[1]), jnp.float32)
    final_state, smooth = lax.scan(advance, initial, blocks)
    return (jnp.swapaxes(smooth, 0, 1).reshape(rows_here, length, channels), final_state)


def ema_carry(rate, eta, incoming):
    block_len = min(64, SEQ_DEV)
    blocks_count = SEQ_DEV // block_len
    lag_values = jnp.arange(block_len, dtype=jnp.float32)
    leading = jnp.exp(-(lag_values[:, None, None] + 1.0) * rate[None]) * eta[None]
    block_decay = jnp.exp(-block_len * rate)

    def advance(carried, unused):
        return (
            block_decay * carried,
            jnp.einsum("tdh,bdh->btd", leading, carried, precision=TOP_PRECISION),
        )

    _, smooth = lax.scan(advance, incoming, None, length=blocks_count)
    return jnp.swapaxes(smooth, 0, 1).reshape(incoming.shape[0], SEQ_DEV, incoming.shape[1])


def per_device(
    tokens,
    cotangent,
    lengths,
    w_mx,
    w_value,
    w_out,
    w_up,
    w_down,
    ema_rate,
    ema_in,
    ema_out,
    gains,
    qk_affine,
):
    gathered = (
        lax.all_gather(w_mx, ("dp", "seq"), axis=0, tiled=True),
        lax.all_gather(w_value, ("dp", "seq"), axis=0, tiled=True),
        lax.all_gather(w_out, ("dp", "seq"), axis=0, tiled=True),
        lax.all_gather(w_up, ("dp", "seq"), axis=0, tiled=True),
        lax.all_gather(w_down, ("dp", "seq"), axis=0, tiled=True),
        lax.all_gather(ema_rate, ("dp", "seq"), axis=0, tiled=True),
        lax.all_gather(ema_in, ("dp", "seq"), axis=0, tiled=True),
        lax.all_gather(ema_out, ("dp", "seq"), axis=0, tiled=True),
        lax.all_gather(gains, ("dp", "seq"), axis=0, tiled=True),
    )
    mx_full, value_full, out_full, up_full, down_full, rate_low, beta_low, eta_low, gain_low = (
        gathered
    )
    rate = rate_low.astype(jnp.float32)
    beta = beta_low.astype(jnp.float32)
    eta = eta_low.astype(jnp.float32)
    gain_all = gain_low.astype(jnp.float32)
    gain_first = gain_all[:, 0]
    gain_second = gain_all[:, 1]
    omega_gain = gain_all[:, 2]
    affine = qk_affine.astype(jnp.float32)
    rows_here = tokens.shape[0]
    spans_dev = SEQ_DEV // SPAN
    score_scale = Z ** (-0.5)
    inputs = tokens.astype(jnp.float32)
    seq_pos = lax.axis_index("seq") * SEQ_DEV + jnp.arange(SEQ_DEV, dtype=jnp.int32)
    valid_rows = (seq_pos[None, :] < lengths[:, None]).astype(jnp.float32)[:, :, None]
    inverse1 = lax.rsqrt(jnp.mean(inputs * inputs, axis=-1, keepdims=True) + EPSILON)
    unit1 = inputs * inverse1
    normed = unit1 * gain_first
    normed_low = normed.astype(jnp.bfloat16)
    value_pre = jnp.einsum(
        "bsd,dv->bsv", normed_low, value_full, preferred_element_type=jnp.float32
    )
    value_low = jax.nn.silu(value_pre).astype(jnp.bfloat16)
    (smooth_local, end_local), pull_local = jax.vjp(ema_local, rate, beta, eta, normed)
    growth = jnp.exp(-SEQ_DEV * rate)
    start_state = prefix(
        (growth, end_local),
        "seq",
        chain_combine,
        (jnp.ones_like(growth), jnp.zeros_like(end_local)),
    )[1]
    smooth_carry, pull_carry = jax.vjp(ema_carry, rate, eta, start_state)
    blend = smooth_local + smooth_carry + omega_gain * normed
    shifted_low = jax.nn.silu(blend).astype(jnp.bfloat16)
    mixed = jnp.einsum("bsd,dk->bsk", shifted_low, mx_full, preferred_element_type=jnp.float32)
    update = jax.nn.sigmoid(mixed[..., :D])
    shared_pre = mixed[..., D : D + Z]
    shared = jax.nn.silu(shared_pre)
    reset_pre = mixed[..., D + Z : D + Z + V]
    reset = jax.nn.silu(reset_pre)
    direct = mixed[..., D + Z + V :]
    query_low = (
        (shared * affine[0] + affine[1]).astype(jnp.bfloat16).reshape(rows_here, spans_dev, SPAN, Z)
    )
    key_low = (shared * affine[2]).astype(jnp.bfloat16).reshape(rows_here, spans_dev, SPAN, Z)
    value_tiles = value_low.reshape(rows_here, spans_dev, SPAN, V)
    scores = (
        jnp.einsum("bnqz,bnkz->bnqk", query_low, key_low, preferred_element_type=jnp.float32)
        * score_scale
    )
    causal = jnp.arange(SPAN)[:, None] >= jnp.arange(SPAN)[None, :]
    masked = jnp.where(causal, scores, -1e30)
    peak = jnp.max(masked, axis=-1, keepdims=True)
    expo = jnp.exp(masked - peak)
    attention_weights = expo / jnp.sum(expo, axis=-1, keepdims=True)
    probs_low = attention_weights.astype(jnp.bfloat16)
    attended_output = jnp.einsum(
        "bnqk,bnkv->bnqv", probs_low, value_tiles, preferred_element_type=jnp.float32
    ).reshape(rows_here, SEQ_DEV, V)
    gated_low = (reset * attended_output).astype(jnp.bfloat16)
    cand_pre = direct + jnp.einsum(
        "bsv,vd->bsd", gated_low, out_full, preferred_element_type=jnp.float32
    )
    candidate = jax.nn.silu(cand_pre)
    attn_branch = update * (candidate - inputs)
    middle = inputs + attn_branch
    inverse2 = lax.rsqrt(jnp.mean(middle * middle, axis=-1, keepdims=True) + EPSILON)
    unit2 = middle * inverse2
    normed2_low = (unit2 * gain_second).astype(jnp.bfloat16)
    up_pre = jnp.einsum("bsd,df->bsf", normed2_low, up_full, preferred_element_type=jnp.float32)
    hidden_low = jax.nn.silu(up_pre).astype(jnp.bfloat16)
    ffn_branch = jnp.einsum(
        "bsf,fd->bsd", hidden_low, down_full, preferred_element_type=jnp.float32
    )
    output = middle + ffn_branch
    again = (
        lax.all_gather(w_mx, ("dp", "seq"), axis=0, tiled=True),
        lax.all_gather(w_value, ("dp", "seq"), axis=0, tiled=True),
        lax.all_gather(w_out, ("dp", "seq"), axis=0, tiled=True),
        lax.all_gather(w_up, ("dp", "seq"), axis=0, tiled=True),
        lax.all_gather(w_down, ("dp", "seq"), axis=0, tiled=True),
    )
    mixer_backward, value_back, out_back, up_back, down_back = again
    grad_out = cotangent.astype(jnp.float32) * valid_rows
    grad_out_low = grad_out.astype(jnp.bfloat16)
    grad_down = jnp.einsum(
        "bsf,bsd->fd", hidden_low, grad_out_low, preferred_element_type=jnp.float32
    )
    grad_hidden = jnp.einsum(
        "bsd,fd->bsf", grad_out_low, down_back, preferred_element_type=jnp.float32
    )
    grad_up_low = (grad_hidden * silu_slope(up_pre)).astype(jnp.bfloat16)
    grad_up = jnp.einsum(
        "bsd,bsf->df", normed2_low, grad_up_low, preferred_element_type=jnp.float32
    )
    grad_normed2 = jnp.einsum(
        "bsf,df->bsd", grad_up_low, up_back, preferred_element_type=jnp.float32
    )
    grad_gain_second = jnp.sum(grad_normed2 * unit2, axis=(0, 1))
    scaled2 = grad_normed2 * gain_second
    grad_middle = grad_out + inverse2 * (
        scaled2 - unit2 * jnp.mean(scaled2 * unit2, axis=-1, keepdims=True)
    )
    grad_update = grad_middle * (candidate - inputs)
    grad_cand_pre = grad_middle * update * silu_slope(cand_pre)
    grad_cand_low = grad_cand_pre.astype(jnp.bfloat16)
    grad_out_proj = jnp.einsum(
        "bsv,bsd->vd", gated_low, grad_cand_low, preferred_element_type=jnp.float32
    )
    grad_gated = jnp.einsum(
        "bsd,vd->bsv", grad_cand_low, out_back, preferred_element_type=jnp.float32
    )
    grad_reset = grad_gated * attended_output
    grad_attended_low = (
        (grad_gated * reset).astype(jnp.bfloat16).reshape(rows_here, spans_dev, SPAN, V)
    )
    grad_probs = jnp.einsum(
        "bnqv,bnkv->bnqk", grad_attended_low, value_tiles, preferred_element_type=jnp.float32
    )
    grad_values = jnp.einsum(
        "bnqk,bnqv->bnkv", probs_low, grad_attended_low, preferred_element_type=jnp.float32
    ).reshape(rows_here, SEQ_DEV, V)
    grad_scores_low = (
        attention_weights
        * (grad_probs - jnp.sum(grad_probs * attention_weights, axis=-1, keepdims=True))
    ).astype(jnp.bfloat16)
    grad_query = (
        jnp.einsum("bnqk,bnkz->bnqz", grad_scores_low, key_low, preferred_element_type=jnp.float32)
        * score_scale
    ).reshape(rows_here, SEQ_DEV, Z)
    grad_key = (
        jnp.einsum(
            "bnqk,bnqz->bnkz", grad_scores_low, query_low, preferred_element_type=jnp.float32
        )
        * score_scale
    ).reshape(rows_here, SEQ_DEV, Z)
    grad_affine = jnp.stack(
        [
            jnp.sum(grad_query * shared, axis=(0, 1)),
            jnp.sum(grad_query, axis=(0, 1)),
            jnp.sum(grad_key * shared, axis=(0, 1)),
        ]
    )
    grad_shared = grad_query * affine[0] + grad_key * affine[2]
    grad_mixed_low = jnp.concatenate(
        [
            grad_update * update * (1.0 - update),
            grad_shared * silu_slope(shared_pre),
            grad_reset * silu_slope(reset_pre),
            grad_cand_pre,
        ],
        axis=-1,
    ).astype(jnp.bfloat16)
    grad_mx = jnp.einsum(
        "bsd,bsk->dk", shifted_low, grad_mixed_low, preferred_element_type=jnp.float32
    )
    grad_shifted = jnp.einsum(
        "bsk,dk->bsd", grad_mixed_low, mixer_backward, preferred_element_type=jnp.float32
    )
    grad_blend = grad_shifted * silu_slope(blend)
    grad_omega = jnp.sum(grad_blend * normed, axis=(0, 1))
    grad_value_low = (grad_values * silu_slope(value_pre)).astype(jnp.bfloat16)
    grad_value_proj = jnp.einsum(
        "bsd,bsv->dv", normed_low, grad_value_low, preferred_element_type=jnp.float32
    )
    grad_normed = grad_blend * omega_gain + jnp.einsum(
        "bsv,dv->bsd", grad_value_low, value_back, preferred_element_type=jnp.float32
    )
    rate_from_carry, eta_from_carry, direct_adjoint = pull_carry(grad_blend)
    later_adjoint = prefix_2(
        (growth, direct_adjoint),
        "seq",
        chain_combine,
        (jnp.ones_like(growth), jnp.zeros_like(direct_adjoint)),
    )[1]
    rate_from_local, grad_beta, eta_from_local, normed_from_ema = pull_local(
        (grad_blend, later_adjoint)
    )
    rate_from_growth = jnp.sum(later_adjoint * start_state, axis=0) * (-SEQ_DEV * growth)
    grad_rate = rate_from_carry + rate_from_local + rate_from_growth
    grad_eta = eta_from_carry + eta_from_local
    grad_normed = grad_normed + normed_from_ema
    grad_gain_first = jnp.sum(grad_normed * unit1, axis=(0, 1))
    scaled1 = grad_normed * gain_first
    grad_tokens = grad_middle * (1.0 - update) + inverse1 * (
        scaled1 - unit1 * jnp.mean(scaled1 * unit1, axis=-1, keepdims=True)
    )
    grad_gains = jnp.stack([grad_gain_first, grad_gain_second, grad_omega], axis=1)
    shards = (
        lax.psum_scatter(grad_mx, ("dp", "seq"), scatter_dimension=0, tiled=True),
        lax.psum_scatter(grad_value_proj, ("dp", "seq"), scatter_dimension=0, tiled=True),
        lax.psum_scatter(grad_out_proj, ("dp", "seq"), scatter_dimension=0, tiled=True),
        lax.psum_scatter(grad_up, ("dp", "seq"), scatter_dimension=0, tiled=True),
        lax.psum_scatter(grad_down, ("dp", "seq"), scatter_dimension=0, tiled=True),
        lax.psum_scatter(grad_rate, ("dp", "seq"), scatter_dimension=0, tiled=True),
        lax.psum_scatter(grad_beta, ("dp", "seq"), scatter_dimension=0, tiled=True),
        lax.psum_scatter(grad_eta, ("dp", "seq"), scatter_dimension=0, tiled=True),
        lax.psum_scatter(grad_gains, ("dp", "seq"), scatter_dimension=0, tiled=True),
    )
    squares = jnp.stack(
        [
            jnp.sum(valid_rows * output * output),
            jnp.sum(valid_rows * attn_branch * attn_branch),
            jnp.sum(valid_rows * ffn_branch * ffn_branch),
            jnp.sum(valid_rows),
        ]
    )
    affine_total, square_total = lax.psum((grad_affine, squares), ("dp", "seq"))
    rms_values = jnp.sqrt(square_total[:3] / (square_total[3] * D))
    return (
        output.astype(jnp.bfloat16),
        grad_tokens,
        shards[0],
        shards[1],
        shards[2],
        shards[3],
        shards[4],
        shards[5],
        shards[6],
        shards[7],
        shards[8],
        affine_total,
        rms_values,
    )


HA, HB = 3200, 768
RA, RB = 48, 96

CHUNKS = [(0, 0, 640, "xy"), (0, 640, 640, "yx"), (0, 1280, 640, "xy"), (0, 1920, 640, "yx"), (0, 2560, 640, "xy"), (1, 0, 384, "yx"), (1, 384, 384, "xy")]

class Pos:
    def __init__(s):
        s.dp, s.sq = lax.axis_index("dp"), lax.axis_index("seq")
        s.x, s.c, s.z, s.y = s.dp // 2, s.dp % 2, s.sq // 2, s.sq % 2
        s.sib = (s.dp + 1 - 2 * s.c, s.sq)
        s.xn = (s.dp + 2 - 4 * s.x, s.sq)
        s.yn = (s.dp, s.sq + 1 - 2 * s.y)
        s.up = (s.dp, jnp.minimum(s.sq + 2, s.sq + 2 * (3 - s.z)))
        s.dn = (s.dp, jnp.maximum(s.sq - 2, s.y))
        s.dpx = s.dp + 2 - 4 * s.x

def rcopy(src, dst, ss, rs, dev):
    return pltpu.make_async_remote_copy(src_ref=src, dst_ref=dst, send_sem=ss, recv_sem=rs, device_id=dev, device_id_type=MESH)

def barrier(pos):
    bar = pltpu.get_barrier_semaphore()
    sig = lambda d: pl.semaphore_signal(bar, inc=1, device_id=d, device_id_type=MESH)
    sig(pos.sib); sig(pos.xn); sig(pos.yn)
    @pl.when(pos.z < 3)
    def _(): sig(pos.up)
    @pl.when(pos.z > 0)
    def _(): sig(pos.dn)
    pl.semaphore_wait(bar, 3 + jnp.minimum(pos.z, 1) + jnp.minimum(3 - pos.z, 1))

def at(ref, rows, nrows, half, w, off, width):
    r = pl.ds(pl.multiple_of(rows, 48), nrows)
    c = pl.ds(pl.multiple_of(half * w + off, 128), width)
    return ref.at[r, c]

class Gather:
    def __init__(s, pos, bufs, ss, rs):
        s.p, s.bufs, s.ss, s.rs = pos, bufs, ss, rs
    def geom(s, i):
        b, off, width, order = CHUNKS[i]
        return s.bufs[b], (RA, RB)[b], (HA, HB)[b], off, width, order
    def unit(s, i, dp, z, half, n=1):
        ref, R, W, off, width, _ = s.geom(i)
        return at(ref, (dp * 4 + z) * R, n * R, half, W, off, width)
    def cp(s, i, k, ref, dev):
        return rcopy(ref, ref, s.ss.at[i, k], s.rs.at[i, k], dev)
    def z0(s, i):
        p = s.p
        u = s.unit(i, p.dp, p.z, p.y)
        @pl.when(p.z < 3)
        def _(): rcopy(u, u, s.ss.at[i, 0], s.rs.at[i, p.z], p.up).start()
        @pl.when(p.z > 0)
        def _(): rcopy(u, u, s.ss.at[i, 1], s.rs.at[i, p.z], p.dn).start()
    def zrecv(s, i, zz):
        u = s.unit(i, s.p.dp, zz, s.p.y)
        rcopy(u, u, s.ss.at[i, 0], s.rs.at[i, zz], s.p.up).wait_recv()
        return u
    def zhop(s, i, h):
        p = s.p
        @pl.when(p.z >= h)
        def _():
            u = s.zrecv(i, p.z - h)
            @pl.when(p.z < 3)
            def _(): rcopy(u, u, s.ss.at[i, 1 + h], s.rs.at[i, p.z - h], p.up).start()
        @pl.when(p.z + h <= 3)
        def _():
            u = s.zrecv(i, p.z + h)
            @pl.when(p.z > 0)
            def _(): rcopy(u, u, s.ss.at[i, 10 + h], s.rs.at[i, p.z + h], p.dn).start()
    def s1(s, i):
        p = s.p; order = CHUNKS[i][3]
        u = s.unit(i, p.dp, 0, p.y, 4)
        s.cp(i, 4, u, p.xn if order == "xy" else p.yn).start()
        s.cp(i, 7, u, p.sib).start()
    def s1_in(s, i):
        p = s.p; order = CHUNKS[i][3]
        return s.unit(i, p.dpx, 0, p.y, 4) if order == "xy" else s.unit(i, p.dp, 0, 1 - p.y, 4)
    def s2(s, i):
        p = s.p; order = CHUNKS[i][3]
        r = s.s1_in(i)
        s.cp(i, 4, r, p.xn).wait_recv()
        nxt = p.yn if order == "xy" else p.xn
        u = s.unit(i, p.dp, 0, p.y, 4)
        s.cp(i, 5, u, nxt).start()
        s.cp(i, 6, r, nxt).start()
        s.cp(i, 8, r, p.sib).start()
    def s2_in(s, i):
        p = s.p; order = CHUNKS[i][3]
        if order == "xy":
            return s.unit(i, p.dp, 0, 1 - p.y, 4), s.unit(i, p.dpx, 0, 1 - p.y, 4)
        return s.unit(i, p.dpx, 0, p.y, 4), s.unit(i, p.dpx, 0, 1 - p.y, 4)
    def s3(s, i):
        p = s.p
        for k, r in enumerate(s.s2_in(i)):
            s.cp(i, 5 + k, r, p.sib).wait_recv()
            s.cp(i, 9 + k, r, p.sib).start()
    def s4(s, i):
        p = s.p
        u = s.unit(i, p.dp, 0, p.y, 4)
        for k in (7, 8, 9, 10):
            s.cp(i, k, u, p.sib).wait_recv()
    def drain(s, i):
        p = s.p
        u1 = s.unit(i, p.dp, 0, p.y)
        u = s.unit(i, p.dp, 0, p.y, 4)
        for k in (4, 5, 6, 7, 8, 9, 10):
            s.cp(i, k, u, p.sib).wait_send()
        w = lambda k: rcopy(u1, u1, s.ss.at[i, k], s.rs.at[i, 0], p.sib).wait_send()
        @pl.when(p.z < 3)
        def _(): w(0)
        @pl.when(p.z > 0)
        def _(): w(1)
        for h in (1, 2):
            @pl.when((p.z >= h) & (p.z < 3))
            def _(): w(1 + h)
            @pl.when((p.z + h <= 3) & (p.z > 0))
            def _(): w(10 + h)

def first_exchange(pos, wa_ref, wb_ref, WA, WB, land, ss, rs):
    p = pos
    ca = rcopy(wa_ref.at[:, pl.ds(pl.multiple_of((1 - p.y) * HA, 128), HA)], land, ss.at[0], rs.at[0], p.yn)
    ca.start()
    mine = (p.dp * 4 + p.z) * RB + p.y * 48
    other = (p.dp * 4 + p.z) * RB + (1 - p.y) * 48
    cb = rcopy(wb_ref.at[:, pl.ds(pl.multiple_of((1 - p.y) * HB, 128), HB)], at(WB, mine, 48, 1 - p.y, HB, 0, HB), ss.at[1], rs.at[1], p.yn)
    cb.start()
    at_own = at(WB, mine, 48, p.y, HB, 0, HB)
    loc = pltpu.make_async_copy(wb_ref.at[:, pl.ds(pl.multiple_of(p.y * HB, 128), HB)], at_own, ss.at[2])
    loc.start()
    ca.wait()
    own = wa_ref[:, pl.ds(pl.multiple_of(p.y * HA, 128), HA)].astype(jnp.float32)
    got = land[...].astype(jnp.float32)
    f = (p.y == 0)
    lo = jnp.where(f, own, got); hi = jnp.where(f, got, own)
    WA[pl.ds(pl.multiple_of((p.dp * 4 + p.z) * RA, 16), RA), pl.ds(pl.multiple_of(p.y * HA, 128), HA)] = jnp.concatenate([lo, hi], axis=0).astype(jnp.bfloat16)
    cb.wait(); loc.wait()

def ag_kernel(wa_ref, wb_ref, oa_ref, ob_ref, WA, WB, land, s0, r0, ss, rs, osem):
    pos = Pos()
    barrier(pos)
    first_exchange(pos, wa_ref, wb_ref, WA, WB, land, s0, r0)
    g = Gather(pos, (WA, WB), ss, rs)
    n = len(CHUNKS)
    for i in range(n): g.z0(i)
    for t in range(n + 3):
        if 0 <= t - 3 < n: g.s3(t - 3)
        if 0 <= t - 2 < n: g.s2(t - 2)
        if t < n:
            g.zhop(t, 1)
            g.zhop(t, 2)
            g.zhop(t, 3)
            g.s1(t)
    for i in range(n): g.s4(i)
    for i in range(n): g.drain(i)
    a = pltpu.make_async_copy(WA, oa_ref, osem.at[0]); b = pltpu.make_async_copy(WB, ob_ref, osem.at[1])
    a.start(); b.start(); a.wait(); b.wait()

def gather_call(wa, wb):
    n = len(CHUNKS)
    return pl.pallas_call(
        ag_kernel,
        out_shape=(jax.ShapeDtypeStruct((768, 2 * HA), jnp.bfloat16), jax.ShapeDtypeStruct((1536, 2 * HB), jnp.bfloat16)),
        in_specs=[pl.BlockSpec(memory_space=pltpu.VMEM)] * 2,
        out_specs=[pl.BlockSpec(memory_space=pl.ANY)] * 2,
        scratch_shapes=[pltpu.VMEM((768, 2 * HA), jnp.bfloat16), pltpu.VMEM((1536, 2 * HB), jnp.bfloat16), pltpu.VMEM((24, HA), jnp.bfloat16),
            pltpu.SemaphoreType.DMA((3,)), pltpu.SemaphoreType.DMA((3,)), pltpu.SemaphoreType.DMA((n, 13)), pltpu.SemaphoreType.DMA((n, 13)), pltpu.SemaphoreType.DMA((2,))],
        compiler_params=pltpu.CompilerParams(collective_id=0, has_side_effects=True, vmem_limit_bytes=60 * 2**20),
    )(wa, wb)


class Scatter:
    NS = 14
    def __init__(s, pos, P, L1, L2, L3, L4, F, G, out, ss, rs):
        s.p, s.P, s.L1, s.L2, s.L3, s.L4, s.F, s.G, s.out, s.ss, s.rs = pos, P, L1, L2, L3, L4, F, G, out, ss, rs
    def geom(s, i):
        b, off, w, order = CHUNKS[i]
        return b, (RA, RB)[b], (HA, HB)[b], off, w, order
    def rows(s, i, xx, c, z=0):
        R = (RA, RB)[CHUNKS[i][0]]
        return pl.multiple_of(((xx * 2 + c) * 4 + z) * R, 48)
    def cols(s, i, yy):
        b, R, W, off, w, _ = s.geom(i)
        return pl.ds(pl.multiple_of(yy * W + off, 128), w)
    def piece(s, i, xx, c, yy, z=0, n=4):
        b, R, W, off, w, _ = s.geom(i)
        return s.P[b].at[pl.ds(s.rows(i, xx, c, z), n * R), s.cols(i, yy)]
    def cp(s, i, k, src, dst, dev):
        return rcopy(src, dst, s.ss.at[i, k], s.rs.at[i, k], dev)
    def add(s, dst, src, nrows):
        def body(r, _):
            rr = pl.ds(pl.multiple_of(r * 48, 48), 48)
            dst[rr, :] = (dst[rr, :].astype(f32) + src[rr, :].astype(f32)).astype(bf16)
            return 0
        lax.fori_loop(0, nrows // 48, body, 0)
    def l1(s, i, xx, yy):
        b, R, W, off, w, _ = s.geom(i)
        return s.L1[b].at[xx, :, s.cols(i, yy)]
    def st0(s, i):
        p = s.p
        for k, (xx, yy) in enumerate(((0, 0), (0, 1), (1, 0), (1, 1))):
            s.cp(i, k, s.piece(i, xx, 1 - p.c, yy), s.l1(i, xx, yy), p.sib).start()
    def a0(s, i):
        b, R, W, off, w, _ = s.geom(i)
        for k, (xx, yy) in enumerate(((0, 0), (0, 1), (1, 0), (1, 1))):
            l = s.l1(i, xx, yy)
            s.cp(i, k, l, l, s.p.sib).wait_recv()
            s.add(s.piece(i, xx, s.p.c, yy), l, 4 * R)
    def l2(s, i, k):
        b, R, W, off, w, _ = s.geom(i)
        return s.L2[b].at[k, :, pl.ds(off, w)]
    def l3(s, i):
        b, R, W, off, w, _ = s.geom(i)
        return s.L3[b].at[:, pl.ds(off, w)]
    def st1(s, i):
        p, order = s.p, s.geom(i)[5]
        for k in (0, 1):
            src = s.piece(i, k, p.c, 1 - p.y) if order == "xy" else s.piece(i, 1 - p.x, p.c, k)
            s.cp(i, 4 + k, src, s.l2(i, k), p.yn if order == "xy" else p.xn).start()
    def a1(s, i):
        p = s.p; b, R, W, off, w, order = s.geom(i)
        for k in (0, 1):
            l = s.l2(i, k)
            s.cp(i, 4 + k, l, l, p.xn).wait_recv()
            s.add(s.piece(i, k, p.c, p.y) if order == "xy" else s.piece(i, p.x, p.c, k), l, 4 * R)
    def st2(s, i):
        p, order = s.p, s.geom(i)[5]
        src = s.piece(i, 1 - p.x, p.c, p.y) if order == "xy" else s.piece(i, p.x, p.c, 1 - p.y)
        s.cp(i, 6, src, s.l3(i), p.xn if order == "xy" else p.yn).start()
    def a2(s, i):
        p = s.p; b, R, W, off, w, order = s.geom(i)
        l = s.l3(i)
        s.cp(i, 6, l, l, p.xn).wait_recv()
        s.add(s.piece(i, p.x, p.c, p.y), l, 4 * R)
    def l4(s, i, d, t):
        b, R, W, off, w, _ = s.geom(i)
        return s.L4[b].at[d, t, :, pl.ds(off, w)]
    def own(s, i, t):
        p = s.p
        return s.piece(i, p.x, p.c, p.y, t, 1)
    def zsem(s, d, t):
        return 6 + t if d == 0 else 10 + t
    def zflow(s, i, d, z):
        p = s.p; R = s.geom(i)[1]
        first = z == (0, 3)[d]
        mine = () if first else (z,)
        on = tuple(range(3, z, -1)) if d == 0 else tuple(range(0, z))
        for t in on:
            l = s.l4(i, d, t)
            if not first:
                s.cp(i, s.zsem(d, t), l, l, p.sib).wait_recv()
                s.add(l, s.own(i, t), R)
            s.cp(i, s.zsem(d, t), s.own(i, t) if first else l, l, p.up if d == 0 else p.dn).start()
        for t in mine:
            l = s.l4(i, d, t)
            s.cp(i, s.zsem(d, t), l, l, p.sib).wait_recv()
    def zstep(s, i, h):
        p = s.p
        for z, d in ((h, 0), (3 - h, 1)):
            @pl.when(p.z == z)
            def _(): s.zflow(i, d, z)
    def fin(s, i):
        p = s.p; b, R, W, off, w, _ = s.geom(i)
        u = s.own(i, p.z)
        hu, hd = (p.z > 0), (p.z < 3)
        lu, ld = s.l4(i, 0, p.z), s.l4(i, 1, p.z)
        F, G, out = s.F[b], s.G[b], s.out[b]
        h = R // 2
        for z in range(4):
            @pl.when(p.z == z)
            def _():
                t = u[...].astype(f32)
                if z > 0: t = t + lu[...].astype(f32)
                if z < 3: t = t + ld[...].astype(f32)
                F[:, pl.ds(off, w)] = t
        src = F.at[pl.ds(pl.multiple_of((1 - p.y) * h, 8), h), pl.ds(off, w)]
        s.cp(i, 13, src, G.at[:, pl.ds(off, w)], p.yn).start()
        out[:, s.cols(i, p.y)] = F[pl.ds(pl.multiple_of(p.y * h, 8), h), pl.ds(off, w)]
    def last(s, i):
        p = s.p; b, R, W, off, w, _ = s.geom(i)
        l = s.G[b].at[:, pl.ds(off, w)]
        s.cp(i, 13, l, l, p.yn).wait_recv()
        s.out[b][:, s.cols(i, 1 - p.y)] = l[...]
    def drain(s, i):
        p = s.p; b, R, W, off, w, _ = s.geom(i)
        for k, ref in [(k, s.l1(i, 0, 0)) for k in range(4)] + [(4, s.l2(i, 0)), (5, s.l2(i, 1)), (6, s.l3(i)), (13, s.G[b].at[:, pl.ds(off, w)])]:
            s.cp(i, k, ref, ref, p.sib).wait_send()
        for d in (0, 1):
            for t in ((1, 2, 3), (0, 1, 2))[d]:
                l = s.l4(i, d, t)
                @pl.when((p.z < t) if d == 0 else (p.z > t))
                def _(): s.cp(i, s.zsem(d, t), l, l, p.sib).wait_send()

def rs_schedule(g, n, before=lambda i: None):
    for t in range(n + 9):
        if t < n: before(t); g.st0(t)
        if 0 <= t - 1 < n: g.a0(t - 1); g.st1(t - 1)
        if 0 <= t - 2 < n: g.a1(t - 2); g.st2(t - 2)
        if 0 <= t - 3 < n: g.a2(t - 3); g.zstep(t - 3, 0)
        for h in (1, 2, 3):
            if 0 <= t - 3 - h < n: g.zstep(t - 3 - h, h)
        if 0 <= t - 6 < n: g.fin(t - 6)
        if 0 <= t - 7 < n: g.last(t - 7)
    for i in range(n): g.drain(i)

def rs_kernel(pa_ref, pb_ref, oa, ob, PA, PB, L1A, L1B, L2A, L2B, L3A, L3B, L4A, L4B, FA, FB, GA, GB, ss, rs, ls):
    pos = Pos(); barrier(pos)
    n = len(CHUNKS)
    a = pltpu.make_async_copy(pa_ref, PA, ls.at[0]); b = pltpu.make_async_copy(pb_ref, PB, ls.at[1])
    a.start(); b.start(); a.wait(); b.wait()
    g = Scatter(pos, (PA, PB), (L1A, L1B), (L2A, L2B), (L3A, L3B), (L4A, L4B), (FA, FB), (GA, GB), (oa, ob), ss, rs)
    rs_schedule(g, n)

def rs_scratch():
    n = len(CHUNKS)
    V = pltpu.VMEM
    return [V((768, 2 * HA), bf16), V((1536, 2 * HB), bf16), V((2, 192, 2 * HA), bf16), V((2, 384, 2 * HB), bf16),
        V((2, 192, HA), bf16), V((2, 384, HB), bf16), V((192, HA), bf16), V((384, HB), bf16),
        V((2, 4, 48, HA), bf16), V((2, 4, 96, HB), bf16), V((48, HA), f32), V((96, HB), f32), V((24, HA), f32), V((48, HB), f32),
        pltpu.SemaphoreType.DMA((n, Scatter.NS)), pltpu.SemaphoreType.DMA((n, Scatter.NS)), pltpu.SemaphoreType.DMA((2,))]

def scatter_call(pa, pb):
    return pl.pallas_call(rs_kernel,
        out_shape=(jax.ShapeDtypeStruct((24, 2 * HA), f32), jax.ShapeDtypeStruct((48, 2 * HB), f32)),
        in_specs=[pl.BlockSpec(memory_space=pl.ANY)] * 2,
        out_specs=[pl.BlockSpec(memory_space=pltpu.VMEM)] * 2,
        scratch_shapes=rs_scratch(),
        compiler_params=pltpu.CompilerParams(collective_id=1, has_side_effects=True, vmem_limit_bytes=60 * 2**20))(pa, pb)

NK = 32
NB = 2

def lanes(j): return pl.ds(pl.multiple_of(j * 128, 128), 128)
def rows_(i): return pl.ds(pl.multiple_of(i * 8, 8), 8)
def tree(xs):
    xs = list(xs)
    while len(xs) > 1:
        xs = [xs[i] + xs[i + 1] if i + 1 < len(xs) else xs[i] for i in range(0, len(xs), 2)]
    return xs[0]

def fwd_states(U, rate, S, END, j, unroll=2):
    ln = lanes(j)
    r = rate[0:16, ln]
    w = [jnp.exp(r * (s - 7.0)) for s in range(8)]
    q8 = jnp.exp(r * -8.0)
    def body(k, st):
        new = []
        for b in range(NB):
            S[b * NK + k, :, ln] = st[b]
            parts = [w[s] * U[b * NK + k, pl.ds(s, 1), ln] for s in range(8)]
            new.append(q8 * st[b] + tree(parts))
        return tuple(new)
    st = lax.fori_loop(0, NK, body, tuple(jnp.zeros((16, 128), f32) for _ in range(NB)), unroll=unroll)
    for b in range(NB): END[b, :, ln] = st[b]

def conv_tables(rate, ec, j):
    ln = lanes(j)
    it = lax.broadcasted_iota(jnp.int32, (8, 128), 0).astype(f32)
    E, K = [], []
    for h in range(16):
        rb = jnp.broadcast_to(rate[pl.ds(h, 1), ln], (8, 128)); eb = jnp.broadcast_to(ec[pl.ds(h, 1), ln], (8, 128))
        K.append(jnp.exp(-it * rb) * eb)
        E.append(jnp.exp(-(it + 1.0) * rb) * eb)
    return E, tree(K)

def fwd_smooth(U, S, S0, rate, ec, omega, BL, KS, j, unroll=1):
    ln = lanes(j)
    r = rate[0:16, ln]
    q8 = jnp.exp(r * -8.0)
    E, K = conv_tables(rate, ec, j)
    KS[...] = K
    ii = lax.broadcasted_iota(jnp.int32, (8, 128), 0)
    KM = [jnp.where(ii >= l, jnp.broadcast_to(KS[pl.ds(l, 1), :], (8, 128)), 0.0) for l in range(8)]
    om = jnp.broadcast_to(omega[:, ln], (8, 128))
    KM[0] = KM[0] + om
    def body(k, gs):
        new = []
        for b in range(NB):
            i = b * NK + k
            S[i, :, ln] = S[i, :, ln] + gs[b]
            u = U[i, :, ln]
            parts = [KM[0] * u] + [KM[l] * pltpu.roll(u, l, 0) for l in range(1, 8)]
            parts += [E[h] * S[i, pl.ds(h, 1), ln] for h in range(16)]
            BL[i, :, ln] = tree(parts)
            new.append(q8 * gs[b])
        return tuple(new)
    lax.fori_loop(0, NK, body, tuple(S0[b, :, ln] for b in range(NB)), unroll=unroll)

def bwd_states(Gr, U, S, rate, A, DIR, G1, H, CS, j, unroll=1):
    ln = lanes(j)
    r = rate[0:16, ln]
    w = [jnp.exp(r * -float(s)) for s in range(8)]
    q8 = jnp.exp(r * -8.0)
    def body(kk, c):
        k = NK - 1 - kk
        st, g1, h1, C = c
        new, C = [], list(C)
        for b in range(NB):
            i = b * NK + k
            A[i, :, ln] = st[b]
            p = [w[s] * Gr[i, pl.ds(s, 1), ln] for s in range(8)]
            Bg = tree(p)
            B1 = tree([p[s] if s == 1 else p[s] * float(s) for s in range(1, 8)])
            Sk = S[i, :, ln]
            g1 = g1 + Sk * Bg
            h1 = h1 + Sk * B1
            new.append(q8 * st[b] + Bg)
            u, g = U[i, :, ln], Gr[i, :, ln]
            C = [C[l] + g * (pltpu.roll(u, l, 0) if l else u) for l in range(8)]
        return tuple(new), g1, h1, tuple(C)
    z = jnp.zeros((16, 128), f32)
    st, g1, h1, C = lax.fori_loop(0, NK, body, (tuple(z for _ in range(NB)), z, z, tuple(jnp.zeros((8, 128), f32) for _ in range(8))), unroll=unroll)
    for b in range(NB): DIR[b, :, ln] = st[b]
    ii = lax.broadcasted_iota(jnp.int32, (8, 128), 0)
    g1, h1 = g1 * w[1], h1 * w[1]
    for l in range(8):
        cl = jnp.sum(jnp.where(ii >= l, C[l], 0.0), axis=0, keepdims=True)
        t = w[l] * cl
        g1 = g1 + t
        if l: h1 = h1 + t * float(l)
    G1[:, ln] = g1
    H[:, ln] = h1

def bwd_grad(Gr, U, S, A, A0, rate, ec, H, DU, KS, AT, j, unroll=1):
    ln = lanes(j)
    r = rate[0:16, ln]
    q8 = jnp.exp(r * -8.0)
    c8 = 8.0 * jnp.exp(r * -9.0)
    wu = [jnp.exp(r * (s - 8.0)) * (8.0 - s) for s in range(8)]
    it = lax.broadcasted_iota(jnp.int32, (8, 128), 0).astype(f32)
    E, K = [], []
    for h in range(16):
        rb = jnp.broadcast_to(rate[pl.ds(h, 1), ln], (8, 128)); eb = jnp.broadcast_to(ec[pl.ds(h, 1), ln], (8, 128))
        K.append(jnp.exp(-it * rb) * eb)
        E.append(jnp.exp((it - 8.0) * rb) * eb)
    KS[...] = tree(K)
    ii = lax.broadcasted_iota(jnp.int32, (8, 128), 0)
    KM = [jnp.where(ii < 8 - l, jnp.broadcast_to(KS[pl.ds(l, 1), :], (8, 128)), 0.0) for l in range(8)]
    def body(kk, c):
        k = NK - 1 - kk
        gs, h1 = c
        new = []
        for b in range(NB):
            i = b * NK + k
            Ak = A[i, :, ln] + gs[b]
            AT[b] = Ak
            Bu = tree([wu[s] * U[i, pl.ds(s, 1), ln] for s in range(8)])
            h1 = h1 + Ak * (Bu + c8 * S[i, :, ln])
            g = Gr[i, :, ln]
            parts = [KM[0] * g] + [KM[l] * pltpu.roll(g, 8 - l, 0) for l in range(1, 8)]
            parts += [E[h] * AT[b, pl.ds(h, 1), :] for h in range(16)]
            DU[i, :, ln] = tree(parts)
            new.append(q8 * gs[b])
        return tuple(new), h1
    gs, h1 = lax.fori_loop(0, NK, body, (tuple(A0[b, :, ln] for b in range(NB)), H[:, ln]), unroll=unroll)
    H[:, ln] = h1

def six(f):
    def body(j, _):
        f(j); return 0
    lax.fori_loop(0, 6, body, 0)

vm = lambda s, t=f32: pltpu.VMEM(s, t)
SH = jax.ShapeDtypeStruct
CP = pltpu.CompilerParams(vmem_limit_bytes=56 * 2**20)

def ema1(U, rate, unroll=2):
    def k(U, rate, S, END): six(lambda j: fwd_states(U, rate, S, END, j, unroll))
    return pl.pallas_call(k, out_shape=(SH((64, 16, 768), f32), SH((2, 16, 768), f32)), compiler_params=CP)(U, rate)
def ema2(U, S, S0, rate, ec, omega, unroll=1):
    def k(U, Sin, S0, rate, ec, omega, S, BL, KS):
        S[...] = Sin[...]
        six(lambda j: fwd_smooth(U, S, S0, rate, ec, omega, BL, KS, j, unroll))
    return pl.pallas_call(k, out_shape=(SH((64, 16, 768), f32), SH((64, 8, 768), f32)), scratch_shapes=[vm((8, 128))], compiler_params=CP)(U, S, S0, rate, ec, omega)
def emab1(Gr, U, S, rate, unroll=1):
    def k(Gr, U, S, rate, A, DIR, G1, H, CS): six(lambda j: bwd_states(Gr, U, S, rate, A, DIR, G1, H, CS, j, unroll))
    return pl.pallas_call(k, out_shape=(SH((64, 16, 768), f32), SH((2, 16, 768), f32), SH((16, 768), f32), SH((16, 768), f32)), scratch_shapes=[vm((8, 128))], compiler_params=CP)(Gr, U, S, rate)
def emab2(Gr, U, S, A, A0, rate, ec, H, unroll=1):
    def k(Gr, U, S, A, A0, rate, ec, Hin, H, DU, KS, AT):
        H[...] = Hin[...]
        six(lambda j: bwd_grad(Gr, U, S, A, A0, rate, ec, H, DU, KS, AT, j, unroll))
    return pl.pallas_call(k, out_shape=(SH((16, 768), f32), SH((64, 8, 768), f32)), scratch_shapes=[vm((8, 128)), vm((2, 16, 128))], compiler_params=CP)(Gr, U, S, A, A0, rate, ec, H)

def scan_kernel(way, e_ref, rate_ref, z_ref, W, L, ss, rs):
    sq, dp = lax.axis_index("seq"), lax.axis_index("dp")
    bar = pltpu.get_barrier_semaphore()
    n = 8
    has = lambda d: (sq + d < n) if d > 0 else (sq + d >= 0)
    to = lambda d: (dp, jnp.clip(sq + d, 0, n - 1))
    for s in (1, 2, 4):
        for d in (s, -s):
            @pl.when(has(d))
            def _(): pl.semaphore_signal(bar, inc=1, device_id=to(d), device_id_type=MESH)
    pl.semaphore_wait(bar, sum(jnp.clip(sq - s + 1, 0, 1) + jnp.clip(n - s - sq, 0, 1) for s in (1, 2, 4)))
    W[0] = e_ref[...]
    z_ref[...] = jnp.zeros_like(z_ref)
    g = jnp.exp(rate_ref[...] * -256.0)
    g2 = g * g
    grow, keep = (g, g2, g2 * g2), (jnp.ones_like(g), g, g2 * g)
    for k, s in enumerate((1, 2, 4)):
        cp = rcopy(W.at[k], L.at[k], ss.at[k], rs.at[k], to(way * s))
        @pl.when(has(way * s))
        def _(): cp.start()
        if k < 2: W[k + 1] = W[k]
        @pl.when(has(-way * s))
        def _():
            cp.wait_recv()
            z_ref[...] = z_ref[...] + keep[k][None] * L[k]
            if k < 2: W[k + 1] = W[k + 1] + grow[k][None] * L[k]
    for k, s in enumerate((1, 2, 4)):
        @pl.when(has(way * s))
        def _(): rcopy(W.at[k], L.at[k], ss.at[k], rs.at[k], to(way * s)).wait_send()
def scan_call(e, rate, way, cid):
    return pl.pallas_call(functools.partial(scan_kernel, way),
        out_shape=jax.ShapeDtypeStruct(e.shape, f32),
        scratch_shapes=[pltpu.VMEM((3,) + e.shape, f32), pltpu.VMEM((3,) + e.shape, f32), pltpu.SemaphoreType.DMA((3,)), pltpu.SemaphoreType.DMA((3,))],
        compiler_params=pltpu.CompilerParams(collective_id=cid, has_side_effects=True, vmem_limit_bytes=40 * 2**20))(e, rate)

def sigmoid(v): return jax.nn.sigmoid(v)
def dot(a, b): return jnp.dot(a, b, preferred_element_type=f32)
def dot_nt(a, b): return lax.dot_general(a, b, (((1,), (1,)), ((), ())), preferred_element_type=f32)
def dot_tn(a, b): return lax.dot_general(a, b, (((0,), (0,)), ((), ())), preferred_element_type=f32)
def loop(n, f, unroll=1):
    def body(i, _):
        f(i); return 0
    lax.fori_loop(0, n, body, 0, unroll=unroll)
def ds(i, n): return pl.ds(pl.multiple_of(i * n, n), n)
def silu_and_slope(v):
    s = sigmoid(v)
    y = v * s
    return y, s + y * (1.0 - s)

class Params:
    def __init__(s, pos, ref, PRM, ss, rs):
        s.p, s.ref, s.PRM, s.ss, s.rs = pos, ref, PRM, ss, rs
    def r(s, row, n): return s.PRM.at[pl.ds(pl.multiple_of(row, 8), n), :]
    def cp(s, k, src, dst, dev, kr=None):
        return rcopy(src, dst, s.ss.at[k], s.rs.at[k if kr is None else kr], dev)
    def y0(s):
        p = s.p; row = (p.dp * 4 + p.z) * 48 + p.y * 24
        s.cp(0, s.ref, s.r(row, 24), p.yn).start()
        s.PRM[pl.ds(pl.multiple_of(row, 8), 24), :] = s.ref[...]
    def y1(s):
        p = s.p
        l = s.r((p.dp * 4 + p.z) * 48, 24)
        s.cp(0, l, l, p.yn).wait()
    def z0(s):
        p = s.p; u = s.r((p.dp * 4 + p.z) * 48, 48)
        @pl.when(p.z < 3)
        def _(): s.cp(1, u, u, p.up, 1 + p.z).start()
        @pl.when(p.z > 0)
        def _(): s.cp(2, u, u, p.dn, 1 + p.z).start()
    def zhop(s, h):
        p = s.p
        @pl.when(p.z >= h)
        def _():
            u = s.r((p.dp * 4 + p.z - h) * 48, 48)
            s.cp(1, u, u, p.up, 1 + p.z - h).wait_recv()
            @pl.when(p.z < 3)
            def _(): s.cp(2 + h, u, u, p.up, 1 + p.z - h).start()
        @pl.when(p.z + h <= 3)
        def _():
            u = s.r((p.dp * 4 + p.z + h) * 48, 48)
            s.cp(1, u, u, p.up, 1 + p.z + h).wait_recv()
            @pl.when(p.z > 0)
            def _(): s.cp(4 + h, u, u, p.dn, 1 + p.z + h).start()
    def x0(s):
        p = s.p; u = s.r(p.dp * 192, 192)
        s.cp(7, u, u, p.xn).start()
        s.cp(8, u, u, p.sib).start()
    def x1(s):
        p = s.p; u = s.r(p.dpx * 192, 192)
        s.cp(7, u, u, p.xn).wait_recv()
        s.cp(9, u, u, p.sib).start()
    def end(s):
        p = s.p; u = s.r(p.dp * 192, 192)
        s.cp(8, u, u, p.sib).wait_recv()
        s.cp(9, u, u, p.sib).wait_recv()
    def drain(s):
        p = s.p; u = s.r(p.dp * 192, 192); u1 = s.r(p.dp * 192, 48)
        for k in (7, 8, 9): s.cp(k, u, u, p.sib).wait_send()
        w = lambda k: s.cp(k, u1, u1, p.sib).wait_send()
        @pl.when(p.z < 3)
        def _(): w(1)
        @pl.when(p.z > 0)
        def _(): w(2)
        for h in (1, 2):
            @pl.when((p.z >= h) & (p.z < 3))
            def _(): w(2 + h)
            @pl.when((p.z + h <= 3) & (p.z > 0))
            def _(): w(4 + h)

class Scan:
    def __init__(s, pos, way, rate, W, L, Z, GR, ss, rs):
        s.p, s.way, s.rate, s.W, s.L, s.Z, s.GR, s.ss, s.rs = pos, way, rate, W, L, Z, GR, ss, rs
    def has(s, d): return (s.p.sq + d < 8) if d > 0 else (s.p.sq + d >= 0)
    def cp(s, k):
        d = s.way * 2 ** k
        return rcopy(s.W.at[k], s.L.at[k], s.ss.at[k], s.rs.at[k], (s.p.dp, jnp.clip(s.p.sq + d, 0, 7)))
    def send(s, k):
        @pl.when(s.has(s.way * 2 ** k))
        def _(): s.cp(k).start()
    def begin(s):
        g = jnp.exp(s.rate[0:16, :] * -256.0)
        s.GR[0] = g; s.GR[1] = g * g; s.GR[2] = g * g * g
        s.Z[...] = jnp.zeros_like(s.Z)
        s.send(0)
    def step(s, k):
        keep = lambda: (1.0, s.GR[0][None], s.GR[2][None])[k]
        grow = lambda: (s.GR[0][None], s.GR[1][None])[k]
        if k < 2: s.W[k + 1] = s.W[k].astype(s.W.dtype)
        @pl.when(s.has(-s.way * 2 ** k))
        def _():
            s.cp(k).wait_recv()
            s.Z[...] += keep() * s.L[k].astype(f32)
            if k < 2: s.W[k + 1] = (s.W[k + 1].astype(f32) + grow() * s.L[k].astype(f32)).astype(s.W.dtype)
        if k < 2: s.send(k + 1)
    def drain(s):
        for k in range(3):
            @pl.when(s.has(s.way * 2 ** k))
            def _(): s.cp(k).wait_send()

def full_barrier(p):
    bar = pltpu.get_barrier_semaphore()
    sig = lambda d: pl.semaphore_signal(bar, inc=1, device_id=d, device_id_type=MESH)
    sig(p.sib); sig(p.xn); sig(p.yn)
    for d in (1, 2, 4):
        @pl.when(p.sq + d < 8)
        def _(): sig((p.dp, jnp.minimum(p.sq + d, 7)))
        @pl.when(p.sq - d >= 0)
        def _(): sig((p.dp, jnp.maximum(p.sq - d, 0)))
    pl.semaphore_wait(bar, 3 + sum(jnp.clip(p.sq - d + 1, 0, 1) + jnp.clip(8 - d - p.sq, 0, 1) for d in (1, 2, 4)))

def first_exchange_start(p, mx, va, wo, wu, wd, WB, land, s0, r0):
    cps = {}
    @pl.when(p.y == 0)
    def _():
        rcopy(va, land.at[:, pl.ds(0, 1536)], s0.at[0], r0.at[0], p.yn).start()
        rcopy(wu, land.at[:, pl.ds(1536, 1536)], s0.at[1], r0.at[1], p.yn).start()
    @pl.when(p.y == 1)
    def _():
        rcopy(mx, land, s0.at[0], r0.at[0], p.yn).start()
    r = lambda yy: pl.ds(pl.multiple_of((p.dp * 4 + p.z) * RB + yy * 48, 48), 48)
    for yy, (own, far) in ((0, (wo, wd)), (1, (wd, wo))):
        @pl.when(p.y == yy)
        def _():
            rcopy(far, WB.at[r(yy), pl.ds((1 - yy) * HB, HB)], s0.at[2], r0.at[2], p.yn).start()
            pltpu.make_async_copy(own, WB.at[r(yy), pl.ds(yy * HB, HB)], s0.at[3]).start()

def first_exchange_end(p, mx, va, wo, wu, wd, WA, WB, land, s0, r0):
    rows = pl.ds(pl.multiple_of((p.dp * 4 + p.z) * RA, 16), RA)
    v1, v2 = land.at[:, pl.ds(0, 1536)], land.at[:, pl.ds(1536, 1536)]
    put = lambda c, w, lo, hi: WA.__setitem__((rows, pl.ds(c, w)), jnp.concatenate([lo[...].astype(f32), hi[...].astype(f32)], axis=0).astype(bf16))
    u = WB.at[pl.ds(pl.multiple_of((p.dp * 4 + p.z) * RB, 48), 48), pl.ds(0, HB)]
    @pl.when(p.y == 0)
    def _():
        rcopy(mx, land, s0.at[0], r0.at[0], p.yn).wait_recv()
        put(0, HA, mx, land)
    @pl.when(p.y == 1)
    def _():
        rcopy(va, v1, s0.at[0], r0.at[0], p.yn).wait_recv()
        rcopy(wu, v2, s0.at[1], r0.at[1], p.yn).wait_recv()
        put(HA, 1536, v1, va)
        put(HA + 1536, 1536, v2, wu)
        WA[rows, pl.ds(HA + 3072, 128)] = jnp.zeros((RA, 128), bf16)
    rcopy(u, u, s0.at[2], r0.at[2], p.yn).wait_recv()
    pltpu.make_async_copy(u, u, s0.at[3]).wait()
def first_exchange_drain(p, mx, va, wo, wu, wd, land, s0, r0):
    v1 = land.at[:, pl.ds(0, 1536)]
    @pl.when(p.y == 0)
    def _():
        rcopy(va, v1, s0.at[0], r0.at[0], p.yn).wait_send()
        rcopy(wu, v1, s0.at[1], r0.at[1], p.yn).wait_send()
    @pl.when(p.y == 1)
    def _(): rcopy(mx, land, s0.at[0], r0.at[0], p.yn).wait_send()
    rcopy(wo, wo, s0.at[2], r0.at[2], p.yn).wait_send()

def norm_rows(tok, PT, U, NL, i):
    x = tok[ds(i, 64), :].astype(f32)
    r = lax.rsqrt(jnp.mean(x * x, axis=-1, keepdims=True) + EPSILON)
    u = x * r * PT[32:33, :]
    U[ds(i, 8), :, :] = u.reshape(8, 8, 768)
    NL[ds(i, 64), :] = u.astype(bf16)

def sub8(v):
    return v.reshape(v.shape[0] // 8, 8, v.shape[1]).sum(axis=0)

FORWARD_OUT = (("wa", (768, 2 * HA), bf16), ("wb", (1536, 2 * HB), bf16), ("vl", (512, 1536), bf16), ("vs", (512, 1536), bf16),
    ("re", (512, 1536), bf16), ("rs", (512, 1536), bf16), ("at", (512, 1536), bf16), ("gt", (512, 1536), bf16), ("hi", (512, 1536), bf16), ("hs", (512, 1536), bf16),
    ("uc", (512, 768), bf16), ("du", (512, 768), bf16), ("om", (512, 768), bf16), ("sh", (512, 768), bf16), ("bs", (512, 768), bf16), ("n2", (512, 768), bf16),
    ("mi", (512, 768), f32), ("sp", (512, 128), f32), ("pr", (512, 128), f32), ("st", (64, 16, 768), f32), ("pt", (128, 768), f32), ("res", (512, 768), bf16), ("sq", (24, 768), f32))

def forward_kernel(tok, valid, affine, prm, mx, va, wo, wu, wd, *refs):
    no = len(FORWARD_OUT)
    outs, bufs, rest = refs[:no], refs[no:2 * no], refs[2 * no:]
    B = {name: r for (name, _, _), r in zip(FORWARD_OUT, bufs)}
    O = {name: r for (name, _, _), r in zip(FORWARD_OUT, outs)}
    osem = {name: i for i, (name, _, _) in enumerate(FORWARD_OUT)}
    (PRM, land, U, NL, BL, RSF, UPD, DIR, ACC, KS, W, L, Z, GR, s0, r0, sp_, rp_, ss, rs, sx, rx, so) = rest
    WA, WB, PT, S = B["wa"], B["wb"], B["pt"], B["st"]
    p = Pos()
    full_barrier(p)
    out = lambda name: pltpu.make_async_copy(B[name], O[name], so.at[osem[name]])
    def keep(*names):
        for name in names: out(name).start()
    par = Params(p, prm, PRM, sp_, rp_)
    par.y0()
    first_exchange_start(p, mx, va, wo, wu, wd, WB, land, s0, r0)
    g = Gather(p, (WA, WB), ss, rs)
    n = len(CHUNKS)
    def link(t):
        if t < n: g.z0(t)
        if 0 <= t - 1 < n: g.zhop(t - 1, 1)
        if 0 <= t - 2 < n: g.zhop(t - 2, 2)
        if 0 <= t - 3 < n: g.zhop(t - 3, 3); g.s1(t - 3)
        if 0 <= t - 4 < n: g.s2(t - 4)
        if 0 <= t - 5 < n: g.s3(t - 5)
        if 0 <= t - 6 < n: g.s4(t - 6)
    par.y1(); par.z0()
    first_exchange_end(p, mx, va, wo, wu, wd, WA, WB, land, s0, r0)
    link(0); par.zhop(1)
    link(1); par.zhop(2)
    link(2); par.zhop(3); par.x0()
    link(3); par.x1(); par.end()
    for j in range(6): PT[:, j * 128:(j + 1) * 128] = PRM[j * 128:(j + 1) * 128, :].T
    rate, ec, omega = PT.at[0:16, :], PT.at[16:32, :], PT.at[34:35, :]
    loop(8, lambda i: norm_rows(tok, PT, U, NL, i))
    link(4)
    def some(lo, hi, f):
        def body(j, _):
            f(j); return 0
        lax.fori_loop(lo, hi, body, 0)
    states = lambda j: fwd_states(U, rate, S, W.at[0], j, 4)
    some(0, 6, states)
    sc = Scan(p, 1, PT, W, L, Z, GR, sx, rx)
    sc.begin()
    link(5)
    sc.step(0); sc.step(1); sc.step(2)
    smooth = lambda j: fwd_smooth(U, S, Z, rate, ec, omega, BL, KS, j, 2)
    some(0, 3, smooth)
    link(6)
    some(3, 6, smooth)
    def shift_rows(i):
        y, s = silu_and_slope(BL[ds(i, 8), :, :].reshape(64, 768))
        B["sh"][ds(i, 64), :] = y.astype(bf16)
        B["bs"][ds(i, 64), :] = s.astype(bf16)
    loop(8, shift_rows)
    keep("st", "pt", "sh", "bs")
    link(7)
    def value(m):
        ACC[...] = dot(NL[...], WA[:, pl.ds(pl.multiple_of(HA + m * 256, 128), 256)])
        def rows(i):
            y, s = silu_and_slope(ACC[ds(i, 64), :])
            B["vl"][ds(i, 64), ds(m, 256)] = y.astype(bf16)
            B["vs"][ds(i, 64), ds(m, 256)] = s.astype(bf16)
        loop(8, rows)
    some(0, 2, value)
    def mixed(c, w=256): ACC[:, 0:w] = dot(B["sh"][...], WA[:, pl.ds(pl.multiple_of(c, 128), w)])
    def update(m):
        mixed(m * 256)
        loop(8, lambda i: UPD.__setitem__((ds(i, 64), ds(m, 256)), sigmoid(ACC[ds(i, 64), :])))
    def reset(m):
        mixed(896 + m * 256)
        def rows(i):
            y, s = silu_and_slope(ACC[ds(i, 64), :])
            RSF[ds(i, 64), ds(m, 256)] = y
            B["re"][ds(i, 64), ds(m, 256)] = y.astype(bf16)
            B["rs"][ds(i, 64), ds(m, 256)] = s.astype(bf16)
        loop(8, rows)
    def direct(m):
        mixed(2432 + m * 256)
        DIR[:, ds(m, 256)] = ACC[...]
    some(0, 2, update)
    link(8)
    some(2, 6, value)
    keep("vl", "vs")
    some(2, 3, update)
    mixed(768, 128)
    B["sp"][...] = ACC[:, 0:128]
    some(0, 1, reset)
    link(9)
    some(1, 6, reset)
    keep("re", "rs", "sp")
    link(10)
    def attend(b):
        rr = ds(b, 128)
        s = B["sp"][rr, :]
        s = s * sigmoid(s)
        q = (s * affine[0:1, :] + affine[1:2, :]).astype(bf16)
        k = (s * affine[2:3, :]).astype(bf16)
        t = dot_nt(q, k) * Z_SCALE
        ok = lax.broadcasted_iota(jnp.int32, (128, 128), 0) >= lax.broadcasted_iota(jnp.int32, (128, 128), 1)
        t = jnp.where(ok, t, -1e30)
        e = jnp.exp(t - jnp.max(t, axis=-1, keepdims=True))
        e = e / jnp.sum(e, axis=-1, keepdims=True)
        B["pr"][rr, :] = e
        el = e.astype(bf16)
        for m in range(6):
            c = pl.ds(m * 256, 256)
            a = dot(el, B["vl"][rr, c])
            B["at"][rr, c] = a.astype(bf16)
            B["gt"][rr, c] = (a * RSF[rr, c]).astype(bf16)
    loop(4, attend)
    some(0, 3, direct)
    keep("pr", "at", "gt")
    link(11)
    link(12)
    keep("wa", "wb")
    SQ = B["sq"]
    SQ[...] = jnp.zeros_like(SQ)
    def candidate(m):
        ACC[...] = dot(B["gt"][...], WB[:, ds(m, 256)])
        def rows(i):
            r, c = ds(i, 64), ds(m, 256)
            y, s = silu_and_slope(DIR[r, c] + ACC[r, :])
            u = UPD[r, c]
            x = tok[r, c].astype(f32)
            a = u * (y - x)
            B["mi"][r, c] = x + a
            B["uc"][r, c] = (u * s).astype(bf16)
            B["du"][r, c] = (a * (1.0 - u)).astype(bf16)
            B["om"][r, c] = (1.0 - u).astype(bf16)
            SQ[8:16, c] += sub8(valid[r, :] * a * a)
        loop(8, rows)
    some(0, 3, candidate)
    def second(i):
        v = B["mi"][ds(i, 64), :]
        r = lax.rsqrt(jnp.mean(v * v, axis=-1, keepdims=True) + EPSILON)
        B["n2"][ds(i, 64), :] = (v * r * PT[33:34, :]).astype(bf16)
    loop(8, second)
    keep("mi", "uc", "du", "om", "n2")
    def up(m):
        ACC[...] = dot(B["n2"][...], WA[:, pl.ds(pl.multiple_of(HA + 1536 + m * 256, 128), 256)])
        def rows(i):
            y, s = silu_and_slope(ACC[ds(i, 64), :])
            B["hi"][ds(i, 64), ds(m, 256)] = y.astype(bf16)
            B["hs"][ds(i, 64), ds(m, 256)] = s.astype(bf16)
        loop(8, rows)
    some(0, 6, up)
    keep("hi", "hs")
    def down(m):
        ACC[...] = dot(B["hi"][...], WB[:, pl.ds(pl.multiple_of(HB + m * 256, 128), 256)])
        def rows(i):
            r, c = ds(i, 64), ds(m, 256)
            f = ACC[r, :]
            o = B["mi"][r, c] + f
            B["res"][r, c] = o.astype(bf16)
            v = valid[r, :]
            SQ[0:8, c] += sub8(v * o * o)
            SQ[16:24, c] += sub8(v * f * f)
        loop(8, rows)
    some(0, 3, down)
    keep("res", "sq")
    for i in range(n): g.drain(i)
    par.drain(); sc.drain()
    first_exchange_drain(p, mx, va, wo, wu, wd, land, s0, r0)
    for name, _, _ in FORWARD_OUT: out(name).wait()

Z_SCALE = Z ** -0.5
def forward_call(tok, valid, affine, prm, mx, va, wo, wu, wd):
    n = len(CHUNKS)
    v = pltpu.VMEM
    D_ = pltpu.SemaphoreType.DMA
    return pl.pallas_call(forward_kernel,
        out_shape=tuple(jax.ShapeDtypeStruct(s, t) for _, s, t in FORWARD_OUT),
        in_specs=[pl.BlockSpec(memory_space=pltpu.VMEM)] * 9,
        out_specs=[pl.BlockSpec(memory_space=pl.ANY)] * len(FORWARD_OUT),
        scratch_shapes=[v(s, t) for _, s, t in FORWARD_OUT] + [v((768, 128), f32), v((24, HA), bf16), v((64, 8, 768), f32), v((512, 768), bf16),
            v((64, 8, 768), f32), v((512, 1536), f32), v((512, 768), f32), v((512, 768), f32), v((512, 256), f32), v((8, 128), f32),
            v((3, 2, 16, 768), f32), v((3, 2, 16, 768), f32), v((2, 16, 768), f32), v((3, 16, 768), f32),
            D_((4,)), D_((3,)), D_((10,)), D_((10,)), D_((n, 13)), D_((n, 13)), D_((3,)), D_((3,)), D_((len(FORWARD_OUT),))],
        compiler_params=pltpu.CompilerParams(collective_id=0, has_side_effects=True, vmem_limit_bytes=62 * 2**20),
    )(tok, valid, affine, prm, mx, va, wo, wu, wd)


def per_device_tuned(tokens, cotangent, lengths, w_mx, w_value, w_out, w_up, w_down, ema_rate, ema_in, ema_out, gains, qk_affine):
    rate_own, in_own, out_own = (t.astype(f32) for t in (ema_rate, ema_in, ema_out))
    scale_own = jnp.sqrt(-jnp.expm1(-2.0 * rate_own))
    mine = jnp.pad(jnp.concatenate([rate_own, out_own * scale_own * in_own, gains.astype(f32)], axis=1), ((0, 0), (0, 93)))
    seq_pos = lax.axis_index("seq") * SEQ_DEV + jnp.arange(SEQ_DEV, dtype=jnp.int32)
    valid = (seq_pos[None, :] < lengths[:, None]).astype(f32).reshape(512, 1)
    tok = tokens.reshape(512, D)
    affine = jnp.pad(qk_affine.astype(f32), ((0, 5), (0, 0)))
    kept = forward_call(tok, valid, affine, mine, w_mx, w_value, w_out, w_up, w_down)
    K = {name: t for (name, _, _), t in zip(FORWARD_OUT, kept)}
    full_a, full_b = K["wa"], K["wb"]
    small = K["pt"]
    rate, coef = small[:16], small[16:32]
    gain_first, gain_second, omega_gain = small[32], small[33], small[34]
    mx_full, value_full, up_full = full_a[:, :3200], full_a[:, 3200:4736], full_a[:, 4736:6272]
    out_full, down_full = full_b[:, :768], full_b[:, 768:]
    inputs = tok.astype(f32)
    inverse1 = lax.rsqrt(jnp.mean(inputs * inputs, axis=-1, keepdims=True) + EPSILON)
    unit1 = inputs * inverse1
    normed = unit1 * gain_first
    normed_low = normed.astype(bf16)
    u3 = normed.reshape(64, 8, D)
    dn = lambda a, b, ca, cb: lax.dot_general(a, b, (((ca,), (cb,)), ((), ())), preferred_element_type=f32)
    middle = K["mi"]
    inverse2 = lax.rsqrt(jnp.mean(middle * middle, axis=-1, keepdims=True) + EPSILON)
    unit2 = middle * inverse2
    grad_out = cotangent.reshape(512, D).astype(f32) * valid
    g_low = grad_out.astype(bf16)
    grad_down = dn(K["hi"], g_low, 0, 0)
    gu_low = (dn(g_low, down_full, 1, 1) * K["hs"].astype(f32)).astype(bf16)
    grad_up = dn(K["n2"], gu_low, 0, 0)
    grad_n2 = dn(gu_low, up_full, 1, 1)
    grad_gain_second = jnp.sum(grad_n2 * unit2, axis=0)
    scaled2 = grad_n2 * gain_second
    grad_middle = grad_out + inverse2 * (scaled2 - unit2 * jnp.mean(scaled2 * unit2, axis=-1, keepdims=True))
    gc_low = (grad_middle * K["uc"].astype(f32)).astype(bf16)
    grad_out_proj = dn(K["gt"], gc_low, 0, 0)
    grad_gated = dn(gc_low, out_full, 1, 1)
    grad_reset = grad_gated * K["at"].astype(f32)
    go = (grad_gated * K["re"].astype(f32)).astype(bf16).reshape(4, SPAN, V)
    vl = K["vl"].reshape(4, SPAN, V)
    probs = K["pr"].reshape(4, SPAN, SPAN)
    probs_low = probs.astype(bf16)
    grad_probs = jnp.einsum("nqv,nkv->nqk", go, vl, preferred_element_type=f32)
    grad_values = jnp.einsum("nqk,nqv->nkv", probs_low, go, preferred_element_type=f32).reshape(512, V)
    gs = (probs * (grad_probs - jnp.sum(grad_probs * probs, axis=-1, keepdims=True))).astype(bf16)
    shared_pre = K["sp"]
    shared = jax.nn.silu(shared_pre)
    ql = (shared * affine[0] + affine[1]).astype(bf16).reshape(4, SPAN, Z)
    kl = (shared * affine[2]).astype(bf16).reshape(4, SPAN, Z)
    gq = (jnp.einsum("nqk,nkz->nqz", gs, kl, preferred_element_type=f32) * Z_SCALE).reshape(512, Z)
    gk = (jnp.einsum("nqk,nqz->nkz", gs, ql, preferred_element_type=f32) * Z_SCALE).reshape(512, Z)
    grad_affine = jnp.stack([jnp.sum(gq * shared, axis=0), jnp.sum(gq, axis=0), jnp.sum(gk * shared, axis=0)])
    grad_shared = gq * affine[0] + gk * affine[2]
    gm_low = jnp.concatenate([(grad_middle * K["du"].astype(f32)).astype(bf16), (grad_shared * silu_slope(shared_pre)).astype(bf16),
        (grad_reset * K["rs"].astype(f32)).astype(bf16), gc_low], axis=1)
    grad_mx = dn(K["sh"], gm_low, 0, 0)
    grad_blend = dn(gm_low, mx_full, 1, 1) * K["bs"].astype(f32)
    grad_omega = jnp.sum(grad_blend * normed, axis=0)
    gv_low = (grad_values * K["vs"].astype(f32)).astype(bf16)
    grad_value_proj = dn(normed_low, gv_low, 0, 0)
    grad_normed = grad_blend * omega_gain + dn(gv_low, value_full, 1, 1)
    g3 = grad_blend.reshape(64, 8, D)
    states = K["st"]
    adj, direct, g1, h1 = emab1(g3, u3, states, rate, 2)
    later = scan_call(direct, rate, -1, 3)
    h1, du3 = emab2(g3, u3, states, adj, later, rate, coef, h1, 2)
    grad_normed = grad_normed + du3.reshape(normed.shape)
    grad_gain_first = jnp.sum(grad_normed * unit1, axis=0)
    scaled1 = grad_normed * gain_first
    grad_tokens = grad_middle * K["om"].astype(f32) + inverse1 * (
        scaled1 - unit1 * jnp.mean(scaled1 * unit1, axis=-1, keepdims=True)
    )
    pa = jnp.pad(jnp.concatenate([grad_mx, grad_value_proj, grad_up], axis=1).astype(bf16), ((0, 0), (0, 128)))
    pb = jnp.concatenate([grad_out_proj, grad_down], axis=1).astype(bf16)
    oa, ob = scatter_call(pa, pb)
    tiny = jnp.concatenate([g1.T, h1.T, jnp.stack([grad_gain_first, grad_gain_second, grad_omega], axis=1)], axis=1)
    tiny = lax.psum_scatter(jnp.pad(tiny, ((0, 0), (0, 93))), ("dp", "seq"), scatter_dimension=0, tiled=True)
    g1, h1 = tiny[:, :16], tiny[:, 16:32]
    grad_ema_out = in_own * scale_own * g1
    grad_ema_in = out_own * scale_own * g1
    grad_ema_rate = out_own * in_own * (jnp.exp(-2.0 * rate_own) / scale_own * g1 - scale_own * h1)
    squares = jnp.append(jnp.sum(K["sq"].reshape(3, -1), axis=1), jnp.sum(valid))
    affine_total, square_total = lax.psum((grad_affine, squares), ("dp", "seq"))
    rms_values = jnp.sqrt(square_total[:3] / (square_total[3] * D))
    return (K["res"].reshape(tokens.shape), grad_tokens.reshape(tokens.shape), oa[:, :3200], oa[:, 3200:4736], ob[:, :768], oa[:, 4736:6272], ob[:, 768:],
        grad_ema_rate, grad_ema_in, grad_ema_out, tiny[:, 32:35], affine_total, rms_values)


def solution(mesh):
    placed = (
        P("dp", "seq", None),
        P("dp", "seq", None),
        P("dp"),
        P(("dp", "seq"), None),
        P(("dp", "seq"), None),
        P(("dp", "seq"), None),
        P(("dp", "seq"), None),
        P(("dp", "seq"), None),
        P(("dp", "seq"), None),
        P(("dp", "seq"), None),
        P(("dp", "seq"), None),
        P(("dp", "seq"), None),
        P(),
    )
    step = per_device_tuned if dict(mesh.shape) == {"dp": 4, "seq": 8} else per_device
    return jax.shard_map(
        step,
        mesh=mesh,
        in_specs=placed,
        out_specs=(
            P("dp", "seq", None),
            P("dp", "seq", None),
            P(("dp", "seq"), None),
            P(("dp", "seq"), None),
            P(("dp", "seq"), None),
            P(("dp", "seq"), None),
            P(("dp", "seq"), None),
            P(("dp", "seq"), None),
            P(("dp", "seq"), None),
            P(("dp", "seq"), None),
            P(("dp", "seq"), None),
            P(),
            P(),
        ),
        check_vma=False,
    )
```

```python
import functools

import jax
import jax.numpy as jnp
from jax import lax
from jax.experimental import pallas as pl
from jax.experimental.pallas import tpu as pltpu
from jax.sharding import PartitionSpec as P

MESH = pl.DeviceIdType.MESH
bf16, f32 = jnp.bfloat16, jnp.float32
D = 768
Z = 128
V = 1536
SPAN = 128
SEQ_DEV = 256


EPSILON = 1e-06
TOP_PRECISION = lax.Precision.HIGHEST


def prefix(value, axis, join, neutral):
    count, mine = (lax.axis_size(axis), lax.axis_index(axis))
    pieces = jax.tree.map(lambda part: lax.all_gather(part, axis), value)
    so_far = jax.tree.map(
        lambda part, zero: jnp.full_like(part, 0) + jnp.asarray(zero, part.dtype), value, neutral
    )

    def lap(position, so_far):
        longer = join(so_far, jax.tree.map(lambda part: part[position], pieces))
        return jax.tree.map(lambda new, old: jnp.where(position < mine, new, old), longer, so_far)

    return lax.fori_loop(0, count - 1, lap, so_far)


def prefix_2(value, axis, combine, identity):
    length, here = (lax.axis_size(axis), lax.axis_index(axis))
    everything = jax.tree.map(
        lambda part, kind: lax.all_gather(part.astype(kind), axis),
        value,
        jax.tree.map(lambda a: jnp.bfloat16 if a.dtype == jnp.float32 else a.dtype, value),
    )
    start = jax.tree.map(
        lambda part, zero: jnp.broadcast_to(jnp.asarray(zero, part.dtype), part.shape),
        value,
        identity,
    )

    def lap(k, before):
        at = length - 1 - k
        reached = at > here
        new = combine(
            before, jax.tree.map(lambda part, own: part[at].astype(own.dtype), everything, value)
        )
        return jax.tree.map(lambda a, b: jnp.where(reached, a, b), new, before)

    return lax.fori_loop(0, length, lap, start)


def silu_slope(values):
    sigmoid = jax.nn.sigmoid(values)
    return sigmoid * (1.0 + values * (1.0 - sigmoid))


def chain_combine(earlier, later):
    return (earlier[0] * later[0], later[0] * earlier[1] + later[1])


def ema_local(rate, beta, eta, input_signal):
    rows_here, length, channels = input_signal.shape
    block_len = min(64, length)
    blocks_count = length // block_len
    lag_values = jnp.arange(block_len, dtype=jnp.float32)
    powers = jnp.exp(-lag_values[:, None, None] * rate[None])
    scale_in = jnp.sqrt(-jnp.expm1(-2.0 * rate)) * beta
    kernel = jnp.sum(powers * (eta * scale_in)[None], axis=2)
    step_ids = jnp.arange(block_len)
    lag_index = jnp.clip(step_ids[:, None] - step_ids[None, :], 0, block_len - 1)
    toeplitz = jnp.where(
        (step_ids[:, None] >= step_ids[None, :])[:, :, None], kernel[lag_index], 0.0
    )
    leading = jnp.exp(-(lag_values[:, None, None] + 1.0) * rate[None]) * eta[None]
    trailing = powers[::-1] * scale_in[None]
    block_decay = jnp.exp(-block_len * rate)
    blocks = jnp.swapaxes(input_signal.reshape(rows_here, blocks_count, block_len, channels), 0, 1)

    def advance(carried, segment):
        smooth = jnp.einsum("tsd,bsd->btd", toeplitz, segment, precision=TOP_PRECISION)
        smooth = smooth + jnp.einsum("tdh,bdh->btd", leading, carried, precision=TOP_PRECISION)
        carried = block_decay * carried + jnp.einsum(
            "sdh,bsd->bdh", trailing, segment, precision=TOP_PRECISION
        )
        return (carried, smooth)

    initial = jnp.zeros((rows_here, channels, rate.shape[1]), jnp.float32)
    final_state, smooth = lax.scan(advance, initial, blocks)
    return (jnp.swapaxes(smooth, 0, 1).reshape(rows_here, length, channels), final_state)


def ema_carry(rate, eta, incoming):
    block_len = min(64, SEQ_DEV)
    blocks_count = SEQ_DEV // block_len
    lag_values = jnp.arange(block_len, dtype=jnp.float32)
    leading = jnp.exp(-(lag_values[:, None, None] + 1.0) * rate[None]) * eta[None]
    block_decay = jnp.exp(-block_len * rate)

    def advance(carried, unused):
        return (
            block_decay * carried,
            jnp.einsum("tdh,bdh->btd", leading, carried, precision=TOP_PRECISION),
        )

    _, smooth = lax.scan(advance, incoming, None, length=blocks_count)
    return jnp.swapaxes(smooth, 0, 1).reshape(incoming.shape[0], SEQ_DEV, incoming.shape[1])


def per_device(
    tokens,
    cotangent,
    lengths,
    w_mx,
    w_value,
    w_out,
    w_up,
    w_down,
    ema_rate,
    ema_in,
    ema_out,
    gains,
    qk_affine,
):
    gathered = (
        lax.all_gather(w_mx, ("dp", "seq"), axis=0, tiled=True),
        lax.all_gather(w_value, ("dp", "seq"), axis=0, tiled=True),
        lax.all_gather(w_out, ("dp", "seq"), axis=0, tiled=True),
        lax.all_gather(w_up, ("dp", "seq"), axis=0, tiled=True),
        lax.all_gather(w_down, ("dp", "seq"), axis=0, tiled=True),
        lax.all_gather(ema_rate, ("dp", "seq"), axis=0, tiled=True),
        lax.all_gather(ema_in, ("dp", "seq"), axis=0, tiled=True),
        lax.all_gather(ema_out, ("dp", "seq"), axis=0, tiled=True),
        lax.all_gather(gains, ("dp", "seq"), axis=0, tiled=True),
    )
    mx_full, value_full, out_full, up_full, down_full, rate_low, beta_low, eta_low, gain_low = (
        gathered
    )
    rate = rate_low.astype(jnp.float32)
    beta = beta_low.astype(jnp.float32)
    eta = eta_low.astype(jnp.float32)
    gain_all = gain_low.astype(jnp.float32)
    gain_first = gain_all[:, 0]
    gain_second = gain_all[:, 1]
    omega_gain = gain_all[:, 2]
    affine = qk_affine.astype(jnp.float32)
    rows_here = tokens.shape[0]
    spans_dev = SEQ_DEV // SPAN
    score_scale = Z ** (-0.5)
    inputs = tokens.astype(jnp.float32)
    seq_pos = lax.axis_index("seq") * SEQ_DEV + jnp.arange(SEQ_DEV, dtype=jnp.int32)
    valid_rows = (seq_pos[None, :] < lengths[:, None]).astype(jnp.float32)[:, :, None]
    inverse1 = lax.rsqrt(jnp.mean(inputs * inputs, axis=-1, keepdims=True) + EPSILON)
    unit1 = inputs * inverse1
    normed = unit1 * gain_first
    normed_low = normed.astype(jnp.bfloat16)
    value_pre = jnp.einsum(
        "bsd,dv->bsv", normed_low, value_full, preferred_element_type=jnp.float32
    )
    value_low = jax.nn.silu(value_pre).astype(jnp.bfloat16)
    (smooth_local, end_local), pull_local = jax.vjp(ema_local, rate, beta, eta, normed)
    growth = jnp.exp(-SEQ_DEV * rate)
    start_state = prefix(
        (growth, end_local),
        "seq",
        chain_combine,
        (jnp.ones_like(growth), jnp.zeros_like(end_local)),
    )[1]
    smooth_carry, pull_carry = jax.vjp(ema_carry, rate, eta, start_state)
    blend = smooth_local + smooth_carry + omega_gain * normed
    shifted_low = jax.nn.silu(blend).astype(jnp.bfloat16)
    mixed = jnp.einsum("bsd,dk->bsk", shifted_low, mx_full, preferred_element_type=jnp.float32)
    update = jax.nn.sigmoid(mixed[..., :D])
    shared_pre = mixed[..., D : D + Z]
    shared = jax.nn.silu(shared_pre)
    reset_pre = mixed[..., D + Z : D + Z + V]
    reset = jax.nn.silu(reset_pre)
    direct = mixed[..., D + Z + V :]
    query_low = (
        (shared * affine[0] + affine[1]).astype(jnp.bfloat16).reshape(rows_here, spans_dev, SPAN, Z)
    )
    key_low = (shared * affine[2]).astype(jnp.bfloat16).reshape(rows_here, spans_dev, SPAN, Z)
    value_tiles = value_low.reshape(rows_here, spans_dev, SPAN, V)
    scores = (
        jnp.einsum("bnqz,bnkz->bnqk", query_low, key_low, preferred_element_type=jnp.float32)
        * score_scale
    )
    causal = jnp.arange(SPAN)[:, None] >= jnp.arange(SPAN)[None, :]
    masked = jnp.where(causal, scores, -1e30)
    peak = jnp.max(masked, axis=-1, keepdims=True)
    expo = jnp.exp(masked - peak)
    attention_weights = expo / jnp.sum(expo, axis=-1, keepdims=True)
    probs_low = attention_weights.astype(jnp.bfloat16)
    attended_output = jnp.einsum(
        "bnqk,bnkv->bnqv", probs_low, value_tiles, preferred_element_type=jnp.float32
    ).reshape(rows_here, SEQ_DEV, V)
    gated_low = (reset * attended_output).astype(jnp.bfloat16)
    cand_pre = direct + jnp.einsum(
        "bsv,vd->bsd", gated_low, out_full, preferred_element_type=jnp.float32
    )
    candidate = jax.nn.silu(cand_pre)
    attn_branch = update * (candidate - inputs)
    middle = inputs + attn_branch
    inverse2 = lax.rsqrt(jnp.mean(middle * middle, axis=-1, keepdims=True) + EPSILON)
    unit2 = middle * inverse2
    normed2_low = (unit2 * gain_second).astype(jnp.bfloat16)
    up_pre = jnp.einsum("bsd,df->bsf", normed2_low, up_full, preferred_element_type=jnp.float32)
    hidden_low = jax.nn.silu(up_pre).astype(jnp.bfloat16)
    ffn_branch = jnp.einsum(
        "bsf,fd->bsd", hidden_low, down_full, preferred_element_type=jnp.float32
    )
    output = middle + ffn_branch
    again = (
        lax.all_gather(w_mx, ("dp", "seq"), axis=0, tiled=True),
        lax.all_gather(w_value, ("dp", "seq"), axis=0, tiled=True),
        lax.all_gather(w_out, ("dp", "seq"), axis=0, tiled=True),
        lax.all_gather(w_up, ("dp", "seq"), axis=0, tiled=True),
        lax.all_gather(w_down, ("dp", "seq"), axis=0, tiled=True),
    )
    mixer_backward, value_back, out_back, up_back, down_back = again
    grad_out = cotangent.astype(jnp.float32) * valid_rows
    grad_out_low = grad_out.astype(jnp.bfloat16)
    grad_down = jnp.einsum(
        "bsf,bsd->fd", hidden_low, grad_out_low, preferred_element_type=jnp.float32
    )
    grad_hidden = jnp.einsum(
        "bsd,fd->bsf", grad_out_low, down_back, preferred_element_type=jnp.float32
    )
    grad_up_low = (grad_hidden * silu_slope(up_pre)).astype(jnp.bfloat16)
    grad_up = jnp.einsum(
        "bsd,bsf->df", normed2_low, grad_up_low, preferred_element_type=jnp.float32
    )
    grad_normed2 = jnp.einsum(
        "bsf,df->bsd", grad_up_low, up_back, preferred_element_type=jnp.float32
    )
    grad_gain_second = jnp.sum(grad_normed2 * unit2, axis=(0, 1))
    scaled2 = grad_normed2 * gain_second
    grad_middle = grad_out + inverse2 * (
        scaled2 - unit2 * jnp.mean(scaled2 * unit2, axis=-1, keepdims=True)
    )
    grad_update = grad_middle * (candidate - inputs)
    grad_cand_pre = grad_middle * update * silu_slope(cand_pre)
    grad_cand_low = grad_cand_pre.astype(jnp.bfloat16)
    grad_out_proj = jnp.einsum(
        "bsv,bsd->vd", gated_low, grad_cand_low, preferred_element_type=jnp.float32
    )
    grad_gated = jnp.einsum(
        "bsd,vd->bsv", grad_cand_low, out_back, preferred_element_type=jnp.float32
    )
    grad_reset = grad_gated * attended_output
    grad_attended_low = (
        (grad_gated * reset).astype(jnp.bfloat16).reshape(rows_here, spans_dev, SPAN, V)
    )
    grad_probs = jnp.einsum(
        "bnqv,bnkv->bnqk", grad_attended_low, value_tiles, preferred_element_type=jnp.float32
    )
    grad_values = jnp.einsum(
        "bnqk,bnqv->bnkv", probs_low, grad_attended_low, preferred_element_type=jnp.float32
    ).reshape(rows_here, SEQ_DEV, V)
    grad_scores_low = (
        attention_weights
        * (grad_probs - jnp.sum(grad_probs * attention_weights, axis=-1, keepdims=True))
    ).astype(jnp.bfloat16)
    grad_query = (
        jnp.einsum("bnqk,bnkz->bnqz", grad_scores_low, key_low, preferred_element_type=jnp.float32)
        * score_scale
    ).reshape(rows_here, SEQ_DEV, Z)
    grad_key = (
        jnp.einsum(
            "bnqk,bnqz->bnkz", grad_scores_low, query_low, preferred_element_type=jnp.float32
        )
        * score_scale
    ).reshape(rows_here, SEQ_DEV, Z)
    grad_affine = jnp.stack(
        [
            jnp.sum(grad_query * shared, axis=(0, 1)),
            jnp.sum(grad_query, axis=(0, 1)),
            jnp.sum(grad_key * shared, axis=(0, 1)),
        ]
    )
    grad_shared = grad_query * affine[0] + grad_key * affine[2]
    grad_mixed_low = jnp.concatenate(
        [
            grad_update * update * (1.0 - update),
            grad_shared * silu_slope(shared_pre),
            grad_reset * silu_slope(reset_pre),
            grad_cand_pre,
        ],
        axis=-1,
    ).astype(jnp.bfloat16)
    grad_mx = jnp.einsum(
        "bsd,bsk->dk", shifted_low, grad_mixed_low, preferred_element_type=jnp.float32
    )
    grad_shifted = jnp.einsum(
        "bsk,dk->bsd", grad_mixed_low, mixer_backward, preferred_element_type=jnp.float32
    )
    grad_blend = grad_shifted * silu_slope(blend)
    grad_omega = jnp.sum(grad_blend * normed, axis=(0, 1))
    grad_value_low = (grad_values * silu_slope(value_pre)).astype(jnp.bfloat16)
    grad_value_proj = jnp.einsum(
        "bsd,bsv->dv", normed_low, grad_value_low, preferred_element_type=jnp.float32
    )
    grad_normed = grad_blend * omega_gain + jnp.einsum(
        "bsv,dv->bsd", grad_value_low, value_back, preferred_element_type=jnp.float32
    )
    rate_from_carry, eta_from_carry, direct_adjoint = pull_carry(grad_blend)
    later_adjoint = prefix_2(
        (growth, direct_adjoint),
        "seq",
        chain_combine,
        (jnp.ones_like(growth), jnp.zeros_like(direct_adjoint)),
    )[1]
    rate_from_local, grad_beta, eta_from_local, normed_from_ema = pull_local(
        (grad_blend, later_adjoint)
    )
    rate_from_growth = jnp.sum(later_adjoint * start_state, axis=0) * (-SEQ_DEV * growth)
    grad_rate = rate_from_carry + rate_from_local + rate_from_growth
    grad_eta = eta_from_carry + eta_from_local
    grad_normed = grad_normed + normed_from_ema
    grad_gain_first = jnp.sum(grad_normed * unit1, axis=(0, 1))
    scaled1 = grad_normed * gain_first
    grad_tokens = grad_middle * (1.0 - update) + inverse1 * (
        scaled1 - unit1 * jnp.mean(scaled1 * unit1, axis=-1, keepdims=True)
    )
    grad_gains = jnp.stack([grad_gain_first, grad_gain_second, grad_omega], axis=1)
    shards = (
        lax.psum_scatter(grad_mx, ("dp", "seq"), scatter_dimension=0, tiled=True),
        lax.psum_scatter(grad_value_proj, ("dp", "seq"), scatter_dimension=0, tiled=True),
        lax.psum_scatter(grad_out_proj, ("dp", "seq"), scatter_dimension=0, tiled=True),
        lax.psum_scatter(grad_up, ("dp", "seq"), scatter_dimension=0, tiled=True),
        lax.psum_scatter(grad_down, ("dp", "seq"), scatter_dimension=0, tiled=True),
        lax.psum_scatter(grad_rate, ("dp", "seq"), scatter_dimension=0, tiled=True),
        lax.psum_scatter(grad_beta, ("dp", "seq"), scatter_dimension=0, tiled=True),
        lax.psum_scatter(grad_eta, ("dp", "seq"), scatter_dimension=0, tiled=True),
        lax.psum_scatter(grad_gains, ("dp", "seq"), scatter_dimension=0, tiled=True),
    )
    squares = jnp.stack(
        [
            jnp.sum(valid_rows * output * output),
            jnp.sum(valid_rows * attn_branch * attn_branch),
            jnp.sum(valid_rows * ffn_branch * ffn_branch),
            jnp.sum(valid_rows),
        ]
    )
    affine_total, square_total = lax.psum((grad_affine, squares), ("dp", "seq"))
    rms_values = jnp.sqrt(square_total[:3] / (square_total[3] * D))
    return (
        output.astype(jnp.bfloat16),
        grad_tokens,
        shards[0],
        shards[1],
        shards[2],
        shards[3],
        shards[4],
        shards[5],
        shards[6],
        shards[7],
        shards[8],
        affine_total,
        rms_values,
    )


HA, HB = 3200, 768
RA, RB = 48, 96

CHUNKS = [(0, 0, 640, "xy"), (0, 640, 640, "yx"), (0, 1280, 640, "xy"), (0, 1920, 640, "yx"), (0, 2560, 640, "xy"), (1, 0, 384, "yx"), (1, 384, 384, "xy")]

class Pos:
    def __init__(s):
        s.dp, s.sq = lax.axis_index("dp"), lax.axis_index("seq")
        s.x, s.c, s.z, s.y = s.dp // 2, s.dp % 2, s.sq // 2, s.sq % 2
        s.sib = (s.dp + 1 - 2 * s.c, s.sq)
        s.xn = (s.dp + 2 - 4 * s.x, s.sq)
        s.yn = (s.dp, s.sq + 1 - 2 * s.y)
        s.up = (s.dp, jnp.minimum(s.sq + 2, s.sq + 2 * (3 - s.z)))
        s.dn = (s.dp, jnp.maximum(s.sq - 2, s.y))
        s.dpx = s.dp + 2 - 4 * s.x

def rcopy(src, dst, ss, rs, dev):
    return pltpu.make_async_remote_copy(src_ref=src, dst_ref=dst, send_sem=ss, recv_sem=rs, device_id=dev, device_id_type=MESH)

def barrier(pos):
    bar = pltpu.get_barrier_semaphore()
    sig = lambda d: pl.semaphore_signal(bar, inc=1, device_id=d, device_id_type=MESH)
    sig(pos.sib); sig(pos.xn); sig(pos.yn)
    @pl.when(pos.z < 3)
    def _(): sig(pos.up)
    @pl.when(pos.z > 0)
    def _(): sig(pos.dn)
    pl.semaphore_wait(bar, 3 + jnp.minimum(pos.z, 1) + jnp.minimum(3 - pos.z, 1))

def at(ref, rows, nrows, half, w, off, width):
    r = pl.ds(pl.multiple_of(rows, 48), nrows)
    c = pl.ds(pl.multiple_of(half * w + off, 128), width)
    return ref.at[r, c]

class Gather:
    def __init__(s, pos, bufs, ss, rs):
        s.p, s.bufs, s.ss, s.rs = pos, bufs, ss, rs
    def geom(s, i):
        b, off, width, order = CHUNKS[i]
        return s.bufs[b], (RA, RB)[b], (HA, HB)[b], off, width, order
    def unit(s, i, dp, z, half, n=1):
        ref, R, W, off, width, _ = s.geom(i)
        return at(ref, (dp * 4 + z) * R, n * R, half, W, off, width)
    def cp(s, i, k, ref, dev):
        return rcopy(ref, ref, s.ss.at[i, k], s.rs.at[i, k], dev)
    def z0(s, i):
        p = s.p
        u = s.unit(i, p.dp, p.z, p.y)
        @pl.when(p.z < 3)
        def _(): rcopy(u, u, s.ss.at[i, 0], s.rs.at[i, p.z], p.up).start()
        @pl.when(p.z > 0)
        def _(): rcopy(u, u, s.ss.at[i, 1], s.rs.at[i, p.z], p.dn).start()
    def zrecv(s, i, zz):
        u = s.unit(i, s.p.dp, zz, s.p.y)
        rcopy(u, u, s.ss.at[i, 0], s.rs.at[i, zz], s.p.up).wait_recv()
        return u
    def zhop(s, i, h):
        p = s.p
        @pl.when(p.z >= h)
        def _():
            u = s.zrecv(i, p.z - h)
            @pl.when(p.z < 3)
            def _(): rcopy(u, u, s.ss.at[i, 1 + h], s.rs.at[i, p.z - h], p.up).start()
        @pl.when(p.z + h <= 3)
        def _():
            u = s.zrecv(i, p.z + h)
            @pl.when(p.z > 0)
            def _(): rcopy(u, u, s.ss.at[i, 10 + h], s.rs.at[i, p.z + h], p.dn).start()
    def s1(s, i):
        p = s.p; order = CHUNKS[i][3]
        u = s.unit(i, p.dp, 0, p.y, 4)
        s.cp(i, 4, u, p.xn if order == "xy" else p.yn).start()
        s.cp(i, 7, u, p.sib).start()
    def s1_in(s, i):
        p = s.p; order = CHUNKS[i][3]
        return s.unit(i, p.dpx, 0, p.y, 4) if order == "xy" else s.unit(i, p.dp, 0, 1 - p.y, 4)
    def s2(s, i):
        p = s.p; order = CHUNKS[i][3]
        r = s.s1_in(i)
        s.cp(i, 4, r, p.xn).wait_recv()
        nxt = p.yn if order == "xy" else p.xn
        u = s.unit(i, p.dp, 0, p.y, 4)
        s.cp(i, 5, u, nxt).start()
        s.cp(i, 6, r, nxt).start()
        s.cp(i, 8, r, p.sib).start()
    def s2_in(s, i):
        p = s.p; order = CHUNKS[i][3]
        if order == "xy":
            return s.unit(i, p.dp, 0, 1 - p.y, 4), s.unit(i, p.dpx, 0, 1 - p.y, 4)
        return s.unit(i, p.dpx, 0, p.y, 4), s.unit(i, p.dpx, 0, 1 - p.y, 4)
    def s3(s, i):
        p = s.p
        for k, r in enumerate(s.s2_in(i)):
            s.cp(i, 5 + k, r, p.sib).wait_recv()
            s.cp(i, 9 + k, r, p.sib).start()
    def s4(s, i):
        p = s.p
        u = s.unit(i, p.dp, 0, p.y, 4)
        for k in (7, 8, 9, 10):
            s.cp(i, k, u, p.sib).wait_recv()
    def drain(s, i):
        p = s.p
        u1 = s.unit(i, p.dp, 0, p.y)
        u = s.unit(i, p.dp, 0, p.y, 4)
        for k in (4, 5, 6, 7, 8, 9, 10):
            s.cp(i, k, u, p.sib).wait_send()
        w = lambda k: rcopy(u1, u1, s.ss.at[i, k], s.rs.at[i, 0], p.sib).wait_send()
        @pl.when(p.z < 3)
        def _(): w(0)
        @pl.when(p.z > 0)
        def _(): w(1)
        for h in (1, 2):
            @pl.when((p.z >= h) & (p.z < 3))
            def _(): w(1 + h)
            @pl.when((p.z + h <= 3) & (p.z > 0))
            def _(): w(10 + h)


class Scatter:
    NS = 14
    def __init__(s, pos, P, L1, L2, L3, L4, F, G, out, ss, rs):
        s.p, s.P, s.L1, s.L2, s.L3, s.L4, s.F, s.G, s.out, s.ss, s.rs = pos, P, L1, L2, L3, L4, F, G, out, ss, rs
    def geom(s, i):
        b, off, w, order = CHUNKS[i]
        return b, (RA, RB)[b], (HA, HB)[b], off, w, order
    def rows(s, i, xx, c, z=0):
        R = (RA, RB)[CHUNKS[i][0]]
        return pl.multiple_of(((xx * 2 + c) * 4 + z) * R, 48)
    def cols(s, i, yy):
        b, R, W, off, w, _ = s.geom(i)
        return pl.ds(pl.multiple_of(yy * W + off, 128), w)
    def piece(s, i, xx, c, yy, z=0, n=4):
        b, R, W, off, w, _ = s.geom(i)
        return s.P[b].at[pl.ds(s.rows(i, xx, c, z), n * R), s.cols(i, yy)]
    def cp(s, i, k, src, dst, dev):
        return rcopy(src, dst, s.ss.at[i, k], s.rs.at[i, k], dev)
    def add(s, dst, src, nrows):
        def body(r, _):
            rr = pl.ds(pl.multiple_of(r * 48, 48), 48)
            dst[rr, :] = (dst[rr, :].astype(f32) + src[rr, :].astype(f32)).astype(bf16)
            return 0
        lax.fori_loop(0, nrows // 48, body, 0)
    def l1(s, i, xx, yy):
        b, R, W, off, w, _ = s.geom(i)
        return s.L1[b].at[xx, :, s.cols(i, yy)]
    def st0(s, i):
        p = s.p
        for k, (xx, yy) in enumerate(((0, 0), (0, 1), (1, 0), (1, 1))):
            s.cp(i, k, s.piece(i, xx, 1 - p.c, yy), s.l1(i, xx, yy), p.sib).start()
    def a0(s, i):
        b, R, W, off, w, _ = s.geom(i)
        for k, (xx, yy) in enumerate(((0, 0), (0, 1), (1, 0), (1, 1))):
            l = s.l1(i, xx, yy)
            s.cp(i, k, l, l, s.p.sib).wait_recv()
            s.add(s.piece(i, xx, s.p.c, yy), l, 4 * R)
    def l2(s, i, k):
        b, R, W, off, w, _ = s.geom(i)
        return s.L2[b].at[k, :, pl.ds(off, w)]
    def l3(s, i):
        b, R, W, off, w, _ = s.geom(i)
        return s.L3[b].at[:, pl.ds(off, w)]
    def st1(s, i):
        p, order = s.p, s.geom(i)[5]
        for k in (0, 1):
            src = s.piece(i, k, p.c, 1 - p.y) if order == "xy" else s.piece(i, 1 - p.x, p.c, k)
            s.cp(i, 4 + k, src, s.l2(i, k), p.yn if order == "xy" else p.xn).start()
    def a1(s, i):
        p = s.p; b, R, W, off, w, order = s.geom(i)
        for k in (0, 1):
            l = s.l2(i, k)
            s.cp(i, 4 + k, l, l, p.xn).wait_recv()
            s.add(s.piece(i, k, p.c, p.y) if order == "xy" else s.piece(i, p.x, p.c, k), l, 4 * R)
    def st2(s, i):
        p, order = s.p, s.geom(i)[5]
        src = s.piece(i, 1 - p.x, p.c, p.y) if order == "xy" else s.piece(i, p.x, p.c, 1 - p.y)
        s.cp(i, 6, src, s.l3(i), p.xn if order == "xy" else p.yn).start()
    def a2(s, i):
        p = s.p; b, R, W, off, w, order = s.geom(i)
        l = s.l3(i)
        s.cp(i, 6, l, l, p.xn).wait_recv()
        s.add(s.piece(i, p.x, p.c, p.y), l, 4 * R)
    def l4(s, i, d, t):
        b, R, W, off, w, _ = s.geom(i)
        return s.L4[b].at[d, t, :, pl.ds(off, w)]
    def own(s, i, t):
        p = s.p
        return s.piece(i, p.x, p.c, p.y, t, 1)
    def zsem(s, d, t):
        return 6 + t if d == 0 else 10 + t
    def zflow(s, i, d, z):
        p = s.p; R = s.geom(i)[1]
        first = z == (0, 3)[d]
        mine = () if first else (z,)
        on = tuple(range(3, z, -1)) if d == 0 else tuple(range(0, z))
        for t in on:
            l = s.l4(i, d, t)
            if not first:
                s.cp(i, s.zsem(d, t), l, l, p.sib).wait_recv()
                s.add(l, s.own(i, t), R)
            s.cp(i, s.zsem(d, t), s.own(i, t) if first else l, l, p.up if d == 0 else p.dn).start()
        for t in mine:
            l = s.l4(i, d, t)
            s.cp(i, s.zsem(d, t), l, l, p.sib).wait_recv()
    def zstep(s, i, h):
        p = s.p
        for z, d in ((h, 0), (3 - h, 1)):
            @pl.when(p.z == z)
            def _(): s.zflow(i, d, z)
    def fin(s, i):
        p = s.p; b, R, W, off, w, _ = s.geom(i)
        u = s.own(i, p.z)
        hu, hd = (p.z > 0), (p.z < 3)
        lu, ld = s.l4(i, 0, p.z), s.l4(i, 1, p.z)
        F, G, out = s.F[b], s.G[b], s.out
        h = R // 2
        for z in range(4):
            @pl.when(p.z == z)
            def _():
                t = u[...].astype(f32)
                if z > 0: t = t + lu[...].astype(f32)
                if z < 3: t = t + ld[...].astype(f32)
                F[:, pl.ds(off, w)] = t
        src = F.at[pl.ds(pl.multiple_of((1 - p.y) * h, 8), h), pl.ds(off, w)]
        s.cp(i, 13, src, G.at[:, pl.ds(off, w)], p.yn).start()
        for yy in (0, 1):
            @pl.when(p.y == yy)
            def _(): out(b, yy, off, w, lambda o, k: F[pl.ds(yy * h, h), pl.ds(off + o, k)])
    def last(s, i):
        p = s.p; b, R, W, off, w, _ = s.geom(i)
        l = s.G[b].at[:, pl.ds(off, w)]
        s.cp(i, 13, l, l, p.yn).wait_recv()
        for yy in (0, 1):
            @pl.when(p.y == 1 - yy)
            def _(): s.out(b, yy, off, w, lambda o, k: l[:, pl.ds(o, k)])
    def drain(s, i):
        p = s.p; b, R, W, off, w, _ = s.geom(i)
        for k, ref in [(k, s.l1(i, 0, 0)) for k in range(4)] + [(4, s.l2(i, 0)), (5, s.l2(i, 1)), (6, s.l3(i)), (13, s.G[b].at[:, pl.ds(off, w)])]:
            s.cp(i, k, ref, ref, p.sib).wait_send()
        for d in (0, 1):
            for t in ((1, 2, 3), (0, 1, 2))[d]:
                l = s.l4(i, d, t)
                @pl.when((p.z < t) if d == 0 else (p.z > t))
                def _(): s.cp(i, s.zsem(d, t), l, l, p.sib).wait_send()

def rs_scratch():
    n = len(CHUNKS)
    V = pltpu.VMEM
    return [V((768, 2 * HA), bf16), V((1536, 2 * HB), bf16), V((2, 192, 2 * HA), bf16), V((2, 384, 2 * HB), bf16),
        V((2, 192, HA), bf16), V((2, 384, HB), bf16), V((192, HA), bf16), V((384, HB), bf16),
        V((2, 4, 48, HA), bf16), V((2, 4, 96, HB), bf16), V((48, HA), f32), V((96, HB), f32), V((24, HA), f32), V((48, HB), f32),
        pltpu.SemaphoreType.DMA((n, Scatter.NS)), pltpu.SemaphoreType.DMA((n, Scatter.NS)), pltpu.SemaphoreType.DMA((2,))]


NK = 32
NB = 2

def lanes(j): return pl.ds(pl.multiple_of(j * 128, 128), 128)
def rows_(i): return pl.ds(pl.multiple_of(i * 8, 8), 8)
def tree(xs):
    xs = list(xs)
    while len(xs) > 1:
        xs = [xs[i] + xs[i + 1] if i + 1 < len(xs) else xs[i] for i in range(0, len(xs), 2)]
    return xs[0]

def fwd_states(U, rate, S, END, j, unroll=2):
    ln = lanes(j)
    r = rate[0:16, ln]
    w = [jnp.exp(r * (s - 7.0)) for s in range(8)]
    q8 = jnp.exp(r * -8.0)
    def body(k, st):
        new = []
        for b in range(NB):
            S[b * NK + k, :, ln] = st[b]
            parts = [w[s] * U[b * NK + k, pl.ds(s, 1), ln] for s in range(8)]
            new.append(q8 * st[b] + tree(parts))
        return tuple(new)
    st = lax.fori_loop(0, NK, body, tuple(jnp.zeros((16, 128), f32) for _ in range(NB)), unroll=unroll)
    for b in range(NB): END[b, :, ln] = st[b]

def conv_tables(rate, ec, j):
    ln = lanes(j)
    it = lax.broadcasted_iota(jnp.int32, (8, 128), 0).astype(f32)
    E, K = [], []
    for h in range(16):
        rb = jnp.broadcast_to(rate[pl.ds(h, 1), ln], (8, 128)); eb = jnp.broadcast_to(ec[pl.ds(h, 1), ln], (8, 128))
        K.append(jnp.exp(-it * rb) * eb)
        E.append(jnp.exp(-(it + 1.0) * rb) * eb)
    return E, tree(K)

def fwd_smooth(U, S, S0, rate, ec, omega, BL, KS, j, unroll=1):
    ln = lanes(j)
    r = rate[0:16, ln]
    q8 = jnp.exp(r * -8.0)
    E, K = conv_tables(rate, ec, j)
    KS[...] = K
    ii = lax.broadcasted_iota(jnp.int32, (8, 128), 0)
    KM = [jnp.where(ii >= l, jnp.broadcast_to(KS[pl.ds(l, 1), :], (8, 128)), 0.0) for l in range(8)]
    om = jnp.broadcast_to(omega[:, ln], (8, 128))
    KM[0] = KM[0] + om
    def body(k, gs):
        new = []
        for b in range(NB):
            i = b * NK + k
            S[i, :, ln] = S[i, :, ln] + gs[b]
            u = U[i, :, ln]
            parts = [KM[0] * u] + [KM[l] * pltpu.roll(u, l, 0) for l in range(1, 8)]
            parts += [E[h] * S[i, pl.ds(h, 1), ln] for h in range(16)]
            BL[i, :, ln] = tree(parts)
            new.append(q8 * gs[b])
        return tuple(new)
    lax.fori_loop(0, NK, body, tuple(S0[b, :, ln] for b in range(NB)), unroll=unroll)

def bwd_states(Gr, U, S, rate, A, DIR, G1, H, CS, j, unroll=1):
    ln = lanes(j)
    r = rate[0:16, ln]
    w = [jnp.exp(r * -float(s)) for s in range(8)]
    q8 = jnp.exp(r * -8.0)
    def body(kk, c):
        k = NK - 1 - kk
        st, g1, h1, C = c
        new, C = [], list(C)
        for b in range(NB):
            i = b * NK + k
            A[i, :, ln] = st[b]
            p = [w[s] * Gr[i, pl.ds(s, 1), ln] for s in range(8)]
            Bg = tree(p)
            B1 = tree([p[s] if s == 1 else p[s] * float(s) for s in range(1, 8)])
            Sk = S[i, :, ln]
            g1 = g1 + Sk * Bg
            h1 = h1 + Sk * B1
            new.append(q8 * st[b] + Bg)
            u, g = U[i, :, ln], Gr[i, :, ln]
            C = [C[l] + g * (pltpu.roll(u, l, 0) if l else u) for l in range(8)]
        return tuple(new), g1, h1, tuple(C)
    z = jnp.zeros((16, 128), f32)
    st, g1, h1, C = lax.fori_loop(0, NK, body, (tuple(z for _ in range(NB)), z, z, tuple(jnp.zeros((8, 128), f32) for _ in range(8))), unroll=unroll)
    for b in range(NB): DIR[b, :, ln] = st[b].astype(DIR.dtype)
    ii = lax.broadcasted_iota(jnp.int32, (8, 128), 0)
    g1, h1 = g1 * w[1], h1 * w[1]
    for l in range(8):
        cl = jnp.sum(jnp.where(ii >= l, C[l], 0.0), axis=0, keepdims=True)
        t = w[l] * cl
        g1 = g1 + t
        if l: h1 = h1 + t * float(l)
    G1[:, ln] = g1
    H[:, ln] = h1

def bwd_grad(Gr, U, S, A, A0, rate, ec, H, DU, KS, AT, j, unroll=1):
    ln = lanes(j)
    r = rate[0:16, ln]
    q8 = jnp.exp(r * -8.0)
    c8 = 8.0 * jnp.exp(r * -9.0)
    wu = [jnp.exp(r * (s - 8.0)) * (8.0 - s) for s in range(8)]
    it = lax.broadcasted_iota(jnp.int32, (8, 128), 0).astype(f32)
    E, K = [], []
    for h in range(16):
        rb = jnp.broadcast_to(rate[pl.ds(h, 1), ln], (8, 128)); eb = jnp.broadcast_to(ec[pl.ds(h, 1), ln], (8, 128))
        K.append(jnp.exp(-it * rb) * eb)
        E.append(jnp.exp((it - 8.0) * rb) * eb)
    KS[...] = tree(K)
    ii = lax.broadcasted_iota(jnp.int32, (8, 128), 0)
    KM = [jnp.where(ii < 8 - l, jnp.broadcast_to(KS[pl.ds(l, 1), :], (8, 128)), 0.0) for l in range(8)]
    def body(kk, c):
        k = NK - 1 - kk
        gs, h1 = c
        new = []
        for b in range(NB):
            i = b * NK + k
            Ak = A[i, :, ln] + gs[b]
            AT[b] = Ak
            Bu = tree([wu[s] * U[i, pl.ds(s, 1), ln] for s in range(8)])
            h1 = h1 + Ak * (Bu + c8 * S[i, :, ln])
            g = Gr[i, :, ln]
            parts = [KM[0] * g] + [KM[l] * pltpu.roll(g, 8 - l, 0) for l in range(1, 8)]
            parts += [E[h] * AT[b, pl.ds(h, 1), :] for h in range(16)]
            DU[i, :, ln] += tree(parts)
            new.append(q8 * gs[b])
        return tuple(new), h1
    gs, h1 = lax.fori_loop(0, NK, body, (tuple(A0[b, :, ln] for b in range(NB)), H[:, ln]), unroll=unroll)
    H[:, ln] = h1


def sigmoid(v): return jax.nn.sigmoid(v)
def dot(a, b): return jnp.dot(a, b, preferred_element_type=f32)
def dot_nt(a, b): return lax.dot_general(a, b, (((1,), (1,)), ((), ())), preferred_element_type=f32)
def dot_tn(a, b): return lax.dot_general(a, b, (((0,), (0,)), ((), ())), preferred_element_type=f32)
def loop(n, f, unroll=1):
    def body(i, _):
        f(i); return 0
    lax.fori_loop(0, n, body, 0, unroll=unroll)
def ds(i, n): return pl.ds(pl.multiple_of(i * n, n), n)
def silu_and_slope(v):
    s = sigmoid(v)
    y = v * s
    return y, s + y * (1.0 - s)

class Params:
    def __init__(s, pos, ref, PRM, ss, rs):
        s.p, s.ref, s.PRM, s.ss, s.rs = pos, ref, PRM, ss, rs
    def r(s, row, n): return s.PRM.at[pl.ds(pl.multiple_of(row, 8), n), :]
    def cp(s, k, src, dst, dev, kr=None):
        return rcopy(src, dst, s.ss.at[k], s.rs.at[k if kr is None else kr], dev)
    def y0(s):
        p = s.p; row = (p.dp * 4 + p.z) * 48 + p.y * 24
        s.cp(0, s.ref, s.r(row, 24), p.yn).start()
        s.PRM[pl.ds(pl.multiple_of(row, 8), 24), :] = s.ref[...]
    def y1(s):
        p = s.p
        l = s.r((p.dp * 4 + p.z) * 48, 24)
        s.cp(0, l, l, p.yn).wait()
    def z0(s):
        p = s.p; u = s.r((p.dp * 4 + p.z) * 48, 48)
        @pl.when(p.z < 3)
        def _(): s.cp(1, u, u, p.up, 1 + p.z).start()
        @pl.when(p.z > 0)
        def _(): s.cp(2, u, u, p.dn, 1 + p.z).start()
    def zhop(s, h):
        p = s.p
        @pl.when(p.z >= h)
        def _():
            u = s.r((p.dp * 4 + p.z - h) * 48, 48)
            s.cp(1, u, u, p.up, 1 + p.z - h).wait_recv()
            @pl.when(p.z < 3)
            def _(): s.cp(2 + h, u, u, p.up, 1 + p.z - h).start()
        @pl.when(p.z + h <= 3)
        def _():
            u = s.r((p.dp * 4 + p.z + h) * 48, 48)
            s.cp(1, u, u, p.up, 1 + p.z + h).wait_recv()
            @pl.when(p.z > 0)
            def _(): s.cp(4 + h, u, u, p.dn, 1 + p.z + h).start()
    def x0(s):
        p = s.p; u = s.r(p.dp * 192, 192)
        s.cp(7, u, u, p.xn).start()
        s.cp(8, u, u, p.sib).start()
    def x1(s):
        p = s.p; u = s.r(p.dpx * 192, 192)
        s.cp(7, u, u, p.xn).wait_recv()
        s.cp(9, u, u, p.sib).start()
    def end(s):
        p = s.p; u = s.r(p.dp * 192, 192)
        s.cp(8, u, u, p.sib).wait_recv()
        s.cp(9, u, u, p.sib).wait_recv()
    def drain(s):
        p = s.p; u = s.r(p.dp * 192, 192); u1 = s.r(p.dp * 192, 48)
        for k in (7, 8, 9): s.cp(k, u, u, p.sib).wait_send()
        w = lambda k: s.cp(k, u1, u1, p.sib).wait_send()
        @pl.when(p.z < 3)
        def _(): w(1)
        @pl.when(p.z > 0)
        def _(): w(2)
        for h in (1, 2):
            @pl.when((p.z >= h) & (p.z < 3))
            def _(): w(2 + h)
            @pl.when((p.z + h <= 3) & (p.z > 0))
            def _(): w(4 + h)

class Scan:
    def __init__(s, pos, way, rate, W, L, Z, GR, ss, rs):
        s.p, s.way, s.rate, s.W, s.L, s.Z, s.GR, s.ss, s.rs = pos, way, rate, W, L, Z, GR, ss, rs
    def has(s, d): return (s.p.sq + d < 8) if d > 0 else (s.p.sq + d >= 0)
    def cp(s, k):
        d = s.way * 2 ** k
        return rcopy(s.W.at[k], s.L.at[k], s.ss.at[k], s.rs.at[k], (s.p.dp, jnp.clip(s.p.sq + d, 0, 7)))
    def send(s, k):
        @pl.when(s.has(s.way * 2 ** k))
        def _(): s.cp(k).start()
    def begin(s):
        g = jnp.exp(s.rate[0:16, :] * -256.0)
        s.GR[0] = g; s.GR[1] = g * g; s.GR[2] = g * g * g
        s.Z[...] = jnp.zeros_like(s.Z)
        s.send(0)
    def step(s, k):
        keep = lambda: (1.0, s.GR[0][None], s.GR[2][None])[k]
        grow = lambda: (s.GR[0][None], s.GR[1][None])[k]
        if k < 2: s.W[k + 1] = s.W[k].astype(s.W.dtype)
        @pl.when(s.has(-s.way * 2 ** k))
        def _():
            s.cp(k).wait_recv()
            s.Z[...] += keep() * s.L[k].astype(f32)
            if k < 2: s.W[k + 1] = (s.W[k + 1].astype(f32) + grow() * s.L[k].astype(f32)).astype(s.W.dtype)
        if k < 2: s.send(k + 1)
    def drain(s):
        for k in range(3):
            @pl.when(s.has(s.way * 2 ** k))
            def _(): s.cp(k).wait_send()

def full_barrier(p):
    bar = pltpu.get_barrier_semaphore()
    sig = lambda d: pl.semaphore_signal(bar, inc=1, device_id=d, device_id_type=MESH)
    sig(p.sib); sig(p.xn); sig(p.yn)
    for d in (1, 2, 4):
        @pl.when(p.sq + d < 8)
        def _(): sig((p.dp, jnp.minimum(p.sq + d, 7)))
        @pl.when(p.sq - d >= 0)
        def _(): sig((p.dp, jnp.maximum(p.sq - d, 0)))
    pl.semaphore_wait(bar, 3 + sum(jnp.clip(p.sq - d + 1, 0, 1) + jnp.clip(8 - d - p.sq, 0, 1) for d in (1, 2, 4)))

def first_exchange_start(p, mx, va, wo, wu, wd, WB, land, s0, r0):
    cps = {}
    @pl.when(p.y == 0)
    def _():
        rcopy(va, land.at[:, pl.ds(0, 1536)], s0.at[0], r0.at[0], p.yn).start()
        rcopy(wu, land.at[:, pl.ds(1536, 1536)], s0.at[1], r0.at[1], p.yn).start()
    @pl.when(p.y == 1)
    def _():
        rcopy(mx, land, s0.at[0], r0.at[0], p.yn).start()
    r = lambda yy: pl.ds(pl.multiple_of((p.dp * 4 + p.z) * RB + yy * 48, 48), 48)
    for yy, (own, far) in ((0, (wo, wd)), (1, (wd, wo))):
        @pl.when(p.y == yy)
        def _():
            rcopy(far, WB.at[r(yy), pl.ds((1 - yy) * HB, HB)], s0.at[2], r0.at[2], p.yn).start()
            pltpu.make_async_copy(own, WB.at[r(yy), pl.ds(yy * HB, HB)], s0.at[3]).start()

def first_exchange_end(p, mx, va, wo, wu, wd, WA, WB, land, s0, r0):
    rows = pl.ds(pl.multiple_of((p.dp * 4 + p.z) * RA, 16), RA)
    v1, v2 = land.at[:, pl.ds(0, 1536)], land.at[:, pl.ds(1536, 1536)]
    put = lambda c, w, lo, hi: WA.__setitem__((rows, pl.ds(c, w)), jnp.concatenate([lo[...].astype(f32), hi[...].astype(f32)], axis=0).astype(bf16))
    u = WB.at[pl.ds(pl.multiple_of((p.dp * 4 + p.z) * RB, 48), 48), pl.ds(0, HB)]
    @pl.when(p.y == 0)
    def _():
        rcopy(mx, land, s0.at[0], r0.at[0], p.yn).wait_recv()
        put(0, HA, mx, land)
    @pl.when(p.y == 1)
    def _():
        rcopy(va, v1, s0.at[0], r0.at[0], p.yn).wait_recv()
        rcopy(wu, v2, s0.at[1], r0.at[1], p.yn).wait_recv()
        put(HA, 1536, v1, va)
        put(HA + 1536, 1536, v2, wu)
        WA[rows, pl.ds(HA + 3072, 128)] = jnp.zeros((RA, 128), bf16)
    rcopy(u, u, s0.at[2], r0.at[2], p.yn).wait_recv()
    pltpu.make_async_copy(u, u, s0.at[3]).wait()
def first_exchange_drain(p, mx, va, wo, wu, wd, land, s0, r0):
    v1 = land.at[:, pl.ds(0, 1536)]
    @pl.when(p.y == 0)
    def _():
        rcopy(va, v1, s0.at[0], r0.at[0], p.yn).wait_send()
        rcopy(wu, v1, s0.at[1], r0.at[1], p.yn).wait_send()
    @pl.when(p.y == 1)
    def _(): rcopy(mx, land, s0.at[0], r0.at[0], p.yn).wait_send()
    rcopy(wo, wo, s0.at[2], r0.at[2], p.yn).wait_send()

def norm_rows(tok, PT, U, NL, i):
    x = tok[ds(i, 64), :].astype(f32)
    r = lax.rsqrt(jnp.mean(x * x, axis=-1, keepdims=True) + EPSILON)
    u = x * r * PT[32:33, :]
    U[ds(i, 8), :, :] = u.reshape(8, 8, 768)
    NL[ds(i, 64), :] = u.astype(bf16)

def sub8(v):
    return v.reshape(v.shape[0] // 8, 8, v.shape[1]).sum(axis=0)

FORWARD_OUT = (("wa", (768, 2 * HA), bf16), ("wb", (1536, 2 * HB), bf16), ("vl", (512, 1536), bf16), ("vs", (512, 1536), bf16),
    ("re", (512, 1536), bf16), ("rs", (512, 1536), bf16), ("at", (512, 1536), bf16), ("gt", (512, 1536), bf16), ("hi", (512, 1536), bf16), ("hs", (512, 1536), bf16),
    ("uc", (512, 768), bf16), ("du", (512, 768), bf16), ("om", (512, 768), bf16), ("sh", (512, 768), bf16), ("bs", (512, 768), bf16), ("n2", (512, 768), bf16),
    ("mi", (512, 768), f32), ("sp", (512, 128), f32), ("pr", (512, 128), f32), ("st", (64, 16, 768), f32), ("pt", (128, 768), f32), ("res", (512, 768), bf16), ("sq", (24, 768), f32))

def forward_kernel(tok, valid, affine, prm, mx, va, wo, wu, wd, *refs):
    no = len(FORWARD_OUT)
    outs, bufs, rest = refs[:no], refs[no:2 * no], refs[2 * no:]
    B = {name: r for (name, _, _), r in zip(FORWARD_OUT, bufs)}
    O = {name: r for (name, _, _), r in zip(FORWARD_OUT, outs)}
    osem = {name: i for i, (name, _, _) in enumerate(FORWARD_OUT)}
    (PRM, land, U, NL, BL, RSF, UPD, DIR, ACC, KS, W, L, Z, GR, s0, r0, sp_, rp_, ss, rs, sx, rx, so) = rest
    WA, WB, PT, S = B["wa"], B["wb"], B["pt"], B["st"]
    p = Pos()
    full_barrier(p)
    out = lambda name: pltpu.make_async_copy(B[name], O[name], so.at[osem[name]])
    def keep(*names):
        for name in names: out(name).start()
    par = Params(p, prm, PRM, sp_, rp_)
    par.y0()
    first_exchange_start(p, mx, va, wo, wu, wd, WB, land, s0, r0)
    g = Gather(p, (WA, WB), ss, rs)
    n = len(CHUNKS)
    def link(t):
        if t < n: g.z0(t)
        if 0 <= t - 1 < n: g.zhop(t - 1, 1)
        if 0 <= t - 2 < n: g.zhop(t - 2, 2)
        if 0 <= t - 3 < n: g.zhop(t - 3, 3); g.s1(t - 3)
        if 0 <= t - 4 < n: g.s2(t - 4)
        if 0 <= t - 5 < n: g.s3(t - 5)
        if 0 <= t - 6 < n: g.s4(t - 6)
    par.y1(); par.z0()
    first_exchange_end(p, mx, va, wo, wu, wd, WA, WB, land, s0, r0)
    link(0); par.zhop(1)
    link(1); par.zhop(2)
    link(2); par.zhop(3); par.x0()
    link(3); par.x1(); par.end()
    for j in range(6): PT[:, j * 128:(j + 1) * 128] = PRM[j * 128:(j + 1) * 128, :].T
    rate, ec, omega = PT.at[0:16, :], PT.at[16:32, :], PT.at[34:35, :]
    loop(8, lambda i: norm_rows(tok, PT, U, NL, i))
    link(4)
    def some(lo, hi, f):
        def body(j, _):
            f(j); return 0
        lax.fori_loop(lo, hi, body, 0)
    states = lambda j: fwd_states(U, rate, S, W.at[0], j, 4)
    some(0, 6, states)
    sc = Scan(p, 1, PT, W, L, Z, GR, sx, rx)
    sc.begin()
    link(5)
    sc.step(0); sc.step(1); sc.step(2)
    smooth = lambda j: fwd_smooth(U, S, Z, rate, ec, omega, BL, KS, j, 2)
    some(0, 3, smooth)
    link(6)
    some(3, 6, smooth)
    def shift_rows(i):
        y, s = silu_and_slope(BL[ds(i, 8), :, :].reshape(64, 768))
        B["sh"][ds(i, 64), :] = y.astype(bf16)
        B["bs"][ds(i, 64), :] = s.astype(bf16)
    loop(8, shift_rows)
    keep("st", "pt", "sh", "bs")
    link(7)
    def value(m):
        ACC[...] = dot(NL[...], WA[:, pl.ds(pl.multiple_of(HA + m * 256, 128), 256)])
        def rows(i):
            y, s = silu_and_slope(ACC[ds(i, 64), :])
            B["vl"][ds(i, 64), ds(m, 256)] = y.astype(bf16)
            B["vs"][ds(i, 64), ds(m, 256)] = s.astype(bf16)
        loop(8, rows)
    some(0, 2, value)
    def mixed(c, w=256): ACC[:, 0:w] = dot(B["sh"][...], WA[:, pl.ds(pl.multiple_of(c, 128), w)])
    def update(m):
        mixed(m * 256)
        loop(8, lambda i: UPD.__setitem__((ds(i, 64), ds(m, 256)), sigmoid(ACC[ds(i, 64), :])))
    def reset(m):
        mixed(896 + m * 256)
        def rows(i):
            y, s = silu_and_slope(ACC[ds(i, 64), :])
            RSF[ds(i, 64), ds(m, 256)] = y
            B["re"][ds(i, 64), ds(m, 256)] = y.astype(bf16)
            B["rs"][ds(i, 64), ds(m, 256)] = s.astype(bf16)
        loop(8, rows)
    def direct(m):
        mixed(2432 + m * 256)
        DIR[:, ds(m, 256)] = ACC[...]
    some(0, 2, update)
    link(8)
    some(2, 6, value)
    keep("vl", "vs")
    some(2, 3, update)
    mixed(768, 128)
    B["sp"][...] = ACC[:, 0:128]
    some(0, 1, reset)
    link(9)
    some(1, 6, reset)
    keep("re", "rs", "sp")
    link(10)
    def attend(b):
        rr = ds(b, 128)
        s = B["sp"][rr, :]
        s = s * sigmoid(s)
        q = (s * affine[0:1, :] + affine[1:2, :]).astype(bf16)
        k = (s * affine[2:3, :]).astype(bf16)
        t = dot_nt(q, k) * Z_SCALE
        ok = lax.broadcasted_iota(jnp.int32, (128, 128), 0) >= lax.broadcasted_iota(jnp.int32, (128, 128), 1)
        t = jnp.where(ok, t, -1e30)
        e = jnp.exp(t - jnp.max(t, axis=-1, keepdims=True))
        e = e / jnp.sum(e, axis=-1, keepdims=True)
        B["pr"][rr, :] = e
        el = e.astype(bf16)
        for m in range(6):
            c = pl.ds(m * 256, 256)
            a = dot(el, B["vl"][rr, c])
            B["at"][rr, c] = a.astype(bf16)
            B["gt"][rr, c] = (a * RSF[rr, c]).astype(bf16)
    loop(4, attend)
    some(0, 3, direct)
    keep("pr", "at", "gt")
    link(11)
    link(12)
    keep("wa", "wb")
    SQ = B["sq"]
    SQ[...] = jnp.zeros_like(SQ)
    def candidate(m):
        ACC[...] = dot(B["gt"][...], WB[:, ds(m, 256)])
        def rows(i):
            r, c = ds(i, 64), ds(m, 256)
            y, s = silu_and_slope(DIR[r, c] + ACC[r, :])
            u = UPD[r, c]
            x = tok[r, c].astype(f32)
            a = u * (y - x)
            B["mi"][r, c] = x + a
            B["uc"][r, c] = (u * s).astype(bf16)
            B["du"][r, c] = (a * (1.0 - u)).astype(bf16)
            B["om"][r, c] = (1.0 - u).astype(bf16)
            SQ[8:16, c] += sub8(valid[r, :] * a * a)
        loop(8, rows)
    some(0, 3, candidate)
    def second(i):
        v = B["mi"][ds(i, 64), :]
        r = lax.rsqrt(jnp.mean(v * v, axis=-1, keepdims=True) + EPSILON)
        B["n2"][ds(i, 64), :] = (v * r * PT[33:34, :]).astype(bf16)
    loop(8, second)
    keep("mi", "uc", "du", "om", "n2")
    def up(m):
        ACC[...] = dot(B["n2"][...], WA[:, pl.ds(pl.multiple_of(HA + 1536 + m * 256, 128), 256)])
        def rows(i):
            y, s = silu_and_slope(ACC[ds(i, 64), :])
            B["hi"][ds(i, 64), ds(m, 256)] = y.astype(bf16)
            B["hs"][ds(i, 64), ds(m, 256)] = s.astype(bf16)
        loop(8, rows)
    some(0, 6, up)
    keep("hi", "hs")
    def down(m):
        ACC[...] = dot(B["hi"][...], WB[:, pl.ds(pl.multiple_of(HB + m * 256, 128), 256)])
        def rows(i):
            r, c = ds(i, 64), ds(m, 256)
            f = ACC[r, :]
            o = B["mi"][r, c] + f
            B["res"][r, c] = o.astype(bf16)
            v = valid[r, :]
            SQ[0:8, c] += sub8(v * o * o)
            SQ[16:24, c] += sub8(v * f * f)
        loop(8, rows)
    some(0, 3, down)
    keep("res", "sq")
    for i in range(n): g.drain(i)
    par.drain(); sc.drain()
    first_exchange_drain(p, mx, va, wo, wu, wd, land, s0, r0)
    for name, _, _ in FORWARD_OUT: out(name).wait()

Z_SCALE = Z ** -0.5
def forward_call(tok, valid, affine, prm, mx, va, wo, wu, wd):
    n = len(CHUNKS)
    v = pltpu.VMEM
    D_ = pltpu.SemaphoreType.DMA
    return pl.pallas_call(forward_kernel,
        out_shape=tuple(jax.ShapeDtypeStruct(s, t) for _, s, t in FORWARD_OUT),
        in_specs=[pl.BlockSpec(memory_space=pltpu.VMEM)] * 9,
        out_specs=[pl.BlockSpec(memory_space=pl.ANY)] * len(FORWARD_OUT),
        scratch_shapes=[v(s, t) for _, s, t in FORWARD_OUT] + [v((768, 128), f32), v((24, HA), bf16), v((64, 8, 768), f32), v((512, 768), bf16),
            v((64, 8, 768), f32), v((512, 1536), f32), v((512, 768), f32), v((512, 768), f32), v((512, 256), f32), v((8, 128), f32),
            v((3, 2, 16, 768), f32), v((3, 2, 16, 768), f32), v((2, 16, 768), f32), v((3, 16, 768), f32),
            D_((4,)), D_((3,)), D_((10,)), D_((10,)), D_((n, 13)), D_((n, 13)), D_((3,)), D_((3,)), D_((len(FORWARD_OUT),))],
        compiler_params=pltpu.CompilerParams(collective_id=0, has_side_effects=True, vmem_limit_bytes=62 * 2**20),
    )(tok, valid, affine, prm, mx, va, wo, wu, wd)

class Tiny:
    def __init__(s, pos, T, L1, L2, L4, OUT, G, ss, rs):
        s.p, s.T, s.L1, s.L2, s.L4, s.OUT, s.G, s.ss, s.rs = pos, T, L1, L2, L4, OUT, G, ss, rs
    def r(s, xx, c, z=0, n=4): return s.T.at[pl.ds(pl.multiple_of(((xx * 2 + c) * 4 + z) * 48, 8), n * 48), :]
    def cp(s, k, src, dst, dev): return rcopy(src, dst, s.ss.at[k], s.rs.at[k], dev)
    def st0(s):
        for xx in (0, 1): s.cp(xx, s.r(xx, 1 - s.p.c), s.L1.at[xx], s.p.sib).start()
    def a0(s):
        p = s.p
        for xx in (0, 1):
            l = s.L1.at[xx]
            s.cp(xx, l, l, p.sib).wait_recv()
            t = s.r(xx, p.c)
            t[...] = t[...] + l[...]
        s.cp(2, s.r(1 - p.x, p.c), s.L2, p.xn).start()
    def a1(s):
        p = s.p
        s.cp(2, s.L2, s.L2, p.xn).wait_recv()
        t = s.r(p.x, p.c)
        t[...] = t[...] + s.L2[...]
    def own(s, t): return s.r(s.p.x, s.p.c, t, 1)
    def zsem(s, d, t): return 2 + t if d == 0 else 6 + t
    def zflow(s, d, z):
        p = s.p
        first = z == (0, 3)[d]
        on = tuple(range(3, z, -1)) if d == 0 else tuple(range(0, z))
        for t in on:
            l = s.L4.at[d, t]
            if not first:
                s.cp(s.zsem(d, t), l, l, p.sib).wait_recv()
                l[...] = l[...] + s.own(t)[...]
            s.cp(s.zsem(d, t), s.own(t) if first else l, l, p.up if d == 0 else p.dn).start()
        if not first:
            l = s.L4.at[d, z]
            s.cp(s.zsem(d, z), l, l, p.sib).wait_recv()
    def zstep(s, h):
        for z, d in ((h, 0), (3 - h, 1)):
            @pl.when(s.p.z == z)
            def _(): s.zflow(d, z)
    def fin(s):
        p = s.p
        for z in range(4):
            @pl.when(p.z == z)
            def _():
                t = s.own(z)
                v = t[...]
                if z > 0: v = v + s.L4[0, z]
                if z < 3: v = v + s.L4[1, z]
                t[...] = v
        row = ((p.x * 2 + p.c) * 4 + p.z) * 48
        far = s.T.at[pl.ds(pl.multiple_of(row + (1 - p.y) * 24, 8), 24), :]
        s.cp(9, far, s.G, p.yn).start()
    def last(s):
        p = s.p
        row = ((p.x * 2 + p.c) * 4 + p.z) * 48
        s.cp(9, s.G, s.G, p.yn).wait_recv()
        s.OUT[...] = s.T[pl.ds(pl.multiple_of(row + p.y * 24, 8), 24), :] + s.G[...]
    def drain(s):
        p = s.p
        for k, l in ((0, s.L1.at[0]), (1, s.L1.at[1]), (2, s.L2), (9, s.G)): s.cp(k, l, l, p.sib).wait_send()
        for d in (0, 1):
            for t in ((1, 2, 3), (0, 1, 2))[d]:
                l = s.L4.at[d, t]
                @pl.when((p.z < t) if d == 0 else (p.z > t))
                def _(): s.cp(s.zsem(d, t), l, l, p.sib).wait_send()

class Total:
    def __init__(s, pos, R, L, ss, rs):
        p = pos
        z1 = (p.dp, p.sq + 2 - 4 * (p.z % 2)); z2 = (p.dp, p.sq + 4 - 8 * (p.z // 2))
        s.to, s.R, s.L, s.ss, s.rs = (p.sib, p.xn, p.yn, z1, z2), R, L, ss, rs
    def cp(s, k): return rcopy(s.R.at[k], s.L.at[k], s.ss.at[k], s.rs.at[k], s.to[k])
    def send(s, k): s.cp(k).start()
    def step(s, k):
        s.cp(k).wait_recv()
        s.R[k + 1] = s.R[k] + s.L[k]
        if k < 4: s.send(k + 1)
    def drain(s):
        for k in range(5): s.cp(k).wait_send()

BACK_IN = ("wa", "wb", "vl", "vs", "re", "rs", "at", "gt", "hi", "hs", "uc", "du", "om", "sh", "bs", "n2", "mi", "sp", "pr", "st", "pt", "tok", "cot")
ORDER = (5, 6, 0, 1, 2, 3, 4)
ENTER = {5: 0, 6: 1, 0: 4, 1: 5, 2: 6, 3: 7, 4: 8}

def backward_kernel(valid, affine, sq, *refs):
    ni = len(BACK_IN)
    I = dict(zip(BACK_IN, refs[:ni]))
    (o_mx, o_va, o_up, o_wo, o_wd, o_gt, o_tiny, o_red) = refs[ni:ni + 8]
    (WA, WB, L1A, L1B, L2A, L2B, L3A, L3B, L4A, L4B, FA, FB, GA, GB_, TOK, PT, U, X0, X1, GT, GG, G1, H, KS, AT, ACC, W, L, Zb, GR,
     T, TL1, TL2, TL4, TG, TP, RR, RL, ss, rs, sx, rx, st_, rt_, sr, rr_, li, lo) = refs[ni + 8:]
    p = Pos()
    sem = {name: i for i, name in enumerate(BACK_IN)}
    def load(name, dst): pltpu.make_async_copy(I[name], dst, li.at[sem[name]]).start()
    def ready(name, dst): pltpu.make_async_copy(I[name], dst, li.at[sem[name]]).wait()
    n = len(CHUNKS)
    parts = ((0, 1536), (1536, 3072))
    def put(b, half, off, w, get):
        if b == 1: (o_wo, o_wd)[half][:, pl.ds(off, w)] = get(0, w)
        elif half == 0: o_mx[:, pl.ds(off, w)] = get(0, w)
        else:
            for (lo_, hi_), o in zip(parts, (o_va, o_up)):
                a, e = max(off, lo_), min(off + w, hi_)
                if a < e: o[:, pl.ds(a - lo_, e - a)] = get(a - off, e - a)
    g = Scatter(p, (WA, WB), (L1A, L1B), (L2A, L2B), (L3A, L3B), (L4A, L4B), (FA, FB), (GA, GB_), put, ss, rs)
    def link(t):
        for i in ORDER:
            r = t - ENTER[i]
            if r == 0: g.st0(i)
            if r == 1: g.a0(i); g.st1(i)
            if r == 2: g.a1(i); g.st2(i)
            if r == 3: g.a2(i); g.zstep(i, 0)
            if r in (4, 5, 6): g.zstep(i, r - 3)
            if r == 6: g.fin(i)
            if r == 7: g.last(i)
    v = lambda s, t: pltpu.VMEM(s, t)
    big, mid = v((512, 1536), bf16), v((512, 768), bf16)
    rate, ec, omega = PT.at[0:16, :], PT.at[16:32, :], PT.at[34:35, :]
    gain1, gain2 = PT.at[32:33, :], PT.at[33:34, :]
    def some(lo, hi, f):
        def body(j, _):
            f(j); return 0
        lax.fori_loop(lo, hi, body, 0)
    def at3(X, i): return X[ds(i, 8), :, :].reshape(64, 768)
    def dense(P0, P1, P2, P3, P4, P5, P6, GMX, Q0, Q1, Q2, Q3, Q4, SP, PR):
        load("cot", Q4); load("wb", WB); load("hi", P1); load("hs", P0); load("wa", WA); load("n2", Q1); load("tok", TOK); load("pt", PT)
        load("gt", P3); load("mi", X0); load("uc", Q2); load("du", Q3); load("rs", P4); load("vl", P5); load("vs", P6); load("sp", SP); load("pr", PR)
        full_barrier(p)
        GG[...] = jnp.zeros_like(GG)
        ready("cot", Q4)
        def low(i): Q0[ds(i, 64), :] = (Q4[ds(i, 64), :].astype(f32) * valid[ds(i, 64), :]).astype(bf16)
        loop(8, low)
        ready("wb", WB); ready("hs", P0); ready("hi", P1)
        def f_hidden(m):
            c = ds(m, 256)
            ACC[...] = dot_nt(Q0[...], WB[c, HB:])
            WB[c, HB:] = dot_tn(P1[:, c], Q0[...]).astype(bf16)
            def rows(i):
                r = ds(i, 64)
                P2[r, c] = (ACC[r, :] * P0[r, c].astype(f32)).astype(bf16)
            loop(8, rows)
        some(0, 6, f_hidden)
        load("at", P0); load("re", P1)
        ready("wa", WA); ready("n2", Q1)
        def f_up(m):
            c = ds(m, 256)
            X1[:, :, c] = dot_nt(P2[...], WA[c, HA + 1536:HA + 3072]).reshape(64, 8, 256)
            WA[c, HA + 1536:HA + 3072] = dot_tn(Q1[:, c], P2[...]).astype(bf16)
        some(0, 3, f_up)
        ready("mi", X0); ready("uc", Q2); ready("du", Q3); ready("pt", PT)
        load("sh", Q0);
        load("om", Q1)
        ready("om", Q1)
        def f_norm2(i):
            r = ds(i, 64)
            m_, k = at3(X0, i), at3(X1, i)
            inv = lax.rsqrt(jnp.mean(m_ * m_, axis=-1, keepdims=True) + EPSILON)
            unit = m_ * inv
            GG[0:8, :] += sub8(k * unit)
            k = k * gain2[...]
            gm = Q4[r, :].astype(f32) * valid[r, :] + inv * (k - unit * jnp.mean(k * unit, axis=-1, keepdims=True))
            GMX[r, 0:768] = (gm * Q3[r, :].astype(f32)).astype(bf16)
            GMX[r, 2432:3200] = (gm * Q2[r, :].astype(f32)).astype(bf16)
            GT[r, :] = gm * Q1[r, :].astype(f32)
        loop(8, f_norm2)
        ready("gt", P3); ready("at", P0); ready("re", P1); ready("rs", P4)
        def f_gated(m):
            c = ds(m, 256)
            ACC[...] = dot_nt(GMX[:, 2432:3200], WB[c, 0:HB])
            WB[c, 0:HB] = dot_tn(P3[:, c], GMX[:, 2432:3200]).astype(bf16)
            c2 = pl.ds(pl.multiple_of(896 + m * 256, 128), 256)
            def rows(i):
                r = ds(i, 64)
                a = ACC[r, :]
                P2[r, c] = (a * P1[r, c].astype(f32)).astype(bf16)
                GMX[r, c2] = (a * P0[r, c].astype(f32) * P4[r, c].astype(f32)).astype(bf16)
            loop(8, rows)
        some(0, 6, f_gated)
        link(0)
        load("bs", Q1)
        ready("tok", TOK)
        loop(8, lambda i: norm_rows(TOK, PT, U, Q2, i))
        link(1)
        ready("vl", P5); ready("vs", P6); ready("sp", SP); ready("pr", PR)
        RR[0] = jnp.zeros((8, 128), f32)
        def f_attend(b):
            r = ds(b, 128)
            pr = PR[r, :]
            gp = dot_nt(P2[r, :], P5[r, :])
            gs = (pr * (gp - jnp.sum(gp * pr, axis=-1, keepdims=True))).astype(bf16)
            el = pr.astype(bf16)
            for m in range(6):
                c = pl.ds(m * 256, 256)
                P6[r, c] = (dot_tn(el, P2[r, c]) * P6[r, c].astype(f32)).astype(bf16)
            s, slope = silu_and_slope(SP[r, :])
            q = (s * affine[0:1, :] + affine[1:2, :]).astype(bf16)
            k = (s * affine[2:3, :]).astype(bf16)
            gq = dot(gs, k) * Z_SCALE
            gk = dot_tn(gs, q) * Z_SCALE
            GMX[r, 768:896] = ((gq * affine[0:1, :] + gk * affine[2:3, :]) * slope).astype(bf16)
            for i, t in enumerate((gq * s, gq, gk * s)):
                RR[0, i:i + 1, :] += jnp.sum(t, axis=0, keepdims=True)
        loop(4, f_attend)
        link(2)
        ready("bs", Q1); ready("sh", Q0)
        def f_blend(m):
            c = ds(m, 256)
            ACC[...] = dot_nt(GMX[...], WA[c, 0:HA])
            X1[:, :, c] = dot_nt(P6[...], WA[c, HA:HA + 1536]).reshape(64, 8, 256)
            def rows(i):
                r, k = ds(i, 64), ds(i, 8)
                gb = ACC[r, :] * Q1[r, c].astype(f32)
                X0[k, :, c] = gb.reshape(8, 8, 256)
                GG[8:16, c] += sub8(gb * U[k, :, c].reshape(64, 256))
                X1[k, :, c] += (gb * omega[:, c]).reshape(8, 8, 256)
            loop(8, rows)
        some(0, 3, f_blend)
        link(3)
        for i in range(5):
            lo_, w = CHUNKS[i][1], CHUNKS[i][2]
            WA[:, lo_:lo_ + w] = dot_tn(Q0[...], GMX[:, lo_:lo_ + w]).astype(bf16)
            e = min(lo_ + w, 1536)
            if lo_ < e: WA[:, HA + lo_:HA + e] = dot_tn(Q2[...], P6[:, lo_:e]).astype(bf16)
            if lo_ + w == HA: WA[:, 2 * HA - 128:] = jnp.zeros((768, 128), bf16)
            link(4 + i)
    pl.run_scoped(dense, big, big, big, big, big, big, big, v((512, HA), bf16), mid, mid, mid, mid, mid, v((512, 128), f32), v((512, 128), f32))
    tot = Total(p, RR, RL, sr, rr_)
    for k in range(3):
        t = sub8(sq[pl.ds(k * 8, 8), :]).sum(axis=0, keepdims=True)
        RR[0, 3 + k:4 + k, :] = sum(t[:, j * 128:(j + 1) * 128] for j in range(6))
    RR[0, 6:7, :] = jnp.broadcast_to(jnp.sum(valid[...], axis=0, keepdims=True) * (1.0 / 128.0), (1, 128))
    tot.send(0)
    def average(S, A):
        load("st", S)
        ready("st", S)
        back = lambda j: bwd_states(X0, U, S, rate, A, W.at[0], G1, H, KS, j, 2)
        some(0, 3, back)
        link(9)
        some(3, 6, back)
        sc = Scan(p, -1, PT, W, L, Zb, GR, sx, rx)
        sc.begin()
        tot.step(0)
        link(10)
        sc.step(0)
        tot.step(1)
        sc.step(1)
        tot.step(2)
        sc.step(2)
        link(11)
        grad = lambda j: bwd_grad(X0, U, S, A, Zb, rate, ec, H, X1, KS, AT, j, 2)
        some(0, 3, grad)
        tot.step(3)
        link(12)
        some(3, 6, grad)
        tot.step(4)
        sc.drain()
    pl.run_scoped(average, v((64, 16, 768), f32), v((64, 16, 768), f32))
    o_red[...] = RR[5]
    GG[16:24, :] = jnp.zeros((8, 768), f32)
    def f_last(i):
        r = ds(i, 64)
        x = TOK[r, :].astype(f32)
        inv = lax.rsqrt(jnp.mean(x * x, axis=-1, keepdims=True) + EPSILON)
        unit = x * inv
        gn = at3(X1, i)
        GG[16:24, :] += sub8(gn * unit)
        k = gn * gain1[...]
        GT[r, :] += inv * (k - unit * jnp.mean(k * unit, axis=-1, keepdims=True))
    loop(8, f_last)
    fin = pltpu.make_async_copy(GT, o_gt, lo.at[0])
    fin.start()
    TP[...] = jnp.zeros_like(TP)
    TP[0:16, :] = G1[...]
    TP[16:32, :] = H[...]
    for k, i in ((32, 2), (33, 0), (34, 1)):
        TP[k:k + 1, :] = jnp.sum(GG[pl.ds(i * 8, 8), :], axis=0, keepdims=True)
    for j in range(6): T[j * 128:(j + 1) * 128, :] = TP[:, j * 128:(j + 1) * 128].T
    tiny = Tiny(p, T, TL1, TL2, TL4, o_tiny, TG, st_, rt_)
    tiny.st0()
    link(13)
    tiny.a0()
    link(14)
    tiny.a1(); tiny.zstep(0)
    link(15)
    for h in (1, 2, 3): tiny.zstep(h)
    tiny.fin()
    link(16)
    tiny.last()
    for i in range(n): g.drain(i)
    tiny.drain(); tot.drain()
    fin.wait()

def backward_call(valid, affine, sq, ins):
    n = len(CHUNKS)
    v = pltpu.VMEM
    D_ = pltpu.SemaphoreType.DMA
    sds = jax.ShapeDtypeStruct
    vm_, any_ = pl.BlockSpec(memory_space=pltpu.VMEM), pl.BlockSpec(memory_space=pl.ANY)
    return pl.pallas_call(backward_kernel,
        out_shape=(sds((24, 3200), f32), sds((24, 1536), f32), sds((24, 1536), f32), sds((48, 768), f32), sds((48, 768), f32), sds((512, 768), f32), sds((24, 128), f32), sds((8, 128), f32)),
        in_specs=[vm_] * 3 + [any_] * len(ins),
        out_specs=[vm_] * 5 + [any_] + [vm_] * 2,
        scratch_shapes=rs_scratch()[:14] + [v((512, 768), bf16), v((128, 768), f32), v((64, 8, 768), f32), v((64, 8, 768), f32), v((64, 8, 768), f32), v((512, 768), f32),
            v((24, 768), f32), v((16, 768), f32), v((16, 768), f32), v((8, 128), f32), v((2, 16, 128), f32), v((512, 256), f32),
            v((3, 2, 16, 768), bf16), v((3, 2, 16, 768), bf16), v((2, 16, 768), f32), v((3, 16, 768), f32),
            v((768, 128), f32), v((2, 192, 128), f32), v((192, 128), f32), v((2, 4, 48, 128), f32), v((24, 128), f32), v((128, 768), f32),
            v((6, 8, 128), f32), v((5, 8, 128), f32),
            D_((n, Scatter.NS)), D_((n, Scatter.NS)), D_((3,)), D_((3,)), D_((10,)), D_((10,)), D_((5,)), D_((5,)), D_((len(BACK_IN),)), D_((1,))],
        compiler_params=pltpu.CompilerParams(collective_id=1, has_side_effects=True, vmem_limit_bytes=63 * 2**20),
    )(valid, affine, sq, *ins)


def per_device_tuned(tokens, cotangent, lengths, w_mx, w_value, w_out, w_up, w_down, ema_rate, ema_in, ema_out, gains, qk_affine):
    rate_own, in_own, out_own = (t.astype(f32) for t in (ema_rate, ema_in, ema_out))
    scale_own = jnp.sqrt(-jnp.expm1(-2.0 * rate_own))
    mine = jnp.pad(jnp.concatenate([rate_own, out_own * scale_own * in_own, gains.astype(f32)], axis=1), ((0, 0), (0, 93)))
    seq_pos = lax.axis_index("seq") * SEQ_DEV + jnp.arange(SEQ_DEV, dtype=jnp.int32)
    valid = (seq_pos[None, :] < lengths[:, None]).astype(f32).reshape(512, 1)
    tok = tokens.reshape(512, D)
    affine = jnp.pad(qk_affine.astype(f32), ((0, 5), (0, 0)))
    kept = forward_call(tok, valid, affine, mine, w_mx, w_value, w_out, w_up, w_down)
    K = {name: t for (name, _, _), t in zip(FORWARD_OUT, kept)}
    K["tok"], K["cot"], K["mi"] = tok, cotangent.reshape(512, D), K["mi"].reshape(64, 8, 768)
    g_mx, g_va, g_up, g_wo, g_wd, g_tok, tiny, red = backward_call(valid, affine, K["sq"], [K[name] for name in BACK_IN])
    g1, h1 = tiny[:, :16], tiny[:, 16:32]
    grad_ema_out = in_own * scale_own * g1
    grad_ema_in = out_own * scale_own * g1
    grad_ema_rate = out_own * in_own * (jnp.exp(-2.0 * rate_own) / scale_own * g1 - scale_own * h1)
    sums = jnp.sum(red[3:7], axis=1)
    rms_values = jnp.sqrt(sums[:3] / (sums[3] * D))
    return (K["res"].reshape(tokens.shape), g_tok.reshape(tokens.shape), g_mx, g_va, g_wo, g_up, g_wd,
        grad_ema_rate, grad_ema_in, grad_ema_out, tiny[:, 32:35], red[:3], rms_values)


def solution(mesh):
    placed = (
        P("dp", "seq", None),
        P("dp", "seq", None),
        P("dp"),
        P(("dp", "seq"), None),
        P(("dp", "seq"), None),
        P(("dp", "seq"), None),
        P(("dp", "seq"), None),
        P(("dp", "seq"), None),
        P(("dp", "seq"), None),
        P(("dp", "seq"), None),
        P(("dp", "seq"), None),
        P(("dp", "seq"), None),
        P(),
    )
    step = per_device_tuned if dict(mesh.shape) == {"dp": 4, "seq": 8} else per_device
    return jax.shard_map(
        step,
        mesh=mesh,
        in_specs=placed,
        out_specs=(
            P("dp", "seq", None),
            P("dp", "seq", None),
            P(("dp", "seq"), None),
            P(("dp", "seq"), None),
            P(("dp", "seq"), None),
            P(("dp", "seq"), None),
            P(("dp", "seq"), None),
            P(("dp", "seq"), None),
            P(("dp", "seq"), None),
            P(("dp", "seq"), None),
            P(("dp", "seq"), None),
            P(),
            P(),
        ),
        check_vma=False,
    )
```

```python
import functools

import jax
import jax.numpy as jnp
from jax import lax
from jax.experimental import pallas as pl
from jax.experimental.pallas import tpu as pltpu
from jax.sharding import PartitionSpec as P

MESH = pl.DeviceIdType.MESH
bf16, f32 = jnp.bfloat16, jnp.float32
D = 768
Z = 128
V = 1536
SPAN = 128
SEQ_DEV = 256


EPSILON = 1e-06
TOP_PRECISION = lax.Precision.HIGHEST


def prefix(value, axis, join, neutral):
    count, mine = (lax.axis_size(axis), lax.axis_index(axis))
    pieces = jax.tree.map(lambda part: lax.all_gather(part, axis), value)
    so_far = jax.tree.map(
        lambda part, zero: jnp.full_like(part, 0) + jnp.asarray(zero, part.dtype), value, neutral
    )

    def lap(position, so_far):
        longer = join(so_far, jax.tree.map(lambda part: part[position], pieces))
        return jax.tree.map(lambda new, old: jnp.where(position < mine, new, old), longer, so_far)

    return lax.fori_loop(0, count - 1, lap, so_far)


def prefix_2(value, axis, combine, identity):
    length, here = (lax.axis_size(axis), lax.axis_index(axis))
    everything = jax.tree.map(
        lambda part, kind: lax.all_gather(part.astype(kind), axis),
        value,
        jax.tree.map(lambda a: jnp.bfloat16 if a.dtype == jnp.float32 else a.dtype, value),
    )
    start = jax.tree.map(
        lambda part, zero: jnp.broadcast_to(jnp.asarray(zero, part.dtype), part.shape),
        value,
        identity,
    )

    def lap(k, before):
        at = length - 1 - k
        reached = at > here
        new = combine(
            before, jax.tree.map(lambda part, own: part[at].astype(own.dtype), everything, value)
        )
        return jax.tree.map(lambda a, b: jnp.where(reached, a, b), new, before)

    return lax.fori_loop(0, length, lap, start)


def silu_slope(values):
    sigmoid = jax.nn.sigmoid(values)
    return sigmoid * (1.0 + values * (1.0 - sigmoid))


def chain_combine(earlier, later):
    return (earlier[0] * later[0], later[0] * earlier[1] + later[1])


def ema_local(rate, beta, eta, input_signal):
    rows_here, length, channels = input_signal.shape
    block_len = min(64, length)
    blocks_count = length // block_len
    lag_values = jnp.arange(block_len, dtype=jnp.float32)
    powers = jnp.exp(-lag_values[:, None, None] * rate[None])
    scale_in = jnp.sqrt(-jnp.expm1(-2.0 * rate)) * beta
    kernel = jnp.sum(powers * (eta * scale_in)[None], axis=2)
    step_ids = jnp.arange(block_len)
    lag_index = jnp.clip(step_ids[:, None] - step_ids[None, :], 0, block_len - 1)
    toeplitz = jnp.where(
        (step_ids[:, None] >= step_ids[None, :])[:, :, None], kernel[lag_index], 0.0
    )
    leading = jnp.exp(-(lag_values[:, None, None] + 1.0) * rate[None]) * eta[None]
    trailing = powers[::-1] * scale_in[None]
    block_decay = jnp.exp(-block_len * rate)
    blocks = jnp.swapaxes(input_signal.reshape(rows_here, blocks_count, block_len, channels), 0, 1)

    def advance(carried, segment):
        smooth = jnp.einsum("tsd,bsd->btd", toeplitz, segment, precision=TOP_PRECISION)
        smooth = smooth + jnp.einsum("tdh,bdh->btd", leading, carried, precision=TOP_PRECISION)
        carried = block_decay * carried + jnp.einsum(
            "sdh,bsd->bdh", trailing, segment, precision=TOP_PRECISION
        )
        return (carried, smooth)

    initial = jnp.zeros((rows_here, channels, rate.shape[1]), jnp.float32)
    final_state, smooth = lax.scan(advance, initial, blocks)
    return (jnp.swapaxes(smooth, 0, 1).reshape(rows_here, length, channels), final_state)


def ema_carry(rate, eta, incoming):
    block_len = min(64, SEQ_DEV)
    blocks_count = SEQ_DEV // block_len
    lag_values = jnp.arange(block_len, dtype=jnp.float32)
    leading = jnp.exp(-(lag_values[:, None, None] + 1.0) * rate[None]) * eta[None]
    block_decay = jnp.exp(-block_len * rate)

    def advance(carried, unused):
        return (
            block_decay * carried,
            jnp.einsum("tdh,bdh->btd", leading, carried, precision=TOP_PRECISION),
        )

    _, smooth = lax.scan(advance, incoming, None, length=blocks_count)
    return jnp.swapaxes(smooth, 0, 1).reshape(incoming.shape[0], SEQ_DEV, incoming.shape[1])


def per_device(
    tokens,
    cotangent,
    lengths,
    w_mx,
    w_value,
    w_out,
    w_up,
    w_down,
    ema_rate,
    ema_in,
    ema_out,
    gains,
    qk_affine,
):
    gathered = (
        lax.all_gather(w_mx, ("dp", "seq"), axis=0, tiled=True),
        lax.all_gather(w_value, ("dp", "seq"), axis=0, tiled=True),
        lax.all_gather(w_out, ("dp", "seq"), axis=0, tiled=True),
        lax.all_gather(w_up, ("dp", "seq"), axis=0, tiled=True),
        lax.all_gather(w_down, ("dp", "seq"), axis=0, tiled=True),
        lax.all_gather(ema_rate, ("dp", "seq"), axis=0, tiled=True),
        lax.all_gather(ema_in, ("dp", "seq"), axis=0, tiled=True),
        lax.all_gather(ema_out, ("dp", "seq"), axis=0, tiled=True),
        lax.all_gather(gains, ("dp", "seq"), axis=0, tiled=True),
    )
    mx_full, value_full, out_full, up_full, down_full, rate_low, beta_low, eta_low, gain_low = (
        gathered
    )
    rate = rate_low.astype(jnp.float32)
    beta = beta_low.astype(jnp.float32)
    eta = eta_low.astype(jnp.float32)
    gain_all = gain_low.astype(jnp.float32)
    gain_first = gain_all[:, 0]
    gain_second = gain_all[:, 1]
    omega_gain = gain_all[:, 2]
    affine = qk_affine.astype(jnp.float32)
    rows_here = tokens.shape[0]
    spans_dev = SEQ_DEV // SPAN
    score_scale = Z ** (-0.5)
    inputs = tokens.astype(jnp.float32)
    seq_pos = lax.axis_index("seq") * SEQ_DEV + jnp.arange(SEQ_DEV, dtype=jnp.int32)
    valid_rows = (seq_pos[None, :] < lengths[:, None]).astype(jnp.float32)[:, :, None]
    inverse1 = lax.rsqrt(jnp.mean(inputs * inputs, axis=-1, keepdims=True) + EPSILON)
    unit1 = inputs * inverse1
    normed = unit1 * gain_first
    normed_low = normed.astype(jnp.bfloat16)
    value_pre = jnp.einsum(
        "bsd,dv->bsv", normed_low, value_full, preferred_element_type=jnp.float32
    )
    value_low = jax.nn.silu(value_pre).astype(jnp.bfloat16)
    (smooth_local, end_local), pull_local = jax.vjp(ema_local, rate, beta, eta, normed)
    growth = jnp.exp(-SEQ_DEV * rate)
    start_state = prefix(
        (growth, end_local),
        "seq",
        chain_combine,
        (jnp.ones_like(growth), jnp.zeros_like(end_local)),
    )[1]
    smooth_carry, pull_carry = jax.vjp(ema_carry, rate, eta, start_state)
    blend = smooth_local + smooth_carry + omega_gain * normed
    shifted_low = jax.nn.silu(blend).astype(jnp.bfloat16)
    mixed = jnp.einsum("bsd,dk->bsk", shifted_low, mx_full, preferred_element_type=jnp.float32)
    update = jax.nn.sigmoid(mixed[..., :D])
    shared_pre = mixed[..., D : D + Z]
    shared = jax.nn.silu(shared_pre)
    reset_pre = mixed[..., D + Z : D + Z + V]
    reset = jax.nn.silu(reset_pre)
    direct = mixed[..., D + Z + V :]
    query_low = (
        (shared * affine[0] + affine[1]).astype(jnp.bfloat16).reshape(rows_here, spans_dev, SPAN, Z)
    )
    key_low = (shared * affine[2]).astype(jnp.bfloat16).reshape(rows_here, spans_dev, SPAN, Z)
    value_tiles = value_low.reshape(rows_here, spans_dev, SPAN, V)
    scores = (
        jnp.einsum("bnqz,bnkz->bnqk", query_low, key_low, preferred_element_type=jnp.float32)
        * score_scale
    )
    causal = jnp.arange(SPAN)[:, None] >= jnp.arange(SPAN)[None, :]
    masked = jnp.where(causal, scores, -1e30)
    peak = jnp.max(masked, axis=-1, keepdims=True)
    expo = jnp.exp(masked - peak)
    attention_weights = expo / jnp.sum(expo, axis=-1, keepdims=True)
    probs_low = attention_weights.astype(jnp.bfloat16)
    attended_output = jnp.einsum(
        "bnqk,bnkv->bnqv", probs_low, value_tiles, preferred_element_type=jnp.float32
    ).reshape(rows_here, SEQ_DEV, V)
    gated_low = (reset * attended_output).astype(jnp.bfloat16)
    cand_pre = direct + jnp.einsum(
        "bsv,vd->bsd", gated_low, out_full, preferred_element_type=jnp.float32
    )
    candidate = jax.nn.silu(cand_pre)
    attn_branch = update * (candidate - inputs)
    middle = inputs + attn_branch
    inverse2 = lax.rsqrt(jnp.mean(middle * middle, axis=-1, keepdims=True) + EPSILON)
    unit2 = middle * inverse2
    normed2_low = (unit2 * gain_second).astype(jnp.bfloat16)
    up_pre = jnp.einsum("bsd,df->bsf", normed2_low, up_full, preferred_element_type=jnp.float32)
    hidden_low = jax.nn.silu(up_pre).astype(jnp.bfloat16)
    ffn_branch = jnp.einsum(
        "bsf,fd->bsd", hidden_low, down_full, preferred_element_type=jnp.float32
    )
    output = middle + ffn_branch
    again = (
        lax.all_gather(w_mx, ("dp", "seq"), axis=0, tiled=True),
        lax.all_gather(w_value, ("dp", "seq"), axis=0, tiled=True),
        lax.all_gather(w_out, ("dp", "seq"), axis=0, tiled=True),
        lax.all_gather(w_up, ("dp", "seq"), axis=0, tiled=True),
        lax.all_gather(w_down, ("dp", "seq"), axis=0, tiled=True),
    )
    mixer_backward, value_back, out_back, up_back, down_back = again
    grad_out = cotangent.astype(jnp.float32) * valid_rows
    grad_out_low = grad_out.astype(jnp.bfloat16)
    grad_down = jnp.einsum(
        "bsf,bsd->fd", hidden_low, grad_out_low, preferred_element_type=jnp.float32
    )
    grad_hidden = jnp.einsum(
        "bsd,fd->bsf", grad_out_low, down_back, preferred_element_type=jnp.float32
    )
    grad_up_low = (grad_hidden * silu_slope(up_pre)).astype(jnp.bfloat16)
    grad_up = jnp.einsum(
        "bsd,bsf->df", normed2_low, grad_up_low, preferred_element_type=jnp.float32
    )
    grad_normed2 = jnp.einsum(
        "bsf,df->bsd", grad_up_low, up_back, preferred_element_type=jnp.float32
    )
    grad_gain_second = jnp.sum(grad_normed2 * unit2, axis=(0, 1))
    scaled2 = grad_normed2 * gain_second
    grad_middle = grad_out + inverse2 * (
        scaled2 - unit2 * jnp.mean(scaled2 * unit2, axis=-1, keepdims=True)
    )
    grad_update = grad_middle * (candidate - inputs)
    grad_cand_pre = grad_middle * update * silu_slope(cand_pre)
    grad_cand_low = grad_cand_pre.astype(jnp.bfloat16)
    grad_out_proj = jnp.einsum(
        "bsv,bsd->vd", gated_low, grad_cand_low, preferred_element_type=jnp.float32
    )
    grad_gated = jnp.einsum(
        "bsd,vd->bsv", grad_cand_low, out_back, preferred_element_type=jnp.float32
    )
    grad_reset = grad_gated * attended_output
    grad_attended_low = (
        (grad_gated * reset).astype(jnp.bfloat16).reshape(rows_here, spans_dev, SPAN, V)
    )
    grad_probs = jnp.einsum(
        "bnqv,bnkv->bnqk", grad_attended_low, value_tiles, preferred_element_type=jnp.float32
    )
    grad_values = jnp.einsum(
        "bnqk,bnqv->bnkv", probs_low, grad_attended_low, preferred_element_type=jnp.float32
    ).reshape(rows_here, SEQ_DEV, V)
    grad_scores_low = (
        attention_weights
        * (grad_probs - jnp.sum(grad_probs * attention_weights, axis=-1, keepdims=True))
    ).astype(jnp.bfloat16)
    grad_query = (
        jnp.einsum("bnqk,bnkz->bnqz", grad_scores_low, key_low, preferred_element_type=jnp.float32)
        * score_scale
    ).reshape(rows_here, SEQ_DEV, Z)
    grad_key = (
        jnp.einsum(
            "bnqk,bnqz->bnkz", grad_scores_low, query_low, preferred_element_type=jnp.float32
        )
        * score_scale
    ).reshape(rows_here, SEQ_DEV, Z)
    grad_affine = jnp.stack(
        [
            jnp.sum(grad_query * shared, axis=(0, 1)),
            jnp.sum(grad_query, axis=(0, 1)),
            jnp.sum(grad_key * shared, axis=(0, 1)),
        ]
    )
    grad_shared = grad_query * affine[0] + grad_key * affine[2]
    grad_mixed_low = jnp.concatenate(
        [
            grad_update * update * (1.0 - update),
            grad_shared * silu_slope(shared_pre),
            grad_reset * silu_slope(reset_pre),
            grad_cand_pre,
        ],
        axis=-1,
    ).astype(jnp.bfloat16)
    grad_mx = jnp.einsum(
        "bsd,bsk->dk", shifted_low, grad_mixed_low, preferred_element_type=jnp.float32
    )
    grad_shifted = jnp.einsum(
        "bsk,dk->bsd", grad_mixed_low, mixer_backward, preferred_element_type=jnp.float32
    )
    grad_blend = grad_shifted * silu_slope(blend)
    grad_omega = jnp.sum(grad_blend * normed, axis=(0, 1))
    grad_value_low = (grad_values * silu_slope(value_pre)).astype(jnp.bfloat16)
    grad_value_proj = jnp.einsum(
        "bsd,bsv->dv", normed_low, grad_value_low, preferred_element_type=jnp.float32
    )
    grad_normed = grad_blend * omega_gain + jnp.einsum(
        "bsv,dv->bsd", grad_value_low, value_back, preferred_element_type=jnp.float32
    )
    rate_from_carry, eta_from_carry, direct_adjoint = pull_carry(grad_blend)
    later_adjoint = prefix_2(
        (growth, direct_adjoint),
        "seq",
        chain_combine,
        (jnp.ones_like(growth), jnp.zeros_like(direct_adjoint)),
    )[1]
    rate_from_local, grad_beta, eta_from_local, normed_from_ema = pull_local(
        (grad_blend, later_adjoint)
    )
    rate_from_growth = jnp.sum(later_adjoint * start_state, axis=0) * (-SEQ_DEV * growth)
    grad_rate = rate_from_carry + rate_from_local + rate_from_growth
    grad_eta = eta_from_carry + eta_from_local
    grad_normed = grad_normed + normed_from_ema
    grad_gain_first = jnp.sum(grad_normed * unit1, axis=(0, 1))
    scaled1 = grad_normed * gain_first
    grad_tokens = grad_middle * (1.0 - update) + inverse1 * (
        scaled1 - unit1 * jnp.mean(scaled1 * unit1, axis=-1, keepdims=True)
    )
    grad_gains = jnp.stack([grad_gain_first, grad_gain_second, grad_omega], axis=1)
    shards = (
        lax.psum_scatter(grad_mx, ("dp", "seq"), scatter_dimension=0, tiled=True),
        lax.psum_scatter(grad_value_proj, ("dp", "seq"), scatter_dimension=0, tiled=True),
        lax.psum_scatter(grad_out_proj, ("dp", "seq"), scatter_dimension=0, tiled=True),
        lax.psum_scatter(grad_up, ("dp", "seq"), scatter_dimension=0, tiled=True),
        lax.psum_scatter(grad_down, ("dp", "seq"), scatter_dimension=0, tiled=True),
        lax.psum_scatter(grad_rate, ("dp", "seq"), scatter_dimension=0, tiled=True),
        lax.psum_scatter(grad_beta, ("dp", "seq"), scatter_dimension=0, tiled=True),
        lax.psum_scatter(grad_eta, ("dp", "seq"), scatter_dimension=0, tiled=True),
        lax.psum_scatter(grad_gains, ("dp", "seq"), scatter_dimension=0, tiled=True),
    )
    squares = jnp.stack(
        [
            jnp.sum(valid_rows * output * output),
            jnp.sum(valid_rows * attn_branch * attn_branch),
            jnp.sum(valid_rows * ffn_branch * ffn_branch),
            jnp.sum(valid_rows),
        ]
    )
    affine_total, square_total = lax.psum((grad_affine, squares), ("dp", "seq"))
    rms_values = jnp.sqrt(square_total[:3] / (square_total[3] * D))
    return (
        output.astype(jnp.bfloat16),
        grad_tokens,
        shards[0],
        shards[1],
        shards[2],
        shards[3],
        shards[4],
        shards[5],
        shards[6],
        shards[7],
        shards[8],
        affine_total,
        rms_values,
    )


HA, HB = 3200, 768
RA, RB = 48, 96

CHUNKS = [(0, 0, 256, "xy"), (0, 256, 256, "yx"), (0, 512, 384, "xy"), (0, 896, 384, "yx"), (0, 1280, 384, "xy"), (0, 1664, 384, "yx"),
    (0, 2048, 384, "xy"), (0, 2432, 384, "yx"), (0, 2816, 256, "xy"), (0, 3072, 128, "yx"),
    (1, 0, 256, "xy"), (1, 256, 128, "yx"), (1, 384, 128, "xy"), (1, 512, 256, "yx")]
GATHER_GROUPS = ((0, 1), (2, 3), (4, 5), (6, 7), (8, 9, 11, 12), (10, 13))
SCATTER_GROUPS = ((10, 13), (11, 12), (0, 1), (2, 3), (4, 5), (6, 7), (8, 9))

class Pos:
    def __init__(s):
        s.dp, s.sq = lax.axis_index("dp"), lax.axis_index("seq")
        s.x, s.c, s.z, s.y = s.dp // 2, s.dp % 2, s.sq // 2, s.sq % 2
        s.sib = (s.dp + 1 - 2 * s.c, s.sq)
        s.xn = (s.dp + 2 - 4 * s.x, s.sq)
        s.yn = (s.dp, s.sq + 1 - 2 * s.y)
        s.dpx = s.dp + 2 - 4 * s.x
    def zof(s, d): return (s.z + d) % 4
    def zn(s, d): return (s.dp, s.zof(d) * 2 + s.y)

def rcopy(src, dst, ss, rs, dev):
    return pltpu.make_async_remote_copy(src_ref=src, dst_ref=dst, send_sem=ss, recv_sem=rs, device_id=dev, device_id_type=MESH)

def full_barrier(p):
    bar = pltpu.get_barrier_semaphore()
    sig = lambda d: pl.semaphore_signal(bar, inc=1, device_id=d, device_id_type=MESH)
    for d in (p.sib, p.xn, p.yn, p.zn(1), p.zn(2), p.zn(3)): sig(d)
    @pl.when(p.sq < 7)
    def _(): sig((p.dp, jnp.minimum(p.sq + 1, 7)))
    @pl.when(p.sq > 0)
    def _(): sig((p.dp, jnp.maximum(p.sq - 1, 0)))
    pl.semaphore_wait(bar, 6 + jnp.clip(p.sq, 0, 1) + jnp.clip(7 - p.sq, 0, 1))

def at(ref, rows, nrows, half, w, off, width):
    return ref.at[pl.ds(pl.multiple_of(rows, 48), nrows), pl.ds(pl.multiple_of(half * w + off, 128), width)]

class Gather:
    def __init__(s, pos, bufs, ss, rs):
        s.p, s.bufs, s.ss, s.rs = pos, bufs, ss, rs
    def unit(s, i, dp, z, half, n=1):
        b, off, width, _ = CHUNKS[i]
        R = (RA, RB)[b]
        return at(s.bufs[b], (dp * 4 + z) * R, n * R, half, (HA, HB)[b], off, width)
    def cp(s, i, k, ref, dev):
        return rcopy(ref, ref, s.ss.at[i, k], s.rs.at[i, k], dev)
    def z0(s, i):
        p = s.p
        u = s.unit(i, p.dp, p.z, p.y)
        for d in (1, 3, 2): rcopy(u, u, s.ss.at[i, d - 1], s.rs.at[i, p.z], p.zn(d)).start()
    def s1(s, i):
        p = s.p
        for d in (1, 2, 3):
            u = s.unit(i, p.dp, p.zof(d), p.y)
            rcopy(u, u, s.ss.at[i, 0], s.rs.at[i, p.zof(d)], p.sib).wait_recv()
        u = s.unit(i, p.dp, 0, p.y, 4)
        s.cp(i, 4, u, p.xn if CHUNKS[i][3] == "xy" else p.yn).start()
        s.cp(i, 7, u, p.sib).start()
    def s1_in(s, i):
        p = s.p
        return s.unit(i, p.dpx, 0, p.y, 4) if CHUNKS[i][3] == "xy" else s.unit(i, p.dp, 0, 1 - p.y, 4)
    def s2(s, i):
        p = s.p
        r = s.s1_in(i)
        s.cp(i, 4, r, p.xn).wait_recv()
        nxt = p.yn if CHUNKS[i][3] == "xy" else p.xn
        s.cp(i, 5, s.unit(i, p.dp, 0, p.y, 4), nxt).start()
        s.cp(i, 6, r, nxt).start()
        s.cp(i, 8, r, p.sib).start()
    def s2_in(s, i):
        p = s.p
        if CHUNKS[i][3] == "xy":
            return s.unit(i, p.dp, 0, 1 - p.y, 4), s.unit(i, p.dpx, 0, 1 - p.y, 4)
        return s.unit(i, p.dpx, 0, p.y, 4), s.unit(i, p.dpx, 0, 1 - p.y, 4)
    def s3(s, i):
        for k, r in enumerate(s.s2_in(i)):
            s.cp(i, 5 + k, r, s.p.sib).wait_recv()
            s.cp(i, 9 + k, r, s.p.sib).start()
    def s4(s, i):
        u = s.unit(i, s.p.dp, 0, s.p.y, 4)
        for k in (7, 8, 9, 10): s.cp(i, k, u, s.p.sib).wait_recv()
    def tick(s, t):
        at_ = lambda k: GATHER_GROUPS[k] if 0 <= k < len(GATHER_GROUPS) else ()
        for i in at_(t): s.s1(i)
        for i in at_(t - 1): s.s2(i)
        for i in at_(t + 1): s.z0(i)
        for i in at_(t - 2): s.s3(i)
        for i in at_(t - 3): s.s4(i)
    def drain(s):
        p = s.p
        for i in range(len(CHUNKS)):
            u1 = s.unit(i, p.dp, 0, p.y)
            u = s.unit(i, p.dp, 0, p.y, 4)
            for k in (4, 5, 6, 7, 8, 9, 10): s.cp(i, k, u, p.sib).wait_send()
            for k in (0, 1, 2): s.cp(i, k, u1, p.sib).wait_send()

class Scatter:
    NS = 11
    def __init__(s, pos, P, L1, L2, L3, L4, F, G, out, ss, rs):
        s.p, s.P, s.L1, s.L2, s.L3, s.L4, s.F, s.G, s.out, s.ss, s.rs = pos, P, L1, L2, L3, L4, F, G, out, ss, rs
    def geom(s, i):
        b, off, w, order = CHUNKS[i]
        return b, (RA, RB)[b], (HA, HB)[b], off, w, order
    def cols(s, i, yy):
        b, R, W, off, w, _ = s.geom(i)
        return pl.ds(pl.multiple_of(yy * W + off, 128), w)
    def piece(s, i, xx, c, yy, z=0, n=4):
        b, R, W, off, w, _ = s.geom(i)
        return s.P[b].at[pl.ds(pl.multiple_of(((xx * 2 + c) * 4 + z) * R, 48), n * R), s.cols(i, yy)]
    def cp(s, i, k, src, dst, dev):
        return rcopy(src, dst, s.ss.at[i, k], s.rs.at[i, k], dev)
    def add(s, dst, src, nrows):
        def body(r, _):
            rr = pl.ds(pl.multiple_of(r * 48, 48), 48)
            dst[rr, :] = (dst[rr, :].astype(f32) + src[rr, :].astype(f32)).astype(bf16)
            return 0
        lax.fori_loop(0, nrows // 48, body, 0)
    def l1(s, i, xx, yy):
        return s.L1[CHUNKS[i][0]].at[xx, :, s.cols(i, yy)]
    def st0(s, i):
        p = s.p
        for k, (xx, yy) in enumerate(((0, 0), (0, 1), (1, 0), (1, 1))):
            s.cp(i, k, s.piece(i, xx, 1 - p.c, yy), s.l1(i, xx, yy), p.sib).start()
    def a0(s, i):
        R = s.geom(i)[1]
        for k, (xx, yy) in enumerate(((0, 0), (0, 1), (1, 0), (1, 1))):
            l = s.l1(i, xx, yy)
            s.cp(i, k, l, l, s.p.sib).wait_recv()
            s.add(s.piece(i, xx, s.p.c, yy), l, 4 * R)
    def l2(s, i, k):
        b, R, W, off, w, _ = s.geom(i)
        return s.L2[b].at[k, :, pl.ds(off, w)]
    def l3(s, i):
        b, R, W, off, w, _ = s.geom(i)
        return s.L3[b].at[:, pl.ds(off, w)]
    def st1(s, i):
        p, order = s.p, s.geom(i)[5]
        for k in (0, 1):
            src = s.piece(i, k, p.c, 1 - p.y) if order == "xy" else s.piece(i, 1 - p.x, p.c, k)
            s.cp(i, 4 + k, src, s.l2(i, k), p.yn if order == "xy" else p.xn).start()
    def a1(s, i):
        p = s.p; b, R, W, off, w, order = s.geom(i)
        for k in (0, 1):
            l = s.l2(i, k)
            s.cp(i, 4 + k, l, l, p.xn).wait_recv()
            s.add(s.piece(i, k, p.c, p.y) if order == "xy" else s.piece(i, p.x, p.c, k), l, 4 * R)
    def st2(s, i):
        p, order = s.p, s.geom(i)[5]
        src = s.piece(i, 1 - p.x, p.c, p.y) if order == "xy" else s.piece(i, p.x, p.c, 1 - p.y)
        s.cp(i, 6, src, s.l3(i), p.xn if order == "xy" else p.yn).start()
    def a2(s, i):
        l = s.l3(i)
        s.cp(i, 6, l, l, s.p.xn).wait_recv()
        s.add(s.piece(i, s.p.x, s.p.c, s.p.y), l, 4 * s.geom(i)[1])
    def l4(s, i, k):
        b, R, W, off, w, _ = s.geom(i)
        return s.L4[b].at[k, :, pl.ds(off, w)]
    def zsend(s, i):
        p = s.p
        for d in (1, 3, 2):
            rcopy(s.piece(i, p.x, p.c, p.y, p.zof(d), 1), s.l4(i, 3 - d), s.ss.at[i, 6 + d], s.rs.at[i, 10 - d], p.zn(d)).start()
    def fin(s, i):
        p = s.p; b, R, W, off, w, _ = s.geom(i)
        F, G, out = s.F[b], s.G[b], s.out
        h = R // 2
        t = s.piece(i, p.x, p.c, p.y, p.z, 1)[...].astype(f32)
        for k in range(3):
            l = s.l4(i, k)
            s.cp(i, 7 + k, l, l, p.sib).wait_recv()
            t = t + l[...].astype(f32)
        F[:, pl.ds(off, w)] = t
        src = F.at[pl.ds(pl.multiple_of((1 - p.y) * h, 8), h), pl.ds(off, w)]
        s.cp(i, 10, src, G.at[:, pl.ds(off, w)], p.yn).start()
        for yy in (0, 1):
            @pl.when(p.y == yy)
            def _(): out(b, yy, off, w, lambda o, k: F[pl.ds(yy * h, h), pl.ds(off + o, k)])
    def last(s, i):
        p = s.p; b, R, W, off, w, _ = s.geom(i)
        l = s.G[b].at[:, pl.ds(off, w)]
        s.cp(i, 10, l, l, p.yn).wait_recv()
        for yy in (0, 1):
            @pl.when(p.y == 1 - yy)
            def _(): s.out(b, yy, off, w, lambda o, k: l[:, pl.ds(o, k)])
    def tick(s, t, enter):
        st = [(t - e, grp) for e, grp in zip(enter, SCATTER_GROUPS)]
        for r, grp in st:
            for i in grp:
                if r == 1: s.a0(i); s.st1(i)
        for r, grp in st:
            for i in grp:
                if r == 2: s.a1(i); s.st2(i)
        for r, grp in st:
            for i in grp:
                if r == 0: s.st0(i)
                if r == 3: s.a2(i); s.zsend(i)
                if r == 4: s.fin(i)
                if r == 5: s.last(i)
    def drain(s):
        p = s.p
        for i in range(len(CHUNKS)):
            b, R, W, off, w, _ = s.geom(i)
            for k, ref in [(k, s.l1(i, 0, 0)) for k in range(4)] + [(4, s.l2(i, 0)), (5, s.l2(i, 1)), (6, s.l3(i)), (10, s.G[b].at[:, pl.ds(off, w)])] + [(7 + k, s.l4(i, k)) for k in range(3)]:
                s.cp(i, k, ref, ref, p.sib).wait_send()

def rs_scratch():
    v = pltpu.VMEM
    return [v((768, 2 * HA), bf16), v((1536, 2 * HB), bf16), v((2, 192, 2 * HA), bf16), v((2, 384, 2 * HB), bf16),
        v((2, 192, HA), bf16), v((2, 384, HB), bf16), v((192, HA), bf16), v((384, HB), bf16),
        v((3, 48, HA), bf16), v((3, 96, HB), bf16), v((48, HA), f32), v((96, HB), f32), v((24, HA), f32), v((48, HB), f32)]

NK = 32
NB = 2

def lanes(j): return pl.ds(pl.multiple_of(j * 128, 128), 128)
def rows_(i): return pl.ds(pl.multiple_of(i * 8, 8), 8)
def tree(xs):
    xs = list(xs)
    while len(xs) > 1:
        xs = [xs[i] + xs[i + 1] if i + 1 < len(xs) else xs[i] for i in range(0, len(xs), 2)]
    return xs[0]

def fwd_states(U, rate, S, END, j, unroll=2):
    ln = lanes(j)
    r = rate[0:16, ln]
    w = [jnp.exp(r * (s - 7.0)) for s in range(8)]
    q8 = jnp.exp(r * -8.0)
    def body(k, st):
        new = []
        for b in range(NB):
            S[b * NK + k, :, ln] = st[b]
            parts = [w[s] * U[b * NK + k, pl.ds(s, 1), ln] for s in range(8)]
            new.append(q8 * st[b] + tree(parts))
        return tuple(new)
    st = lax.fori_loop(0, NK, body, tuple(jnp.zeros((16, 128), f32) for _ in range(NB)), unroll=unroll)
    for b in range(NB): END[b, :, ln] = st[b]

def conv_tables(rate, ec, j):
    ln = lanes(j)
    it = lax.broadcasted_iota(jnp.int32, (8, 128), 0).astype(f32)
    E, K = [], []
    for h in range(16):
        rb = jnp.broadcast_to(rate[pl.ds(h, 1), ln], (8, 128)); eb = jnp.broadcast_to(ec[pl.ds(h, 1), ln], (8, 128))
        K.append(jnp.exp(-it * rb) * eb)
        E.append(jnp.exp(-(it + 1.0) * rb) * eb)
    return E, tree(K)

def fwd_smooth(U, S, S0, rate, ec, omega, BL, KS, j, unroll=1):
    ln = lanes(j)
    r = rate[0:16, ln]
    q8 = jnp.exp(r * -8.0)
    E, K = conv_tables(rate, ec, j)
    KS[...] = K
    ii = lax.broadcasted_iota(jnp.int32, (8, 128), 0)
    KM = [jnp.where(ii >= l, jnp.broadcast_to(KS[pl.ds(l, 1), :], (8, 128)), 0.0) for l in range(8)]
    om = jnp.broadcast_to(omega[:, ln], (8, 128))
    KM[0] = KM[0] + om
    def body(k, gs):
        new = []
        for b in range(NB):
            i = b * NK + k
            S[i, :, ln] = S[i, :, ln] + gs[b]
            u = U[i, :, ln]
            parts = [KM[0] * u] + [KM[l] * pltpu.roll(u, l, 0) for l in range(1, 8)]
            parts += [E[h] * S[i, pl.ds(h, 1), ln] for h in range(16)]
            BL[i, :, ln] = tree(parts)
            new.append(q8 * gs[b])
        return tuple(new)
    lax.fori_loop(0, NK, body, tuple(S0[b, :, ln] for b in range(NB)), unroll=unroll)

def bwd_states(Gr, U, S, rate, A, DIR, G1, H, CS, j, unroll=1):
    ln = lanes(j)
    r = rate[0:16, ln]
    w = [jnp.exp(r * -float(s)) for s in range(8)]
    q8 = jnp.exp(r * -8.0)
    def body(kk, c):
        k = NK - 1 - kk
        st, g1, h1, C = c
        new, C = [], list(C)
        for b in range(NB):
            i = b * NK + k
            A[i, :, ln] = st[b]
            p = [w[s] * Gr[i, pl.ds(s, 1), ln] for s in range(8)]
            Bg = tree(p)
            B1 = tree([p[s] if s == 1 else p[s] * float(s) for s in range(1, 8)])
            Sk = S[i, :, ln]
            g1 = g1 + Sk * Bg
            h1 = h1 + Sk * B1
            new.append(q8 * st[b] + Bg)
            u, g = U[i, :, ln], Gr[i, :, ln]
            C = [C[l] + g * (pltpu.roll(u, l, 0) if l else u) for l in range(8)]
        return tuple(new), g1, h1, tuple(C)
    z = jnp.zeros((16, 128), f32)
    st, g1, h1, C = lax.fori_loop(0, NK, body, (tuple(z for _ in range(NB)), z, z, tuple(jnp.zeros((8, 128), f32) for _ in range(8))), unroll=unroll)
    for b in range(NB): DIR[b, :, ln] = st[b].astype(DIR.dtype)
    ii = lax.broadcasted_iota(jnp.int32, (8, 128), 0)
    g1, h1 = g1 * w[1], h1 * w[1]
    for l in range(8):
        cl = jnp.sum(jnp.where(ii >= l, C[l], 0.0), axis=0, keepdims=True)
        t = w[l] * cl
        g1 = g1 + t
        if l: h1 = h1 + t * float(l)
    G1[:, ln] = g1
    H[:, ln] = h1

def bwd_grad(Gr, U, S, A, A0, rate, ec, H, DU, KS, AT, j, unroll=1):
    ln = lanes(j)
    r = rate[0:16, ln]
    q8 = jnp.exp(r * -8.0)
    c8 = 8.0 * jnp.exp(r * -9.0)
    wu = [jnp.exp(r * (s - 8.0)) * (8.0 - s) for s in range(8)]
    it = lax.broadcasted_iota(jnp.int32, (8, 128), 0).astype(f32)
    E, K = [], []
    for h in range(16):
        rb = jnp.broadcast_to(rate[pl.ds(h, 1), ln], (8, 128)); eb = jnp.broadcast_to(ec[pl.ds(h, 1), ln], (8, 128))
        K.append(jnp.exp(-it * rb) * eb)
        E.append(jnp.exp((it - 8.0) * rb) * eb)
    KS[...] = tree(K)
    ii = lax.broadcasted_iota(jnp.int32, (8, 128), 0)
    KM = [jnp.where(ii < 8 - l, jnp.broadcast_to(KS[pl.ds(l, 1), :], (8, 128)), 0.0) for l in range(8)]
    def body(kk, c):
        k = NK - 1 - kk
        gs, h1 = c
        new = []
        for b in range(NB):
            i = b * NK + k
            Ak = A[i, :, ln] + gs[b]
            AT[b] = Ak
            Bu = tree([wu[s] * U[i, pl.ds(s, 1), ln] for s in range(8)])
            h1 = h1 + Ak * (Bu + c8 * S[i, :, ln])
            g = Gr[i, :, ln]
            parts = [KM[0] * g] + [KM[l] * pltpu.roll(g, 8 - l, 0) for l in range(1, 8)]
            parts += [E[h] * AT[b, pl.ds(h, 1), :] for h in range(16)]
            DU[i, :, ln] += tree(parts)
            new.append(q8 * gs[b])
        return tuple(new), h1
    gs, h1 = lax.fori_loop(0, NK, body, (tuple(A0[b, :, ln] for b in range(NB)), H[:, ln]), unroll=unroll)
    H[:, ln] = h1


def sigmoid(v): return jax.nn.sigmoid(v)
def dot(a, b): return jnp.dot(a, b, preferred_element_type=f32)
def dot_nt(a, b): return lax.dot_general(a, b, (((1,), (1,)), ((), ())), preferred_element_type=f32)
def dot_tn(a, b): return lax.dot_general(a, b, (((0,), (0,)), ((), ())), preferred_element_type=f32)
def loop(n, f, unroll=1):
    def body(i, _):
        f(i); return 0
    lax.fori_loop(0, n, body, 0, unroll=unroll)
def ds(i, n): return pl.ds(pl.multiple_of(i * n, n), n)
def silu_and_slope(v):
    s = sigmoid(v)
    y = v * s
    return y, s + y * (1.0 - s)

class Params:
    def __init__(s, pos, ref, PRM, ss, rs):
        s.p, s.ref, s.PRM, s.ss, s.rs = pos, ref, PRM, ss, rs
    def r(s, row, n): return s.PRM.at[pl.ds(pl.multiple_of(row, 8), n), :]
    def cp(s, k, src, dst, dev, kr=None):
        return rcopy(src, dst, s.ss.at[k], s.rs.at[k if kr is None else kr], dev)
    def y0(s):
        p = s.p; row = (p.dp * 4 + p.z) * 48 + p.y * 24
        s.cp(0, s.ref, s.r(row, 24), p.yn).start()
        s.PRM[pl.ds(pl.multiple_of(row, 8), 24), :] = s.ref[...]
    def y1(s):
        p = s.p
        l = s.r((p.dp * 4 + p.z) * 48, 24)
        s.cp(0, l, l, p.yn).wait()
    def z0(s):
        p = s.p; u = s.r((p.dp * 4 + p.z) * 48, 48)
        for d in (1, 3, 2): s.cp(d, u, u, p.zn(d), 1 + p.z).start()
    def x0(s):
        p = s.p; u = s.r(p.dp * 192, 192)
        for d in (1, 2, 3):
            l = s.r((p.dp * 4 + p.zof(d)) * 48, 48)
            s.cp(1, l, l, p.sib, 1 + p.zof(d)).wait_recv()
        s.cp(7, u, u, p.xn).start()
        s.cp(8, u, u, p.sib).start()
    def x1(s):
        p = s.p; u = s.r(p.dpx * 192, 192)
        s.cp(7, u, u, p.xn).wait_recv()
        s.cp(9, u, u, p.sib).start()
    def end(s):
        p = s.p; u = s.r(p.dp * 192, 192)
        s.cp(8, u, u, p.sib).wait_recv()
        s.cp(9, u, u, p.sib).wait_recv()
    def drain(s):
        p = s.p; u = s.r(p.dp * 192, 192); u1 = s.r(p.dp * 192, 48)
        for k in (7, 8, 9): s.cp(k, u, u, p.sib).wait_send()
        for k in (1, 2, 3): s.cp(k, u1, u1, p.sib).wait_send()

class Scan:
    def __init__(s, pos, way, rate, W, L, Z, GR, ss, rs):
        s.p, s.way, s.rate, s.W, s.L, s.Z, s.GR, s.ss, s.rs = pos, way, rate, W, L, Z, GR, ss, rs
    def has(s, d): return (s.p.sq + d < 8) if d > 0 else (s.p.sq + d >= 0)
    def cp(s, k):
        d = s.way * 2 ** k
        return rcopy(s.W.at[k], s.L.at[k], s.ss.at[k], s.rs.at[k], (s.p.dp, jnp.clip(s.p.sq + d, 0, 7)))
    def send(s, k):
        @pl.when(s.has(s.way * 2 ** k))
        def _(): s.cp(k).start()
    def begin(s):
        g = jnp.exp(s.rate[0:16, :] * -256.0)
        s.GR[0] = g; s.GR[1] = g * g; s.GR[2] = g * g * g
        s.Z[...] = jnp.zeros_like(s.Z)
        s.send(0)
    def step(s, k):
        keep = lambda: (1.0, s.GR[0][None], s.GR[2][None])[k]
        grow = lambda: (s.GR[0][None], s.GR[1][None])[k]
        if k < 2: s.W[k + 1] = s.W[k].astype(s.W.dtype)
        @pl.when(s.has(-s.way * 2 ** k))
        def _():
            s.cp(k).wait_recv()
            s.Z[...] += keep() * s.L[k].astype(f32)
            if k < 2: s.W[k + 1] = (s.W[k + 1].astype(f32) + grow() * s.L[k].astype(f32)).astype(s.W.dtype)
        if k < 2: s.send(k + 1)
    def drain(s):
        for k in range(3):
            @pl.when(s.has(s.way * 2 ** k))
            def _(): s.cp(k).wait_send()

def first_exchange_start(p, mx, va, wo, wu, wd, WB, land, s0, r0):
    cps = {}
    @pl.when(p.y == 0)
    def _():
        rcopy(va, land.at[:, pl.ds(0, 1536)], s0.at[0], r0.at[0], p.yn).start()
        rcopy(wu, land.at[:, pl.ds(1536, 1536)], s0.at[1], r0.at[1], p.yn).start()
    @pl.when(p.y == 1)
    def _():
        rcopy(mx, land, s0.at[0], r0.at[0], p.yn).start()
    r = lambda yy: pl.ds(pl.multiple_of((p.dp * 4 + p.z) * RB + yy * 48, 48), 48)
    for yy, (own, far) in ((0, (wo, wd)), (1, (wd, wo))):
        @pl.when(p.y == yy)
        def _():
            rcopy(far, WB.at[r(yy), pl.ds((1 - yy) * HB, HB)], s0.at[2], r0.at[2], p.yn).start()
            pltpu.make_async_copy(own, WB.at[r(yy), pl.ds(yy * HB, HB)], s0.at[3]).start()

def first_exchange_end(p, mx, va, wo, wu, wd, WA, WB, land, s0, r0):
    rows = pl.ds(pl.multiple_of((p.dp * 4 + p.z) * RA, 16), RA)
    v1, v2 = land.at[:, pl.ds(0, 1536)], land.at[:, pl.ds(1536, 1536)]
    put = lambda c, w, lo, hi: WA.__setitem__((rows, pl.ds(c, w)), jnp.concatenate([lo[...].astype(f32), hi[...].astype(f32)], axis=0).astype(bf16))
    u = WB.at[pl.ds(pl.multiple_of((p.dp * 4 + p.z) * RB, 48), 48), pl.ds(0, HB)]
    @pl.when(p.y == 0)
    def _():
        rcopy(mx, land, s0.at[0], r0.at[0], p.yn).wait_recv()
        put(0, HA, mx, land)
    @pl.when(p.y == 1)
    def _():
        rcopy(va, v1, s0.at[0], r0.at[0], p.yn).wait_recv()
        rcopy(wu, v2, s0.at[1], r0.at[1], p.yn).wait_recv()
        put(HA, 1536, v1, va)
        put(HA + 1536, 1536, v2, wu)
        WA[rows, pl.ds(HA + 3072, 128)] = jnp.zeros((RA, 128), bf16)
    rcopy(u, u, s0.at[2], r0.at[2], p.yn).wait_recv()
    pltpu.make_async_copy(u, u, s0.at[3]).wait()
def first_exchange_drain(p, mx, va, wo, wu, wd, land, s0, r0):
    v1 = land.at[:, pl.ds(0, 1536)]
    @pl.when(p.y == 0)
    def _():
        rcopy(va, v1, s0.at[0], r0.at[0], p.yn).wait_send()
        rcopy(wu, v1, s0.at[1], r0.at[1], p.yn).wait_send()
    @pl.when(p.y == 1)
    def _(): rcopy(mx, land, s0.at[0], r0.at[0], p.yn).wait_send()
    rcopy(wo, wo, s0.at[2], r0.at[2], p.yn).wait_send()

def norm_rows(tok, PT, U, NL, i):
    x = tok[ds(i, 64), :].astype(f32)
    r = lax.rsqrt(jnp.mean(x * x, axis=-1, keepdims=True) + EPSILON)
    u = x * r * PT[32:33, :]
    U[ds(i, 8), :, :] = u.reshape(8, 8, 768)
    NL[ds(i, 64), :] = u.astype(bf16)

def sub8(v):
    return v.reshape(v.shape[0] // 8, 8, v.shape[1]).sum(axis=0)

FORWARD_OUT = (("wa", (768, 2 * HA), bf16), ("wb", (1536, 2 * HB), bf16), ("vl", (512, 1536), bf16), ("vs", (512, 1536), bf16),
    ("re", (512, 1536), bf16), ("rs", (512, 1536), bf16), ("at", (512, 1536), bf16), ("gt", (512, 1536), bf16), ("hi", (512, 1536), bf16), ("hs", (512, 1536), bf16),
    ("uc", (512, 768), bf16), ("du", (512, 768), bf16), ("om", (512, 768), bf16), ("sh", (512, 768), bf16), ("bs", (512, 768), bf16), ("n2", (512, 768), bf16),
    ("mi", (512, 768), f32), ("sp", (512, 128), f32), ("pr", (512, 128), f32), ("st", (64, 16, 768), f32), ("pt", (128, 768), f32), ("res", (512, 768), bf16), ("sq", (24, 768), f32))

def forward_kernel(tok, valid, affine, prm, mx, va, wo, wu, wd, *refs):
    no = len(FORWARD_OUT)
    outs, bufs, rest = refs[:no], refs[no:2 * no], refs[2 * no:]
    B = {name: r for (name, _, _), r in zip(FORWARD_OUT, bufs)}
    O = {name: r for (name, _, _), r in zip(FORWARD_OUT, outs)}
    osem = {name: i for i, (name, _, _) in enumerate(FORWARD_OUT)}
    (PRM, land, U, NL, BL, RSF, UPD, DIR, ACC, KS, W, L, Z, GR, s0, r0, sp_, rp_, ss, rs, sx, rx, so) = rest
    WA, WB, PT, S = B["wa"], B["wb"], B["pt"], B["st"]
    p = Pos()
    full_barrier(p)
    out = lambda name: pltpu.make_async_copy(B[name], O[name], so.at[osem[name]])
    def keep(*names):
        for name in names: out(name).start()
    par = Params(p, prm, PRM, sp_, rp_)
    par.y0()
    first_exchange_start(p, mx, va, wo, wu, wd, WB, land, s0, r0)
    g = Gather(p, (WA, WB), ss, rs)
    link = g.tick
    par.y1(); par.z0()
    first_exchange_end(p, mx, va, wo, wu, wd, WA, WB, land, s0, r0)
    for i in GATHER_GROUPS[0]: g.z0(i)
    par.x0(); par.x1(); par.end()
    link(0)
    for j in range(6): PT[:, j * 128:(j + 1) * 128] = PRM[j * 128:(j + 1) * 128, :].T
    rate, ec, omega = PT.at[0:16, :], PT.at[16:32, :], PT.at[34:35, :]
    loop(8, lambda i: norm_rows(tok, PT, U, NL, i))
    def some(lo, hi, f):
        def body(j, _):
            f(j); return 0
        lax.fori_loop(lo, hi, body, 0)
    states = lambda j: fwd_states(U, rate, S, W.at[0], j, 4)
    some(0, 6, states)
    sc = Scan(p, 1, PT, W, L, Z, GR, sx, rx)
    sc.begin()
    link(1)
    sc.step(0); sc.step(1); sc.step(2)
    smooth = lambda j: fwd_smooth(U, S, Z, rate, ec, omega, BL, KS, j, 2)
    some(0, 6, smooth)
    link(2)
    def shift_rows(i):
        y, s = silu_and_slope(BL[ds(i, 8), :, :].reshape(64, 768))
        B["sh"][ds(i, 64), :] = y.astype(bf16)
        B["bs"][ds(i, 64), :] = s.astype(bf16)
    loop(8, shift_rows)
    keep("st", "pt", "sh", "bs")
    def value(m):
        ACC[...] = dot(NL[...], WA[:, pl.ds(pl.multiple_of(HA + m * 256, 128), 256)])
        def rows(i):
            y, s = silu_and_slope(ACC[ds(i, 64), :])
            B["vl"][ds(i, 64), ds(m, 256)] = y.astype(bf16)
            B["vs"][ds(i, 64), ds(m, 256)] = s.astype(bf16)
        loop(8, rows)
    def mixed(c, w=256): ACC[:, 0:w] = dot(B["sh"][...], WA[:, pl.ds(pl.multiple_of(c, 128), w)])
    def update(m):
        mixed(m * 256)
        loop(8, lambda i: UPD.__setitem__((ds(i, 64), ds(m, 256)), sigmoid(ACC[ds(i, 64), :])))
    def reset(m):
        mixed(896 + m * 256)
        def rows(i):
            y, s = silu_and_slope(ACC[ds(i, 64), :])
            RSF[ds(i, 64), ds(m, 256)] = y
            B["re"][ds(i, 64), ds(m, 256)] = y.astype(bf16)
            B["rs"][ds(i, 64), ds(m, 256)] = s.astype(bf16)
        loop(8, rows)
    def direct(m):
        mixed(2432 + m * 256)
        DIR[:, ds(m, 256)] = ACC[...]
    def attend(b):
        rr = ds(b, 128)
        s = B["sp"][rr, :]
        s = s * sigmoid(s)
        q = (s * affine[0:1, :] + affine[1:2, :]).astype(bf16)
        k = (s * affine[2:3, :]).astype(bf16)
        t = dot_nt(q, k) * Z_SCALE
        ok = lax.broadcasted_iota(jnp.int32, (128, 128), 0) >= lax.broadcasted_iota(jnp.int32, (128, 128), 1)
        t = jnp.where(ok, t, -1e30)
        e = jnp.exp(t - jnp.max(t, axis=-1, keepdims=True))
        e = e / jnp.sum(e, axis=-1, keepdims=True)
        B["pr"][rr, :] = e
        el = e.astype(bf16)
        for m in range(6):
            c = pl.ds(m * 256, 256)
            a = dot(el, B["vl"][rr, c])
            B["at"][rr, c] = a.astype(bf16)
            B["gt"][rr, c] = (a * RSF[rr, c]).astype(bf16)
    link(3)
    some(0, 2, value)
    some(0, 2, update)
    link(4)
    some(2, 5, value)
    some(2, 3, update)
    mixed(768, 128)
    B["sp"][...] = ACC[:, 0:128]
    some(0, 1, reset)
    link(5)
    some(5, 6, value)
    keep("vl", "vs", "sp")
    some(1, 4, reset)
    link(6)
    some(4, 6, reset)
    keep("re", "rs")
    some(0, 1, direct)
    loop(4, attend)
    keep("pr", "at", "gt")
    link(7)
    some(1, 3, direct)
    link(8)
    keep("wa", "wb")
    SQ = B["sq"]
    SQ[...] = jnp.zeros_like(SQ)
    def candidate(m):
        ACC[...] = dot(B["gt"][...], WB[:, ds(m, 256)])
        def rows(i):
            r, c = ds(i, 64), ds(m, 256)
            y, s = silu_and_slope(DIR[r, c] + ACC[r, :])
            u = UPD[r, c]
            x = tok[r, c].astype(f32)
            a = u * (y - x)
            B["mi"][r, c] = x + a
            B["uc"][r, c] = (u * s).astype(bf16)
            B["du"][r, c] = (a * (1.0 - u)).astype(bf16)
            B["om"][r, c] = (1.0 - u).astype(bf16)
            SQ[8:16, c] += sub8(valid[r, :] * a * a)
        loop(8, rows)
    some(0, 3, candidate)
    def second(i):
        v = B["mi"][ds(i, 64), :]
        r = lax.rsqrt(jnp.mean(v * v, axis=-1, keepdims=True) + EPSILON)
        B["n2"][ds(i, 64), :] = (v * r * PT[33:34, :]).astype(bf16)
    loop(8, second)
    keep("mi", "uc", "du", "om", "n2")
    def up(m):
        ACC[...] = dot(B["n2"][...], WA[:, pl.ds(pl.multiple_of(HA + 1536 + m * 256, 128), 256)])
        def rows(i):
            y, s = silu_and_slope(ACC[ds(i, 64), :])
            B["hi"][ds(i, 64), ds(m, 256)] = y.astype(bf16)
            B["hs"][ds(i, 64), ds(m, 256)] = s.astype(bf16)
        loop(8, rows)
    some(0, 6, up)
    keep("hi", "hs")
    def down(m):
        ACC[...] = dot(B["hi"][...], WB[:, pl.ds(pl.multiple_of(HB + m * 256, 128), 256)])
        def rows(i):
            r, c = ds(i, 64), ds(m, 256)
            f = ACC[r, :]
            o = B["mi"][r, c] + f
            B["res"][r, c] = o.astype(bf16)
            v = valid[r, :]
            SQ[0:8, c] += sub8(v * o * o)
            SQ[16:24, c] += sub8(v * f * f)
        loop(8, rows)
    some(0, 3, down)
    keep("res", "sq")
    g.drain()
    par.drain(); sc.drain()
    first_exchange_drain(p, mx, va, wo, wu, wd, land, s0, r0)
    for name, _, _ in FORWARD_OUT: out(name).wait()

Z_SCALE = Z ** -0.5
def forward_call(tok, valid, affine, prm, mx, va, wo, wu, wd):
    n = len(CHUNKS)
    v = pltpu.VMEM
    D_ = pltpu.SemaphoreType.DMA
    return pl.pallas_call(forward_kernel,
        out_shape=tuple(jax.ShapeDtypeStruct(s, t) for _, s, t in FORWARD_OUT),
        in_specs=[pl.BlockSpec(memory_space=pltpu.VMEM)] * 9,
        out_specs=[pl.BlockSpec(memory_space=pl.ANY)] * len(FORWARD_OUT),
        scratch_shapes=[v(s, t) for _, s, t in FORWARD_OUT] + [v((768, 128), f32), v((24, HA), bf16), v((64, 8, 768), f32), v((512, 768), bf16),
            v((64, 8, 768), f32), v((512, 1536), f32), v((512, 768), f32), v((512, 768), f32), v((512, 256), f32), v((8, 128), f32),
            v((3, 2, 16, 768), f32), v((3, 2, 16, 768), f32), v((2, 16, 768), f32), v((3, 16, 768), f32),
            D_((4,)), D_((3,)), D_((10,)), D_((10,)), D_((n, 11)), D_((n, 11)), D_((3,)), D_((3,)), D_((len(FORWARD_OUT),))],
        compiler_params=pltpu.CompilerParams(collective_id=0, has_side_effects=True, vmem_limit_bytes=62 * 2**20),
    )(tok, valid, affine, prm, mx, va, wo, wu, wd)

class Tiny:
    def __init__(s, pos, T, L1, L2, L4, OUT, G, ss, rs):
        s.p, s.T, s.L1, s.L2, s.L4, s.OUT, s.G, s.ss, s.rs = pos, T, L1, L2, L4, OUT, G, ss, rs
    def r(s, xx, c, z=0, n=4): return s.T.at[pl.ds(pl.multiple_of(((xx * 2 + c) * 4 + z) * 48, 8), n * 48), :]
    def cp(s, k, src, dst, dev): return rcopy(src, dst, s.ss.at[k], s.rs.at[k], dev)
    def st0(s):
        for xx in (0, 1): s.cp(xx, s.r(xx, 1 - s.p.c), s.L1.at[xx], s.p.sib).start()
    def a0(s):
        p = s.p
        for xx in (0, 1):
            l = s.L1.at[xx]
            s.cp(xx, l, l, p.sib).wait_recv()
            t = s.r(xx, p.c)
            t[...] = t[...] + l[...]
        s.cp(2, s.r(1 - p.x, p.c), s.L2, p.xn).start()
    def a1(s):
        p = s.p
        s.cp(2, s.L2, s.L2, p.xn).wait_recv()
        t = s.r(p.x, p.c)
        t[...] = t[...] + s.L2[...]
    def zsend(s):
        p = s.p
        for d in (1, 3, 2): rcopy(s.r(p.x, p.c, p.zof(d), 1), s.L4.at[3 - d], s.ss.at[2 + d], s.rs.at[6 - d], p.zn(d)).start()
    def fin(s):
        p = s.p
        t = s.r(p.x, p.c, p.z, 1)
        v = t[...]
        for k in range(3):
            l = s.L4.at[k]
            s.cp(3 + k, l, l, p.sib).wait_recv()
            v = v + l[...]
        t[...] = v
        row = ((p.x * 2 + p.c) * 4 + p.z) * 48
        far = s.T.at[pl.ds(pl.multiple_of(row + (1 - p.y) * 24, 8), 24), :]
        s.cp(9, far, s.G, p.yn).start()
    def last(s):
        p = s.p
        row = ((p.x * 2 + p.c) * 4 + p.z) * 48
        s.cp(9, s.G, s.G, p.yn).wait_recv()
        s.OUT[...] = s.T[pl.ds(pl.multiple_of(row + p.y * 24, 8), 24), :] + s.G[...]
    def drain(s):
        p = s.p
        for k, l in ((0, s.L1.at[0]), (1, s.L1.at[1]), (2, s.L2), (9, s.G)): s.cp(k, l, l, p.sib).wait_send()
        for k in range(3): s.cp(3 + k, s.L4.at[k], s.L4.at[k], p.sib).wait_send()

class Total:
    def __init__(s, pos, R, L, ss, rs):
        p = pos
        z1 = (p.dp, p.sq + 2 - 4 * (p.z % 2)); z2 = (p.dp, p.sq + 4 - 8 * (p.z // 2))
        s.to, s.R, s.L, s.ss, s.rs = (p.sib, p.xn, p.yn, z1, z2), R, L, ss, rs
    def cp(s, k): return rcopy(s.R.at[k], s.L.at[k], s.ss.at[k], s.rs.at[k], s.to[k])
    def send(s, k): s.cp(k).start()
    def step(s, k):
        s.cp(k).wait_recv()
        s.R[k + 1] = s.R[k] + s.L[k]
        if k < 4: s.send(k + 1)
    def drain(s):
        for k in range(5): s.cp(k).wait_send()

BACK_IN = ("wa", "wb", "vl", "vs", "re", "rs", "at", "gt", "hi", "hs", "uc", "du", "om", "sh", "bs", "n2", "mi", "sp", "pr", "st", "pt", "tok", "cot")
ENTER = (0, 1, 3, 4, 5, 6, 7)

def backward_kernel(valid, affine, sq, *refs):
    ni = len(BACK_IN)
    I = dict(zip(BACK_IN, refs[:ni]))
    (o_mx, o_va, o_up, o_wo, o_wd, o_gt, o_tiny, o_red) = refs[ni:ni + 8]
    (WA, WB, L1A, L1B, L2A, L2B, L3A, L3B, L4A, L4B, FA, FB, GA, GB_, TOK, PT, U, X0, X1, GT, GG, G1, H, KS, AT, ACC, W, L, Zb, GR,
     T, TL1, TL2, TL4, TG, TP, RR, RL, ss, rs, sx, rx, st_, rt_, sr, rr_, li, lo, lw) = refs[ni + 8:]
    p = Pos()
    sem = {name: i for i, name in enumerate(BACK_IN)}
    def load(name, dst): pltpu.make_async_copy(I[name], dst, li.at[sem[name]]).start()
    def ready(name, dst): pltpu.make_async_copy(I[name], dst, li.at[sem[name]]).wait()
    whole = ((WB, "wb", HB, HB), (WA, "wa", HA + 1536, 1536), (WB, "wb", 0, HB), (WA, "wa", 0, HA + 1536))
    def part_copy(k):
        ref, name, c, w = whole[k]
        return pltpu.make_async_copy(I[name].at[:, pl.ds(c, w)], ref.at[:, pl.ds(c, w)], lw.at[k])
    def part(k): part_copy(k).start()
    parts = ((0, 1536), (1536, 3072))
    def put(b, half, off, w, get):
        if b == 1: (o_wo, o_wd)[half][:, pl.ds(off, w)] = get(0, w)
        elif half == 0: o_mx[:, pl.ds(off, w)] = get(0, w)
        else:
            for (lo_, hi_), o in zip(parts, (o_va, o_up)):
                a, e = max(off, lo_), min(off + w, hi_)
                if a < e: o[:, pl.ds(a - lo_, e - a)] = get(a - off, e - a)
    g = Scatter(p, (WA, WB), (L1A, L1B), (L2A, L2B), (L3A, L3B), (L4A, L4B), (FA, FB), (GA, GB_), put, ss, rs)
    def link(t): g.tick(t, ENTER)
    v = lambda s, t: pltpu.VMEM(s, t)
    big, mid = v((512, 1536), bf16), v((512, 768), bf16)
    rate, ec, omega = PT.at[0:16, :], PT.at[16:32, :], PT.at[34:35, :]
    gain1, gain2 = PT.at[32:33, :], PT.at[33:34, :]
    def some(lo, hi, f):
        def body(j, _):
            f(j); return 0
        lax.fori_loop(lo, hi, body, 0)
    def at3(X, i): return X[ds(i, 8), :, :].reshape(64, 768)
    def dense(P0, P1, P2, P3, P4, P5, P6, GMX, Q0, Q1, Q2, Q3, Q4, SP, PR, SHT, NLT):
        load("cot", Q4); part(0); load("hs", P0); load("hi", P1); part(1); load("n2", Q1); load("mi", X0); load("uc", Q2); load("du", Q3); load("pt", PT)
        part(2); load("gt", P3); load("rs", P4); load("vl", P5); load("vs", P6); load("sp", SP); load("pr", PR); part(3); load("tok", TOK)
        full_barrier(p)
        GG[...] = jnp.zeros_like(GG)
        ready("cot", Q4)
        def low(i): Q0[ds(i, 64), :] = (Q4[ds(i, 64), :].astype(f32) * valid[ds(i, 64), :]).astype(bf16)
        loop(8, low)
        part_copy(0).wait(); ready("hs", P0); ready("hi", P1)
        def f_hidden(m):
            c = ds(m, 256)
            ACC[...] = dot_nt(Q0[...], WB[c, HB:])
            WB[c, HB:] = dot_tn(P1[:, c], Q0[...]).astype(bf16)
            def rows(i):
                r = ds(i, 64)
                P2[r, c] = (ACC[r, :] * P0[r, c].astype(f32)).astype(bf16)
            loop(8, rows)
        some(0, 6, f_hidden)
        load("at", P0); load("re", P1)
        part_copy(1).wait(); ready("n2", Q1)
        def f_up(m):
            c = ds(m, 256)
            X1[:, :, c] = dot_nt(P2[...], WA[c, HA + 1536:HA + 3072]).reshape(64, 8, 256)
            WA[c, HA + 1536:HA + 3072] = dot_tn(Q1[:, c], P2[...]).astype(bf16)
        some(0, 3, f_up)
        ready("mi", X0); ready("uc", Q2); ready("du", Q3); ready("pt", PT)
        load("sh", Q0);
        load("om", Q1)
        ready("om", Q1)
        def f_norm2(i):
            r = ds(i, 64)
            m_, k = at3(X0, i), at3(X1, i)
            inv = lax.rsqrt(jnp.mean(m_ * m_, axis=-1, keepdims=True) + EPSILON)
            unit = m_ * inv
            GG[0:8, :] += sub8(k * unit)
            k = k * gain2[...]
            gm = Q4[r, :].astype(f32) * valid[r, :] + inv * (k - unit * jnp.mean(k * unit, axis=-1, keepdims=True))
            GMX[r, 0:768] = (gm * Q3[r, :].astype(f32)).astype(bf16)
            GMX[r, 2432:3200] = (gm * Q2[r, :].astype(f32)).astype(bf16)
            GT[r, :] = gm * Q1[r, :].astype(f32)
        loop(8, f_norm2)
        part_copy(2).wait(); ready("gt", P3); ready("at", P0); ready("re", P1); ready("rs", P4)
        def f_gated(m):
            c = ds(m, 256)
            ACC[...] = dot_nt(GMX[:, 2432:3200], WB[c, 0:HB])
            WB[c, 0:HB] = dot_tn(P3[:, c], GMX[:, 2432:3200]).astype(bf16)
            c2 = pl.ds(pl.multiple_of(896 + m * 256, 128), 256)
            def rows(i):
                r = ds(i, 64)
                a = ACC[r, :]
                P2[r, c] = (a * P1[r, c].astype(f32)).astype(bf16)
                GMX[r, c2] = (a * P0[r, c].astype(f32) * P4[r, c].astype(f32)).astype(bf16)
            loop(8, rows)
        some(0, 6, f_gated)
        link(0)
        load("bs", Q1)
        ready("tok", TOK)
        loop(8, lambda i: norm_rows(TOK, PT, U, Q2, i))
        link(1)
        ready("vl", P5); ready("vs", P6); ready("sp", SP); ready("pr", PR)
        RR[0] = jnp.zeros((8, 128), f32)
        def f_attend(b):
            r = ds(b, 128)
            pr = PR[r, :]
            gp = dot_nt(P2[r, :], P5[r, :])
            gs = (pr * (gp - jnp.sum(gp * pr, axis=-1, keepdims=True))).astype(bf16)
            el = pr.astype(bf16)
            for m in range(6):
                c = pl.ds(m * 256, 256)
                P6[r, c] = (dot_tn(el, P2[r, c]) * P6[r, c].astype(f32)).astype(bf16)
            s, slope = silu_and_slope(SP[r, :])
            q = (s * affine[0:1, :] + affine[1:2, :]).astype(bf16)
            k = (s * affine[2:3, :]).astype(bf16)
            gq = dot(gs, k) * Z_SCALE
            gk = dot_tn(gs, q) * Z_SCALE
            GMX[r, 768:896] = ((gq * affine[0:1, :] + gk * affine[2:3, :]) * slope).astype(bf16)
            for i, t in enumerate((gq * s, gq, gk * s)):
                RR[0, i:i + 1, :] += jnp.sum(t, axis=0, keepdims=True)
        loop(4, f_attend)
        link(2)
        part_copy(3).wait(); ready("bs", Q1); ready("sh", Q0)
        def f_blend(m):
            c = ds(m, 256)
            ACC[...] = dot_nt(GMX[...], WA[c, 0:HA])
            X1[:, :, c] = dot_nt(P6[...], WA[c, HA:HA + 1536]).reshape(64, 8, 256)
            def rows(i):
                r, k = ds(i, 64), ds(i, 8)
                gb = ACC[r, :] * Q1[r, c].astype(f32)
                X0[k, :, c] = gb.reshape(8, 8, 256)
                GG[8:16, c] += sub8(gb * U[k, :, c].reshape(64, 256))
                X1[k, :, c] += (gb * omega[:, c]).reshape(8, 8, 256)
            loop(8, rows)
        some(0, 3, f_blend)
        SHT[...] = Q0[...].T
        NLT[...] = Q2[...].T
        for k, (lo_, hi_) in enumerate(((0, 512), (512, 1280), (1280, 2048), (2048, 2816), (2816, 3200))):
            WA[:, lo_:hi_] = dot(SHT[...], GMX[:, lo_:hi_]).astype(bf16)
            e = min(hi_, 1536)
            if lo_ < e: WA[:, HA + lo_:HA + e] = dot(NLT[...], P6[:, lo_:e]).astype(bf16)
            if hi_ == HA: WA[:, 2 * HA - 128:] = jnp.zeros((768, 128), bf16)
            link(3 + k)
    pl.run_scoped(dense, big, big, big, big, big, big, big, v((512, HA), bf16), mid, mid, mid, mid, mid, v((512, 128), f32), v((512, 128), f32), v((768, 512), bf16), v((768, 512), bf16))
    tot = Total(p, RR, RL, sr, rr_)
    for k in range(3):
        t = sub8(sq[pl.ds(k * 8, 8), :]).sum(axis=0, keepdims=True)
        RR[0, 3 + k:4 + k, :] = sum(t[:, j * 128:(j + 1) * 128] for j in range(6))
    RR[0, 6:7, :] = jnp.broadcast_to(jnp.sum(valid[...], axis=0, keepdims=True) * (1.0 / 128.0), (1, 128))
    tot.send(0)
    def average(S, A):
        load("st", S)
        ready("st", S)
        back = lambda j: bwd_states(X0, U, S, rate, A, W.at[0], G1, H, KS, j, 2)
        some(0, 3, back)
        link(8)
        some(3, 6, back)
        sc = Scan(p, -1, PT, W, L, Zb, GR, sx, rx)
        sc.begin()
        tot.step(0)
        link(9)
        sc.step(0)
        tot.step(1)
        sc.step(1)
        tot.step(2)
        sc.step(2)
        link(10)
        grad = lambda j: bwd_grad(X0, U, S, A, Zb, rate, ec, H, X1, KS, AT, j, 2)
        some(0, 3, grad)
        tot.step(3)
        link(11)
        some(3, 6, grad)
        tot.step(4)
        sc.drain()
    pl.run_scoped(average, v((64, 16, 768), f32), v((64, 16, 768), f32))
    o_red[...] = RR[5]
    GG[16:24, :] = jnp.zeros((8, 768), f32)
    def f_last(i):
        r = ds(i, 64)
        x = TOK[r, :].astype(f32)
        inv = lax.rsqrt(jnp.mean(x * x, axis=-1, keepdims=True) + EPSILON)
        unit = x * inv
        gn = at3(X1, i)
        GG[16:24, :] += sub8(gn * unit)
        k = gn * gain1[...]
        GT[r, :] += inv * (k - unit * jnp.mean(k * unit, axis=-1, keepdims=True))
    loop(8, f_last)
    fin = pltpu.make_async_copy(GT, o_gt, lo.at[0])
    fin.start()
    TP[...] = jnp.zeros_like(TP)
    TP[0:16, :] = G1[...]
    TP[16:32, :] = H[...]
    for k, i in ((32, 2), (33, 0), (34, 1)):
        TP[k:k + 1, :] = jnp.sum(GG[pl.ds(i * 8, 8), :], axis=0, keepdims=True)
    for j in range(6): T[j * 128:(j + 1) * 128, :] = TP[:, j * 128:(j + 1) * 128].T
    tiny = Tiny(p, T, TL1, TL2, TL4, o_tiny, TG, st_, rt_)
    tiny.st0()
    tiny.a0()
    tiny.a1(); tiny.zsend()
    link(12)
    tiny.fin()
    tiny.last()
    g.drain()
    tiny.drain(); tot.drain()
    fin.wait()

def backward_call(valid, affine, sq, ins):
    n = len(CHUNKS)
    v = pltpu.VMEM
    D_ = pltpu.SemaphoreType.DMA
    sds = jax.ShapeDtypeStruct
    vm_, any_ = pl.BlockSpec(memory_space=pltpu.VMEM), pl.BlockSpec(memory_space=pl.ANY)
    return pl.pallas_call(backward_kernel,
        out_shape=(sds((24, 3200), f32), sds((24, 1536), f32), sds((24, 1536), f32), sds((48, 768), f32), sds((48, 768), f32), sds((512, 768), f32), sds((24, 128), f32), sds((8, 128), f32)),
        in_specs=[vm_] * 3 + [any_] * len(ins),
        out_specs=[vm_] * 5 + [any_] + [vm_] * 2,
        scratch_shapes=rs_scratch() + [v((512, 768), bf16), v((128, 768), f32), v((64, 8, 768), f32), v((64, 8, 768), f32), v((64, 8, 768), f32), v((512, 768), f32),
            v((24, 768), f32), v((16, 768), f32), v((16, 768), f32), v((8, 128), f32), v((2, 16, 128), f32), v((512, 256), f32),
            v((3, 2, 16, 768), bf16), v((3, 2, 16, 768), bf16), v((2, 16, 768), f32), v((3, 16, 768), f32),
            v((768, 128), f32), v((2, 192, 128), f32), v((192, 128), f32), v((3, 48, 128), f32), v((24, 128), f32), v((128, 768), f32),
            v((6, 8, 128), f32), v((5, 8, 128), f32),
            D_((n, Scatter.NS)), D_((n, Scatter.NS)), D_((3,)), D_((3,)), D_((10,)), D_((10,)), D_((5,)), D_((5,)), D_((len(BACK_IN),)), D_((1,)), D_((4,))],
        compiler_params=pltpu.CompilerParams(collective_id=1, has_side_effects=True, vmem_limit_bytes=63 * 2**20),
    )(valid, affine, sq, *ins)


def per_device_tuned(tokens, cotangent, lengths, w_mx, w_value, w_out, w_up, w_down, ema_rate, ema_in, ema_out, gains, qk_affine):
    rate_own, in_own, out_own = (t.astype(f32) for t in (ema_rate, ema_in, ema_out))
    scale_own = jnp.sqrt(-jnp.expm1(-2.0 * rate_own))
    mine = jnp.pad(jnp.concatenate([rate_own, out_own * scale_own * in_own, gains.astype(f32)], axis=1), ((0, 0), (0, 93)))
    seq_pos = lax.axis_index("seq") * SEQ_DEV + jnp.arange(SEQ_DEV, dtype=jnp.int32)
    valid = (seq_pos[None, :] < lengths[:, None]).astype(f32).reshape(512, 1)
    tok = tokens.reshape(512, D)
    affine = jnp.pad(qk_affine.astype(f32), ((0, 5), (0, 0)))
    kept = forward_call(tok, valid, affine, mine, w_mx, w_value, w_out, w_up, w_down)
    K = {name: t for (name, _, _), t in zip(FORWARD_OUT, kept)}
    K["tok"], K["cot"], K["mi"] = tok, cotangent.reshape(512, D), K["mi"].reshape(64, 8, 768)
    g_mx, g_va, g_up, g_wo, g_wd, g_tok, tiny, red = backward_call(valid, affine, K["sq"], [K[name] for name in BACK_IN])
    g1, h1 = tiny[:, :16], tiny[:, 16:32]
    grad_ema_out = in_own * scale_own * g1
    grad_ema_in = out_own * scale_own * g1
    grad_ema_rate = out_own * in_own * (jnp.exp(-2.0 * rate_own) / scale_own * g1 - scale_own * h1)
    sums = jnp.sum(red[3:7], axis=1)
    rms_values = jnp.sqrt(sums[:3] / (sums[3] * D))
    return (K["res"].reshape(tokens.shape), g_tok.reshape(tokens.shape), g_mx, g_va, g_wo, g_up, g_wd,
        grad_ema_rate, grad_ema_in, grad_ema_out, tiny[:, 32:35], red[:3], rms_values)


def solution(mesh):
    placed = (
        P("dp", "seq", None),
        P("dp", "seq", None),
        P("dp"),
        P(("dp", "seq"), None),
        P(("dp", "seq"), None),
        P(("dp", "seq"), None),
        P(("dp", "seq"), None),
        P(("dp", "seq"), None),
        P(("dp", "seq"), None),
        P(("dp", "seq"), None),
        P(("dp", "seq"), None),
        P(("dp", "seq"), None),
        P(),
    )
    step = per_device_tuned if dict(mesh.shape) == {"dp": 4, "seq": 8} else per_device
    return jax.shard_map(
        step,
        mesh=mesh,
        in_specs=placed,
        out_specs=(
            P("dp", "seq", None),
            P("dp", "seq", None),
            P(("dp", "seq"), None),
            P(("dp", "seq"), None),
            P(("dp", "seq"), None),
            P(("dp", "seq"), None),
            P(("dp", "seq"), None),
            P(("dp", "seq"), None),
            P(("dp", "seq"), None),
            P(("dp", "seq"), None),
            P(("dp", "seq"), None),
            P(),
            P(),
        ),
        check_vma=False,
    )
```

```python
import functools

import jax
import jax.numpy as jnp
from jax import lax
from jax.experimental import pallas as pl
from jax.experimental.pallas import tpu as pltpu
from jax.sharding import PartitionSpec as P

MESH = pl.DeviceIdType.MESH
bf16, f32 = jnp.bfloat16, jnp.float32
D = 768
Z = 128
V = 1536
SPAN = 128
SEQ_DEV = 256


EPSILON = 1e-06
TOP_PRECISION = lax.Precision.HIGHEST


def prefix(value, axis, join, neutral):
    count, mine = (lax.axis_size(axis), lax.axis_index(axis))
    pieces = jax.tree.map(lambda part: lax.all_gather(part, axis), value)
    so_far = jax.tree.map(
        lambda part, zero: jnp.full_like(part, 0) + jnp.asarray(zero, part.dtype), value, neutral
    )

    def lap(position, so_far):
        longer = join(so_far, jax.tree.map(lambda part: part[position], pieces))
        return jax.tree.map(lambda new, old: jnp.where(position < mine, new, old), longer, so_far)

    return lax.fori_loop(0, count - 1, lap, so_far)


def prefix_2(value, axis, combine, identity):
    length, here = (lax.axis_size(axis), lax.axis_index(axis))
    everything = jax.tree.map(
        lambda part, kind: lax.all_gather(part.astype(kind), axis),
        value,
        jax.tree.map(lambda a: jnp.bfloat16 if a.dtype == jnp.float32 else a.dtype, value),
    )
    start = jax.tree.map(
        lambda part, zero: jnp.broadcast_to(jnp.asarray(zero, part.dtype), part.shape),
        value,
        identity,
    )

    def lap(k, before):
        at = length - 1 - k
        reached = at > here
        new = combine(
            before, jax.tree.map(lambda part, own: part[at].astype(own.dtype), everything, value)
        )
        return jax.tree.map(lambda a, b: jnp.where(reached, a, b), new, before)

    return lax.fori_loop(0, length, lap, start)


def silu_slope(values):
    sigmoid = jax.nn.sigmoid(values)
    return sigmoid * (1.0 + values * (1.0 - sigmoid))


def chain_combine(earlier, later):
    return (earlier[0] * later[0], later[0] * earlier[1] + later[1])


def ema_local(rate, beta, eta, input_signal):
    rows_here, length, channels = input_signal.shape
    block_len = min(64, length)
    blocks_count = length // block_len
    lag_values = jnp.arange(block_len, dtype=jnp.float32)
    powers = jnp.exp(-lag_values[:, None, None] * rate[None])
    scale_in = jnp.sqrt(-jnp.expm1(-2.0 * rate)) * beta
    kernel = jnp.sum(powers * (eta * scale_in)[None], axis=2)
    step_ids = jnp.arange(block_len)
    lag_index = jnp.clip(step_ids[:, None] - step_ids[None, :], 0, block_len - 1)
    toeplitz = jnp.where(
        (step_ids[:, None] >= step_ids[None, :])[:, :, None], kernel[lag_index], 0.0
    )
    leading = jnp.exp(-(lag_values[:, None, None] + 1.0) * rate[None]) * eta[None]
    trailing = powers[::-1] * scale_in[None]
    block_decay = jnp.exp(-block_len * rate)
    blocks = jnp.swapaxes(input_signal.reshape(rows_here, blocks_count, block_len, channels), 0, 1)

    def advance(carried, segment):
        smooth = jnp.einsum("tsd,bsd->btd", toeplitz, segment, precision=TOP_PRECISION)
        smooth = smooth + jnp.einsum("tdh,bdh->btd", leading, carried, precision=TOP_PRECISION)
        carried = block_decay * carried + jnp.einsum(
            "sdh,bsd->bdh", trailing, segment, precision=TOP_PRECISION
        )
        return (carried, smooth)

    initial = jnp.zeros((rows_here, channels, rate.shape[1]), jnp.float32)
    final_state, smooth = lax.scan(advance, initial, blocks)
    return (jnp.swapaxes(smooth, 0, 1).reshape(rows_here, length, channels), final_state)


def ema_carry(rate, eta, incoming):
    block_len = min(64, SEQ_DEV)
    blocks_count = SEQ_DEV // block_len
    lag_values = jnp.arange(block_len, dtype=jnp.float32)
    leading = jnp.exp(-(lag_values[:, None, None] + 1.0) * rate[None]) * eta[None]
    block_decay = jnp.exp(-block_len * rate)

    def advance(carried, unused):
        return (
            block_decay * carried,
            jnp.einsum("tdh,bdh->btd", leading, carried, precision=TOP_PRECISION),
        )

    _, smooth = lax.scan(advance, incoming, None, length=blocks_count)
    return jnp.swapaxes(smooth, 0, 1).reshape(incoming.shape[0], SEQ_DEV, incoming.shape[1])


def per_device(
    tokens,
    cotangent,
    lengths,
    w_mx,
    w_value,
    w_out,
    w_up,
    w_down,
    ema_rate,
    ema_in,
    ema_out,
    gains,
    qk_affine,
):
    gathered = (
        lax.all_gather(w_mx, ("dp", "seq"), axis=0, tiled=True),
        lax.all_gather(w_value, ("dp", "seq"), axis=0, tiled=True),
        lax.all_gather(w_out, ("dp", "seq"), axis=0, tiled=True),
        lax.all_gather(w_up, ("dp", "seq"), axis=0, tiled=True),
        lax.all_gather(w_down, ("dp", "seq"), axis=0, tiled=True),
        lax.all_gather(ema_rate, ("dp", "seq"), axis=0, tiled=True),
        lax.all_gather(ema_in, ("dp", "seq"), axis=0, tiled=True),
        lax.all_gather(ema_out, ("dp", "seq"), axis=0, tiled=True),
        lax.all_gather(gains, ("dp", "seq"), axis=0, tiled=True),
    )
    mx_full, value_full, out_full, up_full, down_full, rate_low, beta_low, eta_low, gain_low = (
        gathered
    )
    rate = rate_low.astype(jnp.float32)
    beta = beta_low.astype(jnp.float32)
    eta = eta_low.astype(jnp.float32)
    gain_all = gain_low.astype(jnp.float32)
    gain_first = gain_all[:, 0]
    gain_second = gain_all[:, 1]
    omega_gain = gain_all[:, 2]
    affine = qk_affine.astype(jnp.float32)
    rows_here = tokens.shape[0]
    spans_dev = SEQ_DEV // SPAN
    score_scale = Z ** (-0.5)
    inputs = tokens.astype(jnp.float32)
    seq_pos = lax.axis_index("seq") * SEQ_DEV + jnp.arange(SEQ_DEV, dtype=jnp.int32)
    valid_rows = (seq_pos[None, :] < lengths[:, None]).astype(jnp.float32)[:, :, None]
    inverse1 = lax.rsqrt(jnp.mean(inputs * inputs, axis=-1, keepdims=True) + EPSILON)
    unit1 = inputs * inverse1
    normed = unit1 * gain_first
    normed_low = normed.astype(jnp.bfloat16)
    value_pre = jnp.einsum(
        "bsd,dv->bsv", normed_low, value_full, preferred_element_type=jnp.float32
    )
    value_low = jax.nn.silu(value_pre).astype(jnp.bfloat16)
    (smooth_local, end_local), pull_local = jax.vjp(ema_local, rate, beta, eta, normed)
    growth = jnp.exp(-SEQ_DEV * rate)
    start_state = prefix(
        (growth, end_local),
        "seq",
        chain_combine,
        (jnp.ones_like(growth), jnp.zeros_like(end_local)),
    )[1]
    smooth_carry, pull_carry = jax.vjp(ema_carry, rate, eta, start_state)
    blend = smooth_local + smooth_carry + omega_gain * normed
    shifted_low = jax.nn.silu(blend).astype(jnp.bfloat16)
    mixed = jnp.einsum("bsd,dk->bsk", shifted_low, mx_full, preferred_element_type=jnp.float32)
    update = jax.nn.sigmoid(mixed[..., :D])
    shared_pre = mixed[..., D : D + Z]
    shared = jax.nn.silu(shared_pre)
    reset_pre = mixed[..., D + Z : D + Z + V]
    reset = jax.nn.silu(reset_pre)
    direct = mixed[..., D + Z + V :]
    query_low = (
        (shared * affine[0] + affine[1]).astype(jnp.bfloat16).reshape(rows_here, spans_dev, SPAN, Z)
    )
    key_low = (shared * affine[2]).astype(jnp.bfloat16).reshape(rows_here, spans_dev, SPAN, Z)
    value_tiles = value_low.reshape(rows_here, spans_dev, SPAN, V)
    scores = (
        jnp.einsum("bnqz,bnkz->bnqk", query_low, key_low, preferred_element_type=jnp.float32)
        * score_scale
    )
    causal = jnp.arange(SPAN)[:, None] >= jnp.arange(SPAN)[None, :]
    masked = jnp.where(causal, scores, -1e30)
    peak = jnp.max(masked, axis=-1, keepdims=True)
    expo = jnp.exp(masked - peak)
    attention_weights = expo / jnp.sum(expo, axis=-1, keepdims=True)
    probs_low = attention_weights.astype(jnp.bfloat16)
    attended_output = jnp.einsum(
        "bnqk,bnkv->bnqv", probs_low, value_tiles, preferred_element_type=jnp.float32
    ).reshape(rows_here, SEQ_DEV, V)
    gated_low = (reset * attended_output).astype(jnp.bfloat16)
    cand_pre = direct + jnp.einsum(
        "bsv,vd->bsd", gated_low, out_full, preferred_element_type=jnp.float32
    )
    candidate = jax.nn.silu(cand_pre)
    attn_branch = update * (candidate - inputs)
    middle = inputs + attn_branch
    inverse2 = lax.rsqrt(jnp.mean(middle * middle, axis=-1, keepdims=True) + EPSILON)
    unit2 = middle * inverse2
    normed2_low = (unit2 * gain_second).astype(jnp.bfloat16)
    up_pre = jnp.einsum("bsd,df->bsf", normed2_low, up_full, preferred_element_type=jnp.float32)
    hidden_low = jax.nn.silu(up_pre).astype(jnp.bfloat16)
    ffn_branch = jnp.einsum(
        "bsf,fd->bsd", hidden_low, down_full, preferred_element_type=jnp.float32
    )
    output = middle + ffn_branch
    again = (
        lax.all_gather(w_mx, ("dp", "seq"), axis=0, tiled=True),
        lax.all_gather(w_value, ("dp", "seq"), axis=0, tiled=True),
        lax.all_gather(w_out, ("dp", "seq"), axis=0, tiled=True),
        lax.all_gather(w_up, ("dp", "seq"), axis=0, tiled=True),
        lax.all_gather(w_down, ("dp", "seq"), axis=0, tiled=True),
    )
    mixer_backward, value_back, out_back, up_back, down_back = again
    grad_out = cotangent.astype(jnp.float32) * valid_rows
    grad_out_low = grad_out.astype(jnp.bfloat16)
    grad_down = jnp.einsum(
        "bsf,bsd->fd", hidden_low, grad_out_low, preferred_element_type=jnp.float32
    )
    grad_hidden = jnp.einsum(
        "bsd,fd->bsf", grad_out_low, down_back, preferred_element_type=jnp.float32
    )
    grad_up_low = (grad_hidden * silu_slope(up_pre)).astype(jnp.bfloat16)
    grad_up = jnp.einsum(
        "bsd,bsf->df", normed2_low, grad_up_low, preferred_element_type=jnp.float32
    )
    grad_normed2 = jnp.einsum(
        "bsf,df->bsd", grad_up_low, up_back, preferred_element_type=jnp.float32
    )
    grad_gain_second = jnp.sum(grad_normed2 * unit2, axis=(0, 1))
    scaled2 = grad_normed2 * gain_second
    grad_middle = grad_out + inverse2 * (
        scaled2 - unit2 * jnp.mean(scaled2 * unit2, axis=-1, keepdims=True)
    )
    grad_update = grad_middle * (candidate - inputs)
    grad_cand_pre = grad_middle * update * silu_slope(cand_pre)
    grad_cand_low = grad_cand_pre.astype(jnp.bfloat16)
    grad_out_proj = jnp.einsum(
        "bsv,bsd->vd", gated_low, grad_cand_low, preferred_element_type=jnp.float32
    )
    grad_gated = jnp.einsum(
        "bsd,vd->bsv", grad_cand_low, out_back, preferred_element_type=jnp.float32
    )
    grad_reset = grad_gated * attended_output
    grad_attended_low = (
        (grad_gated * reset).astype(jnp.bfloat16).reshape(rows_here, spans_dev, SPAN, V)
    )
    grad_probs = jnp.einsum(
        "bnqv,bnkv->bnqk", grad_attended_low, value_tiles, preferred_element_type=jnp.float32
    )
    grad_values = jnp.einsum(
        "bnqk,bnqv->bnkv", probs_low, grad_attended_low, preferred_element_type=jnp.float32
    ).reshape(rows_here, SEQ_DEV, V)
    grad_scores_low = (
        attention_weights
        * (grad_probs - jnp.sum(grad_probs * attention_weights, axis=-1, keepdims=True))
    ).astype(jnp.bfloat16)
    grad_query = (
        jnp.einsum("bnqk,bnkz->bnqz", grad_scores_low, key_low, preferred_element_type=jnp.float32)
        * score_scale
    ).reshape(rows_here, SEQ_DEV, Z)
    grad_key = (
        jnp.einsum(
            "bnqk,bnqz->bnkz", grad_scores_low, query_low, preferred_element_type=jnp.float32
        )
        * score_scale
    ).reshape(rows_here, SEQ_DEV, Z)
    grad_affine = jnp.stack(
        [
            jnp.sum(grad_query * shared, axis=(0, 1)),
            jnp.sum(grad_query, axis=(0, 1)),
            jnp.sum(grad_key * shared, axis=(0, 1)),
        ]
    )
    grad_shared = grad_query * affine[0] + grad_key * affine[2]
    grad_mixed_low = jnp.concatenate(
        [
            grad_update * update * (1.0 - update),
            grad_shared * silu_slope(shared_pre),
            grad_reset * silu_slope(reset_pre),
            grad_cand_pre,
        ],
        axis=-1,
    ).astype(jnp.bfloat16)
    grad_mx = jnp.einsum(
        "bsd,bsk->dk", shifted_low, grad_mixed_low, preferred_element_type=jnp.float32
    )
    grad_shifted = jnp.einsum(
        "bsk,dk->bsd", grad_mixed_low, mixer_backward, preferred_element_type=jnp.float32
    )
    grad_blend = grad_shifted * silu_slope(blend)
    grad_omega = jnp.sum(grad_blend * normed, axis=(0, 1))
    grad_value_low = (grad_values * silu_slope(value_pre)).astype(jnp.bfloat16)
    grad_value_proj = jnp.einsum(
        "bsd,bsv->dv", normed_low, grad_value_low, preferred_element_type=jnp.float32
    )
    grad_normed = grad_blend * omega_gain + jnp.einsum(
        "bsv,dv->bsd", grad_value_low, value_back, preferred_element_type=jnp.float32
    )
    rate_from_carry, eta_from_carry, direct_adjoint = pull_carry(grad_blend)
    later_adjoint = prefix_2(
        (growth, direct_adjoint),
        "seq",
        chain_combine,
        (jnp.ones_like(growth), jnp.zeros_like(direct_adjoint)),
    )[1]
    rate_from_local, grad_beta, eta_from_local, normed_from_ema = pull_local(
        (grad_blend, later_adjoint)
    )
    rate_from_growth = jnp.sum(later_adjoint * start_state, axis=0) * (-SEQ_DEV * growth)
    grad_rate = rate_from_carry + rate_from_local + rate_from_growth
    grad_eta = eta_from_carry + eta_from_local
    grad_normed = grad_normed + normed_from_ema
    grad_gain_first = jnp.sum(grad_normed * unit1, axis=(0, 1))
    scaled1 = grad_normed * gain_first
    grad_tokens = grad_middle * (1.0 - update) + inverse1 * (
        scaled1 - unit1 * jnp.mean(scaled1 * unit1, axis=-1, keepdims=True)
    )
    grad_gains = jnp.stack([grad_gain_first, grad_gain_second, grad_omega], axis=1)
    shards = (
        lax.psum_scatter(grad_mx, ("dp", "seq"), scatter_dimension=0, tiled=True),
        lax.psum_scatter(grad_value_proj, ("dp", "seq"), scatter_dimension=0, tiled=True),
        lax.psum_scatter(grad_out_proj, ("dp", "seq"), scatter_dimension=0, tiled=True),
        lax.psum_scatter(grad_up, ("dp", "seq"), scatter_dimension=0, tiled=True),
        lax.psum_scatter(grad_down, ("dp", "seq"), scatter_dimension=0, tiled=True),
        lax.psum_scatter(grad_rate, ("dp", "seq"), scatter_dimension=0, tiled=True),
        lax.psum_scatter(grad_beta, ("dp", "seq"), scatter_dimension=0, tiled=True),
        lax.psum_scatter(grad_eta, ("dp", "seq"), scatter_dimension=0, tiled=True),
        lax.psum_scatter(grad_gains, ("dp", "seq"), scatter_dimension=0, tiled=True),
    )
    squares = jnp.stack(
        [
            jnp.sum(valid_rows * output * output),
            jnp.sum(valid_rows * attn_branch * attn_branch),
            jnp.sum(valid_rows * ffn_branch * ffn_branch),
            jnp.sum(valid_rows),
        ]
    )
    affine_total, square_total = lax.psum((grad_affine, squares), ("dp", "seq"))
    rms_values = jnp.sqrt(square_total[:3] / (square_total[3] * D))
    return (
        output.astype(jnp.bfloat16),
        grad_tokens,
        shards[0],
        shards[1],
        shards[2],
        shards[3],
        shards[4],
        shards[5],
        shards[6],
        shards[7],
        shards[8],
        affine_total,
        rms_values,
    )


HA, HB = 3200, 768
RA, RB = 48, 96

MXL, VAL, UPL, ONE, DWL = 1664, 1664, 2432, 768, 384
KINDS = ((0, 0, 1664), (0, 1664, 768), (0, 2432, 768), (1, 0, 384), (1, 384, 384))
GATHER_CHUNKS = ((0, 1664, 128, "xy"), (0, 1792, 128, "yx"), (0, 1920, 256, "xy"), (0, 2176, 256, "yx"), (0, 0, 384, "xy"), (0, 384, 384, "yx"), (0, 768, 384, "xy"), (0, 1152, 512, "yx"), (1, 0, 128, "xy"), (1, 128, 256, "yx"), (0, 2432, 128, "xy"), (0, 2560, 128, "yx"), (0, 2688, 128, "z"), (0, 2816, 128, "z"), (0, 2944, 128, "z"), (0, 3072, 128, "z"), (1, 384, 128, "xy"), (1, 512, 256, "yx"))
SCATTER_CHUNKS = ((1, 384, 128, "xy"), (1, 512, 128, "yx"), (1, 640, 128, "yx"), (0, 2432, 384, "xy"), (0, 2816, 384, "yx"), (1, 0, 256, "xy"), (1, 256, 128, "yx"), (0, 1664, 512, "yx"), (0, 2176, 256, "xy"), (0, 0, 384, "xy"), (0, 384, 384, "yx"), (0, 768, 256, "xy"), (0, 1024, 256, "yx"), (0, 1280, 128, "xy"), (0, 1408, 256, "yx"))

class Pos:
    def __init__(s):
        s.dp, s.sq = lax.axis_index("dp"), lax.axis_index("seq")
        s.x, s.c, s.z, s.y = s.dp // 2, s.dp % 2, s.sq // 2, s.sq % 2
        s.sib = (s.dp + 1 - 2 * s.c, s.sq)
        s.xn = (s.dp + 2 - 4 * s.x, s.sq)
        s.yn = (s.dp, s.sq + 1 - 2 * s.y)
        s.dpx = s.dp + 2 - 4 * s.x
    def zof(s, d): return (s.z + d) % 4
    def zn(s, d): return (s.dp, s.zof(d) * 2 + s.y)

def rcopy(src, dst, ss, rs, dev):
    return pltpu.make_async_remote_copy(src_ref=src, dst_ref=dst, send_sem=ss, recv_sem=rs, device_id=dev, device_id_type=MESH)

def full_barrier(p):
    bar = pltpu.get_barrier_semaphore()
    sig = lambda d: pl.semaphore_signal(bar, inc=1, device_id=d, device_id_type=MESH)
    for d in (p.sib, p.xn, p.yn, p.zn(1), p.zn(2), p.zn(3)): sig(d)
    pl.semaphore_wait(bar, 6)

def at(ref, rows, nrows, half, w, off, width):
    return ref.at[pl.ds(pl.multiple_of(rows, 48), nrows), pl.ds(pl.multiple_of(half * w + off, 128), width)]

class Gather:
    def __init__(s, pos, bufs, ss, rs):
        s.p, s.bufs, s.ss, s.rs, s.here = pos, bufs, ss, rs, set()
    def unit(s, i, dp, z, half, n=1):
        b, off, width, _ = GATHER_CHUNKS[i]
        R = (RA, RB)[b]
        return at(s.bufs[b], (dp * 4 + z) * R, n * R, half, (HA, HB)[b], off, width)
    def cp(s, i, k, ref, dev):
        return rcopy(ref, ref, s.ss.at[i, k], s.rs.at[i, k], dev)
    def z0(s, i):
        p = s.p
        u = s.unit(i, p.dp, p.z, p.y)
        for d in (1, 3, 2): rcopy(u, u, s.ss.at[i, d - 1], s.rs.at[i, p.z], p.zn(d)).start()
    def s1(s, i):
        p = s.p
        for d in (1, 2, 3):
            u = s.unit(i, p.dp, p.zof(d), p.y)
            rcopy(u, u, s.ss.at[i, 0], s.rs.at[i, p.zof(d)], p.sib).wait_recv()
        u = s.unit(i, p.dp, 0, p.y, 4)
        s.cp(i, 4, u, p.xn if GATHER_CHUNKS[i][3] == "xy" else p.yn).start()
        s.cp(i, 7, u, p.sib).start()
    def s2(s, i):
        p = s.p
        xy = GATHER_CHUNKS[i][3] == "xy"
        r = s.unit(i, p.dpx, 0, p.y, 4) if xy else s.unit(i, p.dp, 0, 1 - p.y, 4)
        s.cp(i, 4, r, p.xn).wait_recv()
        nxt = p.yn if xy else p.xn
        s.cp(i, 5, s.unit(i, p.dp, 0, p.y, 4), nxt).start()
        s.cp(i, 6, r, nxt).start()
        s.cp(i, 8, r, p.sib).start()
    def s3(s, i, k):
        p = s.p
        if GATHER_CHUNKS[i][3] == "xy": r = s.unit(i, (p.dp, p.dpx)[k], 0, 1 - p.y, 4)
        else: r = s.unit(i, p.dpx, 0, (p.y, 1 - p.y)[k], 4)
        s.cp(i, 5 + k, r, p.sib).wait_recv()
        s.cp(i, 9 + k, r, p.sib).start()
    def sa(s, i): s.s3(i, 0)
    def sb(s, i): s.s3(i, 1)
    def need(s, b, lo, hi):
        for i, (bb, off, w, _) in enumerate(GATHER_CHUNKS):
            if bb == b and off < hi and off + w > lo and i not in s.here:
                s.here.add(i)
                u = s.unit(i, s.p.dp, 0, s.p.y, 4)
                for k in (7, 8, 9, 10): s.cp(i, k, u, s.p.sib).wait_recv()
    def c1(s, i):
        s.cp(i, 4, s.unit(i, s.p.dp, s.p.z, s.p.y), s.p.xn).start()
    def c2(s, i):
        p = s.p
        r = s.unit(i, p.dpx, p.z, p.y)
        s.cp(i, 4, r, p.xn).wait_recv()
        s.cp(i, 5, s.unit(i, p.dp, p.z, p.y), p.yn).start()
        s.cp(i, 6, r, p.yn).start()
    def four(s, i, z):
        p = s.p
        return [s.unit(i, d, z, h) for d in (p.dp, p.dpx) for h in (p.y, 1 - p.y)]
    def c3(s, i):
        p = s.p
        us = s.four(i, p.z)
        s.cp(i, 5, us[1], p.yn).wait_recv()
        s.cp(i, 6, us[3], p.yn).wait_recv()
        for d in (1, 3, 2):
            for k, u in enumerate(us):
                rcopy(u, u, s.ss.at[i, 7 + 4 * d + k], s.rs.at[i, 11 + 4 * (d - 1) + k], p.zn(d)).start()
    def c4(s, i):
        p = s.p
        for d in (1, 2, 3):
            for k, u in enumerate(s.four(i, p.z)):
                rcopy(u, u, s.ss.at[i, 0], s.rs.at[i, 11 + 4 * (d - 1) + k], p.sib).wait_recv()
        for k, (d, h) in enumerate(((p.dp, p.y), (p.dpx, p.y), (p.dp, 1 - p.y), (p.dpx, 1 - p.y))):
            s.cp(i, 7 + k, s.unit(i, d, 0, h, 4), p.sib).start()
    def steps(s): return (s.z0, s.s1, s.s2, s.sa, s.sb, s.c1, s.c2, s.c3, s.c4)
    def drain(s):
        p = s.p
        for i, (_, _, _, order) in enumerate(GATHER_CHUNKS):
            u1 = s.unit(i, p.dp, 0, p.y)
            u = s.unit(i, p.dp, 0, p.y, 4)
            one = (4, 5, 6) + tuple(range(11, 23)) if order == "z" else (0, 1, 2)
            for k in one: s.cp(i, k, u1, p.sib).wait_send()
            for k in range(4, 11):
                if k not in one: s.cp(i, k, u, p.sib).wait_send()

class Scatter:
    NS = 11
    def __init__(s, pos, P, L1, L2, L3, L4, F, G, out, ss, rs):
        s.p, s.P, s.L1, s.L2, s.L3, s.L4, s.F, s.G, s.out, s.ss, s.rs = pos, P, L1, L2, L3, L4, F, G, out, ss, rs
    def geom(s, i):
        b, off, w, order = SCATTER_CHUNKS[i]
        return b, (RA, RB)[b], (HA, HB)[b], off, w, order
    def cols(s, i, yy):
        b, R, W, off, w, _ = s.geom(i)
        return pl.ds(pl.multiple_of(yy * W + off, 128), w)
    def piece(s, i, xx, c, yy, z=0, n=4):
        b, R, W, off, w, _ = s.geom(i)
        return s.P[b].at[pl.ds(pl.multiple_of(((xx * 2 + c) * 4 + z) * R, 48), n * R), s.cols(i, yy)]
    def cp(s, i, k, src, dst, dev):
        return rcopy(src, dst, s.ss.at[i, k], s.rs.at[i, k], dev)
    def add(s, dst, src, nrows):
        def body(r, _):
            rr = pl.ds(pl.multiple_of(r * 48, 48), 48)
            dst[rr, :] = (dst[rr, :].astype(f32) + src[rr, :].astype(f32)).astype(bf16)
            return 0
        lax.fori_loop(0, nrows // 48, body, 0)
    def l1(s, i, xx, yy):
        return s.L1[SCATTER_CHUNKS[i][0]].at[xx, :, s.cols(i, yy)]
    def st0(s, i):
        p = s.p
        for k, (xx, yy) in enumerate(((0, 0), (0, 1), (1, 0), (1, 1))):
            s.cp(i, k, s.piece(i, xx, 1 - p.c, yy), s.l1(i, xx, yy), p.sib).start()
    def a0(s, i):
        R = s.geom(i)[1]
        for k, (xx, yy) in enumerate(((0, 0), (0, 1), (1, 0), (1, 1))):
            l = s.l1(i, xx, yy)
            s.cp(i, k, l, l, s.p.sib).wait_recv()
            s.add(s.piece(i, xx, s.p.c, yy), l, 4 * R)
    def l2(s, i, k):
        b, R, W, off, w, _ = s.geom(i)
        return s.L2[b].at[k, :, pl.ds(off, w)]
    def l3(s, i):
        b, R, W, off, w, _ = s.geom(i)
        return s.L3[b].at[:, pl.ds(off, w)]
    def st1(s, i):
        p, order = s.p, s.geom(i)[5]
        for k in (0, 1):
            src = s.piece(i, k, p.c, 1 - p.y) if order == "xy" else s.piece(i, 1 - p.x, p.c, k)
            s.cp(i, 4 + k, src, s.l2(i, k), p.yn if order == "xy" else p.xn).start()
    def a1(s, i):
        p = s.p; b, R, W, off, w, order = s.geom(i)
        for k in (0, 1):
            l = s.l2(i, k)
            s.cp(i, 4 + k, l, l, p.xn).wait_recv()
            s.add(s.piece(i, k, p.c, p.y) if order == "xy" else s.piece(i, p.x, p.c, k), l, 4 * R)
    def st2(s, i):
        p, order = s.p, s.geom(i)[5]
        src = s.piece(i, 1 - p.x, p.c, p.y) if order == "xy" else s.piece(i, p.x, p.c, 1 - p.y)
        s.cp(i, 6, src, s.l3(i), p.xn if order == "xy" else p.yn).start()
    def a2(s, i):
        l = s.l3(i)
        s.cp(i, 6, l, l, s.p.xn).wait_recv()
        s.add(s.piece(i, s.p.x, s.p.c, s.p.y), l, 4 * s.geom(i)[1])
    def l4(s, i, k):
        b, R, W, off, w, _ = s.geom(i)
        return s.L4[b].at[k, :, pl.ds(off, w)]
    def zsend(s, i):
        p = s.p
        for d in (1, 3, 2):
            rcopy(s.piece(i, p.x, p.c, p.y, p.zof(d), 1), s.l4(i, 3 - d), s.ss.at[i, 6 + d], s.rs.at[i, 10 - d], p.zn(d)).start()
    def fin(s, i):
        p = s.p; b, R, W, off, w, _ = s.geom(i)
        F, G, out = s.F[b], s.G[b], s.out
        h = R // 2
        t = s.piece(i, p.x, p.c, p.y, p.z, 1)[...].astype(f32)
        for k in range(3):
            l = s.l4(i, k)
            s.cp(i, 7 + k, l, l, p.sib).wait_recv()
            t = t + l[...].astype(f32)
        F[:, pl.ds(off, w)] = t
        src = F.at[pl.ds(pl.multiple_of((1 - p.y) * h, 8), h), pl.ds(off, w)]
        s.cp(i, 10, src, G.at[:, pl.ds(off, w)], p.yn).start()
        for yy in (0, 1):
            @pl.when(p.y == yy)
            def _(): out(b, yy, off, w, lambda o, k: F[pl.ds(yy * h, h), pl.ds(off + o, k)])
    def last(s, i):
        p = s.p; b, R, W, off, w, _ = s.geom(i)
        l = s.G[b].at[:, pl.ds(off, w)]
        s.cp(i, 10, l, l, p.yn).wait_recv()
        for yy in (0, 1):
            @pl.when(p.y == 1 - yy)
            def _(): s.out(b, yy, off, w, lambda o, k: l[:, pl.ds(o, k)])
    def r0(s, i): s.st0(i)
    def r1(s, i): s.a0(i); s.st1(i)
    def r2(s, i): s.a1(i); s.st2(i)
    def r3(s, i): s.a2(i); s.zsend(i)
    def r4(s, i): s.fin(i)
    def r5(s, i): s.last(i)
    def steps(s): return (s.r0, s.r1, s.r2, s.r3, s.r4, s.r5)
    def drain(s):
        p = s.p
        for i in range(len(SCATTER_CHUNKS)):
            b, R, W, off, w, _ = s.geom(i)
            for k, ref in [(k, s.l1(i, 0, 0)) for k in range(4)] + [(4, s.l2(i, 0)), (5, s.l2(i, 1)), (6, s.l3(i)), (10, s.G[b].at[:, pl.ds(off, w)])] + [(7 + k, s.l4(i, k)) for k in range(3)]:
                s.cp(i, k, ref, ref, p.sib).wait_send()

def rs_scratch():
    v = pltpu.VMEM
    return [v((768, 2 * HA), bf16), v((1536, 2 * HB), bf16), v((2, 192, 2 * HA), bf16), v((2, 384, 2 * HB), bf16),
        v((2, 192, HA), bf16), v((2, 384, HB), bf16), v((192, HA), bf16), v((384, HB), bf16),
        v((3, 48, HA), bf16), v((3, 96, HB), bf16), v((48, HA), f32), v((96, HB), f32), v((24, HA), f32), v((48, HB), f32)]

NK = 32
NB = 2

def lanes(j): return pl.ds(pl.multiple_of(j * 128, 128), 128)
def rows_(i): return pl.ds(pl.multiple_of(i * 8, 8), 8)
def tree(xs):
    xs = list(xs)
    while len(xs) > 1:
        xs = [xs[i] + xs[i + 1] if i + 1 < len(xs) else xs[i] for i in range(0, len(xs), 2)]
    return xs[0]

def fwd_states(U, rate, S, END, j, unroll=2):
    ln = lanes(j)
    r = rate[0:16, ln]
    w = [jnp.exp(r * (s - 7.0)) for s in range(8)]
    q8 = jnp.exp(r * -8.0)
    def body(k, st):
        new = []
        for b in range(NB):
            S[b * NK + k, :, ln] = st[b]
            parts = [w[s] * U[b * NK + k, pl.ds(s, 1), ln] for s in range(8)]
            new.append(q8 * st[b] + tree(parts))
        return tuple(new)
    st = lax.fori_loop(0, NK, body, tuple(jnp.zeros((16, 128), f32) for _ in range(NB)), unroll=unroll)
    for b in range(NB): END[b, :, ln] = st[b].astype(END.dtype)

def conv_tables(rate, ec, j):
    ln = lanes(j)
    it = lax.broadcasted_iota(jnp.int32, (8, 128), 0).astype(f32)
    E, K = [], []
    for h in range(16):
        rb = jnp.broadcast_to(rate[pl.ds(h, 1), ln], (8, 128)); eb = jnp.broadcast_to(ec[pl.ds(h, 1), ln], (8, 128))
        K.append(jnp.exp(-it * rb) * eb)
        E.append(jnp.exp(-(it + 1.0) * rb) * eb)
    return E, tree(K)

def fwd_smooth(U, S, S0, rate, ec, omega, BL, KS, j, unroll=1):
    ln = lanes(j)
    r = rate[0:16, ln]
    q8 = jnp.exp(r * -8.0)
    E, K = conv_tables(rate, ec, j)
    KS[...] = K
    ii = lax.broadcasted_iota(jnp.int32, (8, 128), 0)
    KM = [jnp.where(ii >= l, jnp.broadcast_to(KS[pl.ds(l, 1), :], (8, 128)), 0.0) for l in range(8)]
    om = jnp.broadcast_to(omega[:, ln], (8, 128))
    KM[0] = KM[0] + om
    def body(k, gs):
        new = []
        for b in range(NB):
            i = b * NK + k
            S[i, :, ln] = S[i, :, ln] + gs[b]
            u = U[i, :, ln]
            parts = [KM[0] * u] + [KM[l] * pltpu.roll(u, l, 0) for l in range(1, 8)]
            parts += [E[h] * S[i, pl.ds(h, 1), ln] for h in range(16)]
            BL[i, :, ln] = tree(parts)
            new.append(q8 * gs[b])
        return tuple(new)
    lax.fori_loop(0, NK, body, tuple(S0[b, :, ln] for b in range(NB)), unroll=unroll)

def bwd_states(Gr, U, S, rate, A, DIR, G1, H, CS, j, unroll=1):
    ln = lanes(j)
    r = rate[0:16, ln]
    w = [jnp.exp(r * -float(s)) for s in range(8)]
    q8 = jnp.exp(r * -8.0)
    def body(kk, c):
        k = NK - 1 - kk
        st, g1, h1, C = c
        new, C = [], list(C)
        for b in range(NB):
            i = b * NK + k
            A[i, :, ln] = st[b]
            p = [Gr[i, pl.ds(0, 1), ln]] + [w[s] * Gr[i, pl.ds(s, 1), ln] for s in range(1, 8)]
            later = B1 = p[7]
            for t in range(6, 0, -1):
                later = later + p[t]
                B1 = B1 + later
            Bg = later + p[0]
            Sk = S[i, :, ln]
            g1 = g1 + Sk * Bg
            h1 = h1 + Sk * B1
            new.append(q8 * st[b] + Bg)
            u, g = U[i, :, ln], Gr[i, :, ln]
            C = [C[l] + g * (pltpu.roll(u, l, 0) if l else u) for l in range(8)]
        return tuple(new), g1, h1, tuple(C)
    z = jnp.zeros((16, 128), f32)
    st, g1, h1, C = lax.fori_loop(0, NK, body, (tuple(z for _ in range(NB)), z, z, tuple(jnp.zeros((8, 128), f32) for _ in range(8))), unroll=unroll)
    for b in range(NB): DIR[b, :, ln] = st[b].astype(DIR.dtype)
    ii = lax.broadcasted_iota(jnp.int32, (8, 128), 0)
    g1, h1 = g1 * w[1], h1 * w[1]
    for l in range(8):
        cl = jnp.sum(jnp.where(ii >= l, C[l], 0.0), axis=0, keepdims=True)
        t = w[l] * cl
        g1 = g1 + t
        if l: h1 = h1 + t * float(l)
    G1[:, ln] = g1
    H[:, ln] = h1

def bwd_grad(Gr, U, S, A, A0, rate, ec, H, DU, KS, AT, j, unroll=1):
    ln = lanes(j)
    r = rate[0:16, ln]
    q8 = jnp.exp(r * -8.0)
    c8 = 8.0 * jnp.exp(r * -9.0)
    wu = [jnp.exp(r * (s - 8.0)) * (8.0 - s) for s in range(8)]
    it = lax.broadcasted_iota(jnp.int32, (8, 128), 0).astype(f32)
    E, K = [], []
    for h in range(16):
        rb = jnp.broadcast_to(rate[pl.ds(h, 1), ln], (8, 128)); eb = jnp.broadcast_to(ec[pl.ds(h, 1), ln], (8, 128))
        K.append(jnp.exp(-it * rb) * eb)
        E.append(jnp.exp((it - 8.0) * rb) * eb)
    KS[...] = tree(K)
    ii = lax.broadcasted_iota(jnp.int32, (8, 128), 0)
    KM = [jnp.where(ii < 8 - l, jnp.broadcast_to(KS[pl.ds(l, 1), :], (8, 128)), 0.0) for l in range(8)]
    def body(kk, c):
        k = NK - 1 - kk
        gs, h1 = c
        new = []
        for b in range(NB):
            i = b * NK + k
            Ak = A[i, :, ln] + gs[b]
            AT[b] = Ak
            Bu = tree([wu[s] * U[i, pl.ds(s, 1), ln] for s in range(8)])
            h1 = h1 + Ak * (Bu + c8 * S[i, :, ln])
            g = Gr[i, :, ln]
            parts = [KM[0] * g] + [KM[l] * pltpu.roll(g, 8 - l, 0) for l in range(1, 8)]
            parts += [E[h] * AT[b, pl.ds(h, 1), :] for h in range(16)]
            DU[i, :, ln] += tree(parts)
            new.append(q8 * gs[b])
        return tuple(new), h1
    gs, h1 = lax.fori_loop(0, NK, body, (tuple(A0[b, :, ln] for b in range(NB)), H[:, ln]), unroll=unroll)
    H[:, ln] = h1


def sigmoid(v): return jax.nn.sigmoid(v)
def dot(a, b): return jnp.dot(a, b, preferred_element_type=f32)
def dot_nt(a, b): return lax.dot_general(a, b, (((1,), (1,)), ((), ())), preferred_element_type=f32)
def dot_tn(a, b): return lax.dot_general(a, b, (((0,), (0,)), ((), ())), preferred_element_type=f32)
def loop(n, f, unroll=1):
    def body(i, _):
        f(i); return 0
    lax.fori_loop(0, n, body, 0, unroll=unroll)
def ds(i, n): return pl.ds(pl.multiple_of(i * n, n), n)
def silu_and_slope(v):
    s = sigmoid(v)
    y = v * s
    return y, s + y * (1.0 - s)

class Params:
    def __init__(s, pos, ref, PRM, ss, rs):
        s.p, s.ref, s.PRM, s.ss, s.rs = pos, ref, PRM, ss, rs
    def r(s, row, n): return s.PRM.at[pl.ds(pl.multiple_of(row, 8), n), :]
    def cp(s, k, src, dst, dev, kr=None):
        return rcopy(src, dst, s.ss.at[k], s.rs.at[k if kr is None else kr], dev)
    def y0(s):
        p = s.p; row = (p.dp * 4 + p.z) * 48 + p.y * 24
        s.cp(0, s.ref, s.r(row, 24), p.yn).start()
        s.PRM[pl.ds(pl.multiple_of(row, 8), 24), :] = s.ref[...]
    def y1(s):
        p = s.p
        l = s.r((p.dp * 4 + p.z) * 48, 24)
        s.cp(0, l, l, p.yn).wait()
    def z0(s):
        p = s.p; u = s.r((p.dp * 4 + p.z) * 48, 48)
        for d in (1, 3, 2): s.cp(d, u, u, p.zn(d), 1 + p.z).start()
    def x0(s):
        p = s.p; u = s.r(p.dp * 192, 192)
        for d in (1, 2, 3):
            l = s.r((p.dp * 4 + p.zof(d)) * 48, 48)
            s.cp(1, l, l, p.sib, 1 + p.zof(d)).wait_recv()
        s.cp(7, u, u, p.xn).start()
        s.cp(8, u, u, p.sib).start()
    def x1(s):
        p = s.p; u = s.r(p.dpx * 192, 192)
        s.cp(7, u, u, p.xn).wait_recv()
        s.cp(9, u, u, p.sib).start()
    def end(s):
        p = s.p; u = s.r(p.dp * 192, 192)
        s.cp(8, u, u, p.sib).wait_recv()
        s.cp(9, u, u, p.sib).wait_recv()
    def drain(s):
        p = s.p; u = s.r(p.dp * 192, 192); u1 = s.r(p.dp * 192, 48)
        for k in (7, 8, 9): s.cp(k, u, u, p.sib).wait_send()
        for k in (1, 2, 3): s.cp(k, u1, u1, p.sib).wait_send()

class Scan:
    def __init__(s, pos, way, rate, E, L, Z, ss, rs):
        s.p, s.way, s.rate, s.E, s.L, s.Z, s.ss, s.rs = pos, way, rate, E, L, Z, ss, rs
    def grow(s, k): return jnp.exp(s.rate[0:16, :] * (-256.0 * k))[None]
    def cp(s, d):
        return rcopy(s.E.at[0 if d == 0 else 1], s.L.at[d], s.ss.at[d], s.rs.at[d], s.p.yn if d == 0 else s.p.zn(s.way * d))
    def sc0(s): s.cp(0).start()
    def sc1(s):
        p = s.p
        s.cp(0).wait_recv()
        own, got = s.E[0].astype(f32), s.L[0].astype(f32)
        second = p.y == (1 if s.way > 0 else 0)
        s.Z[...] = jnp.where(second, got, 0.0)
        pair = jnp.where(second, own, got) + s.grow(1) * jnp.where(second, got, own)
        s.E[1] = pair.astype(s.E.dtype)
        for d in (1, 2, 3):
            @pl.when((p.z + d <= 3) if s.way > 0 else (p.z - d >= 0))
            def _(): s.cp(d).start()
    def sc2(s):
        p = s.p
        k = (p.y if s.way > 0 else 1 - p.y).astype(f32)
        for d in (1, 2, 3):
            @pl.when((p.z - d >= 0) if s.way > 0 else (p.z + d <= 3))
            def _():
                s.cp(d).wait_recv()
                s.Z[...] += s.grow(k + 2.0 * (d - 1)) * s.L[d].astype(f32)
    def drain(s):
        p = s.p
        s.cp(0).wait_send()
        for d in (1, 2, 3):
            @pl.when((p.z + d <= 3) if s.way > 0 else (p.z - d >= 0))
            def _(): s.cp(d).wait_send()

class Halves:
    def __init__(s, pos, mx, va, wo, wu, wd, WA, WB, land, ss, rs):
        s.p, s.mx, s.va, s.wo, s.wu, s.wd, s.WA, s.WB, s.land, s.ss, s.rs = pos, mx, va, wo, wu, wd, WA, WB, land, ss, rs
    def pieces(s, y):
        return ((s.va, y * 768, VAL, 768), (s.mx, y * MXL, 0, 1536 if y else MXL), (s.wu, y * 768, UPL, 768))
    def rb(s, yy): return pl.ds(pl.multiple_of((s.p.dp * 4 + s.p.z) * RB + yy * 48, 48), 48)
    def wb(s, yy, half, k): return s.WB.at[s.rb(yy), pl.ds(half * HB + k * DWL, DWL)]
    def start(s):
        p = s.p
        for yy in (0, 1):
            @pl.when(p.y == yy)
            def _():
                for k, (ref, a, c, w) in enumerate(s.pieces(1 - yy)):
                    rcopy(ref.at[:, pl.ds(a, w)], s.land.at[:, pl.ds(c, w)], s.ss.at[k], s.rs.at[k], p.yn).start()
                for k, ref in enumerate((s.wo, s.wd)):
                    rcopy(ref.at[:, pl.ds((1 - yy) * DWL, DWL)], s.wb(yy, 1 - yy, k), s.ss.at[3 + k], s.rs.at[3 + k], p.yn).start()
                    pltpu.make_async_copy(ref.at[:, pl.ds(yy * DWL, DWL)], s.wb(yy, yy, k), s.ss.at[5 + k]).start()
    def end(s, ks):
        p = s.p
        rows = pl.ds(pl.multiple_of((p.dp * 4 + p.z) * RA, 16), RA)
        for yy in (0, 1):
            @pl.when(p.y == yy)
            def _():
                for k, (ref, a, c, w) in enumerate(s.pieces(yy)):
                    if k not in ks: continue
                    l = s.land.at[:, pl.ds(c, w)]
                    rcopy(l, l, s.ss.at[k], s.rs.at[k], p.yn).wait_recv()
                    both = (ref[:, pl.ds(a, w)], l[...]) if yy == 0 else (l[...], ref[:, pl.ds(a, w)])
                    s.WA[rows, pl.ds(yy * HA + c, w)] = jnp.concatenate([t.astype(f32) for t in both], axis=0).astype(bf16)
                if yy == 1 and 1 in ks: s.WA[rows, pl.ds(HA + 1536, 128)] = jnp.zeros((RA, 128), bf16)
        if 1 in ks:
            u = s.wb(0, 0, 0)
            for k in (0, 1):
                rcopy(u, u, s.ss.at[3 + k], s.rs.at[3 + k], p.yn).wait_recv()
                pltpu.make_async_copy(u, u, s.ss.at[5 + k]).wait()
    def hv0(s): s.end((0,))
    def hv1(s): s.end((1, 2))
    def drain(s):
        p = s.p
        for yy in (0, 1):
            @pl.when(p.y == yy)
            def _():
                for k, (ref, a, c, w) in enumerate(s.pieces(1 - yy)):
                    l = s.land.at[:, pl.ds(c, w)]
                    rcopy(l, l, s.ss.at[k], s.rs.at[k], p.yn).wait_send()
        u = s.wb(0, 0, 0)
        for k in (0, 1): rcopy(u, u, s.ss.at[3 + k], s.rs.at[3 + k], p.yn).wait_send()

def norm_rows(tok, PT, U, NL, i):
    x = tok[ds(i, 64), :].astype(f32)
    r = lax.rsqrt(jnp.mean(x * x, axis=-1, keepdims=True) + EPSILON)
    u = x * r * PT[32:33, :]
    U[ds(i, 8), :, :] = u.reshape(8, 8, 768)
    NL[ds(i, 64), :] = u.astype(bf16)

def run_plan(plan, steps):
    for e in plan:
        if e % 100 == 0: steps[0][e // 100]()
        else: steps[1][e // 100](e % 100 - 1)

def sub8(v):
    return v.reshape(v.shape[0] // 8, 8, v.shape[1]).sum(axis=0)

FORWARD_OUT = (("wa", (768, 2 * HA), bf16), ("wb", (1536, 2 * HB), bf16), ("vl", (512, 1536), bf16), ("vs", (512, 1536), bf16),
    ("re", (512, 1536), bf16), ("rs", (512, 1536), bf16), ("at", (512, 1536), bf16), ("gt", (512, 1536), bf16), ("hi", (512, 1536), bf16), ("hs", (512, 1536), bf16),
    ("uc", (512, 768), bf16), ("du", (512, 768), bf16), ("om", (512, 768), bf16), ("sh", (512, 768), bf16), ("bs", (512, 768), bf16), ("n2", (512, 768), bf16),
    ("mi", (512, 768), f32), ("sp", (512, 128), f32), ("pr", (512, 128), f32), ("st", (64, 16, 768), f32), ("pt", (128, 768), f32), ("res", (512, 768), bf16), ("sq", (24, 768), f32))

FORWARD_PLAN = (
    0, 100, 200, 300, 704, 701, 500, 400, 703, 804, 600, 1213, 707, 801, 803, 1216, 1313, 700, 901, 708, 904, 903, 800, 1215, 1001, 702, 1,
    1101, 2, 705, 1316, 807, 808, 1315, 3, 4, 5, 6, 1003, 706, 1214, 712, 900, 805, 908, 1103, 802, 710, 806, 902, 812, 1000, 1004, 1104,
    905, 912, 907, 906, 1008, 709, 1002, 1005, 1102, 1108, 201, 717, 711, 202, 810, 101, 102, 809, 1007, 718, 103, 1314, 104, 105, 106,
    1006, 1107, 811, 1416, 817, 1106, 1100, 1012, 909, 401, 910, 203, 1112, 1105, 818, 911, 402, 1413, 1200, 301, 917, 302, 1009, 303, 1109,
    1414, 403, 918, 1010, 501, 1516, 1110, 1011, 1513, 1415, 502, 503, 504, 1111, 1300, 1017, 1514, 1018, 1117, 1400, 601, 1515, 602, 1118,
    603, 1500,
)

def forward_kernel(tok, valid, affine, prm, mx, va, wo, wu, wd, *refs):
    no = len(FORWARD_OUT)
    outs, bufs, rest = refs[:no], refs[no:2 * no], refs[2 * no:]
    B = {name: r for (name, _, _), r in zip(FORWARD_OUT, bufs)}
    O = {name: r for (name, _, _), r in zip(FORWARD_OUT, outs)}
    osem = {name: i for i, (name, _, _) in enumerate(FORWARD_OUT)}
    (PRM, land, U, NL, BL, RSF, UPD, DIR, ACC, KS, E, L, Z, s0, r0, sp_, rp_, ss, rs, sx, rx, so, sw) = rest
    WA, WB, PT, S = B["wa"], B["wb"], B["pt"], B["st"]
    p = Pos()
    full_barrier(p)
    out = lambda name: pltpu.make_async_copy(B[name], O[name], so.at[osem[name]])
    def keep(*names):
        for name in names: out(name).start()
    def weight(k, h):
        b, c, w = KINDS[k]
        a, o = ((WA, O["wa"]), (WB, O["wb"]))[b]
        cols = pl.ds((HA, HB)[b] * h + c, w)
        return pltpu.make_async_copy(a.at[:, cols], o.at[:, cols], sw.at[k, h])
    def keep_weight(k):
        for h in (0, 1): weight(k, h).start()
    par = Params(p, prm, PRM, sp_, rp_)
    hv = Halves(p, mx, va, wo, wu, wd, WA, WB, land, s0, r0)
    g = Gather(p, (WA, WB), ss, rs)
    rate, ec, omega = PT.at[0:16, :], PT.at[16:32, :], PT.at[34:35, :]
    sc = Scan(p, 1, PT, E, L, Z, sx, rx)
    SQ = B["sq"]
    def par1(): par.y1(); par.z0()
    def pt():
        par.end()
        for j in range(6): PT[:, j * 128:(j + 1) * 128] = PRM[j * 128:(j + 1) * 128, :].T
    def norm(): loop(8, lambda i: norm_rows(tok, PT, U, NL, i))
    def st(j): fwd_states(U, rate, S, E.at[0], j, 4)
    def sm(j):
        if j == 0: sc.sc2()
        fwd_smooth(U, S, Z, rate, ec, omega, BL, KS, j, 2)
    def sh():
        def rows(i):
            y, s = silu_and_slope(BL[ds(i, 8), :, :].reshape(64, 768))
            B["sh"][ds(i, 64), :] = y.astype(bf16)
            B["bs"][ds(i, 64), :] = s.astype(bf16)
        loop(8, rows)
        keep("st", "pt", "sh", "bs")
    def both(name, slope, m, c, w=256):
        def rows(i):
            y, s = silu_and_slope(ACC[ds(i, 64), 0:256])
            B[name][ds(i, 64), ds(m, 256)] = y.astype(bf16)
            B[slope][ds(i, 64), ds(m, 256)] = s.astype(bf16)
            if name == "re": RSF[ds(i, 64), ds(m, 256)] = y
        loop(8, rows)
    def mul(x, ref, c, w=256): ACC[:, 0:w] = dot(x[...], ref[:, c:c + w])
    def va_(k):
        g.need(0, VAL + 256 * k, VAL + 256 * k + 256)
        for h in (0, 1):
            mul(NL, WA, h * HA + VAL + 256 * k)
            both("vl", "vs", 3 * h + k, 0)
        if k == 2: keep("vl", "vs"); keep_weight(1)
    def mu(k):
        g.need(0, 256 * k, 256 * k + 256)
        mul(B["sh"], WA, 256 * k)
        loop(8, lambda i: UPD.__setitem__((ds(i, 64), ds(k, 256)), sigmoid(ACC[ds(i, 64), 0:256])))
        mul(B["sh"], WA, HA + 256 * k)
        both("re", "rs", 3 + k, 0)
    def ms():
        g.need(0, 768, 896)
        mul(B["sh"], WA, 768, 128)
        B["sp"][...] = ACC[:, 0:128]
    def md(k):
        g.need(0, 768 + 256 * k, 1152 + 256 * k)
        mul(B["sh"], WA, 896 + 256 * k)
        both("re", "rs", k, 0)
        DIR[:, ds(k, 256)] = dot(B["sh"][...], WA[:, HA + 768 + 256 * k:HA + 1024 + 256 * k])
    def at_(b):
        rr = ds(b, 128)
        s = B["sp"][rr, :]
        s = s * sigmoid(s)
        q = (s * affine[0:1, :] + affine[1:2, :]).astype(bf16)
        k = (s * affine[2:3, :]).astype(bf16)
        t = dot_nt(q, k) * Z_SCALE
        ok = lax.broadcasted_iota(jnp.int32, (128, 128), 0) >= lax.broadcasted_iota(jnp.int32, (128, 128), 1)
        t = jnp.where(ok, t, -1e30)
        e = jnp.exp(t - jnp.max(t, axis=-1, keepdims=True))
        e = e / jnp.sum(e, axis=-1, keepdims=True)
        B["pr"][rr, :] = e
        el = e.astype(bf16)
        for m in range(6):
            c = pl.ds(m * 256, 256)
            a = dot(el, B["vl"][rr, c])
            B["at"][rr, c] = a.astype(bf16)
            B["gt"][rr, c] = (a * RSF[rr, c]).astype(bf16)
        if b == 3: keep("re", "rs", "sp", "pr", "at", "gt"); keep_weight(0)
    def ca():
        g.need(1, 0, DWL)
        SQ[...] = jnp.zeros_like(SQ)
        for m in range(2):
            ACC[...] = dot(B["gt"][...], WB[:, m * HB:m * HB + DWL])
            def rows(i):
                r, c = ds(i, 64), pl.ds(m * DWL, DWL)
                y, s = silu_and_slope(DIR[r, c] + ACC[r, :])
                u = UPD[r, c]
                x = tok[r, c].astype(f32)
                a = u * (y - x)
                B["mi"][r, c] = x + a
                B["uc"][r, c] = (u * s).astype(bf16)
                B["du"][r, c] = (a * (1.0 - u)).astype(bf16)
                B["om"][r, c] = (1.0 - u).astype(bf16)
                SQ[8:16, c] += sub8(valid[r, :] * a * a)
            loop(8, rows)
        keep_weight(3)
    def n2():
        def rows(i):
            v = B["mi"][ds(i, 64), :]
            r = lax.rsqrt(jnp.mean(v * v, axis=-1, keepdims=True) + EPSILON)
            B["n2"][ds(i, 64), :] = (v * r * PT[33:34, :]).astype(bf16)
        loop(8, rows)
        keep("mi", "uc", "du", "om", "n2")
    def up(k):
        g.need(0, UPL + 256 * k, UPL + 256 * k + 256)
        for h in (0, 1):
            mul(B["n2"], WA, h * HA + UPL + 256 * k)
            both("hi", "hs", 3 * h + k, 0)
    def do():
        keep("hi", "hs"); keep_weight(2)
        g.need(1, DWL, 2 * DWL)
        keep_weight(4)
        for m in range(2):
            ACC[...] = dot(B["hi"][...], WB[:, m * HB + DWL:m * HB + 2 * DWL])
            def rows(i):
                r, c = ds(i, 64), pl.ds(m * DWL, DWL)
                f = ACC[r, :]
                o = B["mi"][r, c] + f
                B["res"][r, c] = o.astype(bf16)
                v = valid[r, :]
                SQ[0:8, c] += sub8(v * o * o)
                SQ[16:24, c] += sub8(v * f * f)
            loop(8, rows)
        keep("res", "sq")
    steps = (par.y0, hv.start, par1, hv.hv0, hv.hv1, par.x0, par.x1, pt, norm, sc.sc0, sc.sc1, sh, ms, ca, n2, do), (st, sm, va_, mu, md, at_, up) + g.steps()
    run_plan(FORWARD_PLAN, steps)
    g.drain(); par.drain(); sc.drain(); hv.drain()
    for name, _, _ in FORWARD_OUT[2:]: out(name).wait()
    for k in range(len(KINDS)):
        for h in (0, 1): weight(k, h).wait()

Z_SCALE = Z ** -0.5
SCAN_TYPE = f32
def forward_call(tok, valid, affine, prm, mx, va, wo, wu, wd):
    n = len(GATHER_CHUNKS)
    v = pltpu.VMEM
    D_ = pltpu.SemaphoreType.DMA
    return pl.pallas_call(forward_kernel,
        out_shape=tuple(jax.ShapeDtypeStruct(s, t) for _, s, t in FORWARD_OUT),
        in_specs=[pl.BlockSpec(memory_space=pltpu.VMEM)] * 9,
        out_specs=[pl.BlockSpec(memory_space=pl.ANY)] * len(FORWARD_OUT),
        scratch_shapes=[v(s, t) for _, s, t in FORWARD_OUT] + [v((768, 128), f32), v((24, HA), bf16), v((64, 8, 768), f32), v((512, 768), bf16),
            v((64, 8, 768), f32), v((512, 1536), f32), v((512, 768), f32), v((512, 768), f32), v((512, 384), f32), v((8, 128), f32),
            v((2, 2, 16, 768), SCAN_TYPE), v((4, 2, 16, 768), SCAN_TYPE), v((2, 16, 768), f32),
            D_((7,)), D_((5,)), D_((10,)), D_((10,)), D_((n, 23)), D_((n, 23)), D_((4,)), D_((4,)), D_((len(FORWARD_OUT),)), D_((len(KINDS), 2))],
        compiler_params=pltpu.CompilerParams(collective_id=0, has_side_effects=True, vmem_limit_bytes=62 * 2**20),
    )(tok, valid, affine, prm, mx, va, wo, wu, wd)

class Tiny:
    def __init__(s, pos, T, L1, L2, L4, OUT, G, ss, rs):
        s.p, s.T, s.L1, s.L2, s.L4, s.OUT, s.G, s.ss, s.rs = pos, T, L1, L2, L4, OUT, G, ss, rs
    def r(s, xx, c, z=0, n=4): return s.T.at[pl.ds(pl.multiple_of(((xx * 2 + c) * 4 + z) * 48, 8), n * 48), :]
    def cp(s, k, src, dst, dev): return rcopy(src, dst, s.ss.at[k], s.rs.at[k], dev)
    def st0(s):
        for xx in (0, 1): s.cp(xx, s.r(xx, 1 - s.p.c), s.L1.at[xx], s.p.sib).start()
    def a0(s):
        p = s.p
        for xx in (0, 1):
            l = s.L1.at[xx]
            s.cp(xx, l, l, p.sib).wait_recv()
            t = s.r(xx, p.c)
            t[...] = t[...] + l[...]
        s.cp(2, s.r(1 - p.x, p.c), s.L2, p.xn).start()
    def a1(s):
        p = s.p
        s.cp(2, s.L2, s.L2, p.xn).wait_recv()
        t = s.r(p.x, p.c)
        t[...] = t[...] + s.L2[...]
    def zsend(s):
        p = s.p
        for d in (1, 3, 2): rcopy(s.r(p.x, p.c, p.zof(d), 1), s.L4.at[3 - d], s.ss.at[2 + d], s.rs.at[6 - d], p.zn(d)).start()
    def fin(s):
        p = s.p
        t = s.r(p.x, p.c, p.z, 1)
        v = t[...]
        for k in range(3):
            l = s.L4.at[k]
            s.cp(3 + k, l, l, p.sib).wait_recv()
            v = v + l[...]
        t[...] = v
        row = ((p.x * 2 + p.c) * 4 + p.z) * 48
        far = s.T.at[pl.ds(pl.multiple_of(row + (1 - p.y) * 24, 8), 24), :]
        s.cp(9, far, s.G, p.yn).start()
    def last(s):
        p = s.p
        row = ((p.x * 2 + p.c) * 4 + p.z) * 48
        s.cp(9, s.G, s.G, p.yn).wait_recv()
        s.OUT[...] = s.T[pl.ds(pl.multiple_of(row + p.y * 24, 8), 24), :] + s.G[...]
    def drain(s):
        p = s.p
        for k, l in ((0, s.L1.at[0]), (1, s.L1.at[1]), (2, s.L2), (9, s.G)): s.cp(k, l, l, p.sib).wait_send()
        for k in range(3): s.cp(3 + k, s.L4.at[k], s.L4.at[k], p.sib).wait_send()

class Total:
    def __init__(s, pos, R, L, ss, rs):
        p = pos
        z1 = (p.dp, p.sq + 2 - 4 * (p.z % 2)); z2 = (p.dp, p.sq + 4 - 8 * (p.z // 2))
        s.to, s.R, s.L, s.ss, s.rs = (p.sib, p.xn, p.yn, z1, z2), R, L, ss, rs
    def cp(s, k): return rcopy(s.R.at[k], s.L.at[k], s.ss.at[k], s.rs.at[k], s.to[k])
    def send(s, k): s.cp(k).start()
    def step(s, k):
        s.cp(k).wait_recv()
        s.R[k + 1] = s.R[k] + s.L[k]
        if k < 4: s.send(k + 1)
    def drain(s):
        for k in range(5): s.cp(k).wait_send()

BACK_IN = ("wa", "wb", "vl", "vs", "re", "rs", "at", "gt", "hi", "hs", "uc", "du", "om", "sh", "bs", "n2", "mi", "sp", "pr", "st", "pt", "tok", "cot")
MX_PARTS = ((0, 384), (384, 384), (768, 256), (1024, 256), (1280, 128), (1408, 256))
BACKWARD_PLAN = (
    800, 701, 702, 703, 704, 705, 706, 2, 1, 3, 801, 802, 102, 803, 101, 4, 900, 103, 901, 5, 104, 902, 903, 904, 905, 201, 906, 6, 105,
    202, 7, 1001, 1002, 1000, 106, 1003, 1004, 701, 204, 702, 301, 703, 107, 302, 700, 901, 801, 902, 802, 803, 205, 903, 800, 206, 304, 8,
    1106, 203, 1101, 1001, 10, 207, 305, 108, 15, 1102, 1002, 110, 1003, 1105, 306, 1104, 9, 14, 13, 1004, 1005, 303, 307, 1006, 11, 113, 0,
    601, 1103, 114, 208, 100, 111, 213, 602, 308, 210, 109, 12, 1201, 115, 1202, 211, 313, 603, 112, 1203, 1204, 310, 214, 408, 404, 1205,
    1206, 311, 209, 401, 900, 212, 314, 413, 200, 407, 215, 309, 312, 406, 300, 402, 409, 414, 315, 411, 509, 504, 400, 412, 403, 405, 501,
    514, 410, 511, 502, 415, 604, 512, 500, 505, 605, 507, 506, 513, 515, 503, 508, 510, 600,
)
CUT = 37

def backward_kernel(valid, affine, sq, *refs):
    ni = len(BACK_IN)
    I = dict(zip(BACK_IN, refs[:ni]))
    (o_mx, o_va, o_up, o_wo, o_wd, o_gt, o_tiny, o_red) = refs[ni:ni + 8]
    (WA, WB, L1A, L1B, L2A, L2B, L3A, L3B, L4A, L4B, FA, FB, GA, GB_, TOK, PT, U, X0, X1, GT, GG, G1, H, KS, AT, ACC, E, L, Zb,
     T, TL1, TL2, TL4, TG, TP, RR, RL, P6, GMX, Q0, Q1, Q2, SHT, SP, ss, rs, sx, rx, st_, rt_, sr, rr_, li, lo, lw) = refs[ni + 8:]
    p = Pos()
    sem = {name: i for i, name in enumerate(BACK_IN)}
    def load(name, dst): pltpu.make_async_copy(I[name], dst, li.at[sem[name]]).start()
    def ready(*pairs):
        for name, dst in pairs: pltpu.make_async_copy(I[name], dst, li.at[sem[name]]).wait()
    def part_copies(k):
        b, c, w = KINDS[k]
        for h in (0, 1):
            cols = pl.ds((HA, HB)[b] * h + c, w)
            yield pltpu.make_async_copy(I[("wa", "wb")[b]].at[:, cols], (WA, WB)[b].at[:, cols], lw.at[k, h])
    def part(k):
        for cp in part_copies(k): cp.start()
    def part_ready(k):
        for cp in part_copies(k): cp.wait()
    def put(b, half, off, w, get):
        outs = ((o_wo, 0, 384, 384), (o_wd, 384, 768, 384)) if b else ((o_mx, 0, 1536 if half else MXL, MXL), (o_va, VAL, UPL, 768), (o_up, UPL, HA, 768))
        for o, lo_, hi_, step in outs:
            a, e = max(off, lo_), min(off + w, hi_)
            if a < e: o[:, pl.ds(a - lo_ + half * step, e - a)] = get(a - off, e - a)
    g = Scatter(p, (WA, WB), (L1A, L1B), (L2A, L2B), (L3A, L3B), (L4A, L4B), (FA, FB), (GA, GB_), put, ss, rs)
    tot = Total(p, RR, RL, sr, rr_)
    sc = Scan(p, -1, PT, E, L, Zb, sx, rx)
    tiny = Tiny(p, T, TL1, TL2, TL4, o_tiny, TG, st_, rt_)
    v = lambda s, t: pltpu.VMEM(s, t)
    big, mid = v((512, 1536), bf16), v((512, 768), bf16)
    rate, ec, omega = PT.at[0:16, :], PT.at[16:32, :], PT.at[34:35, :]
    gain1, gain2 = PT.at[32:33, :], PT.at[33:34, :]
    def at3(X, i): return X[ds(i, 8), :, :].reshape(64, 768)
    def pair(ref, rows, c, w, step): return jnp.concatenate([ref[rows, c:c + w], ref[rows, c + step:c + step + w]], axis=1)
    def ti2(): tiny.a1(); tiny.zsend()
    def to0():
        for k in range(3):
            t = sub8(sq[pl.ds(k * 8, 8), :]).sum(axis=0, keepdims=True)
            RR[0, 3 + k:4 + k, :] = sum(t[:, j * 128:(j + 1) * 128] for j in range(6))
        RR[0, 6:7, :] = jnp.broadcast_to(jnp.sum(valid[...], axis=0, keepdims=True) * (1.0 / 128.0), (1, 128))
        tot.send(0)
    alone = (sc.sc0, sc.sc1, tiny.st0, tiny.a0, ti2, tiny.fin, tiny.last, to0)
    many = g.steps() + (tot.step,)
    def first(P0, P1, P2, P3, P4, P5, Q3, Q4, PR):
        load("cot", Q4); part(4); load("hs", P0); load("hi", P1); part(2); load("n2", Q1); load("mi", X0); load("uc", Q2); load("du", Q3); load("pt", PT)
        part(3); load("gt", P3); load("rs", P4); load("vl", P5); load("vs", P6); load("sp", SP); load("pr", PR); part(1); load("tok", TOK); part(0)
        full_barrier(p)
        def lo_():
            GG[...] = jnp.zeros_like(GG)
            RR[0] = jnp.zeros((8, 128), f32)
            ready(("cot", Q4))
            def rows(i): Q0[ds(i, 64), :] = (Q4[ds(i, 64), :].astype(f32) * valid[ds(i, 64), :]).astype(bf16)
            loop(8, rows)
            part_ready(4); ready(("hs", P0), ("hi", P1))
        def hi(m):
            c = pl.ds(m * 256, 256)
            ACC[...] = dot_nt(Q0[...], pair(WB, c, DWL, DWL, HB))
            t = dot_tn(P1[:, c], Q0[...]).astype(bf16)
            WB[c, DWL:HB], WB[c, HB + DWL:] = t[:, :DWL], t[:, DWL:]
            def rows(i):
                r = ds(i, 64)
                P2[r, c] = (ACC[r, :] * P0[r, c].astype(f32)).astype(bf16)
            loop(8, rows)
            if m == 5: load("at", P0); load("re", P1)
        def ub(m):
            if m == 0: part_ready(2); ready(("n2", Q1))
            c = pl.ds(m * 256, 256)
            X1[:, :, c] = (dot_nt(P2[:, 0:768], WA[c, UPL:HA]) + dot_nt(P2[:, 768:], WA[c, HA + UPL:])).reshape(64, 8, 256)
            WA[c, UPL:HA] = dot_tn(Q1[:, c], P2[:, 0:768]).astype(bf16)
            WA[c, HA + UPL:] = dot_tn(Q1[:, c], P2[:, 768:]).astype(bf16)
        def nb():
            load("sh", Q0)
            load("om", Q1)
            ready(("mi", X0), ("uc", Q2), ("du", Q3), ("pt", PT), ("om", Q1))
            def rows(i):
                r = ds(i, 64)
                m_, k = at3(X0, i), at3(X1, i)
                inv = lax.rsqrt(jnp.mean(m_ * m_, axis=-1, keepdims=True) + EPSILON)
                unit = m_ * inv
                GG[0:8, :] += sub8(k * unit)
                k = k * gain2[...]
                gm = Q4[r, :].astype(f32) * valid[r, :] + inv * (k - unit * jnp.mean(k * unit, axis=-1, keepdims=True))
                GMX[r, 0:768] = (gm * Q3[r, :].astype(f32)).astype(bf16)
                GMX[r, 2432:3200] = (gm * Q2[r, :].astype(f32)).astype(bf16)
                GT[r, :] = gm * Q1[r, :].astype(f32)
            loop(8, rows)
            load("bs", Q1)
        def ga(m):
            if m == 0: part_ready(3); ready(("gt", P3), ("at", P0), ("re", P1), ("rs", P4))
            c = pl.ds(m * 256, 256)
            gc = GMX[:, 2432:3200]
            ACC[...] = dot_nt(gc, pair(WB, c, 0, DWL, HB))
            t = dot_tn(P3[:, c], gc).astype(bf16)
            WB[c, 0:DWL], WB[c, HB:HB + DWL] = t[:, :DWL], t[:, DWL:]
            c2 = pl.ds(896 + m * 256, 256)
            def rows(i):
                r = ds(i, 64)
                a = ACC[r, :]
                P2[r, c] = (a * P1[r, c].astype(f32)).astype(bf16)
                GMX[r, c2] = (a * P0[r, c].astype(f32) * P4[r, c].astype(f32)).astype(bf16)
            loop(8, rows)
        def nr():
            ready(("tok", TOK))
            loop(8, lambda i: norm_rows(TOK, PT, U, Q2, i))
        def at_(b):
            if b == 0: ready(("vl", P5), ("vs", P6), ("sp", SP), ("pr", PR))
            r = ds(b, 128)
            pr = PR[r, :]
            gp = dot_nt(P2[r, :], P5[r, :])
            gs = (pr * (gp - jnp.sum(gp * pr, axis=-1, keepdims=True))).astype(bf16)
            el = pr.astype(bf16)
            for m in range(6):
                c = pl.ds(m * 256, 256)
                P6[r, c] = (dot_tn(el, P2[r, c]) * P6[r, c].astype(f32)).astype(bf16)
            s, slope = silu_and_slope(SP[r, :])
            q = (s * affine[0:1, :] + affine[1:2, :]).astype(bf16)
            k = (s * affine[2:3, :]).astype(bf16)
            gq = dot(gs, k) * Z_SCALE
            gk = dot_tn(gs, q) * Z_SCALE
            GMX[r, 768:896] = ((gq * affine[0:1, :] + gk * affine[2:3, :]) * slope).astype(bf16)
            for i, t in enumerate((gq * s, gq, gk * s)):
                RR[0, i:i + 1, :] += jnp.sum(t, axis=0, keepdims=True)
        run_plan(BACKWARD_PLAN[:CUT], (alone + (lo_, nb, nr), many + (hi, ub, ga, at_)))
    pl.run_scoped(first, big, big, big, big, big, big, mid, mid, v((512, 128), f32))
    def second(S, A):
        load("st", S)
        def vb(m):
            if m == 0: part_ready(1)
            c = pl.ds(m * 256, 256)
            X1[:, :, c] = (dot_nt(P6[:, 0:768], WA[c, VAL:UPL]) + dot_nt(P6[:, 768:], WA[c, HA + VAL:HA + UPL])).reshape(64, 8, 256)
        def dv(m):
            c = pl.ds(m * 256, 256)
            WA[c, VAL:UPL] = dot_tn(Q2[:, c], P6[:, 0:768]).astype(bf16)
            WA[c, HA + VAL:HA + UPL] = dot_tn(Q2[:, c], P6[:, 768:]).astype(bf16)
        def bl(m):
            if m == 0: part_ready(0); ready(("bs", Q1), ("sh", Q0))
            c = pl.ds(m * 256, 256)
            ACC[...] = dot_nt(GMX[:, 0:MXL], WA[c, 0:MXL]) + dot_nt(GMX[:, MXL:], WA[c, HA:HA + 1536])
            def rows(i):
                r, k = ds(i, 64), ds(i, 8)
                gb = ACC[r, :] * Q1[r, c].astype(f32)
                X0[k, :, c] = gb.reshape(8, 8, 256)
                GG[8:16, c] += sub8(gb * U[k, :, c].reshape(64, 256))
                X1[k, :, c] += (gb * omega[:, c]).reshape(8, 8, 256)
            loop(8, rows)
        def bk(j):
            if j == 0: ready(("st", S))
            bwd_states(X0, U, S, rate, A, E.at[0], G1, H, KS, j, 2)
        def tr(): SHT[...] = Q0[...].T
        def dm(k):
            off, w = MX_PARTS[k]
            WA[:, off:off + w] = dot(SHT[...], GMX[:, off:off + w]).astype(bf16)
            e = min(off + w, 1536)
            if off < e: WA[:, HA + off:HA + e] = dot(SHT[...], GMX[:, MXL + off:MXL + e]).astype(bf16)
            if off + w > 1536: WA[:, HA + 1536:HA + MXL] = jnp.zeros((768, 128), bf16)
        def gr(j):
            if j == 0: sc.sc2()
            bwd_grad(X0, U, S, A, Zb, rate, ec, H, X1, KS, AT, j, 2)
        def la():
            GG[16:24, :] = jnp.zeros((8, 768), f32)
            def rows(i):
                r = ds(i, 64)
                x = TOK[r, :].astype(f32)
                inv = lax.rsqrt(jnp.mean(x * x, axis=-1, keepdims=True) + EPSILON)
                unit = x * inv
                gn = at3(X1, i)
                GG[16:24, :] += sub8(gn * unit)
                k = gn * gain1[...]
                GT[r, :] += inv * (k - unit * jnp.mean(k * unit, axis=-1, keepdims=True))
            loop(8, rows)
            pltpu.make_async_copy(GT, o_gt, lo.at[0]).start()
            TP[...] = jnp.zeros_like(TP)
            TP[0:16, :] = G1[...]
            TP[16:32, :] = H[...]
            for k, i in ((32, 2), (33, 0), (34, 1)):
                TP[k:k + 1, :] = jnp.sum(GG[pl.ds(i * 8, 8), :], axis=0, keepdims=True)
            for j in range(6): T[j * 128:(j + 1) * 128, :] = TP[:, j * 128:(j + 1) * 128].T
        run_plan(BACKWARD_PLAN[CUT:], (alone + (tr, la), many + (vb, dv, bl, bk, dm, gr)))
    pl.run_scoped(second, v((64, 16, 768), f32), v((64, 16, 768), f32))
    o_red[...] = RR[5]
    g.drain(); tiny.drain(); tot.drain(); sc.drain()
    pltpu.make_async_copy(GT, o_gt, lo.at[0]).wait()

def backward_call(valid, affine, sq, ins):
    n = len(SCATTER_CHUNKS)
    v = pltpu.VMEM
    D_ = pltpu.SemaphoreType.DMA
    sds = jax.ShapeDtypeStruct
    vm_, any_ = pl.BlockSpec(memory_space=pltpu.VMEM), pl.BlockSpec(memory_space=pl.ANY)
    return pl.pallas_call(backward_kernel,
        out_shape=(sds((24, 3200), f32), sds((24, 1536), f32), sds((24, 1536), f32), sds((48, 768), f32), sds((48, 768), f32), sds((512, 768), f32), sds((24, 128), f32), sds((8, 128), f32)),
        in_specs=[vm_] * 3 + [any_] * len(ins),
        out_specs=[vm_] * 5 + [any_] + [vm_] * 2,
        scratch_shapes=rs_scratch() + [v((512, 768), bf16), v((128, 768), f32), v((64, 8, 768), f32), v((64, 8, 768), f32), v((64, 8, 768), f32), v((512, 768), f32),
            v((24, 768), f32), v((16, 768), f32), v((16, 768), f32), v((8, 128), f32), v((2, 16, 128), f32), v((512, 256), f32),
            v((2, 2, 16, 768), bf16), v((4, 2, 16, 768), bf16), v((2, 16, 768), f32),
            v((768, 128), f32), v((2, 192, 128), f32), v((192, 128), f32), v((3, 48, 128), f32), v((24, 128), f32), v((128, 768), f32),
            v((6, 8, 128), f32), v((5, 8, 128), f32), v((512, 1536), bf16), v((512, 3200), bf16), v((512, 768), bf16), v((512, 768), bf16), v((512, 768), bf16), v((768, 512), bf16), v((512, 128), f32),
            D_((n, 11)), D_((n, 11)), D_((4,)), D_((4,)), D_((10,)), D_((10,)), D_((5,)), D_((5,)), D_((len(BACK_IN),)), D_((1,)), D_((len(KINDS), 2))],
        compiler_params=pltpu.CompilerParams(collective_id=1, has_side_effects=True, vmem_limit_bytes=63 * 2**20),
    )(valid, affine, sq, *ins)


def per_device_tuned(tokens, cotangent, lengths, w_mx, w_value, w_out, w_up, w_down, ema_rate, ema_in, ema_out, gains, qk_affine):
    rate_own, in_own, out_own = (t.astype(f32) for t in (ema_rate, ema_in, ema_out))
    scale_own = jnp.sqrt(-jnp.expm1(-2.0 * rate_own))
    mine = jnp.pad(jnp.concatenate([rate_own, out_own * scale_own * in_own, gains.astype(f32)], axis=1), ((0, 0), (0, 93)))
    seq_pos = lax.axis_index("seq") * SEQ_DEV + jnp.arange(SEQ_DEV, dtype=jnp.int32)
    valid = (seq_pos[None, :] < lengths[:, None]).astype(f32).reshape(512, 1)
    tok = tokens.reshape(512, D)
    affine = jnp.pad(qk_affine.astype(f32), ((0, 5), (0, 0)))
    kept = forward_call(tok, valid, affine, mine, w_mx, w_value, w_out, w_up, w_down)
    K = {name: t for (name, _, _), t in zip(FORWARD_OUT, kept)}
    K["tok"], K["cot"], K["mi"] = tok, cotangent.reshape(512, D), K["mi"].reshape(64, 8, 768)
    g_mx, g_va, g_up, g_wo, g_wd, g_tok, tiny, red = backward_call(valid, affine, K["sq"], [K[name] for name in BACK_IN])
    g1, h1 = tiny[:, :16], tiny[:, 16:32]
    grad_ema_out = in_own * scale_own * g1
    grad_ema_in = out_own * scale_own * g1
    grad_ema_rate = out_own * in_own * (jnp.exp(-2.0 * rate_own) / scale_own * g1 - scale_own * h1)
    sums = jnp.sum(red[3:7], axis=1)
    rms_values = jnp.sqrt(sums[:3] / (sums[3] * D))
    return (K["res"].reshape(tokens.shape), g_tok.reshape(tokens.shape), g_mx, g_va, g_wo, g_up, g_wd,
        grad_ema_rate, grad_ema_in, grad_ema_out, tiny[:, 32:35], red[:3], rms_values)


def solution(mesh):
    placed = (
        P("dp", "seq", None),
        P("dp", "seq", None),
        P("dp"),
        P(("dp", "seq"), None),
        P(("dp", "seq"), None),
        P(("dp", "seq"), None),
        P(("dp", "seq"), None),
        P(("dp", "seq"), None),
        P(("dp", "seq"), None),
        P(("dp", "seq"), None),
        P(("dp", "seq"), None),
        P(("dp", "seq"), None),
        P(),
    )
    step = per_device_tuned if dict(mesh.shape) == {"dp": 4, "seq": 8} else per_device
    return jax.shard_map(
        step,
        mesh=mesh,
        in_specs=placed,
        out_specs=(
            P("dp", "seq", None),
            P("dp", "seq", None),
            P(("dp", "seq"), None),
            P(("dp", "seq"), None),
            P(("dp", "seq"), None),
            P(("dp", "seq"), None),
            P(("dp", "seq"), None),
            P(("dp", "seq"), None),
            P(("dp", "seq"), None),
            P(("dp", "seq"), None),
            P(("dp", "seq"), None),
            P(),
            P(),
        ),
        check_vma=False,
    )
```

```python
import functools

import jax
import jax.numpy as jnp
from jax import lax
from jax.experimental import pallas as pl
from jax.experimental.pallas import tpu as pltpu
from jax.sharding import PartitionSpec as P

MESH = pl.DeviceIdType.MESH
bf16, f32 = jnp.bfloat16, jnp.float32
D = 768
Z = 128
V = 1536
SPAN = 128
SEQ_DEV = 256


EPSILON = 1e-06
TOP_PRECISION = lax.Precision.HIGHEST


def prefix(value, axis, join, neutral):
    count, mine = (lax.axis_size(axis), lax.axis_index(axis))
    pieces = jax.tree.map(lambda part: lax.all_gather(part, axis), value)
    so_far = jax.tree.map(
        lambda part, zero: jnp.full_like(part, 0) + jnp.asarray(zero, part.dtype), value, neutral
    )

    def lap(position, so_far):
        longer = join(so_far, jax.tree.map(lambda part: part[position], pieces))
        return jax.tree.map(lambda new, old: jnp.where(position < mine, new, old), longer, so_far)

    return lax.fori_loop(0, count - 1, lap, so_far)


def prefix_2(value, axis, combine, identity):
    length, here = (lax.axis_size(axis), lax.axis_index(axis))
    everything = jax.tree.map(
        lambda part, kind: lax.all_gather(part.astype(kind), axis),
        value,
        jax.tree.map(lambda a: jnp.bfloat16 if a.dtype == jnp.float32 else a.dtype, value),
    )
    start = jax.tree.map(
        lambda part, zero: jnp.broadcast_to(jnp.asarray(zero, part.dtype), part.shape),
        value,
        identity,
    )

    def lap(k, before):
        at = length - 1 - k
        reached = at > here
        new = combine(
            before, jax.tree.map(lambda part, own: part[at].astype(own.dtype), everything, value)
        )
        return jax.tree.map(lambda a, b: jnp.where(reached, a, b), new, before)

    return lax.fori_loop(0, length, lap, start)


def silu_slope(values):
    sigmoid = jax.nn.sigmoid(values)
    return sigmoid * (1.0 + values * (1.0 - sigmoid))


def chain_combine(earlier, later):
    return (earlier[0] * later[0], later[0] * earlier[1] + later[1])


def ema_local(rate, beta, eta, input_signal):
    rows_here, length, channels = input_signal.shape
    block_len = min(64, length)
    blocks_count = length // block_len
    lag_values = jnp.arange(block_len, dtype=jnp.float32)
    powers = jnp.exp(-lag_values[:, None, None] * rate[None])
    scale_in = jnp.sqrt(-jnp.expm1(-2.0 * rate)) * beta
    kernel = jnp.sum(powers * (eta * scale_in)[None], axis=2)
    step_ids = jnp.arange(block_len)
    lag_index = jnp.clip(step_ids[:, None] - step_ids[None, :], 0, block_len - 1)
    toeplitz = jnp.where(
        (step_ids[:, None] >= step_ids[None, :])[:, :, None], kernel[lag_index], 0.0
    )
    leading = jnp.exp(-(lag_values[:, None, None] + 1.0) * rate[None]) * eta[None]
    trailing = powers[::-1] * scale_in[None]
    block_decay = jnp.exp(-block_len * rate)
    blocks = jnp.swapaxes(input_signal.reshape(rows_here, blocks_count, block_len, channels), 0, 1)

    def advance(carried, segment):
        smooth = jnp.einsum("tsd,bsd->btd", toeplitz, segment, precision=TOP_PRECISION)
        smooth = smooth + jnp.einsum("tdh,bdh->btd", leading, carried, precision=TOP_PRECISION)
        carried = block_decay * carried + jnp.einsum(
            "sdh,bsd->bdh", trailing, segment, precision=TOP_PRECISION
        )
        return (carried, smooth)

    initial = jnp.zeros((rows_here, channels, rate.shape[1]), jnp.float32)
    final_state, smooth = lax.scan(advance, initial, blocks)
    return (jnp.swapaxes(smooth, 0, 1).reshape(rows_here, length, channels), final_state)


def ema_carry(rate, eta, incoming):
    block_len = min(64, SEQ_DEV)
    blocks_count = SEQ_DEV // block_len
    lag_values = jnp.arange(block_len, dtype=jnp.float32)
    leading = jnp.exp(-(lag_values[:, None, None] + 1.0) * rate[None]) * eta[None]
    block_decay = jnp.exp(-block_len * rate)

    def advance(carried, unused):
        return (
            block_decay * carried,
            jnp.einsum("tdh,bdh->btd", leading, carried, precision=TOP_PRECISION),
        )

    _, smooth = lax.scan(advance, incoming, None, length=blocks_count)
    return jnp.swapaxes(smooth, 0, 1).reshape(incoming.shape[0], SEQ_DEV, incoming.shape[1])


def per_device(
    tokens,
    cotangent,
    lengths,
    w_mx,
    w_value,
    w_out,
    w_up,
    w_down,
    ema_rate,
    ema_in,
    ema_out,
    gains,
    qk_affine,
):
    gathered = (
        lax.all_gather(w_mx, ("dp", "seq"), axis=0, tiled=True),
        lax.all_gather(w_value, ("dp", "seq"), axis=0, tiled=True),
        lax.all_gather(w_out, ("dp", "seq"), axis=0, tiled=True),
        lax.all_gather(w_up, ("dp", "seq"), axis=0, tiled=True),
        lax.all_gather(w_down, ("dp", "seq"), axis=0, tiled=True),
        lax.all_gather(ema_rate, ("dp", "seq"), axis=0, tiled=True),
        lax.all_gather(ema_in, ("dp", "seq"), axis=0, tiled=True),
        lax.all_gather(ema_out, ("dp", "seq"), axis=0, tiled=True),
        lax.all_gather(gains, ("dp", "seq"), axis=0, tiled=True),
    )
    mx_full, value_full, out_full, up_full, down_full, rate_low, beta_low, eta_low, gain_low = (
        gathered
    )
    rate = rate_low.astype(jnp.float32)
    beta = beta_low.astype(jnp.float32)
    eta = eta_low.astype(jnp.float32)
    gain_all = gain_low.astype(jnp.float32)
    gain_first = gain_all[:, 0]
    gain_second = gain_all[:, 1]
    omega_gain = gain_all[:, 2]
    affine = qk_affine.astype(jnp.float32)
    rows_here = tokens.shape[0]
    spans_dev = SEQ_DEV // SPAN
    score_scale = Z ** (-0.5)
    inputs = tokens.astype(jnp.float32)
    seq_pos = lax.axis_index("seq") * SEQ_DEV + jnp.arange(SEQ_DEV, dtype=jnp.int32)
    valid_rows = (seq_pos[None, :] < lengths[:, None]).astype(jnp.float32)[:, :, None]
    inverse1 = lax.rsqrt(jnp.mean(inputs * inputs, axis=-1, keepdims=True) + EPSILON)
    unit1 = inputs * inverse1
    normed = unit1 * gain_first
    normed_low = normed.astype(jnp.bfloat16)
    value_pre = jnp.einsum(
        "bsd,dv->bsv", normed_low, value_full, preferred_element_type=jnp.float32
    )
    value_low = jax.nn.silu(value_pre).astype(jnp.bfloat16)
    (smooth_local, end_local), pull_local = jax.vjp(ema_local, rate, beta, eta, normed)
    growth = jnp.exp(-SEQ_DEV * rate)
    start_state = prefix(
        (growth, end_local),
        "seq",
        chain_combine,
        (jnp.ones_like(growth), jnp.zeros_like(end_local)),
    )[1]
    smooth_carry, pull_carry = jax.vjp(ema_carry, rate, eta, start_state)
    blend = smooth_local + smooth_carry + omega_gain * normed
    shifted_low = jax.nn.silu(blend).astype(jnp.bfloat16)
    mixed = jnp.einsum("bsd,dk->bsk", shifted_low, mx_full, preferred_element_type=jnp.float32)
    update = jax.nn.sigmoid(mixed[..., :D])
    shared_pre = mixed[..., D : D + Z]
    shared = jax.nn.silu(shared_pre)
    reset_pre = mixed[..., D + Z : D + Z + V]
    reset = jax.nn.silu(reset_pre)
    direct = mixed[..., D + Z + V :]
    query_low = (
        (shared * affine[0] + affine[1]).astype(jnp.bfloat16).reshape(rows_here, spans_dev, SPAN, Z)
    )
    key_low = (shared * affine[2]).astype(jnp.bfloat16).reshape(rows_here, spans_dev, SPAN, Z)
    value_tiles = value_low.reshape(rows_here, spans_dev, SPAN, V)
    scores = (
        jnp.einsum("bnqz,bnkz->bnqk", query_low, key_low, preferred_element_type=jnp.float32)
        * score_scale
    )
    causal = jnp.arange(SPAN)[:, None] >= jnp.arange(SPAN)[None, :]
    masked = jnp.where(causal, scores, -1e30)
    peak = jnp.max(masked, axis=-1, keepdims=True)
    expo = jnp.exp(masked - peak)
    attention_weights = expo / jnp.sum(expo, axis=-1, keepdims=True)
    probs_low = attention_weights.astype(jnp.bfloat16)
    attended_output = jnp.einsum(
        "bnqk,bnkv->bnqv", probs_low, value_tiles, preferred_element_type=jnp.float32
    ).reshape(rows_here, SEQ_DEV, V)
    gated_low = (reset * attended_output).astype(jnp.bfloat16)
    cand_pre = direct + jnp.einsum(
        "bsv,vd->bsd", gated_low, out_full, preferred_element_type=jnp.float32
    )
    candidate = jax.nn.silu(cand_pre)
    attn_branch = update * (candidate - inputs)
    middle = inputs + attn_branch
    inverse2 = lax.rsqrt(jnp.mean(middle * middle, axis=-1, keepdims=True) + EPSILON)
    unit2 = middle * inverse2
    normed2_low = (unit2 * gain_second).astype(jnp.bfloat16)
    up_pre = jnp.einsum("bsd,df->bsf", normed2_low, up_full, preferred_element_type=jnp.float32)
    hidden_low = jax.nn.silu(up_pre).astype(jnp.bfloat16)
    ffn_branch = jnp.einsum(
        "bsf,fd->bsd", hidden_low, down_full, preferred_element_type=jnp.float32
    )
    output = middle + ffn_branch
    again = (
        lax.all_gather(w_mx, ("dp", "seq"), axis=0, tiled=True),
        lax.all_gather(w_value, ("dp", "seq"), axis=0, tiled=True),
        lax.all_gather(w_out, ("dp", "seq"), axis=0, tiled=True),
        lax.all_gather(w_up, ("dp", "seq"), axis=0, tiled=True),
        lax.all_gather(w_down, ("dp", "seq"), axis=0, tiled=True),
    )
    mixer_backward, value_back, out_back, up_back, down_back = again
    grad_out = cotangent.astype(jnp.float32) * valid_rows
    grad_out_low = grad_out.astype(jnp.bfloat16)
    grad_down = jnp.einsum(
        "bsf,bsd->fd", hidden_low, grad_out_low, preferred_element_type=jnp.float32
    )
    grad_hidden = jnp.einsum(
        "bsd,fd->bsf", grad_out_low, down_back, preferred_element_type=jnp.float32
    )
    grad_up_low = (grad_hidden * silu_slope(up_pre)).astype(jnp.bfloat16)
    grad_up = jnp.einsum(
        "bsd,bsf->df", normed2_low, grad_up_low, preferred_element_type=jnp.float32
    )
    grad_normed2 = jnp.einsum(
        "bsf,df->bsd", grad_up_low, up_back, preferred_element_type=jnp.float32
    )
    grad_gain_second = jnp.sum(grad_normed2 * unit2, axis=(0, 1))
    scaled2 = grad_normed2 * gain_second
    grad_middle = grad_out + inverse2 * (
        scaled2 - unit2 * jnp.mean(scaled2 * unit2, axis=-1, keepdims=True)
    )
    grad_update = grad_middle * (candidate - inputs)
    grad_cand_pre = grad_middle * update * silu_slope(cand_pre)
    grad_cand_low = grad_cand_pre.astype(jnp.bfloat16)
    grad_out_proj = jnp.einsum(
        "bsv,bsd->vd", gated_low, grad_cand_low, preferred_element_type=jnp.float32
    )
    grad_gated = jnp.einsum(
        "bsd,vd->bsv", grad_cand_low, out_back, preferred_element_type=jnp.float32
    )
    grad_reset = grad_gated * attended_output
    grad_attended_low = (
        (grad_gated * reset).astype(jnp.bfloat16).reshape(rows_here, spans_dev, SPAN, V)
    )
    grad_probs = jnp.einsum(
        "bnqv,bnkv->bnqk", grad_attended_low, value_tiles, preferred_element_type=jnp.float32
    )
    grad_values = jnp.einsum(
        "bnqk,bnqv->bnkv", probs_low, grad_attended_low, preferred_element_type=jnp.float32
    ).reshape(rows_here, SEQ_DEV, V)
    grad_scores_low = (
        attention_weights
        * (grad_probs - jnp.sum(grad_probs * attention_weights, axis=-1, keepdims=True))
    ).astype(jnp.bfloat16)
    grad_query = (
        jnp.einsum("bnqk,bnkz->bnqz", grad_scores_low, key_low, preferred_element_type=jnp.float32)
        * score_scale
    ).reshape(rows_here, SEQ_DEV, Z)
    grad_key = (
        jnp.einsum(
            "bnqk,bnqz->bnkz", grad_scores_low, query_low, preferred_element_type=jnp.float32
        )
        * score_scale
    ).reshape(rows_here, SEQ_DEV, Z)
    grad_affine = jnp.stack(
        [
            jnp.sum(grad_query * shared, axis=(0, 1)),
            jnp.sum(grad_query, axis=(0, 1)),
            jnp.sum(grad_key * shared, axis=(0, 1)),
        ]
    )
    grad_shared = grad_query * affine[0] + grad_key * affine[2]
    grad_mixed_low = jnp.concatenate(
        [
            grad_update * update * (1.0 - update),
            grad_shared * silu_slope(shared_pre),
            grad_reset * silu_slope(reset_pre),
            grad_cand_pre,
        ],
        axis=-1,
    ).astype(jnp.bfloat16)
    grad_mx = jnp.einsum(
        "bsd,bsk->dk", shifted_low, grad_mixed_low, preferred_element_type=jnp.float32
    )
    grad_shifted = jnp.einsum(
        "bsk,dk->bsd", grad_mixed_low, mixer_backward, preferred_element_type=jnp.float32
    )
    grad_blend = grad_shifted * silu_slope(blend)
    grad_omega = jnp.sum(grad_blend * normed, axis=(0, 1))
    grad_value_low = (grad_values * silu_slope(value_pre)).astype(jnp.bfloat16)
    grad_value_proj = jnp.einsum(
        "bsd,bsv->dv", normed_low, grad_value_low, preferred_element_type=jnp.float32
    )
    grad_normed = grad_blend * omega_gain + jnp.einsum(
        "bsv,dv->bsd", grad_value_low, value_back, preferred_element_type=jnp.float32
    )
    rate_from_carry, eta_from_carry, direct_adjoint = pull_carry(grad_blend)
    later_adjoint = prefix_2(
        (growth, direct_adjoint),
        "seq",
        chain_combine,
        (jnp.ones_like(growth), jnp.zeros_like(direct_adjoint)),
    )[1]
    rate_from_local, grad_beta, eta_from_local, normed_from_ema = pull_local(
        (grad_blend, later_adjoint)
    )
    rate_from_growth = jnp.sum(later_adjoint * start_state, axis=0) * (-SEQ_DEV * growth)
    grad_rate = rate_from_carry + rate_from_local + rate_from_growth
    grad_eta = eta_from_carry + eta_from_local
    grad_normed = grad_normed + normed_from_ema
    grad_gain_first = jnp.sum(grad_normed * unit1, axis=(0, 1))
    scaled1 = grad_normed * gain_first
    grad_tokens = grad_middle * (1.0 - update) + inverse1 * (
        scaled1 - unit1 * jnp.mean(scaled1 * unit1, axis=-1, keepdims=True)
    )
    grad_gains = jnp.stack([grad_gain_first, grad_gain_second, grad_omega], axis=1)
    shards = (
        lax.psum_scatter(grad_mx, ("dp", "seq"), scatter_dimension=0, tiled=True),
        lax.psum_scatter(grad_value_proj, ("dp", "seq"), scatter_dimension=0, tiled=True),
        lax.psum_scatter(grad_out_proj, ("dp", "seq"), scatter_dimension=0, tiled=True),
        lax.psum_scatter(grad_up, ("dp", "seq"), scatter_dimension=0, tiled=True),
        lax.psum_scatter(grad_down, ("dp", "seq"), scatter_dimension=0, tiled=True),
        lax.psum_scatter(grad_rate, ("dp", "seq"), scatter_dimension=0, tiled=True),
        lax.psum_scatter(grad_beta, ("dp", "seq"), scatter_dimension=0, tiled=True),
        lax.psum_scatter(grad_eta, ("dp", "seq"), scatter_dimension=0, tiled=True),
        lax.psum_scatter(grad_gains, ("dp", "seq"), scatter_dimension=0, tiled=True),
    )
    squares = jnp.stack(
        [
            jnp.sum(valid_rows * output * output),
            jnp.sum(valid_rows * attn_branch * attn_branch),
            jnp.sum(valid_rows * ffn_branch * ffn_branch),
            jnp.sum(valid_rows),
        ]
    )
    affine_total, square_total = lax.psum((grad_affine, squares), ("dp", "seq"))
    rms_values = jnp.sqrt(square_total[:3] / (square_total[3] * D))
    return (
        output.astype(jnp.bfloat16),
        grad_tokens,
        shards[0],
        shards[1],
        shards[2],
        shards[3],
        shards[4],
        shards[5],
        shards[6],
        shards[7],
        shards[8],
        affine_total,
        rms_values,
    )


HA, HB = 3200, 768
RA, RB = 48, 96

MXL, VAL, UPL, ONE, DWL = 1664, 1664, 2432, 768, 384
KINDS = ((0, 0, 1664), (0, 1664, 768), (0, 2432, 768), (1, 0, 384), (1, 384, 384))
GATHER_CHUNKS = ((0, 1664, 128, "xy"), (0, 1792, 256, "yx"), (0, 2048, 256, "xy"), (0, 2304, 128, "yx"), (0, 0, 256, "xy"), (0, 256, 256, "yx"), (0, 512, 256, "xy"), (0, 768, 384, "yx"), (0, 1152, 256, "xy"), (0, 1408, 256, "yx"), (1, 0, 128, "xy"), (1, 128, 256, "yx"), (0, 2432, 128, "xy"), (0, 2560, 128, "yx"), (0, 2688, 128, "z"), (0, 2816, 128, "z"), (0, 2944, 128, "z"), (0, 3072, 128, "z"), (1, 384, 128, "xy"), (1, 512, 128, "yx"), (1, 640, 128, "xy"))
SCATTER_CHUNKS = ((1, 384, 128, "xy"), (1, 512, 128, "yx"), (1, 640, 128, "yx"), (0, 2432, 512, "xy"), (0, 2944, 256, "yx"), (1, 0, 128, "yx"), (1, 128, 256, "xy"), (0, 1664, 512, "yx"), (0, 2176, 256, "xy"), (0, 0, 384, "yx"), (0, 384, 384, "xy"), (0, 768, 384, "yx"), (0, 1152, 256, "xy"), (0, 1408, 256, "yx"))

class Pos:
    def __init__(s):
        s.dp, s.sq = lax.axis_index("dp"), lax.axis_index("seq")
        s.x, s.c, s.z, s.y = s.dp // 2, s.dp % 2, s.sq // 2, s.sq % 2
        s.sib = (s.dp + 1 - 2 * s.c, s.sq)
        s.xn = (s.dp + 2 - 4 * s.x, s.sq)
        s.yn = (s.dp, s.sq + 1 - 2 * s.y)
        s.dpx = s.dp + 2 - 4 * s.x
    def zof(s, d): return (s.z + d) % 4
    def zn(s, d): return (s.dp, s.zof(d) * 2 + s.y)

def rcopy(src, dst, ss, rs, dev):
    return pltpu.make_async_remote_copy(src_ref=src, dst_ref=dst, send_sem=ss, recv_sem=rs, device_id=dev, device_id_type=MESH)

def full_barrier(p):
    bar = pltpu.get_barrier_semaphore()
    sig = lambda d: pl.semaphore_signal(bar, inc=1, device_id=d, device_id_type=MESH)
    for d in (p.sib, p.xn, p.yn, p.zn(1), p.zn(2), p.zn(3)): sig(d)
    pl.semaphore_wait(bar, 6)

def at(ref, rows, nrows, half, w, off, width):
    return ref.at[pl.ds(pl.multiple_of(rows, 48), nrows), pl.ds(pl.multiple_of(half * w + off, 128), width)]

class Gather:
    def __init__(s, pos, bufs, ss, rs):
        s.p, s.bufs, s.ss, s.rs, s.here = pos, bufs, ss, rs, set()
    def unit(s, i, dp, z, half, n=1):
        b, off, width, _ = GATHER_CHUNKS[i]
        R = (RA, RB)[b]
        return at(s.bufs[b], (dp * 4 + z) * R, n * R, half, (HA, HB)[b], off, width)
    def cp(s, i, k, ref, dev):
        return rcopy(ref, ref, s.ss.at[i, k], s.rs.at[i, k], dev)
    def z0(s, i):
        p = s.p
        u = s.unit(i, p.dp, p.z, p.y)
        for d in (1, 3, 2): rcopy(u, u, s.ss.at[i, d - 1], s.rs.at[i, p.z], p.zn(d)).start()
    def s1(s, i):
        p = s.p
        for d in (1, 2, 3):
            u = s.unit(i, p.dp, p.zof(d), p.y)
            rcopy(u, u, s.ss.at[i, 0], s.rs.at[i, p.zof(d)], p.sib).wait_recv()
        u = s.unit(i, p.dp, 0, p.y, 4)
        s.cp(i, 4, u, p.xn if GATHER_CHUNKS[i][3] == "xy" else p.yn).start()
        s.cp(i, 7, u, p.sib).start()
    def s2(s, i):
        p = s.p
        xy = GATHER_CHUNKS[i][3] == "xy"
        r = s.unit(i, p.dpx, 0, p.y, 4) if xy else s.unit(i, p.dp, 0, 1 - p.y, 4)
        s.cp(i, 4, r, p.xn).wait_recv()
        nxt = p.yn if xy else p.xn
        s.cp(i, 5, s.unit(i, p.dp, 0, p.y, 4), nxt).start()
        s.cp(i, 6, r, nxt).start()
        s.cp(i, 8, r, p.sib).start()
    def s3(s, i, k):
        p = s.p
        if GATHER_CHUNKS[i][3] == "xy": r = s.unit(i, (p.dp, p.dpx)[k], 0, 1 - p.y, 4)
        else: r = s.unit(i, p.dpx, 0, (p.y, 1 - p.y)[k], 4)
        s.cp(i, 5 + k, r, p.sib).wait_recv()
        s.cp(i, 9 + k, r, p.sib).start()
    def sa(s, i): s.s3(i, 0)
    def sb(s, i): s.s3(i, 1)
    def need(s, b, lo, hi):
        for i, (bb, off, w, _) in enumerate(GATHER_CHUNKS):
            if bb == b and off < hi and off + w > lo and i not in s.here:
                s.here.add(i)
                u = s.unit(i, s.p.dp, 0, s.p.y, 4)
                for k in (7, 8, 9, 10): s.cp(i, k, u, s.p.sib).wait_recv()
    def c1(s, i):
        s.cp(i, 4, s.unit(i, s.p.dp, s.p.z, s.p.y), s.p.xn).start()
    def c2(s, i):
        p = s.p
        r = s.unit(i, p.dpx, p.z, p.y)
        s.cp(i, 4, r, p.xn).wait_recv()
        s.cp(i, 5, s.unit(i, p.dp, p.z, p.y), p.yn).start()
        s.cp(i, 6, r, p.yn).start()
    def four(s, i, z):
        p = s.p
        return [s.unit(i, d, z, h) for d in (p.dp, p.dpx) for h in (p.y, 1 - p.y)]
    def c3(s, i):
        p = s.p
        us = s.four(i, p.z)
        s.cp(i, 5, us[1], p.yn).wait_recv()
        s.cp(i, 6, us[3], p.yn).wait_recv()
        for d in (1, 3, 2):
            for k, u in enumerate(us):
                rcopy(u, u, s.ss.at[i, 7 + 4 * d + k], s.rs.at[i, 11 + 4 * (d - 1) + k], p.zn(d)).start()
    def c4(s, i):
        p = s.p
        for d in (1, 2, 3):
            for k, u in enumerate(s.four(i, p.z)):
                rcopy(u, u, s.ss.at[i, 0], s.rs.at[i, 11 + 4 * (d - 1) + k], p.sib).wait_recv()
        for k, (d, h) in enumerate(((p.dp, p.y), (p.dpx, p.y), (p.dp, 1 - p.y), (p.dpx, 1 - p.y))):
            s.cp(i, 7 + k, s.unit(i, d, 0, h, 4), p.sib).start()
    def steps(s): return (s.z0, s.s1, s.s2, s.sa, s.sb, s.c1, s.c2, s.c3, s.c4)
    def drain(s):
        p = s.p
        for i, (_, _, _, order) in enumerate(GATHER_CHUNKS):
            u1 = s.unit(i, p.dp, 0, p.y)
            u = s.unit(i, p.dp, 0, p.y, 4)
            one = (4, 5, 6) + tuple(range(11, 23)) if order == "z" else (0, 1, 2)
            for k in one: s.cp(i, k, u1, p.sib).wait_send()
            for k in range(4, 11):
                if k not in one: s.cp(i, k, u, p.sib).wait_send()

class Scatter:
    NS = 11
    def __init__(s, pos, P, L1, L2, L3, L4, F, G, out, ss, rs):
        s.p, s.P, s.L1, s.L2, s.L3, s.L4, s.F, s.G, s.out, s.ss, s.rs = pos, P, L1, L2, L3, L4, F, G, out, ss, rs
    def geom(s, i):
        b, off, w, order = SCATTER_CHUNKS[i]
        return b, (RA, RB)[b], (HA, HB)[b], off, w, order
    def cols(s, i, yy):
        b, R, W, off, w, _ = s.geom(i)
        return pl.ds(pl.multiple_of(yy * W + off, 128), w)
    def piece(s, i, xx, c, yy, z=0, n=4):
        b, R, W, off, w, _ = s.geom(i)
        return s.P[b].at[pl.ds(pl.multiple_of(((xx * 2 + c) * 4 + z) * R, 48), n * R), s.cols(i, yy)]
    def cp(s, i, k, src, dst, dev):
        return rcopy(src, dst, s.ss.at[i, k], s.rs.at[i, k], dev)
    def add(s, dst, src, nrows):
        def body(r, _):
            rr = pl.ds(pl.multiple_of(r * 48, 48), 48)
            dst[rr, :] = (dst[rr, :].astype(f32) + src[rr, :].astype(f32)).astype(bf16)
            return 0
        lax.fori_loop(0, nrows // 48, body, 0)
    def l1(s, i, xx, yy):
        return s.L1[SCATTER_CHUNKS[i][0]].at[xx, :, s.cols(i, yy)]
    def st0(s, i):
        p = s.p
        for k, (xx, yy) in enumerate(((0, 0), (0, 1), (1, 0), (1, 1))):
            s.cp(i, k, s.piece(i, xx, 1 - p.c, yy), s.l1(i, xx, yy), p.sib).start()
    def a0(s, i):
        R = s.geom(i)[1]
        for k, (xx, yy) in enumerate(((0, 0), (0, 1), (1, 0), (1, 1))):
            l = s.l1(i, xx, yy)
            s.cp(i, k, l, l, s.p.sib).wait_recv()
            s.add(s.piece(i, xx, s.p.c, yy), l, 4 * R)
    def l2(s, i, k):
        b, R, W, off, w, _ = s.geom(i)
        return s.L2[b].at[k, :, pl.ds(off, w)]
    def l3(s, i):
        b, R, W, off, w, _ = s.geom(i)
        return s.L3[b].at[:, pl.ds(off, w)]
    def st1(s, i):
        p, order = s.p, s.geom(i)[5]
        for k in (0, 1):
            src = s.piece(i, k, p.c, 1 - p.y) if order == "xy" else s.piece(i, 1 - p.x, p.c, k)
            s.cp(i, 4 + k, src, s.l2(i, k), p.yn if order == "xy" else p.xn).start()
    def a1(s, i):
        p = s.p; b, R, W, off, w, order = s.geom(i)
        for k in (0, 1):
            l = s.l2(i, k)
            s.cp(i, 4 + k, l, l, p.xn).wait_recv()
            s.add(s.piece(i, k, p.c, p.y) if order == "xy" else s.piece(i, p.x, p.c, k), l, 4 * R)
    def st2(s, i):
        p, order = s.p, s.geom(i)[5]
        src = s.piece(i, 1 - p.x, p.c, p.y) if order == "xy" else s.piece(i, p.x, p.c, 1 - p.y)
        s.cp(i, 6, src, s.l3(i), p.xn if order == "xy" else p.yn).start()
    def a2(s, i):
        l = s.l3(i)
        s.cp(i, 6, l, l, s.p.xn).wait_recv()
        s.add(s.piece(i, s.p.x, s.p.c, s.p.y), l, 4 * s.geom(i)[1])
    def l4(s, i, k):
        b, R, W, off, w, _ = s.geom(i)
        return s.L4[b].at[k, :, pl.ds(off, w)]
    def zsend(s, i):
        p = s.p
        for d in (1, 3, 2):
            rcopy(s.piece(i, p.x, p.c, p.y, p.zof(d), 1), s.l4(i, 3 - d), s.ss.at[i, 6 + d], s.rs.at[i, 10 - d], p.zn(d)).start()
    def fin(s, i):
        p = s.p; b, R, W, off, w, _ = s.geom(i)
        F, G, out = s.F[b], s.G[b], s.out
        h = R // 2
        t = s.piece(i, p.x, p.c, p.y, p.z, 1)[...].astype(f32)
        for k in range(3):
            l = s.l4(i, k)
            s.cp(i, 7 + k, l, l, p.sib).wait_recv()
            t = t + l[...].astype(f32)
        F[:, pl.ds(off, w)] = t
        src = F.at[pl.ds(pl.multiple_of((1 - p.y) * h, 8), h), pl.ds(off, w)]
        s.cp(i, 10, src, G.at[:, pl.ds(off, w)], p.yn).start()
        for yy in (0, 1):
            @pl.when(p.y == yy)
            def _(): out(b, yy, off, w, lambda o, k: F[pl.ds(yy * h, h), pl.ds(off + o, k)])
    def last(s, i):
        p = s.p; b, R, W, off, w, _ = s.geom(i)
        l = s.G[b].at[:, pl.ds(off, w)]
        s.cp(i, 10, l, l, p.yn).wait_recv()
        for yy in (0, 1):
            @pl.when(p.y == 1 - yy)
            def _(): s.out(b, yy, off, w, lambda o, k: l[:, pl.ds(o, k)])
    def r0(s, i): s.st0(i)
    def r1(s, i): s.a0(i); s.st1(i)
    def r2(s, i): s.a1(i); s.st2(i)
    def r3(s, i): s.a2(i); s.zsend(i)
    def r4(s, i): s.fin(i)
    def r5(s, i): s.last(i)
    def steps(s): return (s.r0, s.r1, s.r2, s.r3, s.r4, s.r5)
    def drain(s):
        p = s.p
        for i in range(len(SCATTER_CHUNKS)):
            b, R, W, off, w, _ = s.geom(i)
            for k, ref in [(k, s.l1(i, 0, 0)) for k in range(4)] + [(4, s.l2(i, 0)), (5, s.l2(i, 1)), (6, s.l3(i)), (10, s.G[b].at[:, pl.ds(off, w)])] + [(7 + k, s.l4(i, k)) for k in range(3)]:
                s.cp(i, k, ref, ref, p.sib).wait_send()

def rs_scratch():
    v = pltpu.VMEM
    return [v((768, 2 * HA), bf16), v((1536, 2 * HB), bf16), v((2, 192, 2 * HA), bf16), v((2, 384, 2 * HB), bf16),
        v((2, 192, HA), bf16), v((2, 384, HB), bf16), v((192, HA), bf16), v((384, HB), bf16),
        v((3, 48, HA), bf16), v((3, 96, HB), bf16), v((48, HA), f32), v((96, HB), f32), v((24, HA), f32), v((48, HB), f32)]

NK = 32
NB = 2

def lanes(j): return pl.ds(pl.multiple_of(j * 128, 128), 128)
def rows_(i): return pl.ds(pl.multiple_of(i * 8, 8), 8)
def tree(xs):
    xs = list(xs)
    while len(xs) > 1:
        xs = [xs[i] + xs[i + 1] if i + 1 < len(xs) else xs[i] for i in range(0, len(xs), 2)]
    return xs[0]

def fwd_states(U, rate, S, END, j, unroll=2):
    ln = lanes(j)
    r = rate[0:16, ln]
    w = [jnp.exp(r * (s - 7.0)) for s in range(8)]
    q8 = jnp.exp(r * -8.0)
    def body(k, st):
        new = []
        for b in range(NB):
            S[b * NK + k, :, ln] = st[b]
            parts = [w[s] * U[b * NK + k, pl.ds(s, 1), ln] for s in range(8)]
            new.append(q8 * st[b] + tree(parts))
        return tuple(new)
    st = lax.fori_loop(0, NK, body, tuple(jnp.zeros((16, 128), f32) for _ in range(NB)), unroll=unroll)
    for b in range(NB): END[b, :, ln] = st[b].astype(END.dtype)

def conv_tables(rate, ec, j):
    ln = lanes(j)
    it = lax.broadcasted_iota(jnp.int32, (8, 128), 0).astype(f32)
    E, K = [], []
    for h in range(16):
        rb = jnp.broadcast_to(rate[pl.ds(h, 1), ln], (8, 128)); eb = jnp.broadcast_to(ec[pl.ds(h, 1), ln], (8, 128))
        K.append(jnp.exp(-it * rb) * eb)
        E.append(jnp.exp(-(it + 1.0) * rb) * eb)
    return E, tree(K)

def fwd_smooth(U, S, S0, rate, ec, omega, BL, KS, j, unroll=1):
    ln = lanes(j)
    r = rate[0:16, ln]
    q8 = jnp.exp(r * -8.0)
    E, K = conv_tables(rate, ec, j)
    KS[...] = K
    ii = lax.broadcasted_iota(jnp.int32, (8, 128), 0)
    KM = [jnp.where(ii >= l, jnp.broadcast_to(KS[pl.ds(l, 1), :], (8, 128)), 0.0) for l in range(8)]
    om = jnp.broadcast_to(omega[:, ln], (8, 128))
    KM[0] = KM[0] + om
    def body(k, gs):
        new = []
        for b in range(NB):
            i = b * NK + k
            S[i, :, ln] = S[i, :, ln] + gs[b]
            u = U[i, :, ln]
            parts = [KM[0] * u] + [KM[l] * pltpu.roll(u, l, 0) for l in range(1, 8)]
            parts += [E[h] * S[i, pl.ds(h, 1), ln] for h in range(16)]
            BL[i, :, ln] = tree(parts)
            new.append(q8 * gs[b])
        return tuple(new)
    lax.fori_loop(0, NK, body, tuple(S0[b, :, ln] for b in range(NB)), unroll=unroll)

def bwd_states(Gr, U, S, rate, A, DIR, G1, H, CS, j, unroll=1):
    ln = lanes(j)
    r = rate[0:16, ln]
    w = [jnp.exp(r * -float(s)) for s in range(8)]
    q8 = jnp.exp(r * -8.0)
    def body(kk, c):
        k = NK - 1 - kk
        st, g1, h1, C = c
        new, C = [], list(C)
        for b in range(NB):
            i = b * NK + k
            A[i, :, ln] = st[b]
            p = [Gr[i, pl.ds(0, 1), ln]] + [w[s] * Gr[i, pl.ds(s, 1), ln] for s in range(1, 8)]
            later = B1 = p[7]
            for t in range(6, 0, -1):
                later = later + p[t]
                B1 = B1 + later
            Bg = later + p[0]
            Sk = S[i, :, ln]
            g1 = g1 + Sk * Bg
            h1 = h1 + Sk * B1
            new.append(q8 * st[b] + Bg)
            u, g = U[i, :, ln], Gr[i, :, ln]
            C = [C[l] + g * (pltpu.roll(u, l, 0) if l else u) for l in range(8)]
        return tuple(new), g1, h1, tuple(C)
    z = jnp.zeros((16, 128), f32)
    st, g1, h1, C = lax.fori_loop(0, NK, body, (tuple(z for _ in range(NB)), z, z, tuple(jnp.zeros((8, 128), f32) for _ in range(8))), unroll=unroll)
    for b in range(NB): DIR[b, :, ln] = st[b].astype(DIR.dtype)
    ii = lax.broadcasted_iota(jnp.int32, (8, 128), 0)
    g1, h1 = g1 * w[1], h1 * w[1]
    for l in range(8):
        cl = jnp.sum(jnp.where(ii >= l, C[l], 0.0), axis=0, keepdims=True)
        t = w[l] * cl
        g1 = g1 + t
        if l: h1 = h1 + t * float(l)
    G1[:, ln] = g1
    H[:, ln] = h1

def bwd_grad(Gr, U, S, A, A0, rate, ec, H, DU, KS, AT, j, unroll=1):
    ln = lanes(j)
    r = rate[0:16, ln]
    q8 = jnp.exp(r * -8.0)
    c8 = 8.0 * jnp.exp(r * -9.0)
    wu = [jnp.exp(r * (s - 8.0)) * (8.0 - s) for s in range(8)]
    it = lax.broadcasted_iota(jnp.int32, (8, 128), 0).astype(f32)
    E, K = [], []
    for h in range(16):
        rb = jnp.broadcast_to(rate[pl.ds(h, 1), ln], (8, 128)); eb = jnp.broadcast_to(ec[pl.ds(h, 1), ln], (8, 128))
        K.append(jnp.exp(-it * rb) * eb)
        E.append(jnp.exp((it - 8.0) * rb) * eb)
    KS[...] = tree(K)
    ii = lax.broadcasted_iota(jnp.int32, (8, 128), 0)
    KM = [jnp.where(ii < 8 - l, jnp.broadcast_to(KS[pl.ds(l, 1), :], (8, 128)), 0.0) for l in range(8)]
    def body(kk, c):
        k = NK - 1 - kk
        gs, h1 = c
        new = []
        for b in range(NB):
            i = b * NK + k
            Ak = A[i, :, ln] + gs[b]
            AT[b] = Ak
            Bu = tree([wu[s] * U[i, pl.ds(s, 1), ln] for s in range(8)])
            h1 = h1 + Ak * (Bu + c8 * S[i, :, ln])
            g = Gr[i, :, ln]
            parts = [KM[0] * g] + [KM[l] * pltpu.roll(g, 8 - l, 0) for l in range(1, 8)]
            parts += [E[h] * AT[b, pl.ds(h, 1), :] for h in range(16)]
            DU[i, :, ln] += tree(parts)
            new.append(q8 * gs[b])
        return tuple(new), h1
    gs, h1 = lax.fori_loop(0, NK, body, (tuple(A0[b, :, ln] for b in range(NB)), H[:, ln]), unroll=unroll)
    H[:, ln] = h1


def sigmoid(v): return jax.nn.sigmoid(v)
def dot(a, b): return jnp.dot(a, b, preferred_element_type=f32)
def dot_nt(a, b): return lax.dot_general(a, b, (((1,), (1,)), ((), ())), preferred_element_type=f32)
def dot_tn(a, b): return lax.dot_general(a, b, (((0,), (0,)), ((), ())), preferred_element_type=f32)
def loop(n, f, unroll=1):
    def body(i, _):
        f(i); return 0
    lax.fori_loop(0, n, body, 0, unroll=unroll)
def ds(i, n): return pl.ds(pl.multiple_of(i * n, n), n)
def silu_and_slope(v):
    s = sigmoid(v)
    y = v * s
    return y, s + y * (1.0 - s)

class Params:
    def __init__(s, pos, ref, PRM, ss, rs):
        s.p, s.ref, s.PRM, s.ss, s.rs = pos, ref, PRM, ss, rs
    def r(s, row, n): return s.PRM.at[pl.ds(pl.multiple_of(row, 8), n), :]
    def cp(s, k, src, dst, dev, kr=None):
        return rcopy(src, dst, s.ss.at[k], s.rs.at[k if kr is None else kr], dev)
    def y0(s):
        p = s.p; row = (p.dp * 4 + p.z) * 48 + p.y * 24
        s.cp(0, s.ref, s.r(row, 24), p.yn).start()
        s.PRM[pl.ds(pl.multiple_of(row, 8), 24), :] = s.ref[...]
    def y1(s):
        p = s.p
        l = s.r((p.dp * 4 + p.z) * 48, 24)
        s.cp(0, l, l, p.yn).wait()
    def z0(s):
        p = s.p; u = s.r((p.dp * 4 + p.z) * 48, 48)
        for d in (1, 3, 2): s.cp(d, u, u, p.zn(d), 1 + p.z).start()
    def x0(s):
        p = s.p; u = s.r(p.dp * 192, 192)
        for d in (1, 2, 3):
            l = s.r((p.dp * 4 + p.zof(d)) * 48, 48)
            s.cp(1, l, l, p.sib, 1 + p.zof(d)).wait_recv()
        s.cp(7, u, u, p.xn).start()
        s.cp(8, u, u, p.sib).start()
    def x1(s):
        p = s.p; u = s.r(p.dpx * 192, 192)
        s.cp(7, u, u, p.xn).wait_recv()
        s.cp(9, u, u, p.sib).start()
    def end(s):
        p = s.p; u = s.r(p.dp * 192, 192)
        s.cp(8, u, u, p.sib).wait_recv()
        s.cp(9, u, u, p.sib).wait_recv()
    def drain(s):
        p = s.p; u = s.r(p.dp * 192, 192); u1 = s.r(p.dp * 192, 48)
        for k in (7, 8, 9): s.cp(k, u, u, p.sib).wait_send()
        for k in (1, 2, 3): s.cp(k, u1, u1, p.sib).wait_send()

class Scan:
    def __init__(s, pos, way, rate, E, L, Z, ss, rs):
        s.p, s.way, s.rate, s.E, s.L, s.Z, s.ss, s.rs = pos, way, rate, E, L, Z, ss, rs
    def grow(s, k): return jnp.exp(s.rate[0:16, :] * (-256.0 * k))[None]
    def cp(s, d):
        return rcopy(s.E.at[0 if d == 0 else 1], s.L.at[d], s.ss.at[d], s.rs.at[d], s.p.yn if d == 0 else s.p.zn(s.way * d))
    def sc0(s): s.cp(0).start()
    def sc1(s):
        p = s.p
        s.cp(0).wait_recv()
        own, got = s.E[0].astype(f32), s.L[0].astype(f32)
        second = p.y == (1 if s.way > 0 else 0)
        s.Z[...] = jnp.where(second, got, 0.0)
        pair = jnp.where(second, own, got) + s.grow(1) * jnp.where(second, got, own)
        s.E[1] = pair.astype(s.E.dtype)
        for d in (1, 2, 3):
            @pl.when((p.z + d <= 3) if s.way > 0 else (p.z - d >= 0))
            def _(): s.cp(d).start()
    def sc2(s):
        p = s.p
        k = (p.y if s.way > 0 else 1 - p.y).astype(f32)
        for d in (1, 2, 3):
            @pl.when((p.z - d >= 0) if s.way > 0 else (p.z + d <= 3))
            def _():
                s.cp(d).wait_recv()
                s.Z[...] += s.grow(k + 2.0 * (d - 1)) * s.L[d].astype(f32)
    def drain(s):
        p = s.p
        s.cp(0).wait_send()
        for d in (1, 2, 3):
            @pl.when((p.z + d <= 3) if s.way > 0 else (p.z - d >= 0))
            def _(): s.cp(d).wait_send()

class Halves:
    def __init__(s, pos, mx, va, wo, wu, wd, WA, WB, land, ss, rs):
        s.p, s.mx, s.va, s.wo, s.wu, s.wd, s.WA, s.WB, s.land, s.ss, s.rs = pos, mx, va, wo, wu, wd, WA, WB, land, ss, rs
    def pieces(s, y):
        return ((s.va, y * 768, VAL, 768), (s.mx, y * MXL, 0, 1536 if y else MXL), (s.wu, y * 768, UPL, 768))
    def rb(s, yy): return pl.ds(pl.multiple_of((s.p.dp * 4 + s.p.z) * RB + yy * 48, 48), 48)
    def wb(s, yy, half, k): return s.WB.at[s.rb(yy), pl.ds(half * HB + k * DWL, DWL)]
    def start(s):
        p = s.p
        for yy in (0, 1):
            @pl.when(p.y == yy)
            def _():
                for k, (ref, a, c, w) in enumerate(s.pieces(1 - yy)):
                    rcopy(ref.at[:, pl.ds(a, w)], s.land.at[:, pl.ds(c, w)], s.ss.at[k], s.rs.at[k], p.yn).start()
                for k, ref in enumerate((s.wo, s.wd)):
                    rcopy(ref.at[:, pl.ds((1 - yy) * DWL, DWL)], s.wb(yy, 1 - yy, k), s.ss.at[3 + k], s.rs.at[3 + k], p.yn).start()
                    pltpu.make_async_copy(ref.at[:, pl.ds(yy * DWL, DWL)], s.wb(yy, yy, k), s.ss.at[5 + k]).start()
    def end(s, ks):
        p = s.p
        rows = pl.ds(pl.multiple_of((p.dp * 4 + p.z) * RA, 16), RA)
        for yy in (0, 1):
            @pl.when(p.y == yy)
            def _():
                for k, (ref, a, c, w) in enumerate(s.pieces(yy)):
                    if k not in ks: continue
                    l = s.land.at[:, pl.ds(c, w)]
                    rcopy(l, l, s.ss.at[k], s.rs.at[k], p.yn).wait_recv()
                    both = (ref[:, pl.ds(a, w)], l[...]) if yy == 0 else (l[...], ref[:, pl.ds(a, w)])
                    s.WA[rows, pl.ds(yy * HA + c, w)] = jnp.concatenate([t.astype(f32) for t in both], axis=0).astype(bf16)
                if yy == 1 and 1 in ks: s.WA[rows, pl.ds(HA + 1536, 128)] = jnp.zeros((RA, 128), bf16)
        if 1 in ks:
            u = s.wb(0, 0, 0)
            for k in (0, 1):
                rcopy(u, u, s.ss.at[3 + k], s.rs.at[3 + k], p.yn).wait_recv()
                pltpu.make_async_copy(u, u, s.ss.at[5 + k]).wait()
    def hv0(s): s.end((0,))
    def hv1(s): s.end((1, 2))
    def drain(s):
        p = s.p
        for yy in (0, 1):
            @pl.when(p.y == yy)
            def _():
                for k, (ref, a, c, w) in enumerate(s.pieces(1 - yy)):
                    l = s.land.at[:, pl.ds(c, w)]
                    rcopy(l, l, s.ss.at[k], s.rs.at[k], p.yn).wait_send()
        u = s.wb(0, 0, 0)
        for k in (0, 1): rcopy(u, u, s.ss.at[3 + k], s.rs.at[3 + k], p.yn).wait_send()

def norm_rows(tok, PT, U, NL, i):
    x = tok[ds(i, 64), :].astype(f32)
    r = lax.rsqrt(jnp.mean(x * x, axis=-1, keepdims=True) + EPSILON)
    u = x * r * PT[32:33, :]
    U[ds(i, 8), :, :] = u.reshape(8, 8, 768)
    NL[ds(i, 64), :] = u.astype(bf16)

def run_plan(plan, steps):
    for e in plan:
        if e % 100 == 0: steps[0][e // 100]()
        else: steps[1][e // 100](e % 100 - 1)

def state_scale(rate):
    return jnp.sqrt(jnp.tanh(rate) * (1.0 + jnp.exp(-2.0 * rate)))

def row_masks(lens, valid, p):
    for b in range(2):
        t = lax.broadcasted_iota(jnp.int32, (SEQ_DEV, 1), 0) + p.sq * SEQ_DEV
        valid[b * SEQ_DEV:(b + 1) * SEQ_DEV, :] = jnp.where(t < lens[b], 1.0, 0.0)

def sub8(v):
    return v.reshape(v.shape[0] // 8, 8, v.shape[1]).sum(axis=0)

FORWARD_OUT = (("wa", (768, 2 * HA), bf16), ("wb", (1536, 2 * HB), bf16), ("vl", (512, 1536), bf16), ("vs", (512, 1536), bf16),
    ("re", (512, 1536), bf16), ("rs", (512, 1536), bf16), ("at", (512, 1536), bf16), ("gt", (512, 1536), bf16), ("hi", (512, 1536), bf16), ("hs", (512, 1536), bf16),
    ("uc", (512, 768), bf16), ("du", (512, 768), bf16), ("om", (512, 768), bf16), ("sh", (512, 768), bf16), ("bs", (512, 768), bf16), ("n2", (512, 768), bf16),
    ("mi", (512, 768), f32), ("sp", (512, 128), f32), ("pr", (512, 128), f32), ("st", (64, 16, 768), f32), ("pt", (128, 768), f32), ("res", (512, 768), bf16), ("sq", (24, 768), f32))

FORWARD_PLAN = (
    0, 100, 200, 300, 702, 500, 701, 703, 802, 400, 704, 1216, 1218, 600, 710, 801, 902, 709, 700, 901, 800, 804, 1001, 1002, 705, 803,
    1316, 706, 810, 1, 2, 1101, 1318, 3, 4, 707, 809, 5, 1102, 1217, 903, 714, 6, 805, 900, 904, 910, 713, 708, 1215, 201, 1003, 711, 806,
    909, 1000, 1103, 813, 1004, 807, 906, 808, 907, 202, 905, 908, 1104, 1010, 1006, 712, 1009, 1109, 811, 1110, 101, 102, 1007, 1107, 721,
    103, 104, 812, 720, 913, 814, 1106, 105, 1008, 1005, 106, 821, 1105, 719, 1418, 1100, 203, 820, 912, 1317, 1108, 1315, 301, 401, 1416,
    302, 819, 911, 914, 402, 303, 1415, 1012, 1013, 403, 921, 920, 1200, 501, 1011, 1516, 502, 1111, 1112, 1113, 503, 1417, 1518, 504, 919,
    1300, 1014, 1114, 1021, 1515, 1121, 1400, 601, 1517, 602, 1020, 1019, 1119, 1120, 603, 1500,
)

def forward_kernel(lens, tok, qk, rate_t, in_t, out_t, gain_t, mx, va, wo, wu, wd, *refs):
    no = len(FORWARD_OUT)
    outs, bufs, rest = refs[:no], refs[no:2 * no], refs[2 * no:]
    B = {name: r for (name, _, _), r in zip(FORWARD_OUT, bufs)}
    O = {name: r for (name, _, _), r in zip(FORWARD_OUT, outs)}
    osem = {name: i for i, (name, _, _) in enumerate(FORWARD_OUT)}
    (PRM, land, U, NL, BL, RSF, UPD, DIR, ACC, KS, E, L, Z, valid, affine, prm, s0, r0, sp_, rp_, ss, rs, sx, rx, so, sw) = rest
    WA, WB, PT, S = B["wa"], B["wb"], B["pt"], B["st"]
    p = Pos()
    out = lambda name: pltpu.make_async_copy(B[name], O[name], so.at[osem[name]])
    def keep(*names):
        for name in names: out(name).start()
    def weight(k, h):
        b, c, w = KINDS[k]
        a, o = ((WA, O["wa"]), (WB, O["wb"]))[b]
        cols = pl.ds((HA, HB)[b] * h + c, w)
        return pltpu.make_async_copy(a.at[:, cols], o.at[:, cols], sw.at[k, h])
    def keep_weight(k):
        for h in (0, 1): weight(k, h).start()
    def small():
        PT[...] = jnp.zeros_like(PT)
        r = rate_t[...].astype(f32)
        PT[0:16, 0:24] = r
        PT[16:32, 0:24] = out_t[...].astype(f32) * state_scale(r) * in_t[...].astype(f32)
        PT[32:35, 0:24] = gain_t[...].astype(f32)
        prm[...] = PT[:, 0:128].T[0:24, :]
    small()
    full_barrier(p)
    row_masks(lens, valid, p)
    affine[0:3, :] = qk[...].astype(f32)
    par = Params(p, prm, PRM, sp_, rp_)
    hv = Halves(p, mx, va, wo, wu, wd, WA, WB, land, s0, r0)
    g = Gather(p, (WA, WB), ss, rs)
    rate, ec, omega = PT.at[0:16, :], PT.at[16:32, :], PT.at[34:35, :]
    sc = Scan(p, 1, PT, E, L, Z, sx, rx)
    SQ = B["sq"]
    def par1(): par.y1(); par.z0()
    def pt():
        par.end()
        for j in range(6): PT[:, j * 128:(j + 1) * 128] = PRM[j * 128:(j + 1) * 128, :].T
    def norm(): loop(8, lambda i: norm_rows(tok, PT, U, NL, i))
    def st(j): fwd_states(U, rate, S, E.at[0], j, 4)
    def sm(j):
        if j == 0: sc.sc2()
        fwd_smooth(U, S, Z, rate, ec, omega, BL, KS, j, 2)
    def sh():
        def rows(i):
            y, s = silu_and_slope(BL[ds(i, 8), :, :].reshape(64, 768))
            B["sh"][ds(i, 64), :] = y.astype(bf16)
            B["bs"][ds(i, 64), :] = s.astype(bf16)
        loop(8, rows)
        keep("st", "pt", "sh", "bs")
    def both(name, slope, m, c, w=256):
        def rows(i):
            y, s = silu_and_slope(ACC[ds(i, 64), 0:256])
            B[name][ds(i, 64), ds(m, 256)] = y.astype(bf16)
            B[slope][ds(i, 64), ds(m, 256)] = s.astype(bf16)
            if name == "re": RSF[ds(i, 64), ds(m, 256)] = y
        loop(8, rows)
    def mul(x, ref, c, w=256): ACC[:, 0:w] = dot(x[...], ref[:, c:c + w])
    def va_(k):
        g.need(0, VAL + 256 * k, VAL + 256 * k + 256)
        for h in (0, 1):
            mul(NL, WA, h * HA + VAL + 256 * k)
            both("vl", "vs", 3 * h + k, 0)
        if k == 2: keep("vl", "vs"); keep_weight(1)
    def mu(k):
        g.need(0, 256 * k, 256 * k + 256)
        mul(B["sh"], WA, 256 * k)
        loop(8, lambda i: UPD.__setitem__((ds(i, 64), ds(k, 256)), sigmoid(ACC[ds(i, 64), 0:256])))
        mul(B["sh"], WA, HA + 256 * k)
        both("re", "rs", 3 + k, 0)
    def ms():
        g.need(0, 768, 896)
        mul(B["sh"], WA, 768, 128)
        B["sp"][...] = ACC[:, 0:128]
    def md(k):
        g.need(0, 768 + 256 * k, 1152 + 256 * k)
        mul(B["sh"], WA, 896 + 256 * k)
        both("re", "rs", k, 0)
        DIR[:, ds(k, 256)] = dot(B["sh"][...], WA[:, HA + 768 + 256 * k:HA + 1024 + 256 * k])
    def at_(b):
        rr = ds(b, 128)
        s = B["sp"][rr, :]
        s = s * sigmoid(s)
        q = (s * affine[0:1, :] + affine[1:2, :]).astype(bf16)
        k = (s * affine[2:3, :]).astype(bf16)
        t = dot_nt(q, k) * Z_SCALE
        ok = lax.broadcasted_iota(jnp.int32, (128, 128), 0) >= lax.broadcasted_iota(jnp.int32, (128, 128), 1)
        t = jnp.where(ok, t, -1e30)
        e = jnp.exp(t - jnp.max(t, axis=-1, keepdims=True))
        e = e / jnp.sum(e, axis=-1, keepdims=True)
        B["pr"][rr, :] = e
        el = e.astype(bf16)
        for m in range(6):
            c = pl.ds(m * 256, 256)
            a = dot(el, B["vl"][rr, c])
            B["at"][rr, c] = a.astype(bf16)
            B["gt"][rr, c] = (a * RSF[rr, c]).astype(bf16)
        if b == 3: keep("re", "rs", "sp", "pr", "at", "gt"); keep_weight(0)
    def ca():
        g.need(1, 0, DWL)
        SQ[...] = jnp.zeros_like(SQ)
        for m in range(2):
            ACC[...] = dot(B["gt"][...], WB[:, m * HB:m * HB + DWL])
            def rows(i):
                r, c = ds(i, 64), pl.ds(m * DWL, DWL)
                y, s = silu_and_slope(DIR[r, c] + ACC[r, :])
                u = UPD[r, c]
                x = tok[r, c].astype(f32)
                a = u * (y - x)
                B["mi"][r, c] = x + a
                B["uc"][r, c] = (u * s).astype(bf16)
                B["du"][r, c] = (a * (1.0 - u)).astype(bf16)
                B["om"][r, c] = (1.0 - u).astype(bf16)
                SQ[8:16, c] += sub8(valid[r, :] * a * a)
            loop(8, rows)
        keep_weight(3)
    def n2():
        def rows(i):
            v = B["mi"][ds(i, 64), :]
            r = lax.rsqrt(jnp.mean(v * v, axis=-1, keepdims=True) + EPSILON)
            B["n2"][ds(i, 64), :] = (v * r * PT[33:34, :]).astype(bf16)
        loop(8, rows)
        keep("mi", "uc", "du", "om", "n2")
    def up(k):
        g.need(0, UPL + 256 * k, UPL + 256 * k + 256)
        for h in (0, 1):
            mul(B["n2"], WA, h * HA + UPL + 256 * k)
            both("hi", "hs", 3 * h + k, 0)
    def do():
        keep("hi", "hs"); keep_weight(2)
        g.need(1, DWL, 2 * DWL)
        keep_weight(4)
        for m in range(2):
            ACC[...] = dot(B["hi"][...], WB[:, m * HB + DWL:m * HB + 2 * DWL])
            def rows(i):
                r, c = ds(i, 64), pl.ds(m * DWL, DWL)
                f = ACC[r, :]
                o = B["mi"][r, c] + f
                B["res"][r, c] = o.astype(bf16)
                v = valid[r, :]
                SQ[0:8, c] += sub8(v * o * o)
                SQ[16:24, c] += sub8(v * f * f)
            loop(8, rows)
        keep("res", "sq")
    steps = (par.y0, hv.start, par1, hv.hv0, hv.hv1, par.x0, par.x1, pt, norm, sc.sc0, sc.sc1, sh, ms, ca, n2, do), (st, sm, va_, mu, md, at_, up) + g.steps()
    run_plan(FORWARD_PLAN, steps)
    g.drain(); par.drain(); sc.drain(); hv.drain()
    for name, _, _ in FORWARD_OUT[2:]: out(name).wait()
    for k in range(len(KINDS)):
        for h in (0, 1): weight(k, h).wait()

Z_SCALE = Z ** -0.5
SCAN_TYPE = f32
def forward_call(*args):
    n = len(GATHER_CHUNKS)
    v = pltpu.VMEM
    D_ = pltpu.SemaphoreType.DMA
    return pl.pallas_call(forward_kernel,
        out_shape=tuple(jax.ShapeDtypeStruct(s, t) for _, s, t in FORWARD_OUT),
        in_specs=[pl.BlockSpec(memory_space=pltpu.SMEM)] + [pl.BlockSpec(memory_space=pltpu.VMEM)] * 11,
        out_specs=[pl.BlockSpec(memory_space=pl.ANY)] * len(FORWARD_OUT),
        scratch_shapes=[v(s, t) for _, s, t in FORWARD_OUT] + [v((768, 128), f32), v((24, HA), bf16), v((64, 8, 768), f32), v((512, 768), bf16),
            v((64, 8, 768), f32), v((512, 1536), f32), v((512, 768), f32), v((512, 768), f32), v((512, 384), f32), v((8, 128), f32),
            v((2, 2, 16, 768), SCAN_TYPE), v((4, 2, 16, 768), SCAN_TYPE), v((2, 16, 768), f32),
            v((512, 1), f32), v((8, 128), f32), v((24, 128), f32),
            D_((7,)), D_((5,)), D_((10,)), D_((10,)), D_((n, 23)), D_((n, 23)), D_((4,)), D_((4,)), D_((len(FORWARD_OUT),)), D_((len(KINDS), 2))],
        compiler_params=pltpu.CompilerParams(collective_id=0, has_side_effects=True, vmem_limit_bytes=62 * 2**20),
    )(*args)

class Tiny:
    def __init__(s, pos, T, L1, L2, L4, OUT, G, ss, rs):
        s.p, s.T, s.L1, s.L2, s.L4, s.OUT, s.G, s.ss, s.rs = pos, T, L1, L2, L4, OUT, G, ss, rs
    def r(s, xx, c, z=0, n=4): return s.T.at[pl.ds(pl.multiple_of(((xx * 2 + c) * 4 + z) * 48, 8), n * 48), :]
    def cp(s, k, src, dst, dev): return rcopy(src, dst, s.ss.at[k], s.rs.at[k], dev)
    def st0(s):
        for xx in (0, 1): s.cp(xx, s.r(xx, 1 - s.p.c), s.L1.at[xx], s.p.sib).start()
    def a0(s):
        p = s.p
        for xx in (0, 1):
            l = s.L1.at[xx]
            s.cp(xx, l, l, p.sib).wait_recv()
            t = s.r(xx, p.c)
            t[...] = t[...] + l[...]
        s.cp(2, s.r(1 - p.x, p.c), s.L2, p.xn).start()
    def a1(s):
        p = s.p
        s.cp(2, s.L2, s.L2, p.xn).wait_recv()
        t = s.r(p.x, p.c)
        t[...] = t[...] + s.L2[...]
    def zsend(s):
        p = s.p
        for d in (1, 3, 2): rcopy(s.r(p.x, p.c, p.zof(d), 1), s.L4.at[3 - d], s.ss.at[2 + d], s.rs.at[6 - d], p.zn(d)).start()
    def fin(s):
        p = s.p
        t = s.r(p.x, p.c, p.z, 1)
        v = t[...]
        for k in range(3):
            l = s.L4.at[k]
            s.cp(3 + k, l, l, p.sib).wait_recv()
            v = v + l[...]
        t[...] = v
        row = ((p.x * 2 + p.c) * 4 + p.z) * 48
        far = s.T.at[pl.ds(pl.multiple_of(row + (1 - p.y) * 24, 8), 24), :]
        s.cp(9, far, s.G, p.yn).start()
    def last(s):
        p = s.p
        row = ((p.x * 2 + p.c) * 4 + p.z) * 48
        s.cp(9, s.G, s.G, p.yn).wait_recv()
        s.OUT[...] = s.T[pl.ds(pl.multiple_of(row + p.y * 24, 8), 24), :] + s.G[...]
    def drain(s):
        p = s.p
        for k, l in ((0, s.L1.at[0]), (1, s.L1.at[1]), (2, s.L2), (9, s.G)): s.cp(k, l, l, p.sib).wait_send()
        for k in range(3): s.cp(3 + k, s.L4.at[k], s.L4.at[k], p.sib).wait_send()

class Total:
    def __init__(s, pos, R, L, ss, rs):
        p = pos
        z1 = (p.dp, p.sq + 2 - 4 * (p.z % 2)); z2 = (p.dp, p.sq + 4 - 8 * (p.z // 2))
        s.to, s.R, s.L, s.ss, s.rs = (p.sib, p.xn, p.yn, z1, z2), R, L, ss, rs
    def cp(s, k): return rcopy(s.R.at[k], s.L.at[k], s.ss.at[k], s.rs.at[k], s.to[k])
    def send(s, k): s.cp(k).start()
    def step(s, k):
        s.cp(k).wait_recv()
        s.R[k + 1] = s.R[k] + s.L[k]
        if k < 4: s.send(k + 1)
    def drain(s):
        for k in range(5): s.cp(k).wait_send()

BACK_IN = ("wa", "wb", "vl", "vs", "re", "rs", "at", "gt", "hi", "hs", "uc", "du", "om", "sh", "bs", "n2", "mi", "sp", "pr", "st", "pt", "tok", "cot")
MX_PARTS = ((0, 384), (384, 384), (768, 384), (1152, 256), (1408, 256))
BACKWARD_PLAN = (
    800, 701, 702, 703, 704, 705, 706, 1, 801, 3, 802, 803, 5, 4, 101, 103, 2, 900, 104, 901, 105, 1000, 902, 102, 903, 203, 904, 905, 906,
    205, 6, 1001, 1002, 201, 1003, 7, 1004, 701, 702, 703, 202, 106, 204, 801, 802, 803, 8, 301, 107, 901, 108, 902, 9, 305, 903, 109, 303,
    1001, 304, 1002, 1003, 1004, 1005, 1006, 207, 0, 206, 302, 800, 1101, 10, 100, 208, 700, 209, 1102, 601, 1104, 110, 307, 1105, 11, 1103,
    13, 12, 306, 111, 14, 602, 112, 1201, 1202, 308, 210, 1203, 1204, 211, 113, 309, 212, 114, 310, 1205, 1206, 406, 311, 900, 214, 312,
    200, 409, 300, 603, 403, 407, 314, 401, 213, 410, 412, 503, 400, 404, 507, 411, 313, 402, 414, 408, 405, 509, 500, 504, 604, 512, 514,
    502, 413, 506, 605, 511, 510, 508, 501, 600, 505, 513,
)
CUT = 37

def backward_kernel(lens, qk, sq, *refs):
    ni = len(BACK_IN)
    I = dict(zip(BACK_IN, refs[:ni]))
    (o_mx, o_va, o_up, o_wo, o_wd, o_gt, o_tiny, o_red) = refs[ni:ni + 8]
    (WA, WB, L1A, L1B, L2A, L2B, L3A, L3B, L4A, L4B, FA, FB, GA, GB_, TOK, PT, U, X0, X1, GT, GG, G1, H, KS, AT, ACC, E, L, Zb,
     T, TL1, TL2, TL4, TG, TP, RR, RL, P6, GMX, Q0, Q1, Q2, SHT, SP, valid, affine, ss, rs, sx, rx, st_, rt_, sr, rr_, li, lo, lw) = refs[ni + 8:]
    p = Pos()
    sem = {name: i for i, name in enumerate(BACK_IN)}
    def load(name, dst): pltpu.make_async_copy(I[name], dst, li.at[sem[name]]).start()
    def ready(*pairs):
        for name, dst in pairs: pltpu.make_async_copy(I[name], dst, li.at[sem[name]]).wait()
    def part_copies(k):
        b, c, w = KINDS[k]
        for h in (0, 1):
            cols = pl.ds((HA, HB)[b] * h + c, w)
            yield pltpu.make_async_copy(I[("wa", "wb")[b]].at[:, cols], (WA, WB)[b].at[:, cols], lw.at[k, h])
    def part(k):
        for cp in part_copies(k): cp.start()
    def part_ready(k):
        for cp in part_copies(k): cp.wait()
    def put(b, half, off, w, get):
        outs = ((o_wo, 0, 384, 384), (o_wd, 384, 768, 384)) if b else ((o_mx, 0, 1536 if half else MXL, MXL), (o_va, VAL, UPL, 768), (o_up, UPL, HA, 768))
        for o, lo_, hi_, step in outs:
            a, e = max(off, lo_), min(off + w, hi_)
            if a < e: o[:, pl.ds(a - lo_ + half * step, e - a)] = get(a - off, e - a)
    g = Scatter(p, (WA, WB), (L1A, L1B), (L2A, L2B), (L3A, L3B), (L4A, L4B), (FA, FB), (GA, GB_), put, ss, rs)
    tot = Total(p, RR, RL, sr, rr_)
    sc = Scan(p, -1, PT, E, L, Zb, sx, rx)
    tiny = Tiny(p, T, TL1, TL2, TL4, o_tiny, TG, st_, rt_)
    v = lambda s, t: pltpu.VMEM(s, t)
    big, mid = v((512, 1536), bf16), v((512, 768), bf16)
    rate, ec, omega = PT.at[0:16, :], PT.at[16:32, :], PT.at[34:35, :]
    gain1, gain2 = PT.at[32:33, :], PT.at[33:34, :]
    def at3(X, i): return X[ds(i, 8), :, :].reshape(64, 768)
    def pair(ref, rows, c, w, step): return jnp.concatenate([ref[rows, c:c + w], ref[rows, c + step:c + step + w]], axis=1)
    def ti2(): tiny.a1(); tiny.zsend()
    def to0():
        for k in range(3):
            t = sub8(sq[pl.ds(k * 8, 8), :]).sum(axis=0, keepdims=True)
            RR[0, 3 + k:4 + k, :] = sum(t[:, j * 128:(j + 1) * 128] for j in range(6))
        RR[0, 6:7, :] = jnp.broadcast_to(jnp.sum(valid[...], axis=0, keepdims=True) * (1.0 / 128.0), (1, 128))
        tot.send(0)
    alone = (sc.sc0, sc.sc1, tiny.st0, tiny.a0, ti2, tiny.fin, tiny.last, to0)
    many = g.steps() + (tot.step,)
    def first(P0, P1, P2, P3, P4, P5, Q3, Q4, PR):
        load("cot", Q4); part(4); load("hs", P0); load("hi", P1); part(2); load("n2", Q1); load("mi", X0); load("uc", Q2); load("du", Q3); load("pt", PT)
        part(3); load("gt", P3); load("rs", P4); load("vl", P5); load("vs", P6); load("sp", SP); load("pr", PR); part(1); load("tok", TOK); part(0)
        full_barrier(p)
        row_masks(lens, valid, p)
        affine[0:3, :] = qk[...].astype(f32)
        def lo_():
            GG[...] = jnp.zeros_like(GG)
            RR[0] = jnp.zeros((8, 128), f32)
            ready(("cot", Q4))
            def rows(i): Q0[ds(i, 64), :] = (Q4[ds(i, 64), :].astype(f32) * valid[ds(i, 64), :]).astype(bf16)
            loop(8, rows)
            part_ready(4); ready(("hs", P0), ("hi", P1))
        def hi(m):
            c = pl.ds(m * 256, 256)
            ACC[...] = dot_nt(Q0[...], pair(WB, c, DWL, DWL, HB))
            t = dot_tn(P1[:, c], Q0[...]).astype(bf16)
            WB[c, DWL:HB], WB[c, HB + DWL:] = t[:, :DWL], t[:, DWL:]
            def rows(i):
                r = ds(i, 64)
                P2[r, c] = (ACC[r, :] * P0[r, c].astype(f32)).astype(bf16)
            loop(8, rows)
            if m == 5: load("at", P0); load("re", P1)
        def ub(m):
            if m == 0: part_ready(2); ready(("n2", Q1))
            c = pl.ds(m * 256, 256)
            X1[:, :, c] = (dot_nt(P2[:, 0:768], WA[c, UPL:HA]) + dot_nt(P2[:, 768:], WA[c, HA + UPL:])).reshape(64, 8, 256)
            WA[c, UPL:HA] = dot_tn(Q1[:, c], P2[:, 0:768]).astype(bf16)
            WA[c, HA + UPL:] = dot_tn(Q1[:, c], P2[:, 768:]).astype(bf16)
        def nb():
            load("sh", Q0)
            load("om", Q1)
            ready(("mi", X0), ("uc", Q2), ("du", Q3), ("pt", PT), ("om", Q1))
            def rows(i):
                r = ds(i, 64)
                m_, k = at3(X0, i), at3(X1, i)
                inv = lax.rsqrt(jnp.mean(m_ * m_, axis=-1, keepdims=True) + EPSILON)
                unit = m_ * inv
                GG[0:8, :] += sub8(k * unit)
                k = k * gain2[...]
                gm = Q4[r, :].astype(f32) * valid[r, :] + inv * (k - unit * jnp.mean(k * unit, axis=-1, keepdims=True))
                GMX[r, 0:768] = (gm * Q3[r, :].astype(f32)).astype(bf16)
                GMX[r, 2432:3200] = (gm * Q2[r, :].astype(f32)).astype(bf16)
                GT[r, :] = gm * Q1[r, :].astype(f32)
            loop(8, rows)
            load("bs", Q1)
        def ga(m):
            if m == 0: part_ready(3); ready(("gt", P3), ("at", P0), ("re", P1), ("rs", P4))
            c = pl.ds(m * 256, 256)
            gc = GMX[:, 2432:3200]
            ACC[...] = dot_nt(gc, pair(WB, c, 0, DWL, HB))
            t = dot_tn(P3[:, c], gc).astype(bf16)
            WB[c, 0:DWL], WB[c, HB:HB + DWL] = t[:, :DWL], t[:, DWL:]
            c2 = pl.ds(896 + m * 256, 256)
            def rows(i):
                r = ds(i, 64)
                a = ACC[r, :]
                P2[r, c] = (a * P1[r, c].astype(f32)).astype(bf16)
                GMX[r, c2] = (a * P0[r, c].astype(f32) * P4[r, c].astype(f32)).astype(bf16)
            loop(8, rows)
        def nr():
            ready(("tok", TOK))
            loop(8, lambda i: norm_rows(TOK, PT, U, Q2, i))
        def at_(b):
            if b == 0: ready(("vl", P5), ("vs", P6), ("sp", SP), ("pr", PR))
            r = ds(b, 128)
            pr = PR[r, :]
            gp = dot_nt(P2[r, :], P5[r, :])
            gs = (pr * (gp - jnp.sum(gp * pr, axis=-1, keepdims=True))).astype(bf16)
            el = pr.astype(bf16)
            for m in range(6):
                c = pl.ds(m * 256, 256)
                P6[r, c] = (dot_tn(el, P2[r, c]) * P6[r, c].astype(f32)).astype(bf16)
            s, slope = silu_and_slope(SP[r, :])
            q = (s * affine[0:1, :] + affine[1:2, :]).astype(bf16)
            k = (s * affine[2:3, :]).astype(bf16)
            gq = dot(gs, k) * Z_SCALE
            gk = dot_tn(gs, q) * Z_SCALE
            GMX[r, 768:896] = ((gq * affine[0:1, :] + gk * affine[2:3, :]) * slope).astype(bf16)
            for i, t in enumerate((gq * s, gq, gk * s)):
                RR[0, i:i + 1, :] += jnp.sum(t, axis=0, keepdims=True)
        run_plan(BACKWARD_PLAN[:CUT], (alone + (lo_, nb, nr), many + (hi, ub, ga, at_)))
    pl.run_scoped(first, big, big, big, big, big, big, mid, mid, v((512, 128), f32))
    def second(S, A):
        load("st", S)
        def vb(m):
            if m == 0: part_ready(1)
            c = pl.ds(m * 256, 256)
            X1[:, :, c] = (dot_nt(P6[:, 0:768], WA[c, VAL:UPL]) + dot_nt(P6[:, 768:], WA[c, HA + VAL:HA + UPL])).reshape(64, 8, 256)
        def dv(m):
            c = pl.ds(m * 256, 256)
            WA[c, VAL:UPL] = dot_tn(Q2[:, c], P6[:, 0:768]).astype(bf16)
            WA[c, HA + VAL:HA + UPL] = dot_tn(Q2[:, c], P6[:, 768:]).astype(bf16)
        def bl(m):
            if m == 0: part_ready(0); ready(("bs", Q1), ("sh", Q0))
            c = pl.ds(m * 256, 256)
            ACC[...] = dot_nt(GMX[:, 0:MXL], WA[c, 0:MXL]) + dot_nt(GMX[:, MXL:], WA[c, HA:HA + 1536])
            def rows(i):
                r, k = ds(i, 64), ds(i, 8)
                gb = ACC[r, :] * Q1[r, c].astype(f32)
                X0[k, :, c] = gb.reshape(8, 8, 256)
                GG[8:16, c] += sub8(gb * U[k, :, c].reshape(64, 256))
                X1[k, :, c] += (gb * omega[:, c]).reshape(8, 8, 256)
            loop(8, rows)
        def bk(j):
            if j == 0: ready(("st", S))
            bwd_states(X0, U, S, rate, A, E.at[0], G1, H, KS, j, 2)
        def tr(): SHT[...] = Q0[...].T
        def dm(k):
            off, w = MX_PARTS[k]
            WA[:, off:off + w] = dot(SHT[...], GMX[:, off:off + w]).astype(bf16)
            e = min(off + w, 1536)
            if off < e: WA[:, HA + off:HA + e] = dot(SHT[...], GMX[:, MXL + off:MXL + e]).astype(bf16)
            if off + w > 1536: WA[:, HA + 1536:HA + MXL] = jnp.zeros((768, 128), bf16)
        def gr(j):
            if j == 0: sc.sc2()
            bwd_grad(X0, U, S, A, Zb, rate, ec, H, X1, KS, AT, j, 2)
        def la():
            GG[16:24, :] = jnp.zeros((8, 768), f32)
            def rows(i):
                r = ds(i, 64)
                x = TOK[r, :].astype(f32)
                inv = lax.rsqrt(jnp.mean(x * x, axis=-1, keepdims=True) + EPSILON)
                unit = x * inv
                gn = at3(X1, i)
                GG[16:24, :] += sub8(gn * unit)
                k = gn * gain1[...]
                GT[r, :] += inv * (k - unit * jnp.mean(k * unit, axis=-1, keepdims=True))
            loop(8, rows)
            pltpu.make_async_copy(GT, o_gt, lo.at[0]).start()
            TP[...] = jnp.zeros_like(TP)
            TP[0:16, :] = G1[...]
            TP[16:32, :] = H[...]
            for k, i in ((32, 2), (33, 0), (34, 1)):
                TP[k:k + 1, :] = jnp.sum(GG[pl.ds(i * 8, 8), :], axis=0, keepdims=True)
            for j in range(6): T[j * 128:(j + 1) * 128, :] = TP[:, j * 128:(j + 1) * 128].T
        run_plan(BACKWARD_PLAN[CUT:], (alone + (tr, la), many + (vb, dv, bl, bk, dm, gr)))
    pl.run_scoped(second, v((64, 16, 768), f32), v((64, 16, 768), f32))
    o_red[...] = RR[5]
    g.drain(); tiny.drain(); tot.drain(); sc.drain()
    pltpu.make_async_copy(GT, o_gt, lo.at[0]).wait()

def backward_call(lens, qk, sq, ins):
    n = len(SCATTER_CHUNKS)
    v = pltpu.VMEM
    D_ = pltpu.SemaphoreType.DMA
    sds = jax.ShapeDtypeStruct
    vm_, any_ = pl.BlockSpec(memory_space=pltpu.VMEM), pl.BlockSpec(memory_space=pl.ANY)
    return pl.pallas_call(backward_kernel,
        out_shape=(sds((24, 3200), f32), sds((24, 1536), f32), sds((24, 1536), f32), sds((48, 768), f32), sds((48, 768), f32), sds((512, 768), f32), sds((24, 128), f32), sds((8, 128), f32)),
        in_specs=[pl.BlockSpec(memory_space=pltpu.SMEM)] + [vm_] * 2 + [any_] * len(ins),
        out_specs=[vm_] * 5 + [any_] + [vm_] * 2,
        scratch_shapes=rs_scratch() + [v((512, 768), bf16), v((128, 768), f32), v((64, 8, 768), f32), v((64, 8, 768), f32), v((64, 8, 768), f32), v((512, 768), f32),
            v((24, 768), f32), v((16, 768), f32), v((16, 768), f32), v((8, 128), f32), v((2, 16, 128), f32), v((512, 256), f32),
            v((2, 2, 16, 768), bf16), v((4, 2, 16, 768), bf16), v((2, 16, 768), f32),
            v((768, 128), f32), v((2, 192, 128), f32), v((192, 128), f32), v((3, 48, 128), f32), v((24, 128), f32), v((128, 768), f32),
            v((6, 8, 128), f32), v((5, 8, 128), f32), v((512, 1536), bf16), v((512, 3200), bf16), v((512, 768), bf16), v((512, 768), bf16), v((512, 768), bf16), v((768, 512), bf16), v((512, 128), f32), v((512, 1), f32), v((8, 128), f32),
            D_((n, 11)), D_((n, 11)), D_((4,)), D_((4,)), D_((10,)), D_((10,)), D_((5,)), D_((5,)), D_((len(BACK_IN),)), D_((1,)), D_((len(KINDS), 2))],
        compiler_params=pltpu.CompilerParams(collective_id=1, has_side_effects=True, vmem_limit_bytes=63 * 2**20),
    )(lens, qk, sq, *ins)

def last_kernel(res, gtok, mx, va, wo, wu, wd, tiny, red, rate_t, in_t, out_t, o_res, o_gtok, o_mx, o_va, o_wo, o_wu, o_wd, o_rate, o_in, o_out, o_gain, o_qk, o_rms, *rest):
    mid, ss = rest[:7], rest[7]
    into = [pltpu.make_async_copy(a, m, ss.at[0, k]) for k, (a, m) in enumerate(zip((res, gtok, mx, va, wo, wu, wd), mid))]
    big = [pltpu.make_async_copy(m, o, ss.at[1, k]) for k, (m, o) in enumerate(zip(mid, (o_res, o_gtok, o_mx, o_va, o_wo, o_wu, o_wd)))]
    for cp in into: cp.start()
    for a, b in zip(into, big):
        a.wait()
        b.start()
    t = jnp.concatenate([tiny[...], jnp.zeros((104, 128), f32)], axis=0).T
    g1, h1 = t[0:16, 0:24], t[16:32, 0:24]
    r, a, b = (x[...].astype(f32) for x in (rate_t, in_t, out_t))
    scale = state_scale(r)
    o_out[...] = a * scale * g1
    o_in[...] = b * scale * g1
    o_rate[...] = b * a * (jnp.exp(-2.0 * r) / scale * g1 - scale * h1)
    o_gain[...] = t[32:35, 0:24]
    o_qk[...] = red[0:3, :]
    s = jnp.sum(jnp.concatenate([red[...], jnp.zeros((120, 128), f32)], axis=0).T, axis=0, keepdims=True)
    o_rms[...] = jnp.sqrt(s[:, 3:6] / (s[:, 6:7] * D))
    for cp in big: cp.wait()

def last_call(*args):
    vm_, any_ = pl.BlockSpec(memory_space=pltpu.VMEM), pl.BlockSpec(memory_space=pl.ANY)
    sds = jax.ShapeDtypeStruct
    return pl.pallas_call(last_kernel,
        out_shape=tuple(sds(a.shape, a.dtype) for a in args[:7]) + (sds((16, 24), f32),) * 3 + (sds((3, 24), f32), sds((3, 128), f32), sds((1, 3), f32)),
        in_specs=[any_] * 7 + [vm_] * 5,
        out_specs=[any_] * 7 + [vm_] * 6,
        scratch_shapes=[pltpu.VMEM(a.shape, a.dtype) for a in args[:7]] + [pltpu.SemaphoreType.DMA((2, 7))],
        compiler_params=pltpu.CompilerParams(vmem_limit_bytes=63 * 2**20))(*args)


def per_device_tuned(tokens, cotangent, lengths, w_mx, w_value, w_out, w_up, w_down, ema_rate, ema_in, ema_out, gains, qk_affine):
    tok = tokens.reshape(512, D)
    rate_t, in_t, out_t, gain_t = ema_rate.T, ema_in.T, ema_out.T, gains.T
    kept = forward_call(lengths, tok, qk_affine, rate_t, in_t, out_t, gain_t, w_mx, w_value, w_out, w_up, w_down)
    K = {name: t for (name, _, _), t in zip(FORWARD_OUT, kept)}
    K["tok"], K["cot"], K["mi"] = tok, cotangent.reshape(512, D), K["mi"].reshape(64, 8, 768)
    g_mx, g_va, g_up, g_wo, g_wd, g_tok, tiny, red = backward_call(lengths, qk_affine, K["sq"], [K[name] for name in BACK_IN])
    res, g_tok, g_mx, g_va, g_wo, g_up, g_wd, g_rate, g_in, g_out, g_gain, g_qk, rms = last_call(
        K["res"], g_tok, g_mx, g_va, g_wo, g_up, g_wd, tiny, red, rate_t, in_t, out_t)
    return (res.reshape(tokens.shape), g_tok.reshape(tokens.shape), g_mx, g_va, g_wo, g_up, g_wd, g_rate.T, g_in.T, g_out.T, g_gain.T, g_qk, rms.reshape(3))


def solution(mesh):
    placed = (
        P("dp", "seq", None),
        P("dp", "seq", None),
        P("dp"),
        P(("dp", "seq"), None),
        P(("dp", "seq"), None),
        P(("dp", "seq"), None),
        P(("dp", "seq"), None),
        P(("dp", "seq"), None),
        P(("dp", "seq"), None),
        P(("dp", "seq"), None),
        P(("dp", "seq"), None),
        P(("dp", "seq"), None),
        P(),
    )
    step = per_device_tuned if dict(mesh.shape) == {"dp": 4, "seq": 8} else per_device
    return jax.shard_map(
        step,
        mesh=mesh,
        in_specs=placed,
        out_specs=(
            P("dp", "seq", None),
            P("dp", "seq", None),
            P(("dp", "seq"), None),
            P(("dp", "seq"), None),
            P(("dp", "seq"), None),
            P(("dp", "seq"), None),
            P(("dp", "seq"), None),
            P(("dp", "seq"), None),
            P(("dp", "seq"), None),
            P(("dp", "seq"), None),
            P(("dp", "seq"), None),
            P(),
            P(),
        ),
        check_vma=False,
    )
```

```python
import functools

import jax
import jax.numpy as jnp
from jax import lax
from jax.experimental import pallas as pl
from jax.experimental.pallas import tpu as pltpu
from jax.sharding import PartitionSpec as P

MESH = pl.DeviceIdType.MESH
bf16, f32 = jnp.bfloat16, jnp.float32
D = 768
Z = 128
V = 1536
SPAN = 128
SEQ_DEV = 256


EPSILON = 1e-06
TOP_PRECISION = lax.Precision.HIGHEST


def prefix(value, axis, join, neutral):
    count, mine = (lax.axis_size(axis), lax.axis_index(axis))
    pieces = jax.tree.map(lambda part: lax.all_gather(part, axis), value)
    so_far = jax.tree.map(
        lambda part, zero: jnp.full_like(part, 0) + jnp.asarray(zero, part.dtype), value, neutral
    )

    def lap(position, so_far):
        longer = join(so_far, jax.tree.map(lambda part: part[position], pieces))
        return jax.tree.map(lambda new, old: jnp.where(position < mine, new, old), longer, so_far)

    return lax.fori_loop(0, count - 1, lap, so_far)


def prefix_2(value, axis, combine, identity):
    length, here = (lax.axis_size(axis), lax.axis_index(axis))
    everything = jax.tree.map(
        lambda part, kind: lax.all_gather(part.astype(kind), axis),
        value,
        jax.tree.map(lambda a: jnp.bfloat16 if a.dtype == jnp.float32 else a.dtype, value),
    )
    start = jax.tree.map(
        lambda part, zero: jnp.broadcast_to(jnp.asarray(zero, part.dtype), part.shape),
        value,
        identity,
    )

    def lap(k, before):
        at = length - 1 - k
        reached = at > here
        new = combine(
            before, jax.tree.map(lambda part, own: part[at].astype(own.dtype), everything, value)
        )
        return jax.tree.map(lambda a, b: jnp.where(reached, a, b), new, before)

    return lax.fori_loop(0, length, lap, start)


def silu_slope(values):
    sigmoid = jax.nn.sigmoid(values)
    return sigmoid * (1.0 + values * (1.0 - sigmoid))


def chain_combine(earlier, later):
    return (earlier[0] * later[0], later[0] * earlier[1] + later[1])


def ema_local(rate, beta, eta, input_signal):
    rows_here, length, channels = input_signal.shape
    block_len = min(64, length)
    blocks_count = length // block_len
    lag_values = jnp.arange(block_len, dtype=jnp.float32)
    powers = jnp.exp(-lag_values[:, None, None] * rate[None])
    scale_in = jnp.sqrt(-jnp.expm1(-2.0 * rate)) * beta
    kernel = jnp.sum(powers * (eta * scale_in)[None], axis=2)
    step_ids = jnp.arange(block_len)
    lag_index = jnp.clip(step_ids[:, None] - step_ids[None, :], 0, block_len - 1)
    toeplitz = jnp.where(
        (step_ids[:, None] >= step_ids[None, :])[:, :, None], kernel[lag_index], 0.0
    )
    leading = jnp.exp(-(lag_values[:, None, None] + 1.0) * rate[None]) * eta[None]
    trailing = powers[::-1] * scale_in[None]
    block_decay = jnp.exp(-block_len * rate)
    blocks = jnp.swapaxes(input_signal.reshape(rows_here, blocks_count, block_len, channels), 0, 1)

    def advance(carried, segment):
        smooth = jnp.einsum("tsd,bsd->btd", toeplitz, segment, precision=TOP_PRECISION)
        smooth = smooth + jnp.einsum("tdh,bdh->btd", leading, carried, precision=TOP_PRECISION)
        carried = block_decay * carried + jnp.einsum(
            "sdh,bsd->bdh", trailing, segment, precision=TOP_PRECISION
        )
        return (carried, smooth)

    initial = jnp.zeros((rows_here, channels, rate.shape[1]), jnp.float32)
    final_state, smooth = lax.scan(advance, initial, blocks)
    return (jnp.swapaxes(smooth, 0, 1).reshape(rows_here, length, channels), final_state)


def ema_carry(rate, eta, incoming):
    block_len = min(64, SEQ_DEV)
    blocks_count = SEQ_DEV // block_len
    lag_values = jnp.arange(block_len, dtype=jnp.float32)
    leading = jnp.exp(-(lag_values[:, None, None] + 1.0) * rate[None]) * eta[None]
    block_decay = jnp.exp(-block_len * rate)

    def advance(carried, unused):
        return (
            block_decay * carried,
            jnp.einsum("tdh,bdh->btd", leading, carried, precision=TOP_PRECISION),
        )

    _, smooth = lax.scan(advance, incoming, None, length=blocks_count)
    return jnp.swapaxes(smooth, 0, 1).reshape(incoming.shape[0], SEQ_DEV, incoming.shape[1])


def per_device(
    tokens,
    cotangent,
    lengths,
    w_mx,
    w_value,
    w_out,
    w_up,
    w_down,
    ema_rate,
    ema_in,
    ema_out,
    gains,
    qk_affine,
):
    gathered = (
        lax.all_gather(w_mx, ("dp", "seq"), axis=0, tiled=True),
        lax.all_gather(w_value, ("dp", "seq"), axis=0, tiled=True),
        lax.all_gather(w_out, ("dp", "seq"), axis=0, tiled=True),
        lax.all_gather(w_up, ("dp", "seq"), axis=0, tiled=True),
        lax.all_gather(w_down, ("dp", "seq"), axis=0, tiled=True),
        lax.all_gather(ema_rate, ("dp", "seq"), axis=0, tiled=True),
        lax.all_gather(ema_in, ("dp", "seq"), axis=0, tiled=True),
        lax.all_gather(ema_out, ("dp", "seq"), axis=0, tiled=True),
        lax.all_gather(gains, ("dp", "seq"), axis=0, tiled=True),
    )
    mx_full, value_full, out_full, up_full, down_full, rate_low, beta_low, eta_low, gain_low = (
        gathered
    )
    rate = rate_low.astype(jnp.float32)
    beta = beta_low.astype(jnp.float32)
    eta = eta_low.astype(jnp.float32)
    gain_all = gain_low.astype(jnp.float32)
    gain_first = gain_all[:, 0]
    gain_second = gain_all[:, 1]
    omega_gain = gain_all[:, 2]
    affine = qk_affine.astype(jnp.float32)
    rows_here = tokens.shape[0]
    spans_dev = SEQ_DEV // SPAN
    score_scale = Z ** (-0.5)
    inputs = tokens.astype(jnp.float32)
    seq_pos = lax.axis_index("seq") * SEQ_DEV + jnp.arange(SEQ_DEV, dtype=jnp.int32)
    valid_rows = (seq_pos[None, :] < lengths[:, None]).astype(jnp.float32)[:, :, None]
    inverse1 = lax.rsqrt(jnp.mean(inputs * inputs, axis=-1, keepdims=True) + EPSILON)
    unit1 = inputs * inverse1
    normed = unit1 * gain_first
    normed_low = normed.astype(jnp.bfloat16)
    value_pre = jnp.einsum(
        "bsd,dv->bsv", normed_low, value_full, preferred_element_type=jnp.float32
    )
    value_low = jax.nn.silu(value_pre).astype(jnp.bfloat16)
    (smooth_local, end_local), pull_local = jax.vjp(ema_local, rate, beta, eta, normed)
    growth = jnp.exp(-SEQ_DEV * rate)
    start_state = prefix(
        (growth, end_local),
        "seq",
        chain_combine,
        (jnp.ones_like(growth), jnp.zeros_like(end_local)),
    )[1]
    smooth_carry, pull_carry = jax.vjp(ema_carry, rate, eta, start_state)
    blend = smooth_local + smooth_carry + omega_gain * normed
    shifted_low = jax.nn.silu(blend).astype(jnp.bfloat16)
    mixed = jnp.einsum("bsd,dk->bsk", shifted_low, mx_full, preferred_element_type=jnp.float32)
    update = jax.nn.sigmoid(mixed[..., :D])
    shared_pre = mixed[..., D : D + Z]
    shared = jax.nn.silu(shared_pre)
    reset_pre = mixed[..., D + Z : D + Z + V]
    reset = jax.nn.silu(reset_pre)
    direct = mixed[..., D + Z + V :]
    query_low = (
        (shared * affine[0] + affine[1]).astype(jnp.bfloat16).reshape(rows_here, spans_dev, SPAN, Z)
    )
    key_low = (shared * affine[2]).astype(jnp.bfloat16).reshape(rows_here, spans_dev, SPAN, Z)
    value_tiles = value_low.reshape(rows_here, spans_dev, SPAN, V)
    scores = (
        jnp.einsum("bnqz,bnkz->bnqk", query_low, key_low, preferred_element_type=jnp.float32)
        * score_scale
    )
    causal = jnp.arange(SPAN)[:, None] >= jnp.arange(SPAN)[None, :]
    masked = jnp.where(causal, scores, -1e30)
    peak = jnp.max(masked, axis=-1, keepdims=True)
    expo = jnp.exp(masked - peak)
    attention_weights = expo / jnp.sum(expo, axis=-1, keepdims=True)
    probs_low = attention_weights.astype(jnp.bfloat16)
    attended_output = jnp.einsum(
        "bnqk,bnkv->bnqv", probs_low, value_tiles, preferred_element_type=jnp.float32
    ).reshape(rows_here, SEQ_DEV, V)
    gated_low = (reset * attended_output).astype(jnp.bfloat16)
    cand_pre = direct + jnp.einsum(
        "bsv,vd->bsd", gated_low, out_full, preferred_element_type=jnp.float32
    )
    candidate = jax.nn.silu(cand_pre)
    attn_branch = update * (candidate - inputs)
    middle = inputs + attn_branch
    inverse2 = lax.rsqrt(jnp.mean(middle * middle, axis=-1, keepdims=True) + EPSILON)
    unit2 = middle * inverse2
    normed2_low = (unit2 * gain_second).astype(jnp.bfloat16)
    up_pre = jnp.einsum("bsd,df->bsf", normed2_low, up_full, preferred_element_type=jnp.float32)
    hidden_low = jax.nn.silu(up_pre).astype(jnp.bfloat16)
    ffn_branch = jnp.einsum(
        "bsf,fd->bsd", hidden_low, down_full, preferred_element_type=jnp.float32
    )
    output = middle + ffn_branch
    again = (
        lax.all_gather(w_mx, ("dp", "seq"), axis=0, tiled=True),
        lax.all_gather(w_value, ("dp", "seq"), axis=0, tiled=True),
        lax.all_gather(w_out, ("dp", "seq"), axis=0, tiled=True),
        lax.all_gather(w_up, ("dp", "seq"), axis=0, tiled=True),
        lax.all_gather(w_down, ("dp", "seq"), axis=0, tiled=True),
    )
    mixer_backward, value_back, out_back, up_back, down_back = again
    grad_out = cotangent.astype(jnp.float32) * valid_rows
    grad_out_low = grad_out.astype(jnp.bfloat16)
    grad_down = jnp.einsum(
        "bsf,bsd->fd", hidden_low, grad_out_low, preferred_element_type=jnp.float32
    )
    grad_hidden = jnp.einsum(
        "bsd,fd->bsf", grad_out_low, down_back, preferred_element_type=jnp.float32
    )
    grad_up_low = (grad_hidden * silu_slope(up_pre)).astype(jnp.bfloat16)
    grad_up = jnp.einsum(
        "bsd,bsf->df", normed2_low, grad_up_low, preferred_element_type=jnp.float32
    )
    grad_normed2 = jnp.einsum(
        "bsf,df->bsd", grad_up_low, up_back, preferred_element_type=jnp.float32
    )
    grad_gain_second = jnp.sum(grad_normed2 * unit2, axis=(0, 1))
    scaled2 = grad_normed2 * gain_second
    grad_middle = grad_out + inverse2 * (
        scaled2 - unit2 * jnp.mean(scaled2 * unit2, axis=-1, keepdims=True)
    )
    grad_update = grad_middle * (candidate - inputs)
    grad_cand_pre = grad_middle * update * silu_slope(cand_pre)
    grad_cand_low = grad_cand_pre.astype(jnp.bfloat16)
    grad_out_proj = jnp.einsum(
        "bsv,bsd->vd", gated_low, grad_cand_low, preferred_element_type=jnp.float32
    )
    grad_gated = jnp.einsum(
        "bsd,vd->bsv", grad_cand_low, out_back, preferred_element_type=jnp.float32
    )
    grad_reset = grad_gated * attended_output
    grad_attended_low = (
        (grad_gated * reset).astype(jnp.bfloat16).reshape(rows_here, spans_dev, SPAN, V)
    )
    grad_probs = jnp.einsum(
        "bnqv,bnkv->bnqk", grad_attended_low, value_tiles, preferred_element_type=jnp.float32
    )
    grad_values = jnp.einsum(
        "bnqk,bnqv->bnkv", probs_low, grad_attended_low, preferred_element_type=jnp.float32
    ).reshape(rows_here, SEQ_DEV, V)
    grad_scores_low = (
        attention_weights
        * (grad_probs - jnp.sum(grad_probs * attention_weights, axis=-1, keepdims=True))
    ).astype(jnp.bfloat16)
    grad_query = (
        jnp.einsum("bnqk,bnkz->bnqz", grad_scores_low, key_low, preferred_element_type=jnp.float32)
        * score_scale
    ).reshape(rows_here, SEQ_DEV, Z)
    grad_key = (
        jnp.einsum(
            "bnqk,bnqz->bnkz", grad_scores_low, query_low, preferred_element_type=jnp.float32
        )
        * score_scale
    ).reshape(rows_here, SEQ_DEV, Z)
    grad_affine = jnp.stack(
        [
            jnp.sum(grad_query * shared, axis=(0, 1)),
            jnp.sum(grad_query, axis=(0, 1)),
            jnp.sum(grad_key * shared, axis=(0, 1)),
        ]
    )
    grad_shared = grad_query * affine[0] + grad_key * affine[2]
    grad_mixed_low = jnp.concatenate(
        [
            grad_update * update * (1.0 - update),
            grad_shared * silu_slope(shared_pre),
            grad_reset * silu_slope(reset_pre),
            grad_cand_pre,
        ],
        axis=-1,
    ).astype(jnp.bfloat16)
    grad_mx = jnp.einsum(
        "bsd,bsk->dk", shifted_low, grad_mixed_low, preferred_element_type=jnp.float32
    )
    grad_shifted = jnp.einsum(
        "bsk,dk->bsd", grad_mixed_low, mixer_backward, preferred_element_type=jnp.float32
    )
    grad_blend = grad_shifted * silu_slope(blend)
    grad_omega = jnp.sum(grad_blend * normed, axis=(0, 1))
    grad_value_low = (grad_values * silu_slope(value_pre)).astype(jnp.bfloat16)
    grad_value_proj = jnp.einsum(
        "bsd,bsv->dv", normed_low, grad_value_low, preferred_element_type=jnp.float32
    )
    grad_normed = grad_blend * omega_gain + jnp.einsum(
        "bsv,dv->bsd", grad_value_low, value_back, preferred_element_type=jnp.float32
    )
    rate_from_carry, eta_from_carry, direct_adjoint = pull_carry(grad_blend)
    later_adjoint = prefix_2(
        (growth, direct_adjoint),
        "seq",
        chain_combine,
        (jnp.ones_like(growth), jnp.zeros_like(direct_adjoint)),
    )[1]
    rate_from_local, grad_beta, eta_from_local, normed_from_ema = pull_local(
        (grad_blend, later_adjoint)
    )
    rate_from_growth = jnp.sum(later_adjoint * start_state, axis=0) * (-SEQ_DEV * growth)
    grad_rate = rate_from_carry + rate_from_local + rate_from_growth
    grad_eta = eta_from_carry + eta_from_local
    grad_normed = grad_normed + normed_from_ema
    grad_gain_first = jnp.sum(grad_normed * unit1, axis=(0, 1))
    scaled1 = grad_normed * gain_first
    grad_tokens = grad_middle * (1.0 - update) + inverse1 * (
        scaled1 - unit1 * jnp.mean(scaled1 * unit1, axis=-1, keepdims=True)
    )
    grad_gains = jnp.stack([grad_gain_first, grad_gain_second, grad_omega], axis=1)
    shards = (
        lax.psum_scatter(grad_mx, ("dp", "seq"), scatter_dimension=0, tiled=True),
        lax.psum_scatter(grad_value_proj, ("dp", "seq"), scatter_dimension=0, tiled=True),
        lax.psum_scatter(grad_out_proj, ("dp", "seq"), scatter_dimension=0, tiled=True),
        lax.psum_scatter(grad_up, ("dp", "seq"), scatter_dimension=0, tiled=True),
        lax.psum_scatter(grad_down, ("dp", "seq"), scatter_dimension=0, tiled=True),
        lax.psum_scatter(grad_rate, ("dp", "seq"), scatter_dimension=0, tiled=True),
        lax.psum_scatter(grad_beta, ("dp", "seq"), scatter_dimension=0, tiled=True),
        lax.psum_scatter(grad_eta, ("dp", "seq"), scatter_dimension=0, tiled=True),
        lax.psum_scatter(grad_gains, ("dp", "seq"), scatter_dimension=0, tiled=True),
    )
    squares = jnp.stack(
        [
            jnp.sum(valid_rows * output * output),
            jnp.sum(valid_rows * attn_branch * attn_branch),
            jnp.sum(valid_rows * ffn_branch * ffn_branch),
            jnp.sum(valid_rows),
        ]
    )
    affine_total, square_total = lax.psum((grad_affine, squares), ("dp", "seq"))
    rms_values = jnp.sqrt(square_total[:3] / (square_total[3] * D))
    return (
        output.astype(jnp.bfloat16),
        grad_tokens,
        shards[0],
        shards[1],
        shards[2],
        shards[3],
        shards[4],
        shards[5],
        shards[6],
        shards[7],
        shards[8],
        affine_total,
        rms_values,
    )


HA, HB = 3200, 768
RA, RB = 48, 96

MXL, VAL, UPL, ONE, DWL = 1664, 1664, 2432, 768, 384
KINDS = ((0, 0, 1664), (0, 1664, 768), (0, 2432, 768), (1, 0, 384), (1, 384, 384))
GATHER_CHUNKS = ((0, 1664, 128, "xy"), (0, 1792, 128, "yx"), (0, 1920, 256, "xy"), (0, 2176, 256, "yx"), (0, 0, 384, "xy"), (0, 384, 384, "yx"), (0, 768, 384, "xy"), (0, 1152, 512, "yx"), (1, 0, 128, "xy"), (1, 128, 256, "yx"), (0, 2432, 128, "xy"), (0, 2560, 128, "yx"), (0, 2688, 512, "z"), (1, 384, 128, "xy"), (1, 512, 256, "yx"))
SCATTER_CHUNKS = ((1, 384, 128, "xy"), (1, 512, 128, "yx"), (1, 640, 128, "yx"), (0, 2432, 384, "xy"), (0, 2816, 384, "yx"), (1, 0, 256, "xy"), (1, 256, 128, "yx"), (0, 1664, 512, "yx"), (0, 2176, 256, "xy"), (0, 0, 384, "xy"), (0, 384, 384, "yx"), (0, 768, 256, "xy"), (0, 1024, 256, "yx"), (0, 1280, 128, "xy"), (0, 1408, 256, "yx"))

class Pos:
    def __init__(s):
        s.dp, s.sq = lax.axis_index("dp"), lax.axis_index("seq")
        s.x, s.c, s.z, s.y = s.dp // 2, s.dp % 2, s.sq // 2, s.sq % 2
        s.sib = (s.dp + 1 - 2 * s.c, s.sq)
        s.xn = (s.dp + 2 - 4 * s.x, s.sq)
        s.yn = (s.dp, s.sq + 1 - 2 * s.y)
        s.dpx = s.dp + 2 - 4 * s.x
    def zof(s, d): return (s.z + d) % 4
    def zn(s, d): return (s.dp, s.zof(d) * 2 + s.y)

def rcopy(src, dst, ss, rs, dev):
    return pltpu.make_async_remote_copy(src_ref=src, dst_ref=dst, send_sem=ss, recv_sem=rs, device_id=dev, device_id_type=MESH)

def full_barrier(p, *more):
    bar = pltpu.get_barrier_semaphore()
    sig = lambda d: pl.semaphore_signal(bar, inc=1, device_id=d, device_id_type=MESH)
    for d in (p.sib, p.xn, p.yn, p.zn(1), p.zn(2), p.zn(3)) + more: sig(d)
    pl.semaphore_wait(bar, 6 + len(more))

def at(ref, rows, nrows, half, w, off, width):
    return ref.at[pl.ds(pl.multiple_of(rows, 48), nrows), pl.ds(pl.multiple_of(half * w + off, 128), width)]

class Gather:
    def __init__(s, pos, bufs, ss, rs):
        s.p, s.bufs, s.ss, s.rs, s.here = pos, bufs, ss, rs, set()
    def unit(s, i, dp, z, half, n=1):
        b, off, width, _ = GATHER_CHUNKS[i]
        R = (RA, RB)[b]
        return at(s.bufs[b], (dp * 4 + z) * R, n * R, half, (HA, HB)[b], off, width)
    def cp(s, i, k, ref, dev):
        return rcopy(ref, ref, s.ss.at[i, k], s.rs.at[i, k], dev)
    def z0(s, i):
        p = s.p
        u = s.unit(i, p.dp, p.z, p.y)
        for d in (1, 3, 2): rcopy(u, u, s.ss.at[i, d - 1], s.rs.at[i, p.z], p.zn(d)).start()
    def s1(s, i):
        p = s.p
        for d in (1, 2, 3):
            u = s.unit(i, p.dp, p.zof(d), p.y)
            rcopy(u, u, s.ss.at[i, 0], s.rs.at[i, p.zof(d)], p.sib).wait_recv()
        u = s.unit(i, p.dp, 0, p.y, 4)
        s.cp(i, 4, u, p.xn if GATHER_CHUNKS[i][3] == "xy" else p.yn).start()
        s.cp(i, 7, u, p.sib).start()
    def s2(s, i):
        p = s.p
        xy = GATHER_CHUNKS[i][3] == "xy"
        r = s.unit(i, p.dpx, 0, p.y, 4) if xy else s.unit(i, p.dp, 0, 1 - p.y, 4)
        s.cp(i, 4, r, p.xn).wait_recv()
        nxt = p.yn if xy else p.xn
        s.cp(i, 5, s.unit(i, p.dp, 0, p.y, 4), nxt).start()
        s.cp(i, 6, r, nxt).start()
        s.cp(i, 8, r, p.sib).start()
    def s3(s, i, k):
        p = s.p
        if GATHER_CHUNKS[i][3] == "xy": r = s.unit(i, (p.dp, p.dpx)[k], 0, 1 - p.y, 4)
        else: r = s.unit(i, p.dpx, 0, (p.y, 1 - p.y)[k], 4)
        s.cp(i, 5 + k, r, p.sib).wait_recv()
        s.cp(i, 9 + k, r, p.sib).start()
    def sa(s, i): s.s3(i, 0)
    def sb(s, i): s.s3(i, 1)
    def need(s, b, lo, hi):
        for i, (bb, off, w, _) in enumerate(GATHER_CHUNKS):
            if bb == b and off < hi and off + w > lo and i not in s.here:
                s.here.add(i)
                u = s.unit(i, s.p.dp, 0, s.p.y, 4)
                for k in (7, 8, 9, 10): s.cp(i, k, u, s.p.sib).wait_recv()
    def c1(s, i):
        s.cp(i, 4, s.unit(i, s.p.dp, s.p.z, s.p.y), s.p.xn).start()
    def c2(s, i):
        p = s.p
        r = s.unit(i, p.dpx, p.z, p.y)
        s.cp(i, 4, r, p.xn).wait_recv()
        s.cp(i, 5, s.unit(i, p.dp, p.z, p.y), p.yn).start()
        s.cp(i, 6, r, p.yn).start()
    def four(s, i, z):
        p = s.p
        return [s.unit(i, d, z, h) for d in (p.dp, p.dpx) for h in (p.y, 1 - p.y)]
    def c3(s, i):
        p = s.p
        us = s.four(i, p.z)
        s.cp(i, 5, us[1], p.yn).wait_recv()
        s.cp(i, 6, us[3], p.yn).wait_recv()
        for d in (1, 3, 2):
            for k, u in enumerate(us):
                rcopy(u, u, s.ss.at[i, 7 + 4 * d + k], s.rs.at[i, 11 + 4 * (d - 1) + k], p.zn(d)).start()
    def c4(s, i):
        p = s.p
        for d in (1, 2, 3):
            for k, u in enumerate(s.four(i, p.z)):
                rcopy(u, u, s.ss.at[i, 0], s.rs.at[i, 11 + 4 * (d - 1) + k], p.sib).wait_recv()
        for k, (d, h) in enumerate(((p.dp, p.y), (p.dpx, p.y), (p.dp, 1 - p.y), (p.dpx, 1 - p.y))):
            s.cp(i, 7 + k, s.unit(i, d, 0, h, 4), p.sib).start()
    def steps(s): return (s.z0, s.s1, s.s2, s.sa, s.sb, s.c1, s.c2, s.c3, s.c4)
    def drain(s):
        p = s.p
        for i, (_, _, _, order) in enumerate(GATHER_CHUNKS):
            u1 = s.unit(i, p.dp, 0, p.y)
            u = s.unit(i, p.dp, 0, p.y, 4)
            one = (4, 5, 6) + tuple(range(11, 23)) if order == "z" else (0, 1, 2)
            for k in one: s.cp(i, k, u1, p.sib).wait_send()
            for k in range(4, 11):
                if k not in one: s.cp(i, k, u, p.sib).wait_send()

class Scatter:
    NS = 11
    def __init__(s, pos, P, L1, L2, L3, L4, F, FS, G, out, ss, rs):
        s.FS = FS
        s.p, s.P, s.L1, s.L2, s.L3, s.L4, s.F, s.G, s.out, s.ss, s.rs = pos, P, L1, L2, L3, L4, F, G, out, ss, rs
    def geom(s, i):
        b, off, w, order = SCATTER_CHUNKS[i]
        return b, (RA, RB)[b], (HA, HB)[b], off, w, order
    def cols(s, i, yy):
        b, R, W, off, w, _ = s.geom(i)
        return pl.ds(pl.multiple_of(yy * W + off, 128), w)
    def piece(s, i, xx, c, yy, z=0, n=4):
        b, R, W, off, w, _ = s.geom(i)
        return s.P[b].at[pl.ds(pl.multiple_of(((xx * 2 + c) * 4 + z) * R, 48), n * R), s.cols(i, yy)]
    def cp(s, i, k, src, dst, dev):
        return rcopy(src, dst, s.ss.at[i, k], s.rs.at[i, k], dev)
    def add(s, dst, src, nrows):
        def body(r, _):
            rr = pl.ds(pl.multiple_of(r * 48, 48), 48)
            dst[rr, :] = (dst[rr, :].astype(f32) + src[rr, :].astype(f32)).astype(bf16)
            return 0
        lax.fori_loop(0, nrows // 48, body, 0)
    def l1(s, i, xx, yy):
        return s.L1[SCATTER_CHUNKS[i][0]].at[xx, :, s.cols(i, yy)]
    def st0(s, i):
        p = s.p
        for k, (xx, yy) in enumerate(((0, 0), (0, 1), (1, 0), (1, 1))):
            s.cp(i, k, s.piece(i, xx, 1 - p.c, yy), s.l1(i, xx, yy), p.sib).start()
    def a0(s, i):
        R = s.geom(i)[1]
        for k, (xx, yy) in enumerate(((0, 0), (0, 1), (1, 0), (1, 1))):
            l = s.l1(i, xx, yy)
            s.cp(i, k, l, l, s.p.sib).wait_recv()
            s.add(s.piece(i, xx, s.p.c, yy), l, 4 * R)
    def l2(s, i, k):
        b, R, W, off, w, _ = s.geom(i)
        return s.L2[b].at[k, :, pl.ds(off, w)]
    def l3(s, i):
        b, R, W, off, w, _ = s.geom(i)
        return s.L3[b].at[:, pl.ds(off, w)]
    def st1(s, i):
        p, order = s.p, s.geom(i)[5]
        for k in (0, 1):
            src = s.piece(i, k, p.c, 1 - p.y) if order == "xy" else s.piece(i, 1 - p.x, p.c, k)
            s.cp(i, 4 + k, src, s.l2(i, k), p.yn if order == "xy" else p.xn).start()
    def a1(s, i):
        p = s.p; b, R, W, off, w, order = s.geom(i)
        for k in (0, 1):
            l = s.l2(i, k)
            s.cp(i, 4 + k, l, l, p.xn).wait_recv()
            s.add(s.piece(i, k, p.c, p.y) if order == "xy" else s.piece(i, p.x, p.c, k), l, 4 * R)
    def st2(s, i):
        p, order = s.p, s.geom(i)[5]
        src = s.piece(i, 1 - p.x, p.c, p.y) if order == "xy" else s.piece(i, p.x, p.c, 1 - p.y)
        s.cp(i, 6, src, s.l3(i), p.xn if order == "xy" else p.yn).start()
    def a2(s, i):
        l = s.l3(i)
        s.cp(i, 6, l, l, s.p.xn).wait_recv()
        s.add(s.piece(i, s.p.x, s.p.c, s.p.y), l, 4 * s.geom(i)[1])
    def l4(s, i, k):
        b, R, W, off, w, _ = s.geom(i)
        return s.L4[b].at[k, :, pl.ds(off, w)]
    def zsend(s, i):
        p = s.p
        for d in (1, 3, 2):
            rcopy(s.piece(i, p.x, p.c, p.y, p.zof(d), 1), s.l4(i, 3 - d), s.ss.at[i, 6 + d], s.rs.at[i, 10 - d], p.zn(d)).start()
    def fin(s, i):
        p = s.p; b, R, W, off, w, _ = s.geom(i)
        F, G, out = s.F[b], s.G[b], s.out
        h = R // 2
        t = s.piece(i, p.x, p.c, p.y, p.z, 1)[...].astype(f32)
        for k in range(3):
            l = s.l4(i, k)
            s.cp(i, 7 + k, l, l, p.sib).wait_recv()
            t = t + l[...].astype(f32)
        cols = pl.ds(off, w)
        for yy in (0, 1):
            @pl.when(p.y == yy)
            def _():
                F[:, cols] = t[yy * h:yy * h + h, :]
                s.FS[b][:, cols] = t[(1 - yy) * h:(2 - yy) * h, :].astype(bf16)
                out(b, yy, off, w, lambda o, k: F[:, pl.ds(off + o, k)])
        s.cp(i, 10, s.FS[b].at[:, cols], G.at[:, cols], p.yn).start()
    def last(s, i):
        p = s.p; b, R, W, off, w, _ = s.geom(i)
        l = s.G[b].at[:, pl.ds(off, w)]
        s.cp(i, 10, l, l, p.yn).wait_recv()
        for yy in (0, 1):
            @pl.when(p.y == 1 - yy)
            def _(): s.out(b, yy, off, w, lambda o, k: l[:, pl.ds(o, k)].astype(f32))
    def r0(s, i): s.st0(i)
    def r1(s, i): s.a0(i); s.st1(i)
    def r2(s, i): s.a1(i); s.st2(i)
    def r3(s, i): s.a2(i); s.zsend(i)
    def r4(s, i): s.fin(i)
    def r5(s, i): s.last(i)
    def steps(s): return (s.r0, s.r1, s.r2, s.r3, s.r4, s.r5)
    def drain(s):
        p = s.p
        for i in range(len(SCATTER_CHUNKS)):
            b, R, W, off, w, _ = s.geom(i)
            for k, ref in [(k, s.l1(i, 0, 0)) for k in range(4)] + [(4, s.l2(i, 0)), (5, s.l2(i, 1)), (6, s.l3(i)), (10, s.G[b].at[:, pl.ds(off, w)])] + [(7 + k, s.l4(i, k)) for k in range(3)]:
                s.cp(i, k, ref, ref, p.sib).wait_send()

def rs_scratch():
    v = pltpu.VMEM
    return [v((768, 2 * HA), bf16), v((1536, 2 * HB), bf16), v((2, 192, 2 * HA), bf16), v((2, 384, 2 * HB), bf16),
        v((2, 192, HA), bf16), v((2, 384, HB), bf16), v((192, HA), bf16), v((384, HB), bf16),
        v((3, 48, HA), bf16), v((3, 96, HB), bf16), v((24, HA), f32), v((48, HB), f32), v((24, HA), bf16), v((48, HB), bf16), v((24, HA), bf16), v((48, HB), bf16)]

NK = 32
NB = 2

def lanes(j): return pl.ds(pl.multiple_of(j * 128, 128), 128)
def rows_(i): return pl.ds(pl.multiple_of(i * 8, 8), 8)
def tree(xs):
    xs = list(xs)
    while len(xs) > 1:
        xs = [xs[i] + xs[i + 1] if i + 1 < len(xs) else xs[i] for i in range(0, len(xs), 2)]
    return xs[0]

def fwd_states(U, rate, S, END, j, unroll=2):
    ln = lanes(j)
    r = rate[0:16, ln]
    w = [jnp.exp(r * (s - 7.0)) for s in range(8)]
    q8 = jnp.exp(r * -8.0)
    def body(k, st):
        new = []
        for b in range(NB):
            S[b * NK + k, :, ln] = st[b]
            parts = [w[s] * U[b * NK + k, pl.ds(s, 1), ln] for s in range(8)]
            new.append(q8 * st[b] + tree(parts))
        return tuple(new)
    st = lax.fori_loop(0, NK, body, tuple(jnp.zeros((16, 128), f32) for _ in range(NB)), unroll=unroll)
    for b in range(NB): END[b, :, ln] = st[b].astype(END.dtype)

def conv_tables(rate, ec, j):
    ln = lanes(j)
    it = lax.broadcasted_iota(jnp.int32, (8, 128), 0).astype(f32)
    E, K = [], []
    for h in range(16):
        rb = jnp.broadcast_to(rate[pl.ds(h, 1), ln], (8, 128)); eb = jnp.broadcast_to(ec[pl.ds(h, 1), ln], (8, 128))
        K.append(jnp.exp(-it * rb) * eb)
        E.append(jnp.exp(-(it + 1.0) * rb) * eb)
    return E, tree(K)

def fwd_smooth(U, S, S0, rate, ec, omega, BL, KS, j, unroll=1):
    ln = lanes(j)
    r = rate[0:16, ln]
    q8 = jnp.exp(r * -8.0)
    E, K = conv_tables(rate, ec, j)
    KS[...] = K
    ii = lax.broadcasted_iota(jnp.int32, (8, 128), 0)
    KM = [jnp.where(ii >= l, jnp.broadcast_to(KS[pl.ds(l, 1), :], (8, 128)), 0.0) for l in range(8)]
    om = jnp.broadcast_to(omega[:, ln], (8, 128))
    KM[0] = KM[0] + om
    def body(k, gs):
        new = []
        for b in range(NB):
            i = b * NK + k
            S[i, :, ln] = S[i, :, ln] + gs[b]
            u = U[i, :, ln]
            parts = [KM[0] * u] + [KM[l] * pltpu.roll(u, l, 0) for l in range(1, 8)]
            parts += [E[h] * S[i, pl.ds(h, 1), ln] for h in range(16)]
            BL[i, :, ln] = tree(parts)
            new.append(q8 * gs[b])
        return tuple(new)
    lax.fori_loop(0, NK, body, tuple(S0[b, :, ln] for b in range(NB)), unroll=unroll)

def bwd_states(Gr, U, S, rate, A, DIR, G1, H, CS, j, unroll=1):
    ln = lanes(j)
    r = rate[0:16, ln]
    w = [jnp.exp(r * -float(s)) for s in range(8)]
    q8 = jnp.exp(r * -8.0)
    def body(kk, c):
        k = NK - 1 - kk
        st, g1, h1, C = c
        new, C = [], list(C)
        for b in range(NB):
            i = b * NK + k
            A[i, :, ln] = st[b]
            p = [Gr[i, pl.ds(0, 1), ln]] + [w[s] * Gr[i, pl.ds(s, 1), ln] for s in range(1, 8)]
            later = B1 = p[7]
            for t in range(6, 0, -1):
                later = later + p[t]
                B1 = B1 + later
            Bg = later + p[0]
            Sk = S[i, :, ln]
            g1 = g1 + Sk * Bg
            h1 = h1 + Sk * B1
            new.append(q8 * st[b] + Bg)
            u, g = U[i, :, ln], Gr[i, :, ln]
            C = [C[l] + g * (pltpu.roll(u, l, 0) if l else u) for l in range(8)]
        return tuple(new), g1, h1, tuple(C)
    z = jnp.zeros((16, 128), f32)
    st, g1, h1, C = lax.fori_loop(0, NK, body, (tuple(z for _ in range(NB)), z, z, tuple(jnp.zeros((8, 128), f32) for _ in range(8))), unroll=unroll)
    for b in range(NB): DIR[b, :, ln] = st[b].astype(DIR.dtype)
    ii = lax.broadcasted_iota(jnp.int32, (8, 128), 0)
    g1, h1 = g1 * w[1], h1 * w[1]
    for l in range(8):
        cl = jnp.sum(jnp.where(ii >= l, C[l], 0.0), axis=0, keepdims=True)
        t = w[l] * cl
        g1 = g1 + t
        if l: h1 = h1 + t * float(l)
    G1[:, ln] = g1
    H[:, ln] = h1

def bwd_grad(Gr, U, S, A, A0, rate, ec, H, DU, KS, AT, j, unroll=1):
    ln = lanes(j)
    r = rate[0:16, ln]
    q8 = jnp.exp(r * -8.0)
    c8 = 8.0 * jnp.exp(r * -9.0)
    wu = [jnp.exp(r * (s - 8.0)) * (8.0 - s) for s in range(8)]
    it = lax.broadcasted_iota(jnp.int32, (8, 128), 0).astype(f32)
    E, K = [], []
    for h in range(16):
        rb = jnp.broadcast_to(rate[pl.ds(h, 1), ln], (8, 128)); eb = jnp.broadcast_to(ec[pl.ds(h, 1), ln], (8, 128))
        K.append(jnp.exp(-it * rb) * eb)
        E.append(jnp.exp((it - 8.0) * rb) * eb)
    KS[...] = tree(K)
    ii = lax.broadcasted_iota(jnp.int32, (8, 128), 0)
    KM = [jnp.where(ii < 8 - l, jnp.broadcast_to(KS[pl.ds(l, 1), :], (8, 128)), 0.0) for l in range(8)]
    def body(kk, c):
        k = NK - 1 - kk
        gs, h1 = c
        new = []
        for b in range(NB):
            i = b * NK + k
            Ak = A[i, :, ln] + gs[b]
            AT[b] = Ak
            Bu = tree([wu[s] * U[i, pl.ds(s, 1), ln] for s in range(8)])
            h1 = h1 + Ak * (Bu + c8 * S[i, :, ln])
            g = Gr[i, :, ln]
            parts = [KM[0] * g] + [KM[l] * pltpu.roll(g, 8 - l, 0) for l in range(1, 8)]
            parts += [E[h] * AT[b, pl.ds(h, 1), :] for h in range(16)]
            DU[i, :, ln] += tree(parts)
            new.append(q8 * gs[b])
        return tuple(new), h1
    gs, h1 = lax.fori_loop(0, NK, body, (tuple(A0[b, :, ln] for b in range(NB)), H[:, ln]), unroll=unroll)
    H[:, ln] = h1


def sigmoid(v): return jax.nn.sigmoid(v)
def dot(a, b): return jnp.dot(a, b, preferred_element_type=f32)
def dot_nt(a, b): return lax.dot_general(a, b, (((1,), (1,)), ((), ())), preferred_element_type=f32)
def dot_tn(a, b): return lax.dot_general(a, b, (((0,), (0,)), ((), ())), preferred_element_type=f32)
def loop(n, f):
    for i in range(n): f(i)
def ds(i, n): return pl.ds(i * n if isinstance(i, int) else pl.multiple_of(i * n, n), n)
def silu_and_slope(v):
    s = sigmoid(v)
    y = v * s
    return y, s + y * (1.0 - s)

class Params:
    def __init__(s, pos, ref, PRM, ss, rs):
        s.p, s.ref, s.PRM, s.ss, s.rs = pos, ref, PRM, ss, rs
    def r(s, row, n): return s.PRM.at[pl.ds(pl.multiple_of(row, 8), n), :]
    def cp(s, k, src, dst, dev): return rcopy(src, dst, s.ss.at[k], s.rs.at[k], dev)
    def others(s):
        return tuple((d, f) for d in (0, 1, 3, 2) for f in (1, 0) if d or f)
    def y0(s):
        p = s.p
        own = (p.dp * 4 + p.z) * 48 + p.y * 24
        s.PRM[pl.ds(pl.multiple_of(own, 8), 24), :] = s.ref[...]
        for k, (d, f) in enumerate(s.others()):
            y = 1 - p.y if f else p.y
            s.cp(k, s.ref, s.r(own, 24), (p.dp, p.zof(d) * 2 + y)).start()
    def x0(s):
        p = s.p; u = s.r(p.dp * 192, 192)
        for k in range(7):
            l = s.r(p.dp * 192, 24)
            s.cp(k, l, l, p.sib).wait_recv()
        s.cp(7, u, u, p.xn).start()
        s.cp(8, u, u, p.sib).start()
    def x1(s):
        p = s.p; u = s.r(p.dpx * 192, 192)
        s.cp(7, u, u, p.xn).wait_recv()
        s.cp(9, u, u, p.sib).start()
    def end(s):
        p = s.p; u = s.r(p.dp * 192, 192)
        s.cp(8, u, u, p.sib).wait_recv()
        s.cp(9, u, u, p.sib).wait_recv()
    def drain(s):
        p = s.p; u = s.r(p.dp * 192, 192); u1 = s.r(p.dp * 192, 24)
        for k in (7, 8, 9): s.cp(k, u, u, p.sib).wait_send()
        for k in range(7): s.cp(k, u1, u1, p.sib).wait_send()

class Scan:
    def __init__(s, pos, way, rate, E, L, Z, ss, rs):
        s.p, s.way, s.rate, s.E, s.L, s.Z, s.ss, s.rs = pos, way, rate, E, L, Z, ss, rs
    def grow(s, k): return jnp.exp(s.rate[0:16, :] * (-256.0 * k))[None]
    def cp(s, d):
        return rcopy(s.E.at[0 if d == 0 else 1], s.L.at[d], s.ss.at[d], s.rs.at[d], s.p.yn if d == 0 else s.p.zn(s.way * d))
    def sc0(s): s.cp(0).start()
    def sc1(s):
        p = s.p
        s.cp(0).wait_recv()
        own, got = s.E[0].astype(f32), s.L[0].astype(f32)
        second = p.y == (1 if s.way > 0 else 0)
        s.Z[...] = jnp.where(second, got, 0.0)
        pair = jnp.where(second, own, got) + s.grow(1) * jnp.where(second, got, own)
        s.E[1] = pair.astype(s.E.dtype)
        for d in (1, 2, 3):
            @pl.when((p.z + d <= 3) if s.way > 0 else (p.z - d >= 0))
            def _(): s.cp(d).start()
    def sc2(s):
        p = s.p
        k = (p.y if s.way > 0 else 1 - p.y).astype(f32)
        for d in (1, 2, 3):
            @pl.when((p.z - d >= 0) if s.way > 0 else (p.z + d <= 3))
            def _():
                s.cp(d).wait_recv()
                s.Z[...] += s.grow(k + 2.0 * (d - 1)) * s.L[d].astype(f32)
    def drain(s):
        p = s.p
        s.cp(0).wait_send()
        for d in (1, 2, 3):
            @pl.when((p.z + d <= 3) if s.way > 0 else (p.z - d >= 0))
            def _(): s.cp(d).wait_send()

class Halves:
    def __init__(s, pos, mx, va, wo, wu, wd, WA, WB, land, ss, rs):
        s.p, s.mx, s.va, s.wo, s.wu, s.wd, s.WA, s.WB, s.land, s.ss, s.rs = pos, mx, va, wo, wu, wd, WA, WB, land, ss, rs
    def pieces(s, y):
        return ((s.va, y * 768, VAL, 768), (s.mx, y * MXL, 0, 1536 if y else MXL), (s.wu, y * 768, UPL, 768))
    def rb(s, yy): return pl.ds(pl.multiple_of((s.p.dp * 4 + s.p.z) * RB + yy * 48, 48), 48)
    def wb(s, yy, half, k): return s.WB.at[s.rb(yy), pl.ds(half * HB + k * DWL, DWL)]
    def start(s):
        p = s.p
        for yy in (0, 1):
            @pl.when(p.y == yy)
            def _():
                for k, (ref, a, c, w) in enumerate(s.pieces(1 - yy)):
                    rcopy(ref.at[:, pl.ds(a, w)], s.land.at[:, pl.ds(c, w)], s.ss.at[k], s.rs.at[k], p.yn).start()
                for k, ref in enumerate((s.wo, s.wd)):
                    rcopy(ref.at[:, pl.ds((1 - yy) * DWL, DWL)], s.wb(yy, 1 - yy, k), s.ss.at[3 + k], s.rs.at[3 + k], p.yn).start()
                    pltpu.make_async_copy(ref.at[:, pl.ds(yy * DWL, DWL)], s.wb(yy, yy, k), s.ss.at[5 + k]).start()
    def end(s, ks):
        p = s.p
        rows = pl.ds(pl.multiple_of((p.dp * 4 + p.z) * RA, 16), RA)
        for yy in (0, 1):
            @pl.when(p.y == yy)
            def _():
                for k, (ref, a, c, w) in enumerate(s.pieces(yy)):
                    if k not in ks: continue
                    l = s.land.at[:, pl.ds(c, w)]
                    rcopy(l, l, s.ss.at[k], s.rs.at[k], p.yn).wait_recv()
                    both = (ref[:, pl.ds(a, w)], l[...]) if yy == 0 else (l[...], ref[:, pl.ds(a, w)])
                    s.WA[rows, pl.ds(yy * HA + c, w)] = jnp.concatenate([t.astype(f32) for t in both], axis=0).astype(bf16)
                if yy == 1 and 1 in ks: s.WA[rows, pl.ds(HA + 1536, 128)] = jnp.zeros((RA, 128), bf16)
        if 1 in ks:
            u = s.wb(0, 0, 0)
            for k in (0, 1):
                rcopy(u, u, s.ss.at[3 + k], s.rs.at[3 + k], p.yn).wait_recv()
                pltpu.make_async_copy(u, u, s.ss.at[5 + k]).wait()
    def hv0(s): s.end((0,))
    def hv1(s): s.end((1, 2))
    def drain(s):
        p = s.p
        for yy in (0, 1):
            @pl.when(p.y == yy)
            def _():
                for k, (ref, a, c, w) in enumerate(s.pieces(1 - yy)):
                    l = s.land.at[:, pl.ds(c, w)]
                    rcopy(l, l, s.ss.at[k], s.rs.at[k], p.yn).wait_send()
        u = s.wb(0, 0, 0)
        for k in (0, 1): rcopy(u, u, s.ss.at[3 + k], s.rs.at[3 + k], p.yn).wait_send()

def norm_rows(tok, PT, U, NL, i):
    x = tok[ds(i, 64), :].astype(f32)
    r = lax.rsqrt(jnp.mean(x * x, axis=-1, keepdims=True) + EPSILON)
    u = x * r * PT[32:33, :]
    U[ds(i, 8), :, :] = u.reshape(8, 8, 768)
    NL[ds(i, 64), :] = u.astype(bf16)

def run_plan(plan, steps):
    for e in plan:
        if e % 100 == 0: steps[0][e // 100]()
        else: steps[1][e // 100](e % 100 - 1)

def state_scale(rate):
    return jnp.sqrt(jnp.tanh(rate) * (1.0 + jnp.exp(-2.0 * rate)))

def row_masks(lens, valid, p):
    for b in range(2):
        t = lax.broadcasted_iota(jnp.int32, (SEQ_DEV, 1), 0) + p.sq * SEQ_DEV
        valid[b * SEQ_DEV:(b + 1) * SEQ_DEV, :] = jnp.where(t < lens[b], 1.0, 0.0)

def sub8(v):
    return v.reshape(v.shape[0] // 8, 8, v.shape[1]).sum(axis=0)

FORWARD_OUT = (("wa", (768, 2 * HA), bf16), ("wb", (1536, 2 * HB), bf16), ("vl", (512, 1536), bf16), ("vs", (512, 1536), bf16),
    ("re", (512, 1536), bf16), ("rs", (512, 1536), bf16), ("at", (512, 1536), bf16), ("gt", (512, 1536), bf16), ("hi", (512, 1536), bf16), ("hs", (512, 1536), bf16),
    ("uc", (512, 768), bf16), ("du", (512, 768), bf16), ("om", (512, 768), bf16), ("sh", (512, 768), bf16), ("bs", (512, 768), bf16), ("n2", (512, 768), bf16),
    ("mi", (512, 768), f32), ("sp", (512, 128), f32), ("pr", (512, 128), f32), ("st", (64, 16, 768), f32), ("pt", (128, 768), f32), ("res", (512, 768), bf16), ("sq", (24, 768), f32))

FORWARD_PLAN = (
    0, 100, 300, 704, 200, 702, 500, 701, 703, 400, 600, 804, 1213, 706, 802, 700, 711, 712, 801, 800, 1313, 803, 1, 2, 901, 705, 902, 904,
    806, 3, 714, 1001, 812, 1101, 4, 707, 708, 811, 710, 5, 6, 900, 805, 906, 1004, 903, 905, 807, 1003, 1006, 1000, 808, 912, 1005, 1002,
    1103, 709, 814, 907, 1104, 908, 1102, 201, 1012, 810, 1105, 715, 1007, 911, 101, 102, 103, 1413, 104, 809, 202, 1008, 105, 910, 815,
    1108, 106, 1107, 1100, 909, 203, 1011, 1106, 401, 402, 1200, 914, 1111, 1010, 301, 302, 915, 303, 403, 501, 1110, 502, 1009, 1109, 1112,
    503, 504, 1300, 1513, 1014, 1114, 1015, 1400, 601, 1115, 602, 603, 1500,
)

def forward_kernel(lens, qk, rate_t, in_t, out_t, gain_t, *refs):
    far, refs = refs[:6], refs[6:]
    no = len(FORWARD_OUT)
    outs, bufs, rest = refs[:no], refs[no:2 * no], refs[2 * no:]
    B = {name: r for (name, _, _), r in zip(FORWARD_OUT, bufs)}
    O = {name: r for (name, _, _), r in zip(FORWARD_OUT, outs)}
    osem = {name: i for i, (name, _, _) in enumerate(FORWARD_OUT)}
    (PRM, land, U, NL, BL, RSF, UPD, DIR, ACC, KS, E, L, Z, valid, affine, prm, tok, mx, va, wo, wu, wd, si, s0, r0, sp_, rp_, ss, rs, sx, rx, so, sw) = rest
    WA, WB, PT, S = B["wa"], B["wb"], B["pt"], B["st"]
    p = Pos()
    out = lambda name: pltpu.make_async_copy(B[name], O[name], so.at[osem[name]])
    def keep(*names):
        for name in names: out(name).start()
    def weight(k, h):
        b, c, w = KINDS[k]
        a, o = ((WA, O["wa"]), (WB, O["wb"]))[b]
        cols = pl.ds((HA, HB)[b] * h + c, w)
        return pltpu.make_async_copy(a.at[:, cols], o.at[:, cols], sw.at[k, h])
    def keep_weight(k):
        for h in (0, 1): weight(k, h).start()
    def small():
        PT[...] = jnp.zeros_like(PT)
        r = rate_t[...].astype(f32)
        PT[0:16, 0:24] = r
        PT[16:32, 0:24] = out_t[...].astype(f32) * state_scale(r) * in_t[...].astype(f32)
        PT[32:35, 0:24] = gain_t[...].astype(f32)
        prm[...] = PT[:, 0:128].T[0:24, :]
    near = [pltpu.make_async_copy(a, b, si.at[k]) for k, (a, b) in enumerate(zip(far, (va, mx, wu, wo, wd, tok)))]
    for cp in near: cp.start()
    small()
    full_barrier(p, *((p.dp, p.zof(d) * 2 + 1 - p.y) for d in (1, 2, 3)))
    for cp in near: cp.wait()
    row_masks(lens, valid, p)
    affine[0:3, :] = qk[...].astype(f32)
    par = Params(p, prm, PRM, sp_, rp_)
    hv = Halves(p, mx, va, wo, wu, wd, WA, WB, land, s0, r0)
    g = Gather(p, (WA, WB), ss, rs)
    rate, ec, omega = PT.at[0:16, :], PT.at[16:32, :], PT.at[34:35, :]
    sc = Scan(p, 1, PT, E, L, Z, sx, rx)
    SQ = B["sq"]
    def par1(): pass
    def pt():
        par.end()
        for j in range(6): PT[:, j * 128:(j + 1) * 128] = PRM[j * 128:(j + 1) * 128, :].T
    def norm(): loop(8, lambda i: norm_rows(tok, PT, U, NL, i))
    def st(j): fwd_states(U, rate, S, E.at[0], j, 4)
    def sm(j):
        if j == 0: sc.sc2()
        fwd_smooth(U, S, Z, rate, ec, omega, BL, KS, j, 2)
    def sh():
        def rows(i):
            y, s = silu_and_slope(BL[ds(i, 8), :, :].reshape(64, 768))
            B["sh"][ds(i, 64), :] = y.astype(bf16)
            B["bs"][ds(i, 64), :] = s.astype(bf16)
        loop(8, rows)
        keep("st", "pt", "sh", "bs")
    def both(name, slope, m, c, w=256):
        def rows(i):
            y, s = silu_and_slope(ACC[ds(i, 64), 0:256])
            B[name][ds(i, 64), ds(m, 256)] = y.astype(bf16)
            B[slope][ds(i, 64), ds(m, 256)] = s.astype(bf16)
            if name == "re": RSF[ds(i, 64), ds(m, 256)] = y
        loop(8, rows)
    def mul(x, ref, c, w=256): ACC[:, 0:w] = dot(x[...], ref[:, c:c + w])
    def va_(k):
        g.need(0, VAL + 256 * k, VAL + 256 * k + 256)
        for h in (0, 1):
            mul(NL, WA, h * HA + VAL + 256 * k)
            both("vl", "vs", 3 * h + k, 0)
        if k == 2: keep("vl", "vs"); keep_weight(1)
    def mu(k):
        g.need(0, 256 * k, 256 * k + 256)
        mul(B["sh"], WA, 256 * k)
        loop(8, lambda i: UPD.__setitem__((ds(i, 64), ds(k, 256)), sigmoid(ACC[ds(i, 64), 0:256])))
        mul(B["sh"], WA, HA + 256 * k)
        both("re", "rs", 3 + k, 0)
    def ms():
        g.need(0, 768, 896)
        mul(B["sh"], WA, 768, 128)
        B["sp"][...] = ACC[:, 0:128]
    def md(k):
        g.need(0, 768 + 256 * k, 1152 + 256 * k)
        mul(B["sh"], WA, 896 + 256 * k)
        both("re", "rs", k, 0)
        DIR[:, ds(k, 256)] = dot(B["sh"][...], WA[:, HA + 768 + 256 * k:HA + 1024 + 256 * k])
    def at_(b):
        rr = ds(b, 128)
        s = B["sp"][rr, :]
        s = s * sigmoid(s)
        q = (s * affine[0:1, :] + affine[1:2, :]).astype(bf16)
        k = (s * affine[2:3, :]).astype(bf16)
        t = dot_nt(q, k) * Z_SCALE
        ok = lax.broadcasted_iota(jnp.int32, (128, 128), 0) >= lax.broadcasted_iota(jnp.int32, (128, 128), 1)
        t = jnp.where(ok, t, -1e30)
        e = jnp.exp(t - jnp.max(t, axis=-1, keepdims=True))
        e = e / jnp.sum(e, axis=-1, keepdims=True)
        B["pr"][rr, :] = e
        el = e.astype(bf16)
        for m in range(6):
            c = pl.ds(m * 256, 256)
            a = dot(el, B["vl"][rr, c])
            B["at"][rr, c] = a.astype(bf16)
            B["gt"][rr, c] = (a * RSF[rr, c]).astype(bf16)
        if b == 3: keep("re", "rs", "sp", "pr", "at", "gt"); keep_weight(0)
    def ca():
        g.need(1, 0, DWL)
        SQ[...] = jnp.zeros_like(SQ)
        for m in range(2):
            ACC[...] = dot(B["gt"][...], WB[:, m * HB:m * HB + DWL])
            def rows(i):
                r, c = ds(i, 64), pl.ds(m * DWL, DWL)
                y, s = silu_and_slope(DIR[r, c] + ACC[r, :])
                u = UPD[r, c]
                x = tok[r, c].astype(f32)
                a = u * (y - x)
                B["mi"][r, c] = x + a
                B["uc"][r, c] = (u * s).astype(bf16)
                B["du"][r, c] = (a * (1.0 - u)).astype(bf16)
                B["om"][r, c] = (1.0 - u).astype(bf16)
                SQ[8:16, c] += sub8(valid[r, :] * a * a)
            loop(8, rows)
        keep_weight(3)
    def n2():
        def rows(i):
            v = B["mi"][ds(i, 64), :]
            r = lax.rsqrt(jnp.mean(v * v, axis=-1, keepdims=True) + EPSILON)
            B["n2"][ds(i, 64), :] = (v * r * PT[33:34, :]).astype(bf16)
        loop(8, rows)
        keep("mi", "uc", "du", "om", "n2")
    def up(k):
        g.need(0, UPL + 256 * k, UPL + 256 * k + 256)
        for h in (0, 1):
            mul(B["n2"], WA, h * HA + UPL + 256 * k)
            both("hi", "hs", 3 * h + k, 0)
        if k == 2: keep("hi", "hs"); keep_weight(2)
    def do():
        g.need(1, DWL, 2 * DWL)
        keep_weight(4)
        for m in range(2):
            ACC[...] = dot(B["hi"][...], WB[:, m * HB + DWL:m * HB + 2 * DWL])
            def rows(i):
                r, c = ds(i, 64), pl.ds(m * DWL, DWL)
                f = ACC[r, :]
                o = B["mi"][r, c] + f
                B["res"][r, c] = o.astype(bf16)
                v = valid[r, :]
                SQ[0:8, c] += sub8(v * o * o)
                SQ[16:24, c] += sub8(v * f * f)
            loop(8, rows)
        keep("res", "sq")
    steps = (par.y0, hv.start, par1, hv.hv0, hv.hv1, par.x0, par.x1, pt, norm, sc.sc0, sc.sc1, sh, ms, ca, n2, do), (st, sm, va_, mu, md, at_, up) + g.steps()
    run_plan(FORWARD_PLAN, steps)
    g.drain(); par.drain(); sc.drain(); hv.drain()
    for name, _, _ in FORWARD_OUT[2:]: out(name).wait()
    for k in range(len(KINDS)):
        for h in (0, 1): weight(k, h).wait()

Z_SCALE = Z ** -0.5
SCAN_TYPE = f32
def forward_call(*args):
    n = len(GATHER_CHUNKS)
    v = pltpu.VMEM
    D_ = pltpu.SemaphoreType.DMA
    return pl.pallas_call(forward_kernel,
        out_shape=tuple(jax.ShapeDtypeStruct(s, t) for _, s, t in FORWARD_OUT),
        in_specs=[pl.BlockSpec(memory_space=pltpu.SMEM)] + [pl.BlockSpec(memory_space=pltpu.VMEM)] * 5 + [pl.BlockSpec(memory_space=pl.ANY)] * 6,
        out_specs=[pl.BlockSpec(memory_space=pl.ANY)] * len(FORWARD_OUT),
        scratch_shapes=[v(s, t) for _, s, t in FORWARD_OUT] + [v((768, 128), f32), v((24, HA), bf16), v((64, 8, 768), f32), v((512, 768), bf16),
            v((64, 8, 768), f32), v((512, 1536), f32), v((512, 768), f32), v((512, 768), f32), v((512, 384), f32), v((8, 128), f32),
            v((2, 2, 16, 768), SCAN_TYPE), v((4, 2, 16, 768), SCAN_TYPE), v((2, 16, 768), f32),
            v((512, 1), f32), v((8, 128), f32), v((24, 128), f32),
            v((512, 768), bf16), v((24, 3200), bf16), v((24, 1536), bf16), v((48, 768), bf16), v((24, 1536), bf16), v((48, 768), bf16), D_((6,)),
            D_((7,)), D_((5,)), D_((10,)), D_((10,)), D_((n, 23)), D_((n, 23)), D_((4,)), D_((4,)), D_((len(FORWARD_OUT),)), D_((len(KINDS), 2))],
        compiler_params=pltpu.CompilerParams(collective_id=0, has_side_effects=True, vmem_limit_bytes=62 * 2**20),
    )(*args)

class Tiny:
    def __init__(s, pos, T, L1, L2, L4, OUT, G, ss, rs):
        s.p, s.T, s.L1, s.L2, s.L4, s.OUT, s.G, s.ss, s.rs = pos, T, L1, L2, L4, OUT, G, ss, rs
    def r(s, xx, c, z=0, n=4): return s.T.at[pl.ds(pl.multiple_of(((xx * 2 + c) * 4 + z) * 48, 8), n * 48), :]
    def cp(s, k, src, dst, dev): return rcopy(src, dst, s.ss.at[k], s.rs.at[k], dev)
    def st0(s):
        for xx in (0, 1): s.cp(xx, s.r(xx, 1 - s.p.c), s.L1.at[xx], s.p.sib).start()
    def a0(s):
        p = s.p
        for xx in (0, 1):
            l = s.L1.at[xx]
            s.cp(xx, l, l, p.sib).wait_recv()
            t = s.r(xx, p.c)
            t[...] = t[...] + l[...]
        s.cp(2, s.r(1 - p.x, p.c), s.L2, p.xn).start()
    def a1(s):
        p = s.p
        s.cp(2, s.L2, s.L2, p.xn).wait_recv()
        t = s.r(p.x, p.c)
        t[...] = t[...] + s.L2[...]
    def zsend(s):
        p = s.p
        for d in (1, 3, 2): rcopy(s.r(p.x, p.c, p.zof(d), 1), s.L4.at[3 - d], s.ss.at[2 + d], s.rs.at[6 - d], p.zn(d)).start()
    def fin(s):
        p = s.p
        t = s.r(p.x, p.c, p.z, 1)
        v = t[...]
        for k in range(3):
            l = s.L4.at[k]
            s.cp(3 + k, l, l, p.sib).wait_recv()
            v = v + l[...]
        t[...] = v
        row = ((p.x * 2 + p.c) * 4 + p.z) * 48
        far = s.T.at[pl.ds(pl.multiple_of(row + (1 - p.y) * 24, 8), 24), :]
        s.cp(9, far, s.G, p.yn).start()
    def last(s):
        p = s.p
        row = ((p.x * 2 + p.c) * 4 + p.z) * 48
        s.cp(9, s.G, s.G, p.yn).wait_recv()
        s.OUT[...] = s.T[pl.ds(pl.multiple_of(row + p.y * 24, 8), 24), :] + s.G[...]
    def drain(s):
        p = s.p
        for k, l in ((0, s.L1.at[0]), (1, s.L1.at[1]), (2, s.L2), (9, s.G)): s.cp(k, l, l, p.sib).wait_send()
        for k in range(3): s.cp(3 + k, s.L4.at[k], s.L4.at[k], p.sib).wait_send()

class Total:
    def __init__(s, pos, R, L, ss, rs):
        p = pos
        z1 = (p.dp, p.sq + 2 - 4 * (p.z % 2)); z2 = (p.dp, p.sq + 4 - 8 * (p.z // 2))
        s.to, s.R, s.L, s.ss, s.rs = (p.sib, p.xn, p.yn, z1, z2), R, L, ss, rs
    def cp(s, k): return rcopy(s.R.at[k], s.L.at[k], s.ss.at[k], s.rs.at[k], s.to[k])
    def send(s, k): s.cp(k).start()
    def step(s, k):
        s.cp(k).wait_recv()
        s.R[k + 1] = s.R[k] + s.L[k]
        if k < 4: s.send(k + 1)
    def drain(s):
        for k in range(5): s.cp(k).wait_send()

BACK_IN = ("wa", "wb", "vl", "vs", "re", "rs", "at", "gt", "hi", "hs", "uc", "du", "om", "sh", "bs", "n2", "mi", "sp", "pr", "st", "pt", "tok", "cot")
MX_PARTS = ((0, 384), (384, 384), (768, 256), (1024, 256), (1280, 128), (1408, 256))
BACKWARD_PLAN = (
    800, 701, 702, 703, 704, 705, 706, 3, 801, 1, 802, 803, 103, 2, 4, 5, 101, 900, 901, 102, 104, 902, 903, 904, 905, 906, 1001, 1002, 6,
    7, 105, 1003, 1000, 1004, 701, 106, 702, 201, 703, 204, 901, 902, 107, 903, 800, 205, 301, 1102, 11, 304, 203, 1103, 12, 202, 1001, 111,
    1002, 206, 305, 1003, 112, 1004, 303, 1005, 1006, 302, 0, 207, 700, 801, 802, 803, 211, 8, 601, 9, 212, 100, 1101, 10, 108, 602, 109,
    1104, 306, 110, 307, 603, 1106, 13, 1105, 1201, 209, 113, 14, 1202, 312, 208, 311, 1203, 1204, 15, 114, 604, 210, 309, 1205, 308, 115,
    1206, 213, 402, 900, 200, 310, 403, 215, 214, 300, 404, 313, 412, 409, 314, 406, 503, 410, 315, 401, 411, 502, 405, 407, 512, 504, 400,
    605, 506, 408, 507, 413, 415, 414, 510, 500, 509, 513, 515, 508, 505, 511, 514, 501, 600,
)
CUT = 34

def backward_kernel(lens, qk, sq, *refs):
    ni = len(BACK_IN)
    I = dict(zip(BACK_IN, refs[:ni]))
    (o_mx, o_va, o_up, o_wo, o_wd, o_gt, o_tiny, o_red) = refs[ni:ni + 8]
    (WA, WB, L1A, L1B, L2A, L2B, L3A, L3B, L4A, L4B, FA, FB, FSA, FSB, GA, GB_, TOK, PT, U, X0, X1, GT, GG, G1, H, KS, AT, ACC, E, L, Zb,
     T, TL1, TL2, TL4, TG, TP, RR, RL, P6, GMX, Q0, Q1, Q2, SHT, SP, valid, affine, ss, rs, sx, rx, st_, rt_, sr, rr_, li, lo, lw) = refs[ni + 8:]
    p = Pos()
    sem = {name: i for i, name in enumerate(BACK_IN)}
    def load(name, dst): pltpu.make_async_copy(I[name], dst, li.at[sem[name]]).start()
    def ready(*pairs):
        for name, dst in pairs: pltpu.make_async_copy(I[name], dst, li.at[sem[name]]).wait()
    def part_copies(k):
        b, c, w = KINDS[k]
        for h in (0, 1):
            cols = pl.ds((HA, HB)[b] * h + c, w)
            yield pltpu.make_async_copy(I[("wa", "wb")[b]].at[:, cols], (WA, WB)[b].at[:, cols], lw.at[k, h])
    def part(k):
        for cp in part_copies(k): cp.start()
    def part_ready(k):
        for cp in part_copies(k): cp.wait()
    def put(b, half, off, w, get):
        outs = ((o_wo, 0, 384, 384), (o_wd, 384, 768, 384)) if b else ((o_mx, 0, 1536 if half else MXL, MXL), (o_va, VAL, UPL, 768), (o_up, UPL, HA, 768))
        for o, lo_, hi_, step in outs:
            a, e = max(off, lo_), min(off + w, hi_)
            if a < e: o[:, pl.ds(a - lo_ + half * step, e - a)] = get(a - off, e - a)
    g = Scatter(p, (WA, WB), (L1A, L1B), (L2A, L2B), (L3A, L3B), (L4A, L4B), (FA, FB), (FSA, FSB), (GA, GB_), put, ss, rs)
    tot = Total(p, RR, RL, sr, rr_)
    sc = Scan(p, -1, PT, E, L, Zb, sx, rx)
    tiny = Tiny(p, T, TL1, TL2, TL4, o_tiny, TG, st_, rt_)
    v = lambda s, t: pltpu.VMEM(s, t)
    big, mid = v((512, 1536), bf16), v((512, 768), bf16)
    rate, ec, omega = PT.at[0:16, :], PT.at[16:32, :], PT.at[34:35, :]
    gain1, gain2 = PT.at[32:33, :], PT.at[33:34, :]
    def at3(X, i): return X[ds(i, 8), :, :].reshape(64, 768)
    def pair(ref, rows, c, w, step): return jnp.concatenate([ref[rows, c:c + w], ref[rows, c + step:c + step + w]], axis=1)
    def ti2(): tiny.a1(); tiny.zsend()
    def to0():
        for k in range(3):
            t = sub8(sq[pl.ds(k * 8, 8), :]).sum(axis=0, keepdims=True)
            RR[0, 3 + k:4 + k, :] = sum(t[:, j * 128:(j + 1) * 128] for j in range(6))
        RR[0, 6:7, :] = jnp.broadcast_to(jnp.sum(valid[...], axis=0, keepdims=True) * (1.0 / 128.0), (1, 128))
        tot.send(0)
    alone = (sc.sc0, sc.sc1, tiny.st0, tiny.a0, ti2, tiny.fin, tiny.last, to0)
    many = g.steps() + (tot.step,)
    def first(P0, P1, P2, P3, P4, P5, Q3, Q4, PR):
        load("cot", Q4); part(4); load("hs", P0); load("hi", P1)
        full_barrier(p)
        row_masks(lens, valid, p)
        affine[0:3, :] = qk[...].astype(f32)
        def lo_():
            GG[...] = jnp.zeros_like(GG)
            RR[0] = jnp.zeros((8, 128), f32)
            ready(("cot", Q4))
            def rows(i): Q0[ds(i, 64), :] = (Q4[ds(i, 64), :].astype(f32) * valid[ds(i, 64), :]).astype(bf16)
            loop(8, rows)
            part_ready(4); ready(("hs", P0), ("hi", P1))
            part(2); load("n2", Q1); load("mi", X0); load("uc", Q2); load("du", Q3); load("pt", PT)
            load("gt", P3); load("rs", P4); part(3)
        def hi(m):
            c = pl.ds(m * 256, 256)
            ACC[...] = dot_nt(Q0[...], pair(WB, c, DWL, DWL, HB))
            t = dot_tn(P1[:, c], Q0[...]).astype(bf16)
            WB[c, DWL:HB], WB[c, HB + DWL:] = t[:, :DWL], t[:, DWL:]
            def rows(i):
                r = ds(i, 64)
                P2[r, c] = (ACC[r, :] * P0[r, c].astype(f32)).astype(bf16)
            loop(8, rows)
            if m == 5:
                load("at", P0); load("re", P1)
                load("vl", P5); load("vs", P6); load("sp", SP); load("pr", PR); load("tok", TOK); part(1)
        def ub(m):
            if m == 0: part_ready(2); ready(("n2", Q1))
            c = pl.ds(m * 256, 256)
            X1[:, :, c] = (dot_nt(P2[:, 0:768], WA[c, UPL:HA]) + dot_nt(P2[:, 768:], WA[c, HA + UPL:])).reshape(64, 8, 256)
            WA[c, UPL:HA] = dot_tn(Q1[:, c], P2[:, 0:768]).astype(bf16)
            WA[c, HA + UPL:] = dot_tn(Q1[:, c], P2[:, 768:]).astype(bf16)
        def nb():
            load("sh", Q0)
            load("om", Q1)
            ready(("mi", X0), ("uc", Q2), ("du", Q3), ("pt", PT), ("om", Q1))
            def rows(i):
                r = ds(i, 64)
                m_, k = at3(X0, i), at3(X1, i)
                inv = lax.rsqrt(jnp.mean(m_ * m_, axis=-1, keepdims=True) + EPSILON)
                unit = m_ * inv
                GG[0:8, :] += sub8(k * unit)
                k = k * gain2[...]
                gm = Q4[r, :].astype(f32) * valid[r, :] + inv * (k - unit * jnp.mean(k * unit, axis=-1, keepdims=True))
                GMX[r, 0:768] = (gm * Q3[r, :].astype(f32)).astype(bf16)
                GMX[r, 2432:3200] = (gm * Q2[r, :].astype(f32)).astype(bf16)
                GT[r, :] = gm * Q1[r, :].astype(f32)
            loop(8, rows)
            load("bs", Q1)
            part(0)
        def ga(m):
            if m == 0: part_ready(3); ready(("gt", P3), ("at", P0), ("re", P1), ("rs", P4))
            c = pl.ds(m * 256, 256)
            gc = GMX[:, 2432:3200]
            ACC[...] = dot_nt(gc, pair(WB, c, 0, DWL, HB))
            t = dot_tn(P3[:, c], gc).astype(bf16)
            WB[c, 0:DWL], WB[c, HB:HB + DWL] = t[:, :DWL], t[:, DWL:]
            c2 = pl.ds(896 + m * 256, 256)
            def rows(i):
                r = ds(i, 64)
                a = ACC[r, :]
                P2[r, c] = (a * P1[r, c].astype(f32)).astype(bf16)
                GMX[r, c2] = (a * P0[r, c].astype(f32) * P4[r, c].astype(f32)).astype(bf16)
            loop(8, rows)
        def nr():
            ready(("tok", TOK))
            loop(8, lambda i: norm_rows(TOK, PT, U, Q2, i))
        def at_(b):
            if b == 0: ready(("vl", P5), ("vs", P6), ("sp", SP), ("pr", PR))
            r = ds(b, 128)
            pr = PR[r, :]
            gp = dot_nt(P2[r, :], P5[r, :])
            gs = (pr * (gp - jnp.sum(gp * pr, axis=-1, keepdims=True))).astype(bf16)
            el = pr.astype(bf16)
            for m in range(6):
                c = pl.ds(m * 256, 256)
                P6[r, c] = (dot_tn(el, P2[r, c]) * P6[r, c].astype(f32)).astype(bf16)
            s, slope = silu_and_slope(SP[r, :])
            q = (s * affine[0:1, :] + affine[1:2, :]).astype(bf16)
            k = (s * affine[2:3, :]).astype(bf16)
            gq = dot(gs, k) * Z_SCALE
            gk = dot_tn(gs, q) * Z_SCALE
            GMX[r, 768:896] = ((gq * affine[0:1, :] + gk * affine[2:3, :]) * slope).astype(bf16)
            for i, t in enumerate((gq * s, gq, gk * s)):
                RR[0, i:i + 1, :] += jnp.sum(t, axis=0, keepdims=True)
        run_plan(BACKWARD_PLAN[:CUT], (alone + (lo_, nb, nr), many + (hi, ub, ga, at_)))
    pl.run_scoped(first, big, big, big, big, big, big, mid, mid, v((512, 128), f32))
    def second(S, A):
        load("st", S)
        def vb(m):
            if m == 0: part_ready(1)
            c = pl.ds(m * 256, 256)
            X1[:, :, c] = (dot_nt(P6[:, 0:768], WA[c, VAL:UPL]) + dot_nt(P6[:, 768:], WA[c, HA + VAL:HA + UPL])).reshape(64, 8, 256)
        def dv(m):
            c = pl.ds(m * 256, 256)
            WA[c, VAL:UPL] = dot_tn(Q2[:, c], P6[:, 0:768]).astype(bf16)
            WA[c, HA + VAL:HA + UPL] = dot_tn(Q2[:, c], P6[:, 768:]).astype(bf16)
        def bl(m):
            if m == 0: part_ready(0); ready(("bs", Q1), ("sh", Q0))
            c = pl.ds(m * 256, 256)
            ACC[...] = dot_nt(GMX[:, 0:MXL], WA[c, 0:MXL]) + dot_nt(GMX[:, MXL:], WA[c, HA:HA + 1536])
            def rows(i):
                r, k = ds(i, 64), ds(i, 8)
                gb = ACC[r, :] * Q1[r, c].astype(f32)
                X0[k, :, c] = gb.reshape(8, 8, 256)
                GG[8:16, c] += sub8(gb * U[k, :, c].reshape(64, 256))
                X1[k, :, c] += (gb * omega[:, c]).reshape(8, 8, 256)
            loop(8, rows)
        def bk(j):
            if j == 0: ready(("st", S))
            bwd_states(X0, U, S, rate, A, E.at[0], G1, H, KS, j, 2)
        def tr(): SHT[...] = Q0[...].T
        def dm(k):
            off, w = MX_PARTS[k]
            WA[:, off:off + w] = dot(SHT[...], GMX[:, off:off + w]).astype(bf16)
            e = min(off + w, 1536)
            if off < e: WA[:, HA + off:HA + e] = dot(SHT[...], GMX[:, MXL + off:MXL + e]).astype(bf16)
            if off + w > 1536: WA[:, HA + 1536:HA + MXL] = jnp.zeros((768, 128), bf16)
        def gr(j):
            if j == 0: sc.sc2()
            bwd_grad(X0, U, S, A, Zb, rate, ec, H, X1, KS, AT, j, 2)
        def la():
            GG[16:24, :] = jnp.zeros((8, 768), f32)
            def rows(i):
                r = ds(i, 64)
                x = TOK[r, :].astype(f32)
                inv = lax.rsqrt(jnp.mean(x * x, axis=-1, keepdims=True) + EPSILON)
                unit = x * inv
                gn = at3(X1, i)
                GG[16:24, :] += sub8(gn * unit)
                k = gn * gain1[...]
                GT[r, :] += inv * (k - unit * jnp.mean(k * unit, axis=-1, keepdims=True))
            loop(8, rows)
            pltpu.make_async_copy(GT, o_gt, lo.at[0]).start()
            TP[...] = jnp.zeros_like(TP)
            TP[0:16, :] = G1[...]
            TP[16:32, :] = H[...]
            for k, i in ((32, 2), (33, 0), (34, 1)):
                TP[k:k + 1, :] = jnp.sum(GG[pl.ds(i * 8, 8), :], axis=0, keepdims=True)
            for j in range(6): T[j * 128:(j + 1) * 128, :] = TP[:, j * 128:(j + 1) * 128].T
        run_plan(BACKWARD_PLAN[CUT:], (alone + (tr, la), many + (vb, dv, bl, bk, dm, gr)))
    pl.run_scoped(second, v((64, 16, 768), f32), v((64, 16, 768), f32))
    o_red[...] = RR[5]
    g.drain(); tiny.drain(); tot.drain(); sc.drain()
    pltpu.make_async_copy(GT, o_gt, lo.at[0]).wait()

def backward_call(lens, qk, sq, ins):
    n = len(SCATTER_CHUNKS)
    v = pltpu.VMEM
    D_ = pltpu.SemaphoreType.DMA
    sds = jax.ShapeDtypeStruct
    vm_, any_ = pl.BlockSpec(memory_space=pltpu.VMEM), pl.BlockSpec(memory_space=pl.ANY)
    return pl.pallas_call(backward_kernel,
        out_shape=(sds((24, 3200), f32), sds((24, 1536), f32), sds((24, 1536), f32), sds((48, 768), f32), sds((48, 768), f32), sds((512, 768), f32), sds((24, 128), f32), sds((8, 128), f32)),
        in_specs=[pl.BlockSpec(memory_space=pltpu.SMEM)] + [vm_] * 2 + [any_] * len(ins),
        out_specs=[vm_] * 5 + [any_] + [vm_] * 2,
        scratch_shapes=rs_scratch() + [v((512, 768), bf16), v((128, 768), f32), v((64, 8, 768), f32), v((64, 8, 768), f32), v((64, 8, 768), f32), v((512, 768), f32),
            v((24, 768), f32), v((16, 768), f32), v((16, 768), f32), v((8, 128), f32), v((2, 16, 128), f32), v((512, 256), f32),
            v((2, 2, 16, 768), bf16), v((4, 2, 16, 768), bf16), v((2, 16, 768), f32),
            v((768, 128), f32), v((2, 192, 128), f32), v((192, 128), f32), v((3, 48, 128), f32), v((24, 128), f32), v((128, 768), f32),
            v((6, 8, 128), f32), v((5, 8, 128), f32), v((512, 1536), bf16), v((512, 3200), bf16), v((512, 768), bf16), v((512, 768), bf16), v((512, 768), bf16), v((768, 512), bf16), v((512, 128), f32), v((512, 1), f32), v((8, 128), f32),
            D_((n, 11)), D_((n, 11)), D_((4,)), D_((4,)), D_((10,)), D_((10,)), D_((5,)), D_((5,)), D_((len(BACK_IN),)), D_((1,)), D_((len(KINDS), 2))],
        compiler_params=pltpu.CompilerParams(collective_id=1, has_side_effects=True, vmem_limit_bytes=63 * 2**20),
    )(lens, qk, sq, *ins)

def last_kernel(res, gtok, mx, va, wo, wu, wd, tiny, red, rate_t, in_t, out_t, o_res, o_gtok, o_mx, o_va, o_wo, o_wu, o_wd, o_rate, o_in, o_out, o_gain, o_qk, o_rms, *rest):
    mid, ss = rest[:7], rest[7]
    into = [pltpu.make_async_copy(a, m, ss.at[0, k]) for k, (a, m) in enumerate(zip((res, gtok, mx, va, wo, wu, wd), mid))]
    big = [pltpu.make_async_copy(m, o, ss.at[1, k]) for k, (m, o) in enumerate(zip(mid, (o_res, o_gtok, o_mx, o_va, o_wo, o_wu, o_wd)))]
    for cp in into: cp.start()
    for a, b in zip(into, big):
        a.wait()
        b.start()
    t = jnp.concatenate([tiny[...], jnp.zeros((104, 128), f32)], axis=0).T
    g1, h1 = t[0:16, 0:24], t[16:32, 0:24]
    r, a, b = (x[...].astype(f32) for x in (rate_t, in_t, out_t))
    scale = state_scale(r)
    o_out[...] = a * scale * g1
    o_in[...] = b * scale * g1
    o_rate[...] = b * a * (jnp.exp(-2.0 * r) / scale * g1 - scale * h1)
    o_gain[...] = t[32:35, 0:24]
    o_qk[...] = red[0:3, :]
    s = jnp.sum(jnp.concatenate([red[...], jnp.zeros((120, 128), f32)], axis=0).T, axis=0, keepdims=True)
    o_rms[...] = jnp.sqrt(s[:, 3:6] / (s[:, 6:7] * D))
    for cp in big: cp.wait()

def last_call(*args):
    vm_, any_ = pl.BlockSpec(memory_space=pltpu.VMEM), pl.BlockSpec(memory_space=pl.ANY)
    sds = jax.ShapeDtypeStruct
    return pl.pallas_call(last_kernel,
        out_shape=tuple(sds(a.shape, a.dtype) for a in args[:7]) + (sds((16, 24), f32),) * 3 + (sds((3, 24), f32), sds((3, 128), f32), sds((1, 3), f32)),
        in_specs=[any_] * 7 + [vm_] * 5,
        out_specs=[any_] * 7 + [vm_] * 6,
        scratch_shapes=[pltpu.VMEM(a.shape, a.dtype) for a in args[:7]] + [pltpu.SemaphoreType.DMA((2, 7))],
        compiler_params=pltpu.CompilerParams(vmem_limit_bytes=63 * 2**20))(*args)


def per_device_tuned(tokens, cotangent, lengths, w_mx, w_value, w_out, w_up, w_down, ema_rate, ema_in, ema_out, gains, qk_affine):
    tok = tokens.reshape(512, D)
    rate_t, in_t, out_t, gain_t = ema_rate.T, ema_in.T, ema_out.T, gains.T
    kept = forward_call(lengths, qk_affine, rate_t, in_t, out_t, gain_t, w_value, w_mx, w_up, w_out, w_down, tok)
    K = {name: t for (name, _, _), t in zip(FORWARD_OUT, kept)}
    K["tok"], K["cot"], K["mi"] = tok, cotangent.reshape(512, D), K["mi"].reshape(64, 8, 768)
    g_mx, g_va, g_up, g_wo, g_wd, g_tok, tiny, red = backward_call(lengths, qk_affine, K["sq"], [K[name] for name in BACK_IN])
    res, g_tok, g_mx, g_va, g_wo, g_up, g_wd, g_rate, g_in, g_out, g_gain, g_qk, rms = last_call(
        K["res"], g_tok, g_mx, g_va, g_wo, g_up, g_wd, tiny, red, rate_t, in_t, out_t)
    return (res.reshape(tokens.shape), g_tok.reshape(tokens.shape), g_mx, g_va, g_wo, g_up, g_wd, g_rate.T, g_in.T, g_out.T, g_gain.T, g_qk, rms.reshape(3))


def solution(mesh):
    placed = (
        P("dp", "seq", None),
        P("dp", "seq", None),
        P("dp"),
        P(("dp", "seq"), None),
        P(("dp", "seq"), None),
        P(("dp", "seq"), None),
        P(("dp", "seq"), None),
        P(("dp", "seq"), None),
        P(("dp", "seq"), None),
        P(("dp", "seq"), None),
        P(("dp", "seq"), None),
        P(("dp", "seq"), None),
        P(),
    )
    step = per_device_tuned if dict(mesh.shape) == {"dp": 4, "seq": 8} else per_device
    return jax.shard_map(
        step,
        mesh=mesh,
        in_specs=placed,
        out_specs=(
            P("dp", "seq", None),
            P("dp", "seq", None),
            P(("dp", "seq"), None),
            P(("dp", "seq"), None),
            P(("dp", "seq"), None),
            P(("dp", "seq"), None),
            P(("dp", "seq"), None),
            P(("dp", "seq"), None),
            P(("dp", "seq"), None),
            P(("dp", "seq"), None),
            P(("dp", "seq"), None),
            P(),
            P(),
        ),
        check_vma=False,
    )
```

```python
import functools

import jax
import jax.numpy as jnp
from jax import lax
from jax.experimental import pallas as pl
from jax.experimental.pallas import tpu as pltpu
from jax.sharding import PartitionSpec as P

MESH = pl.DeviceIdType.MESH
bf16, f32 = jnp.bfloat16, jnp.float32
D = 768
Z = 128
V = 1536
SPAN = 128
SEQ_DEV = 256


EPSILON = 1e-06
TOP_PRECISION = lax.Precision.HIGHEST


def prefix(value, axis, join, neutral):
    count, mine = (lax.axis_size(axis), lax.axis_index(axis))
    pieces = jax.tree.map(lambda part: lax.all_gather(part, axis), value)
    so_far = jax.tree.map(
        lambda part, zero: jnp.full_like(part, 0) + jnp.asarray(zero, part.dtype), value, neutral
    )

    def lap(position, so_far):
        longer = join(so_far, jax.tree.map(lambda part: part[position], pieces))
        return jax.tree.map(lambda new, old: jnp.where(position < mine, new, old), longer, so_far)

    return lax.fori_loop(0, count - 1, lap, so_far)


def prefix_2(value, axis, combine, identity):
    length, here = (lax.axis_size(axis), lax.axis_index(axis))
    everything = jax.tree.map(
        lambda part, kind: lax.all_gather(part.astype(kind), axis),
        value,
        jax.tree.map(lambda a: jnp.bfloat16 if a.dtype == jnp.float32 else a.dtype, value),
    )
    start = jax.tree.map(
        lambda part, zero: jnp.broadcast_to(jnp.asarray(zero, part.dtype), part.shape),
        value,
        identity,
    )

    def lap(k, before):
        at = length - 1 - k
        reached = at > here
        new = combine(
            before, jax.tree.map(lambda part, own: part[at].astype(own.dtype), everything, value)
        )
        return jax.tree.map(lambda a, b: jnp.where(reached, a, b), new, before)

    return lax.fori_loop(0, length, lap, start)


def silu_slope(values):
    sigmoid = jax.nn.sigmoid(values)
    return sigmoid * (1.0 + values * (1.0 - sigmoid))


def chain_combine(earlier, later):
    return (earlier[0] * later[0], later[0] * earlier[1] + later[1])


def ema_local(rate, beta, eta, input_signal):
    rows_here, length, channels = input_signal.shape
    block_len = min(64, length)
    blocks_count = length // block_len
    lag_values = jnp.arange(block_len, dtype=jnp.float32)
    powers = jnp.exp(-lag_values[:, None, None] * rate[None])
    scale_in = jnp.sqrt(-jnp.expm1(-2.0 * rate)) * beta
    kernel = jnp.sum(powers * (eta * scale_in)[None], axis=2)
    step_ids = jnp.arange(block_len)
    lag_index = jnp.clip(step_ids[:, None] - step_ids[None, :], 0, block_len - 1)
    toeplitz = jnp.where(
        (step_ids[:, None] >= step_ids[None, :])[:, :, None], kernel[lag_index], 0.0
    )
    leading = jnp.exp(-(lag_values[:, None, None] + 1.0) * rate[None]) * eta[None]
    trailing = powers[::-1] * scale_in[None]
    block_decay = jnp.exp(-block_len * rate)
    blocks = jnp.swapaxes(input_signal.reshape(rows_here, blocks_count, block_len, channels), 0, 1)

    def advance(carried, segment):
        smooth = jnp.einsum("tsd,bsd->btd", toeplitz, segment, precision=TOP_PRECISION)
        smooth = smooth + jnp.einsum("tdh,bdh->btd", leading, carried, precision=TOP_PRECISION)
        carried = block_decay * carried + jnp.einsum(
            "sdh,bsd->bdh", trailing, segment, precision=TOP_PRECISION
        )
        return (carried, smooth)

    initial = jnp.zeros((rows_here, channels, rate.shape[1]), jnp.float32)
    final_state, smooth = lax.scan(advance, initial, blocks)
    return (jnp.swapaxes(smooth, 0, 1).reshape(rows_here, length, channels), final_state)


def ema_carry(rate, eta, incoming):
    block_len = min(64, SEQ_DEV)
    blocks_count = SEQ_DEV // block_len
    lag_values = jnp.arange(block_len, dtype=jnp.float32)
    leading = jnp.exp(-(lag_values[:, None, None] + 1.0) * rate[None]) * eta[None]
    block_decay = jnp.exp(-block_len * rate)

    def advance(carried, unused):
        return (
            block_decay * carried,
            jnp.einsum("tdh,bdh->btd", leading, carried, precision=TOP_PRECISION),
        )

    _, smooth = lax.scan(advance, incoming, None, length=blocks_count)
    return jnp.swapaxes(smooth, 0, 1).reshape(incoming.shape[0], SEQ_DEV, incoming.shape[1])


def per_device(
    tokens,
    cotangent,
    lengths,
    w_mx,
    w_value,
    w_out,
    w_up,
    w_down,
    ema_rate,
    ema_in,
    ema_out,
    gains,
    qk_affine,
):
    gathered = (
        lax.all_gather(w_mx, ("dp", "seq"), axis=0, tiled=True),
        lax.all_gather(w_value, ("dp", "seq"), axis=0, tiled=True),
        lax.all_gather(w_out, ("dp", "seq"), axis=0, tiled=True),
        lax.all_gather(w_up, ("dp", "seq"), axis=0, tiled=True),
        lax.all_gather(w_down, ("dp", "seq"), axis=0, tiled=True),
        lax.all_gather(ema_rate, ("dp", "seq"), axis=0, tiled=True),
        lax.all_gather(ema_in, ("dp", "seq"), axis=0, tiled=True),
        lax.all_gather(ema_out, ("dp", "seq"), axis=0, tiled=True),
        lax.all_gather(gains, ("dp", "seq"), axis=0, tiled=True),
    )
    mx_full, value_full, out_full, up_full, down_full, rate_low, beta_low, eta_low, gain_low = (
        gathered
    )
    rate = rate_low.astype(jnp.float32)
    beta = beta_low.astype(jnp.float32)
    eta = eta_low.astype(jnp.float32)
    gain_all = gain_low.astype(jnp.float32)
    gain_first = gain_all[:, 0]
    gain_second = gain_all[:, 1]
    omega_gain = gain_all[:, 2]
    affine = qk_affine.astype(jnp.float32)
    rows_here = tokens.shape[0]
    spans_dev = SEQ_DEV // SPAN
    score_scale = Z ** (-0.5)
    inputs = tokens.astype(jnp.float32)
    seq_pos = lax.axis_index("seq") * SEQ_DEV + jnp.arange(SEQ_DEV, dtype=jnp.int32)
    valid_rows = (seq_pos[None, :] < lengths[:, None]).astype(jnp.float32)[:, :, None]
    inverse1 = lax.rsqrt(jnp.mean(inputs * inputs, axis=-1, keepdims=True) + EPSILON)
    unit1 = inputs * inverse1
    normed = unit1 * gain_first
    normed_low = normed.astype(jnp.bfloat16)
    value_pre = jnp.einsum(
        "bsd,dv->bsv", normed_low, value_full, preferred_element_type=jnp.float32
    )
    value_low = jax.nn.silu(value_pre).astype(jnp.bfloat16)
    (smooth_local, end_local), pull_local = jax.vjp(ema_local, rate, beta, eta, normed)
    growth = jnp.exp(-SEQ_DEV * rate)
    start_state = prefix(
        (growth, end_local),
        "seq",
        chain_combine,
        (jnp.ones_like(growth), jnp.zeros_like(end_local)),
    )[1]
    smooth_carry, pull_carry = jax.vjp(ema_carry, rate, eta, start_state)
    blend = smooth_local + smooth_carry + omega_gain * normed
    shifted_low = jax.nn.silu(blend).astype(jnp.bfloat16)
    mixed = jnp.einsum("bsd,dk->bsk", shifted_low, mx_full, preferred_element_type=jnp.float32)
    update = jax.nn.sigmoid(mixed[..., :D])
    shared_pre = mixed[..., D : D + Z]
    shared = jax.nn.silu(shared_pre)
    reset_pre = mixed[..., D + Z : D + Z + V]
    reset = jax.nn.silu(reset_pre)
    direct = mixed[..., D + Z + V :]
    query_low = (
        (shared * affine[0] + affine[1]).astype(jnp.bfloat16).reshape(rows_here, spans_dev, SPAN, Z)
    )
    key_low = (shared * affine[2]).astype(jnp.bfloat16).reshape(rows_here, spans_dev, SPAN, Z)
    value_tiles = value_low.reshape(rows_here, spans_dev, SPAN, V)
    scores = (
        jnp.einsum("bnqz,bnkz->bnqk", query_low, key_low, preferred_element_type=jnp.float32)
        * score_scale
    )
    causal = jnp.arange(SPAN)[:, None] >= jnp.arange(SPAN)[None, :]
    masked = jnp.where(causal, scores, -1e30)
    peak = jnp.max(masked, axis=-1, keepdims=True)
    expo = jnp.exp(masked - peak)
    attention_weights = expo / jnp.sum(expo, axis=-1, keepdims=True)
    probs_low = attention_weights.astype(jnp.bfloat16)
    attended_output = jnp.einsum(
        "bnqk,bnkv->bnqv", probs_low, value_tiles, preferred_element_type=jnp.float32
    ).reshape(rows_here, SEQ_DEV, V)
    gated_low = (reset * attended_output).astype(jnp.bfloat16)
    cand_pre = direct + jnp.einsum(
        "bsv,vd->bsd", gated_low, out_full, preferred_element_type=jnp.float32
    )
    candidate = jax.nn.silu(cand_pre)
    attn_branch = update * (candidate - inputs)
    middle = inputs + attn_branch
    inverse2 = lax.rsqrt(jnp.mean(middle * middle, axis=-1, keepdims=True) + EPSILON)
    unit2 = middle * inverse2
    normed2_low = (unit2 * gain_second).astype(jnp.bfloat16)
    up_pre = jnp.einsum("bsd,df->bsf", normed2_low, up_full, preferred_element_type=jnp.float32)
    hidden_low = jax.nn.silu(up_pre).astype(jnp.bfloat16)
    ffn_branch = jnp.einsum(
        "bsf,fd->bsd", hidden_low, down_full, preferred_element_type=jnp.float32
    )
    output = middle + ffn_branch
    again = (
        lax.all_gather(w_mx, ("dp", "seq"), axis=0, tiled=True),
        lax.all_gather(w_value, ("dp", "seq"), axis=0, tiled=True),
        lax.all_gather(w_out, ("dp", "seq"), axis=0, tiled=True),
        lax.all_gather(w_up, ("dp", "seq"), axis=0, tiled=True),
        lax.all_gather(w_down, ("dp", "seq"), axis=0, tiled=True),
    )
    mixer_backward, value_back, out_back, up_back, down_back = again
    grad_out = cotangent.astype(jnp.float32) * valid_rows
    grad_out_low = grad_out.astype(jnp.bfloat16)
    grad_down = jnp.einsum(
        "bsf,bsd->fd", hidden_low, grad_out_low, preferred_element_type=jnp.float32
    )
    grad_hidden = jnp.einsum(
        "bsd,fd->bsf", grad_out_low, down_back, preferred_element_type=jnp.float32
    )
    grad_up_low = (grad_hidden * silu_slope(up_pre)).astype(jnp.bfloat16)
    grad_up = jnp.einsum(
        "bsd,bsf->df", normed2_low, grad_up_low, preferred_element_type=jnp.float32
    )
    grad_normed2 = jnp.einsum(
        "bsf,df->bsd", grad_up_low, up_back, preferred_element_type=jnp.float32
    )
    grad_gain_second = jnp.sum(grad_normed2 * unit2, axis=(0, 1))
    scaled2 = grad_normed2 * gain_second
    grad_middle = grad_out + inverse2 * (
        scaled2 - unit2 * jnp.mean(scaled2 * unit2, axis=-1, keepdims=True)
    )
    grad_update = grad_middle * (candidate - inputs)
    grad_cand_pre = grad_middle * update * silu_slope(cand_pre)
    grad_cand_low = grad_cand_pre.astype(jnp.bfloat16)
    grad_out_proj = jnp.einsum(
        "bsv,bsd->vd", gated_low, grad_cand_low, preferred_element_type=jnp.float32
    )
    grad_gated = jnp.einsum(
        "bsd,vd->bsv", grad_cand_low, out_back, preferred_element_type=jnp.float32
    )
    grad_reset = grad_gated * attended_output
    grad_attended_low = (
        (grad_gated * reset).astype(jnp.bfloat16).reshape(rows_here, spans_dev, SPAN, V)
    )
    grad_probs = jnp.einsum(
        "bnqv,bnkv->bnqk", grad_attended_low, value_tiles, preferred_element_type=jnp.float32
    )
    grad_values = jnp.einsum(
        "bnqk,bnqv->bnkv", probs_low, grad_attended_low, preferred_element_type=jnp.float32
    ).reshape(rows_here, SEQ_DEV, V)
    grad_scores_low = (
        attention_weights
        * (grad_probs - jnp.sum(grad_probs * attention_weights, axis=-1, keepdims=True))
    ).astype(jnp.bfloat16)
    grad_query = (
        jnp.einsum("bnqk,bnkz->bnqz", grad_scores_low, key_low, preferred_element_type=jnp.float32)
        * score_scale
    ).reshape(rows_here, SEQ_DEV, Z)
    grad_key = (
        jnp.einsum(
            "bnqk,bnqz->bnkz", grad_scores_low, query_low, preferred_element_type=jnp.float32
        )
        * score_scale
    ).reshape(rows_here, SEQ_DEV, Z)
    grad_affine = jnp.stack(
        [
            jnp.sum(grad_query * shared, axis=(0, 1)),
            jnp.sum(grad_query, axis=(0, 1)),
            jnp.sum(grad_key * shared, axis=(0, 1)),
        ]
    )
    grad_shared = grad_query * affine[0] + grad_key * affine[2]
    grad_mixed_low = jnp.concatenate(
        [
            grad_update * update * (1.0 - update),
            grad_shared * silu_slope(shared_pre),
            grad_reset * silu_slope(reset_pre),
            grad_cand_pre,
        ],
        axis=-1,
    ).astype(jnp.bfloat16)
    grad_mx = jnp.einsum(
        "bsd,bsk->dk", shifted_low, grad_mixed_low, preferred_element_type=jnp.float32
    )
    grad_shifted = jnp.einsum(
        "bsk,dk->bsd", grad_mixed_low, mixer_backward, preferred_element_type=jnp.float32
    )
    grad_blend = grad_shifted * silu_slope(blend)
    grad_omega = jnp.sum(grad_blend * normed, axis=(0, 1))
    grad_value_low = (grad_values * silu_slope(value_pre)).astype(jnp.bfloat16)
    grad_value_proj = jnp.einsum(
        "bsd,bsv->dv", normed_low, grad_value_low, preferred_element_type=jnp.float32
    )
    grad_normed = grad_blend * omega_gain + jnp.einsum(
        "bsv,dv->bsd", grad_value_low, value_back, preferred_element_type=jnp.float32
    )
    rate_from_carry, eta_from_carry, direct_adjoint = pull_carry(grad_blend)
    later_adjoint = prefix_2(
        (growth, direct_adjoint),
        "seq",
        chain_combine,
        (jnp.ones_like(growth), jnp.zeros_like(direct_adjoint)),
    )[1]
    rate_from_local, grad_beta, eta_from_local, normed_from_ema = pull_local(
        (grad_blend, later_adjoint)
    )
    rate_from_growth = jnp.sum(later_adjoint * start_state, axis=0) * (-SEQ_DEV * growth)
    grad_rate = rate_from_carry + rate_from_local + rate_from_growth
    grad_eta = eta_from_carry + eta_from_local
    grad_normed = grad_normed + normed_from_ema
    grad_gain_first = jnp.sum(grad_normed * unit1, axis=(0, 1))
    scaled1 = grad_normed * gain_first
    grad_tokens = grad_middle * (1.0 - update) + inverse1 * (
        scaled1 - unit1 * jnp.mean(scaled1 * unit1, axis=-1, keepdims=True)
    )
    grad_gains = jnp.stack([grad_gain_first, grad_gain_second, grad_omega], axis=1)
    shards = (
        lax.psum_scatter(grad_mx, ("dp", "seq"), scatter_dimension=0, tiled=True),
        lax.psum_scatter(grad_value_proj, ("dp", "seq"), scatter_dimension=0, tiled=True),
        lax.psum_scatter(grad_out_proj, ("dp", "seq"), scatter_dimension=0, tiled=True),
        lax.psum_scatter(grad_up, ("dp", "seq"), scatter_dimension=0, tiled=True),
        lax.psum_scatter(grad_down, ("dp", "seq"), scatter_dimension=0, tiled=True),
        lax.psum_scatter(grad_rate, ("dp", "seq"), scatter_dimension=0, tiled=True),
        lax.psum_scatter(grad_beta, ("dp", "seq"), scatter_dimension=0, tiled=True),
        lax.psum_scatter(grad_eta, ("dp", "seq"), scatter_dimension=0, tiled=True),
        lax.psum_scatter(grad_gains, ("dp", "seq"), scatter_dimension=0, tiled=True),
    )
    squares = jnp.stack(
        [
            jnp.sum(valid_rows * output * output),
            jnp.sum(valid_rows * attn_branch * attn_branch),
            jnp.sum(valid_rows * ffn_branch * ffn_branch),
            jnp.sum(valid_rows),
        ]
    )
    affine_total, square_total = lax.psum((grad_affine, squares), ("dp", "seq"))
    rms_values = jnp.sqrt(square_total[:3] / (square_total[3] * D))
    return (
        output.astype(jnp.bfloat16),
        grad_tokens,
        shards[0],
        shards[1],
        shards[2],
        shards[3],
        shards[4],
        shards[5],
        shards[6],
        shards[7],
        shards[8],
        affine_total,
        rms_values,
    )


HA, HB = 3200, 768
RA, RB = 48, 96

MXL, VAL, UPL, ONE, DWL = 1664, 1664, 2432, 768, 384
KINDS = ((0, 0, 1664), (0, 1664, 768), (0, 2432, 768), (1, 0, 384), (1, 384, 384))
GATHER_CHUNKS = ((0, 1664, 128, "xy"), (0, 1792, 128, "yx"), (0, 1920, 256, "xy"), (0, 2176, 256, "yx"), (0, 0, 384, "xy"), (0, 384, 384, "yx"), (0, 768, 384, "xy"), (0, 1152, 512, "yx"), (1, 0, 128, "xy"), (1, 128, 256, "yx"), (0, 2432, 128, "xy"), (0, 2560, 128, "yx"), (0, 2688, 512, "z"), (1, 384, 128, "xy"), (1, 512, 256, "yx"))
SCATTER_CHUNKS = ((1, 384, 128, "xy"), (1, 512, 128, "yx"), (1, 640, 128, "yx"), (0, 2432, 384, "xy"), (0, 2816, 384, "yx"), (1, 0, 256, "xy"), (1, 256, 128, "yx"), (0, 1664, 512, "yx"), (0, 2176, 256, "xy"), (0, 0, 384, "xy"), (0, 384, 384, "yx"), (0, 768, 256, "xy"), (0, 1024, 256, "yx"), (0, 1280, 128, "xy"), (0, 1408, 256, "yx"))

class Pos:
    def __init__(s):
        s.dp, s.sq = lax.axis_index("dp"), lax.axis_index("seq")
        s.x, s.c, s.z, s.y = s.dp // 2, s.dp % 2, s.sq // 2, s.sq % 2
        s.sib = (s.dp + 1 - 2 * s.c, s.sq)
        s.xn = (s.dp + 2 - 4 * s.x, s.sq)
        s.yn = (s.dp, s.sq + 1 - 2 * s.y)
        s.dpx = s.dp + 2 - 4 * s.x
    def zof(s, d): return (s.z + d) % 4
    def zn(s, d): return (s.dp, s.zof(d) * 2 + s.y)

def rcopy(src, dst, ss, rs, dev):
    return pltpu.make_async_remote_copy(src_ref=src, dst_ref=dst, send_sem=ss, recv_sem=rs, device_id=dev, device_id_type=MESH)

def full_barrier(p, *more, between=lambda: None):
    bar = pltpu.get_barrier_semaphore()
    for d in (p.sib, p.xn, p.yn, p.zn(1), p.zn(2), p.zn(3)) + more:
        pl.semaphore_signal(bar, inc=1, device_id=d, device_id_type=MESH)
    between()
    pl.semaphore_wait(bar, 6 + len(more))

def at(ref, rows, nrows, half, w, off, width):
    return ref.at[pl.ds(pl.multiple_of(rows, 48), nrows), pl.ds(pl.multiple_of(half * w + off, 128), width)]

class Gather:
    def __init__(s, pos, bufs, ss, rs):
        s.p, s.bufs, s.ss, s.rs, s.here = pos, bufs, ss, rs, set()
    def unit(s, i, dp, z, half, n=1):
        b, off, width, _ = GATHER_CHUNKS[i]
        R = (RA, RB)[b]
        return at(s.bufs[b], (dp * 4 + z) * R, n * R, half, (HA, HB)[b], off, width)
    def cp(s, i, k, ref, dev):
        return rcopy(ref, ref, s.ss.at[i, k], s.rs.at[i, k], dev)
    def z0(s, i):
        p = s.p
        u = s.unit(i, p.dp, p.z, p.y)
        for d in (1, 3, 2): rcopy(u, u, s.ss.at[i, d - 1], s.rs.at[i, p.z], p.zn(d)).start()
    def s1(s, i):
        p = s.p
        for d in (1, 2, 3):
            u = s.unit(i, p.dp, p.zof(d), p.y)
            rcopy(u, u, s.ss.at[i, 0], s.rs.at[i, p.zof(d)], p.sib).wait_recv()
        u = s.unit(i, p.dp, 0, p.y, 4)
        s.cp(i, 4, u, p.xn if GATHER_CHUNKS[i][3] == "xy" else p.yn).start()
        s.cp(i, 7, u, p.sib).start()
    def s2(s, i):
        p = s.p
        xy = GATHER_CHUNKS[i][3] == "xy"
        r = s.unit(i, p.dpx, 0, p.y, 4) if xy else s.unit(i, p.dp, 0, 1 - p.y, 4)
        s.cp(i, 4, r, p.xn).wait_recv()
        nxt = p.yn if xy else p.xn
        s.cp(i, 5, s.unit(i, p.dp, 0, p.y, 4), nxt).start()
        s.cp(i, 6, r, nxt).start()
        s.cp(i, 8, r, p.sib).start()
    def s3(s, i, k):
        p = s.p
        if GATHER_CHUNKS[i][3] == "xy": r = s.unit(i, (p.dp, p.dpx)[k], 0, 1 - p.y, 4)
        else: r = s.unit(i, p.dpx, 0, (p.y, 1 - p.y)[k], 4)
        s.cp(i, 5 + k, r, p.sib).wait_recv()
        s.cp(i, 9 + k, r, p.sib).start()
    def sa(s, i): s.s3(i, 0)
    def sb(s, i): s.s3(i, 1)
    def need(s, b, lo, hi):
        for i, (bb, off, w, _) in enumerate(GATHER_CHUNKS):
            if bb == b and off < hi and off + w > lo and i not in s.here:
                s.here.add(i)
                u = s.unit(i, s.p.dp, 0, s.p.y, 4)
                for k in (7, 8, 9, 10): s.cp(i, k, u, s.p.sib).wait_recv()
    def c1(s, i):
        s.cp(i, 4, s.unit(i, s.p.dp, s.p.z, s.p.y), s.p.xn).start()
    def c2(s, i):
        p = s.p
        r = s.unit(i, p.dpx, p.z, p.y)
        s.cp(i, 4, r, p.xn).wait_recv()
        s.cp(i, 5, s.unit(i, p.dp, p.z, p.y), p.yn).start()
        s.cp(i, 6, r, p.yn).start()
    def four(s, i, z):
        p = s.p
        return [s.unit(i, d, z, h) for d in (p.dp, p.dpx) for h in (p.y, 1 - p.y)]
    def c3(s, i):
        p = s.p
        us = s.four(i, p.z)
        s.cp(i, 5, us[1], p.yn).wait_recv()
        s.cp(i, 6, us[3], p.yn).wait_recv()
        for d in (1, 3, 2):
            for k, u in enumerate(us):
                rcopy(u, u, s.ss.at[i, 7 + 4 * d + k], s.rs.at[i, 11 + 4 * (d - 1) + k], p.zn(d)).start()
    def c4(s, i):
        p = s.p
        for d in (1, 2, 3):
            for k, u in enumerate(s.four(i, p.z)):
                rcopy(u, u, s.ss.at[i, 0], s.rs.at[i, 11 + 4 * (d - 1) + k], p.sib).wait_recv()
        for k, (d, h) in enumerate(((p.dp, p.y), (p.dpx, p.y), (p.dp, 1 - p.y), (p.dpx, 1 - p.y))):
            s.cp(i, 7 + k, s.unit(i, d, 0, h, 4), p.sib).start()
    def steps(s): return (s.z0, s.s1, s.s2, s.sa, s.sb, s.c1, s.c2, s.c3, s.c4)
    def drain(s):
        p = s.p
        for i, (_, _, _, order) in enumerate(GATHER_CHUNKS):
            u1 = s.unit(i, p.dp, 0, p.y)
            u = s.unit(i, p.dp, 0, p.y, 4)
            one = (4, 5, 6) + tuple(range(11, 23)) if order == "z" else (0, 1, 2)
            for k in one: s.cp(i, k, u1, p.sib).wait_send()
            for k in range(4, 11):
                if k not in one: s.cp(i, k, u, p.sib).wait_send()

class Scatter:
    NS = 11
    def __init__(s, pos, P, L1, L2, L3, L4, F, FS, G, out, ss, rs):
        s.FS = FS
        s.p, s.P, s.L1, s.L2, s.L3, s.L4, s.F, s.G, s.out, s.ss, s.rs = pos, P, L1, L2, L3, L4, F, G, out, ss, rs
    def geom(s, i):
        b, off, w, order = SCATTER_CHUNKS[i]
        return b, (RA, RB)[b], (HA, HB)[b], off, w, order
    def cols(s, i, yy):
        b, R, W, off, w, _ = s.geom(i)
        return pl.ds(pl.multiple_of(yy * W + off, 128), w)
    def piece(s, i, xx, c, yy, z=0, n=4):
        b, R, W, off, w, _ = s.geom(i)
        return s.P[b].at[pl.ds(pl.multiple_of(((xx * 2 + c) * 4 + z) * R, 48), n * R), s.cols(i, yy)]
    def cp(s, i, k, src, dst, dev):
        return rcopy(src, dst, s.ss.at[i, k], s.rs.at[i, k], dev)
    def add(s, dst, src, nrows):
        def body(r, _):
            rr = pl.ds(pl.multiple_of(r * 48, 48), 48)
            dst[rr, :] = (dst[rr, :].astype(f32) + src[rr, :].astype(f32)).astype(bf16)
            return 0
        lax.fori_loop(0, nrows // 48, body, 0)
    def l1(s, i, xx, yy):
        return s.L1[SCATTER_CHUNKS[i][0]].at[xx, :, s.cols(i, yy)]
    def st0(s, i):
        p = s.p
        for k, (xx, yy) in enumerate(((0, 0), (0, 1), (1, 0), (1, 1))):
            s.cp(i, k, s.piece(i, xx, 1 - p.c, yy), s.l1(i, xx, yy), p.sib).start()
    def a0(s, i):
        R = s.geom(i)[1]
        for k, (xx, yy) in enumerate(((0, 0), (0, 1), (1, 0), (1, 1))):
            l = s.l1(i, xx, yy)
            s.cp(i, k, l, l, s.p.sib).wait_recv()
            s.add(s.piece(i, xx, s.p.c, yy), l, 4 * R)
    def l2(s, i, k):
        b, R, W, off, w, _ = s.geom(i)
        return s.L2[b].at[k, :, pl.ds(off, w)]
    def l3(s, i):
        b, R, W, off, w, _ = s.geom(i)
        return s.L3[b].at[:, pl.ds(off, w)]
    def st1(s, i):
        p, order = s.p, s.geom(i)[5]
        for k in (0, 1):
            src = s.piece(i, k, p.c, 1 - p.y) if order == "xy" else s.piece(i, 1 - p.x, p.c, k)
            s.cp(i, 4 + k, src, s.l2(i, k), p.yn if order == "xy" else p.xn).start()
    def a1(s, i):
        p = s.p; b, R, W, off, w, order = s.geom(i)
        for k in (0, 1):
            l = s.l2(i, k)
            s.cp(i, 4 + k, l, l, p.xn).wait_recv()
            s.add(s.piece(i, k, p.c, p.y) if order == "xy" else s.piece(i, p.x, p.c, k), l, 4 * R)
    def st2(s, i):
        p, order = s.p, s.geom(i)[5]
        src = s.piece(i, 1 - p.x, p.c, p.y) if order == "xy" else s.piece(i, p.x, p.c, 1 - p.y)
        s.cp(i, 6, src, s.l3(i), p.xn if order == "xy" else p.yn).start()
    def a2(s, i):
        l = s.l3(i)
        s.cp(i, 6, l, l, s.p.xn).wait_recv()
        s.add(s.piece(i, s.p.x, s.p.c, s.p.y), l, 4 * s.geom(i)[1])
    def l4(s, i, k):
        b, R, W, off, w, _ = s.geom(i)
        return s.L4[b].at[k, :, pl.ds(off, w)]
    def zsend(s, i):
        p = s.p
        for d in (1, 3, 2):
            rcopy(s.piece(i, p.x, p.c, p.y, p.zof(d), 1), s.l4(i, 3 - d), s.ss.at[i, 6 + d], s.rs.at[i, 10 - d], p.zn(d)).start()
    def fin(s, i):
        p = s.p; b, R, W, off, w, _ = s.geom(i)
        F, G, out = s.F[b], s.G[b], s.out
        h = R // 2
        t = s.piece(i, p.x, p.c, p.y, p.z, 1)[...].astype(f32)
        for k in range(3):
            l = s.l4(i, k)
            s.cp(i, 7 + k, l, l, p.sib).wait_recv()
            t = t + l[...].astype(f32)
        cols = pl.ds(off, w)
        for yy in (0, 1):
            @pl.when(p.y == yy)
            def _():
                F[:, cols] = t[yy * h:yy * h + h, :]
                s.FS[b][:, cols] = t[(1 - yy) * h:(2 - yy) * h, :].astype(bf16)
                out(b, yy, off, w, lambda o, k: F[:, pl.ds(off + o, k)])
        s.cp(i, 10, s.FS[b].at[:, cols], G.at[:, cols], p.yn).start()
    def last(s, i):
        p = s.p; b, R, W, off, w, _ = s.geom(i)
        l = s.G[b].at[:, pl.ds(off, w)]
        s.cp(i, 10, l, l, p.yn).wait_recv()
        for yy in (0, 1):
            @pl.when(p.y == 1 - yy)
            def _(): s.out(b, yy, off, w, lambda o, k: l[:, pl.ds(o, k)].astype(f32))
    def r0(s, i): s.st0(i)
    def r1(s, i): s.a0(i); s.st1(i)
    def r2(s, i): s.a1(i); s.st2(i)
    def r3(s, i): s.a2(i); s.zsend(i)
    def r4(s, i): s.fin(i)
    def r5(s, i): s.last(i)
    def steps(s): return (s.r0, s.r1, s.r2, s.r3, s.r4, s.r5)
    def drain(s):
        p = s.p
        for i in range(len(SCATTER_CHUNKS)):
            b, R, W, off, w, _ = s.geom(i)
            for k, ref in [(k, s.l1(i, 0, 0)) for k in range(4)] + [(4, s.l2(i, 0)), (5, s.l2(i, 1)), (6, s.l3(i)), (10, s.G[b].at[:, pl.ds(off, w)])] + [(7 + k, s.l4(i, k)) for k in range(3)]:
                s.cp(i, k, ref, ref, p.sib).wait_send()

def rs_scratch():
    v = pltpu.VMEM
    return [v((768, 2 * HA), bf16), v((1536, 2 * HB), bf16), v((2, 192, 2 * HA), bf16), v((2, 384, 2 * HB), bf16),
        v((2, 192, HA), bf16), v((2, 384, HB), bf16), v((192, HA), bf16), v((384, HB), bf16),
        v((3, 48, HA), bf16), v((3, 96, HB), bf16), v((24, HA), f32), v((48, HB), f32), v((24, HA), bf16), v((48, HB), bf16), v((24, HA), bf16), v((48, HB), bf16)]

NK = 32
NB = 2

def lanes(j): return pl.ds(pl.multiple_of(j * 128, 128), 128)
def rows_(i): return pl.ds(pl.multiple_of(i * 8, 8), 8)
def tree(xs):
    xs = list(xs)
    while len(xs) > 1:
        xs = [xs[i] + xs[i + 1] if i + 1 < len(xs) else xs[i] for i in range(0, len(xs), 2)]
    return xs[0]

def fwd_states(U, rate, S, END, j, unroll=2):
    ln = lanes(j)
    r = rate[0:16, ln]
    w = [jnp.exp(r * (s - 7.0)) for s in range(8)]
    q8 = jnp.exp(r * -8.0)
    def body(k, st):
        new = []
        for b in range(NB):
            S[b * NK + k, :, ln] = st[b]
            parts = [w[s] * U[b * NK + k, pl.ds(s, 1), ln] for s in range(8)]
            new.append(q8 * st[b] + tree(parts))
        return tuple(new)
    st = lax.fori_loop(0, NK, body, tuple(jnp.zeros((16, 128), f32) for _ in range(NB)), unroll=unroll)
    for b in range(NB): END[b, :, ln] = st[b].astype(END.dtype)

def conv_tables(rate, ec, j):
    ln = lanes(j)
    it = lax.broadcasted_iota(jnp.int32, (8, 128), 0).astype(f32)
    E, K = [], []
    for h in range(16):
        rb = jnp.broadcast_to(rate[pl.ds(h, 1), ln], (8, 128)); eb = jnp.broadcast_to(ec[pl.ds(h, 1), ln], (8, 128))
        K.append(jnp.exp(-it * rb) * eb)
        E.append(jnp.exp(-(it + 1.0) * rb) * eb)
    return E, tree(K)

def fwd_smooth(U, S, S0, rate, ec, omega, BL, KS, j, unroll=1):
    ln = lanes(j)
    r = rate[0:16, ln]
    q8 = jnp.exp(r * -8.0)
    E, K = conv_tables(rate, ec, j)
    KS[...] = K
    ii = lax.broadcasted_iota(jnp.int32, (8, 128), 0)
    KM = [jnp.where(ii >= l, jnp.broadcast_to(KS[pl.ds(l, 1), :], (8, 128)), 0.0) for l in range(8)]
    om = jnp.broadcast_to(omega[:, ln], (8, 128))
    KM[0] = KM[0] + om
    def body(k, gs):
        new = []
        for b in range(NB):
            i = b * NK + k
            S[i, :, ln] = S[i, :, ln] + gs[b]
            u = U[i, :, ln]
            parts = [KM[0] * u] + [KM[l] * pltpu.roll(u, l, 0) for l in range(1, 8)]
            parts += [E[h] * S[i, pl.ds(h, 1), ln] for h in range(16)]
            BL[i, :, ln] = tree(parts)
            new.append(q8 * gs[b])
        return tuple(new)
    lax.fori_loop(0, NK, body, tuple(S0[b, :, ln] for b in range(NB)), unroll=unroll)

def bwd_states(Gr, U, S, rate, A, DIR, G1, H, CS, j, unroll=1):
    ln = lanes(j)
    r = rate[0:16, ln]
    w = [jnp.exp(r * -float(s)) for s in range(8)]
    q8 = jnp.exp(r * -8.0)
    def body(kk, c):
        k = NK - 1 - kk
        st, g1, h1, C = c
        new, C = [], list(C)
        for b in range(NB):
            i = b * NK + k
            A[i, :, ln] = st[b]
            p = [Gr[i, pl.ds(0, 1), ln]] + [w[s] * Gr[i, pl.ds(s, 1), ln] for s in range(1, 8)]
            later = B1 = p[7]
            for t in range(6, 0, -1):
                later = later + p[t]
                B1 = B1 + later
            Bg = later + p[0]
            Sk = S[i, :, ln]
            g1 = g1 + Sk * Bg
            h1 = h1 + Sk * B1
            new.append(q8 * st[b] + Bg)
            u, g = U[i, :, ln], Gr[i, :, ln]
            C = [C[l] + g * (pltpu.roll(u, l, 0) if l else u) for l in range(8)]
        return tuple(new), g1, h1, tuple(C)
    z = jnp.zeros((16, 128), f32)
    st, g1, h1, C = lax.fori_loop(0, NK, body, (tuple(z for _ in range(NB)), z, z, tuple(jnp.zeros((8, 128), f32) for _ in range(8))), unroll=unroll)
    for b in range(NB): DIR[b, :, ln] = st[b].astype(DIR.dtype)
    ii = lax.broadcasted_iota(jnp.int32, (8, 128), 0)
    g1, h1 = g1 * w[1], h1 * w[1]
    for l in range(8):
        cl = jnp.sum(jnp.where(ii >= l, C[l], 0.0), axis=0, keepdims=True)
        t = w[l] * cl
        g1 = g1 + t
        if l: h1 = h1 + t * float(l)
    G1[:, ln] = g1
    H[:, ln] = h1

def bwd_grad(Gr, U, S, A, A0, rate, ec, H, DU, KS, AT, j, unroll=1):
    ln = lanes(j)
    r = rate[0:16, ln]
    q8 = jnp.exp(r * -8.0)
    c8 = 8.0 * jnp.exp(r * -9.0)
    wu = [jnp.exp(r * (s - 8.0)) * (8.0 - s) for s in range(8)]
    it = lax.broadcasted_iota(jnp.int32, (8, 128), 0).astype(f32)
    E, K = [], []
    for h in range(16):
        rb = jnp.broadcast_to(rate[pl.ds(h, 1), ln], (8, 128)); eb = jnp.broadcast_to(ec[pl.ds(h, 1), ln], (8, 128))
        K.append(jnp.exp(-it * rb) * eb)
        E.append(jnp.exp((it - 8.0) * rb) * eb)
    KS[...] = tree(K)
    ii = lax.broadcasted_iota(jnp.int32, (8, 128), 0)
    KM = [jnp.where(ii < 8 - l, jnp.broadcast_to(KS[pl.ds(l, 1), :], (8, 128)), 0.0) for l in range(8)]
    def body(kk, c):
        k = NK - 1 - kk
        gs, h1 = c
        new = []
        for b in range(NB):
            i = b * NK + k
            Ak = A[i, :, ln] + gs[b]
            AT[b] = Ak
            Bu = tree([wu[s] * U[i, pl.ds(s, 1), ln] for s in range(8)])
            h1 = h1 + Ak * (Bu + c8 * S[i, :, ln])
            g = Gr[i, :, ln]
            parts = [KM[0] * g] + [KM[l] * pltpu.roll(g, 8 - l, 0) for l in range(1, 8)]
            parts += [E[h] * AT[b, pl.ds(h, 1), :] for h in range(16)]
            DU[i, :, ln] += tree(parts)
            new.append(q8 * gs[b])
        return tuple(new), h1
    gs, h1 = lax.fori_loop(0, NK, body, (tuple(A0[b, :, ln] for b in range(NB)), H[:, ln]), unroll=unroll)
    H[:, ln] = h1


def sigmoid(v): return jax.nn.sigmoid(v)
def dot(a, b): return jnp.dot(a, b, preferred_element_type=f32)
def dot_nt(a, b): return lax.dot_general(a, b, (((1,), (1,)), ((), ())), preferred_element_type=f32)
def dot_tn(a, b): return lax.dot_general(a, b, (((0,), (0,)), ((), ())), preferred_element_type=f32)
def loop(n, f):
    for i in range(n): f(i)
def ds(i, n): return pl.ds(i * n if isinstance(i, int) else pl.multiple_of(i * n, n), n)
def silu_and_slope(v):
    s = sigmoid(v)
    y = v * s
    return y, s + y * (1.0 - s)

class Params:
    def __init__(s, pos, ref, PRM, ss, rs):
        s.p, s.ref, s.PRM, s.ss, s.rs = pos, ref, PRM, ss, rs
    def r(s, row, n): return s.PRM.at[pl.ds(pl.multiple_of(row, 8), n), :]
    def cp(s, k, src, dst, dev): return rcopy(src, dst, s.ss.at[k], s.rs.at[k], dev)
    def others(s):
        return tuple((d, f) for d in (0, 1, 3, 2) for f in (1, 0) if d or f)
    def y0(s):
        p = s.p
        own = (p.dp * 4 + p.z) * 48 + p.y * 24
        s.PRM[pl.ds(pl.multiple_of(own, 8), 24), :] = s.ref[...]
        for k, (d, f) in enumerate(s.others()):
            y = 1 - p.y if f else p.y
            s.cp(k, s.ref, s.r(own, 24), (p.dp, p.zof(d) * 2 + y)).start()
    def x0(s):
        p = s.p; u = s.r(p.dp * 192, 192)
        for k in range(7):
            l = s.r(p.dp * 192, 24)
            s.cp(k, l, l, p.sib).wait_recv()
        s.cp(7, u, u, p.xn).start()
        s.cp(8, u, u, p.sib).start()
    def x1(s):
        p = s.p; u = s.r(p.dpx * 192, 192)
        s.cp(7, u, u, p.xn).wait_recv()
        s.cp(9, u, u, p.sib).start()
    def end(s):
        p = s.p; u = s.r(p.dp * 192, 192)
        s.cp(8, u, u, p.sib).wait_recv()
        s.cp(9, u, u, p.sib).wait_recv()
    def drain(s):
        p = s.p; u = s.r(p.dp * 192, 192); u1 = s.r(p.dp * 192, 24)
        for k in (7, 8, 9): s.cp(k, u, u, p.sib).wait_send()
        for k in range(7): s.cp(k, u1, u1, p.sib).wait_send()

class Scan:
    def __init__(s, pos, way, rate, E, L, Z, ss, rs):
        s.p, s.way, s.rate, s.E, s.L, s.Z, s.ss, s.rs = pos, way, rate, E, L, Z, ss, rs
    def grow(s, k): return jnp.exp(s.rate[0:16, :] * (-256.0 * k))[None]
    def cp(s, d):
        return rcopy(s.E.at[0 if d == 0 else 1], s.L.at[d], s.ss.at[d], s.rs.at[d], s.p.yn if d == 0 else s.p.zn(s.way * d))
    def sc0(s): s.cp(0).start()
    def sc1(s):
        p = s.p
        s.cp(0).wait_recv()
        own, got = s.E[0].astype(f32), s.L[0].astype(f32)
        second = p.y == (1 if s.way > 0 else 0)
        s.Z[...] = jnp.where(second, got, 0.0)
        pair = jnp.where(second, own, got) + s.grow(1) * jnp.where(second, got, own)
        s.E[1] = pair.astype(s.E.dtype)
        for d in (1, 2, 3):
            @pl.when((p.z + d <= 3) if s.way > 0 else (p.z - d >= 0))
            def _(): s.cp(d).start()
    def sc2(s):
        p = s.p
        k = (p.y if s.way > 0 else 1 - p.y).astype(f32)
        for d in (1, 2, 3):
            @pl.when((p.z - d >= 0) if s.way > 0 else (p.z + d <= 3))
            def _():
                s.cp(d).wait_recv()
                s.Z[...] += s.grow(k + 2.0 * (d - 1)) * s.L[d].astype(f32)
    def drain(s):
        p = s.p
        s.cp(0).wait_send()
        for d in (1, 2, 3):
            @pl.when((p.z + d <= 3) if s.way > 0 else (p.z - d >= 0))
            def _(): s.cp(d).wait_send()

class Halves:
    def __init__(s, pos, mx, va, wo, wu, wd, WA, WB, land, ss, rs):
        s.p, s.mx, s.va, s.wo, s.wu, s.wd, s.WA, s.WB, s.land, s.ss, s.rs = pos, mx, va, wo, wu, wd, WA, WB, land, ss, rs
    def pieces(s, y):
        return ((s.va, y * 768, VAL, 768), (s.mx, y * MXL, 0, 1536 if y else MXL), (s.wu, y * 768, UPL, 768))
    def rb(s, yy): return pl.ds(pl.multiple_of((s.p.dp * 4 + s.p.z) * RB + yy * 48, 48), 48)
    def wb(s, yy, half, k): return s.WB.at[s.rb(yy), pl.ds(half * HB + k * DWL, DWL)]
    def start(s):
        p = s.p
        for yy in (0, 1):
            @pl.when(p.y == yy)
            def _():
                for k, (ref, a, c, w) in enumerate(s.pieces(1 - yy)):
                    rcopy(ref.at[:, pl.ds(a, w)], s.land.at[:, pl.ds(c, w)], s.ss.at[k], s.rs.at[k], p.yn).start()
                for k, ref in enumerate((s.wo, s.wd)):
                    rcopy(ref.at[:, pl.ds((1 - yy) * DWL, DWL)], s.wb(yy, 1 - yy, k), s.ss.at[3 + k], s.rs.at[3 + k], p.yn).start()
                    pltpu.make_async_copy(ref.at[:, pl.ds(yy * DWL, DWL)], s.wb(yy, yy, k), s.ss.at[5 + k]).start()
    def end(s, ks):
        p = s.p
        rows = pl.ds(pl.multiple_of((p.dp * 4 + p.z) * RA, 16), RA)
        for yy in (0, 1):
            @pl.when(p.y == yy)
            def _():
                for k, (ref, a, c, w) in enumerate(s.pieces(yy)):
                    if k not in ks: continue
                    l = s.land.at[:, pl.ds(c, w)]
                    rcopy(l, l, s.ss.at[k], s.rs.at[k], p.yn).wait_recv()
                    both = (ref[:, pl.ds(a, w)], l[...]) if yy == 0 else (l[...], ref[:, pl.ds(a, w)])
                    s.WA[rows, pl.ds(yy * HA + c, w)] = jnp.concatenate([t.astype(f32) for t in both], axis=0).astype(bf16)
                if yy == 1 and 1 in ks: s.WA[rows, pl.ds(HA + 1536, 128)] = jnp.zeros((RA, 128), bf16)
        if 1 in ks:
            u = s.wb(0, 0, 0)
            for k in (0, 1):
                rcopy(u, u, s.ss.at[3 + k], s.rs.at[3 + k], p.yn).wait_recv()
                pltpu.make_async_copy(u, u, s.ss.at[5 + k]).wait()
    def hv0(s): s.end((0,))
    def hv1(s): s.end((1, 2))
    def drain(s):
        p = s.p
        for yy in (0, 1):
            @pl.when(p.y == yy)
            def _():
                for k, (ref, a, c, w) in enumerate(s.pieces(1 - yy)):
                    l = s.land.at[:, pl.ds(c, w)]
                    rcopy(l, l, s.ss.at[k], s.rs.at[k], p.yn).wait_send()
        u = s.wb(0, 0, 0)
        for k in (0, 1): rcopy(u, u, s.ss.at[3 + k], s.rs.at[3 + k], p.yn).wait_send()

def norm_rows(tok, PT, U, NL, i):
    x = tok[ds(i, 64), :].astype(f32)
    r = lax.rsqrt(jnp.mean(x * x, axis=-1, keepdims=True) + EPSILON)
    u = x * r * PT[32:33, :]
    U[ds(i, 8), :, :] = u.reshape(8, 8, 768)
    NL[ds(i, 64), :] = u.astype(bf16)

def run_plan(plan, steps):
    for e in plan:
        if e % 100 == 0: steps[0][e // 100]()
        else: steps[1][e // 100](e % 100 - 1)

def state_scale(rate):
    return jnp.sqrt(jnp.tanh(rate) * (1.0 + jnp.exp(-2.0 * rate)))

def row_masks(lens, valid, p):
    for b in range(2):
        t = lax.broadcasted_iota(jnp.int32, (SEQ_DEV, 1), 0) + p.sq * SEQ_DEV
        valid[b * SEQ_DEV:(b + 1) * SEQ_DEV, :] = jnp.where(t < lens[b], 1.0, 0.0)

def sub8(v):
    return v.reshape(v.shape[0] // 8, 8, v.shape[1]).sum(axis=0)

FORWARD_OUT = (("wa", (768, 2 * HA), bf16), ("wb", (1536, 2 * HB), bf16), ("vl", (512, 1536), bf16), ("vs", (512, 1536), bf16),
    ("re", (512, 1536), bf16), ("rs", (512, 1536), bf16), ("at", (512, 1536), bf16), ("gt", (512, 1536), bf16), ("hi", (512, 1536), bf16), ("hs", (512, 1536), bf16),
    ("uc", (512, 768), bf16), ("du", (512, 768), bf16), ("om", (512, 768), bf16), ("sh", (512, 768), bf16), ("bs", (512, 768), bf16), ("n2", (512, 768), bf16),
    ("mi", (512, 768), f32), ("sp", (512, 128), f32), ("pr", (512, 128), f32), ("st", (64, 16, 768), f32), ("pt", (128, 768), f32), ("res", (512, 768), bf16), ("sq", (24, 768), f32))

FORWARD_PLAN = (
    0, 100, 300, 704, 200, 702, 500, 701, 703, 400, 600, 804, 1213, 706, 802, 700, 711, 712, 801, 800, 1313, 803, 1, 2, 901, 705, 902, 904,
    806, 3, 714, 1001, 812, 1101, 4, 707, 708, 811, 710, 5, 6, 900, 805, 906, 1004, 903, 905, 807, 1003, 1006, 1000, 808, 912, 1005, 1002,
    1103, 709, 814, 907, 1104, 908, 1102, 201, 1012, 810, 1105, 715, 1007, 911, 101, 102, 103, 1413, 104, 809, 202, 1008, 105, 910, 815,
    1108, 106, 1107, 1100, 909, 203, 1011, 1106, 401, 402, 1200, 914, 1111, 1010, 301, 302, 915, 303, 403, 501, 1110, 502, 1009, 1109, 1112,
    503, 504, 1300, 1513, 1014, 1114, 1015, 1400, 601, 1115, 602, 603, 1500,
)

def forward_kernel(lens, qk, rate_t, in_t, out_t, gain_t, *refs):
    far, refs = refs[:6], refs[6:]
    no = len(FORWARD_OUT)
    outs, bufs, rest = refs[:no], refs[no:2 * no], refs[2 * no:]
    B = {name: r for (name, _, _), r in zip(FORWARD_OUT, bufs)}
    O = {name: r for (name, _, _), r in zip(FORWARD_OUT, outs)}
    osem = {name: i for i, (name, _, _) in enumerate(FORWARD_OUT)}
    (PRM, land, U, NL, BL, RSF, UPD, DIR, ACC, KS, E, L, Z, valid, affine, prm, tok, mx, va, wo, wu, wd, si, s0, r0, sp_, rp_, ss, rs, sx, rx, so, sw) = rest
    WA, WB, PT, S = B["wa"], B["wb"], B["pt"], B["st"]
    p = Pos()
    out = lambda name: pltpu.make_async_copy(B[name], O[name], so.at[osem[name]])
    def keep(*names):
        for name in names: out(name).start()
    def weight(k, h):
        b, c, w = KINDS[k]
        a, o = ((WA, O["wa"]), (WB, O["wb"]))[b]
        cols = pl.ds((HA, HB)[b] * h + c, w)
        return pltpu.make_async_copy(a.at[:, cols], o.at[:, cols], sw.at[k, h])
    def keep_weight(k):
        for h in (0, 1): weight(k, h).start()
    def small():
        PT[...] = jnp.zeros_like(PT)
        r = rate_t[...].astype(f32)
        PT[0:16, 0:24] = r
        PT[16:32, 0:24] = out_t[...].astype(f32) * state_scale(r) * in_t[...].astype(f32)
        PT[32:35, 0:24] = gain_t[...].astype(f32)
        prm[...] = PT[:, 0:128].T[0:24, :]
    near = [pltpu.make_async_copy(a, b, si.at[k]) for k, (a, b) in enumerate(zip(far, (va, mx, wu, wo, wd, tok)))]
    for cp in near: cp.start()
    def between():
        small()
        row_masks(lens, valid, p)
        affine[0:3, :] = qk[...].astype(f32)
        for cp in near: cp.wait()
    full_barrier(p, *((p.dp, p.zof(d) * 2 + 1 - p.y) for d in (1, 2, 3)), between=between)
    par = Params(p, prm, PRM, sp_, rp_)
    hv = Halves(p, mx, va, wo, wu, wd, WA, WB, land, s0, r0)
    g = Gather(p, (WA, WB), ss, rs)
    rate, ec, omega = PT.at[0:16, :], PT.at[16:32, :], PT.at[34:35, :]
    sc = Scan(p, 1, PT, E, L, Z, sx, rx)
    SQ = B["sq"]
    def par1(): pass
    def pt():
        par.end()
        for j in range(6): PT[:, j * 128:(j + 1) * 128] = PRM[j * 128:(j + 1) * 128, :].T
    def norm(): loop(8, lambda i: norm_rows(tok, PT, U, NL, i))
    def st(j): fwd_states(U, rate, S, E.at[0], j, 4)
    def sm(j):
        if j == 0: sc.sc2()
        fwd_smooth(U, S, Z, rate, ec, omega, BL, KS, j, 2)
    def sh():
        def rows(i):
            y, s = silu_and_slope(BL[ds(i, 8), :, :].reshape(64, 768))
            B["sh"][ds(i, 64), :] = y.astype(bf16)
            B["bs"][ds(i, 64), :] = s.astype(bf16)
        loop(8, rows)
        keep("st", "pt", "sh", "bs")
    def both(name, slope, m, c, w=256):
        def rows(i):
            y, s = silu_and_slope(ACC[ds(i, 64), 0:256])
            B[name][ds(i, 64), ds(m, 256)] = y.astype(bf16)
            B[slope][ds(i, 64), ds(m, 256)] = s.astype(bf16)
            if name == "re": RSF[ds(i, 64), ds(m, 256)] = y
        loop(8, rows)
    def mul(x, ref, c, w=256): ACC[:, 0:w] = dot(x[...], ref[:, c:c + w])
    def va_(k):
        g.need(0, VAL + 256 * k, VAL + 256 * k + 256)
        for h in (0, 1):
            mul(NL, WA, h * HA + VAL + 256 * k)
            both("vl", "vs", 3 * h + k, 0)
        if k == 2: keep("vl", "vs"); keep_weight(1)
    def mu(k):
        g.need(0, 256 * k, 256 * k + 256)
        mul(B["sh"], WA, 256 * k)
        loop(8, lambda i: UPD.__setitem__((ds(i, 64), ds(k, 256)), sigmoid(ACC[ds(i, 64), 0:256])))
        mul(B["sh"], WA, HA + 256 * k)
        both("re", "rs", 3 + k, 0)
    def ms():
        g.need(0, 768, 896)
        mul(B["sh"], WA, 768, 128)
        B["sp"][...] = ACC[:, 0:128]
    def md(k):
        g.need(0, 768 + 256 * k, 1152 + 256 * k)
        mul(B["sh"], WA, 896 + 256 * k)
        both("re", "rs", k, 0)
        DIR[:, ds(k, 256)] = dot(B["sh"][...], WA[:, HA + 768 + 256 * k:HA + 1024 + 256 * k])
    def at_(b):
        rr = ds(b, 128)
        s = B["sp"][rr, :]
        s = s * sigmoid(s)
        q = (s * affine[0:1, :] + affine[1:2, :]).astype(bf16)
        k = (s * affine[2:3, :]).astype(bf16)
        t = dot_nt(q, k) * Z_SCALE
        ok = lax.broadcasted_iota(jnp.int32, (128, 128), 0) >= lax.broadcasted_iota(jnp.int32, (128, 128), 1)
        t = jnp.where(ok, t, -1e30)
        e = jnp.exp(t - jnp.max(t, axis=-1, keepdims=True))
        e = e / jnp.sum(e, axis=-1, keepdims=True)
        B["pr"][rr, :] = e
        el = e.astype(bf16)
        for m in range(6):
            c = pl.ds(m * 256, 256)
            a = dot(el, B["vl"][rr, c])
            B["at"][rr, c] = a.astype(bf16)
            B["gt"][rr, c] = (a * RSF[rr, c]).astype(bf16)
        if b == 3: keep("re", "rs", "sp", "pr", "at", "gt"); keep_weight(0)
    def ca():
        g.need(1, 0, DWL)
        SQ[...] = jnp.zeros_like(SQ)
        for m in range(2):
            ACC[...] = dot(B["gt"][...], WB[:, m * HB:m * HB + DWL])
            def rows(i):
                r, c = ds(i, 64), pl.ds(m * DWL, DWL)
                y, s = silu_and_slope(DIR[r, c] + ACC[r, :])
                u = UPD[r, c]
                x = tok[r, c].astype(f32)
                a = u * (y - x)
                B["mi"][r, c] = x + a
                B["uc"][r, c] = (u * s).astype(bf16)
                B["du"][r, c] = (a * (1.0 - u)).astype(bf16)
                B["om"][r, c] = (1.0 - u).astype(bf16)
                SQ[8:16, c] += sub8(valid[r, :] * a * a)
            loop(8, rows)
        keep_weight(3)
    def n2():
        def rows(i):
            v = B["mi"][ds(i, 64), :]
            r = lax.rsqrt(jnp.mean(v * v, axis=-1, keepdims=True) + EPSILON)
            B["n2"][ds(i, 64), :] = (v * r * PT[33:34, :]).astype(bf16)
        loop(8, rows)
        keep("mi", "uc", "du", "om", "n2")
    def up(k):
        g.need(0, UPL + 256 * k, UPL + 256 * k + 256)
        for h in (0, 1):
            mul(B["n2"], WA, h * HA + UPL + 256 * k)
            both("hi", "hs", 3 * h + k, 0)
        if k == 2: keep("hi", "hs"); keep_weight(2)
    def do():
        g.need(1, DWL, 2 * DWL)
        keep_weight(4)
        for m in range(2):
            ACC[...] = dot(B["hi"][...], WB[:, m * HB + DWL:m * HB + 2 * DWL])
            def rows(i):
                r, c = ds(i, 64), pl.ds(m * DWL, DWL)
                f = ACC[r, :]
                o = B["mi"][r, c] + f
                B["res"][r, c] = o.astype(bf16)
                v = valid[r, :]
                SQ[0:8, c] += sub8(v * o * o)
                SQ[16:24, c] += sub8(v * f * f)
            loop(8, rows)
        keep("res", "sq")
    steps = (par.y0, hv.start, par1, hv.hv0, hv.hv1, par.x0, par.x1, pt, norm, sc.sc0, sc.sc1, sh, ms, ca, n2, do), (st, sm, va_, mu, md, at_, up) + g.steps()
    run_plan(FORWARD_PLAN, steps)
    g.drain(); par.drain(); sc.drain(); hv.drain()
    for name, _, _ in FORWARD_OUT[2:]: out(name).wait()
    for k in range(len(KINDS)):
        for h in (0, 1): weight(k, h).wait()

Z_SCALE = Z ** -0.5
SCAN_TYPE = f32
def forward_call(*args):
    n = len(GATHER_CHUNKS)
    v = pltpu.VMEM
    D_ = pltpu.SemaphoreType.DMA
    return pl.pallas_call(forward_kernel,
        out_shape=tuple(jax.ShapeDtypeStruct(s, t) for _, s, t in FORWARD_OUT),
        in_specs=[pl.BlockSpec(memory_space=pltpu.SMEM)] + [pl.BlockSpec(memory_space=pltpu.VMEM)] * 5 + [pl.BlockSpec(memory_space=pl.ANY)] * 6,
        out_specs=[pl.BlockSpec(memory_space=pl.ANY)] * len(FORWARD_OUT),
        scratch_shapes=[v(s, t) for _, s, t in FORWARD_OUT] + [v((768, 128), f32), v((24, HA), bf16), v((64, 8, 768), f32), v((512, 768), bf16),
            v((64, 8, 768), f32), v((512, 1536), f32), v((512, 768), f32), v((512, 768), f32), v((512, 384), f32), v((8, 128), f32),
            v((2, 2, 16, 768), SCAN_TYPE), v((4, 2, 16, 768), SCAN_TYPE), v((2, 16, 768), f32),
            v((512, 1), f32), v((8, 128), f32), v((24, 128), f32),
            v((512, 768), bf16), v((24, 3200), bf16), v((24, 1536), bf16), v((48, 768), bf16), v((24, 1536), bf16), v((48, 768), bf16), D_((6,)),
            D_((7,)), D_((5,)), D_((10,)), D_((10,)), D_((n, 23)), D_((n, 23)), D_((4,)), D_((4,)), D_((len(FORWARD_OUT),)), D_((len(KINDS), 2))],
        compiler_params=pltpu.CompilerParams(collective_id=0, has_side_effects=True, vmem_limit_bytes=62 * 2**20),
    )(*args)

class Tiny:
    def __init__(s, pos, T, L1, L2, L4, OUT, G, ss, rs):
        s.p, s.T, s.L1, s.L2, s.L4, s.OUT, s.G, s.ss, s.rs = pos, T, L1, L2, L4, OUT, G, ss, rs
    def r(s, xx, c, z=0, n=4): return s.T.at[pl.ds(pl.multiple_of(((xx * 2 + c) * 4 + z) * 48, 8), n * 48), :]
    def cp(s, k, src, dst, dev): return rcopy(src, dst, s.ss.at[k], s.rs.at[k], dev)
    def st0(s):
        for xx in (0, 1): s.cp(xx, s.r(xx, 1 - s.p.c), s.L1.at[xx], s.p.sib).start()
    def a0(s):
        p = s.p
        for xx in (0, 1):
            l = s.L1.at[xx]
            s.cp(xx, l, l, p.sib).wait_recv()
            t = s.r(xx, p.c)
            t[...] = t[...] + l[...]
        s.cp(2, s.r(1 - p.x, p.c), s.L2, p.xn).start()
    def a1(s):
        p = s.p
        s.cp(2, s.L2, s.L2, p.xn).wait_recv()
        t = s.r(p.x, p.c)
        t[...] = t[...] + s.L2[...]
    def zsend(s):
        p = s.p
        for d in (1, 3, 2): rcopy(s.r(p.x, p.c, p.zof(d), 1), s.L4.at[3 - d], s.ss.at[2 + d], s.rs.at[6 - d], p.zn(d)).start()
    def fin(s):
        p = s.p
        t = s.r(p.x, p.c, p.z, 1)
        v = t[...]
        for k in range(3):
            l = s.L4.at[k]
            s.cp(3 + k, l, l, p.sib).wait_recv()
            v = v + l[...]
        t[...] = v
        row = ((p.x * 2 + p.c) * 4 + p.z) * 48
        far = s.T.at[pl.ds(pl.multiple_of(row + (1 - p.y) * 24, 8), 24), :]
        s.cp(9, far, s.G, p.yn).start()
    def last(s):
        p = s.p
        row = ((p.x * 2 + p.c) * 4 + p.z) * 48
        s.cp(9, s.G, s.G, p.yn).wait_recv()
        s.OUT[...] = s.T[pl.ds(pl.multiple_of(row + p.y * 24, 8), 24), :] + s.G[...]
    def drain(s):
        p = s.p
        for k, l in ((0, s.L1.at[0]), (1, s.L1.at[1]), (2, s.L2), (9, s.G)): s.cp(k, l, l, p.sib).wait_send()
        for k in range(3): s.cp(3 + k, s.L4.at[k], s.L4.at[k], p.sib).wait_send()

class Total:
    def __init__(s, pos, R, L, ss, rs):
        p = pos
        z1 = (p.dp, p.sq + 2 - 4 * (p.z % 2)); z2 = (p.dp, p.sq + 4 - 8 * (p.z // 2))
        s.to, s.R, s.L, s.ss, s.rs = (p.sib, p.xn, p.yn, z1, z2), R, L, ss, rs
    def cp(s, k): return rcopy(s.R.at[k], s.L.at[k], s.ss.at[k], s.rs.at[k], s.to[k])
    def send(s, k): s.cp(k).start()
    def step(s, k):
        s.cp(k).wait_recv()
        s.R[k + 1] = s.R[k] + s.L[k]
        if k < 4: s.send(k + 1)
    def drain(s):
        for k in range(5): s.cp(k).wait_send()

BACK_IN = ("wa", "wb", "vl", "vs", "re", "rs", "at", "gt", "hi", "hs", "uc", "du", "om", "sh", "bs", "n2", "mi", "sp", "pr", "st", "pt", "tok", "cot")
MX_PARTS = ((0, 384), (384, 384), (768, 256), (1024, 256), (1280, 128), (1408, 256))
BACKWARD_PLAN = (
    800, 701, 702, 703, 704, 705, 706, 3, 801, 1, 802, 803, 103, 2, 4, 5, 101, 900, 901, 102, 104, 902, 903, 904, 905, 906, 1001, 1002, 6,
    7, 105, 1003, 1000, 1004, 701, 106, 702, 201, 703, 204, 901, 902, 107, 903, 800, 205, 301, 1102, 11, 304, 203, 1103, 12, 202, 1001, 111,
    1002, 206, 305, 1003, 112, 1004, 303, 1005, 1006, 302, 0, 207, 700, 801, 802, 803, 211, 8, 601, 9, 212, 100, 1101, 10, 108, 602, 109,
    1104, 306, 110, 307, 603, 1106, 13, 1105, 1201, 209, 113, 14, 1202, 312, 208, 311, 1203, 1204, 15, 114, 604, 210, 309, 1205, 308, 115,
    1206, 213, 402, 900, 200, 310, 403, 215, 214, 300, 404, 313, 412, 409, 314, 406, 503, 410, 315, 401, 411, 502, 405, 407, 512, 504, 400,
    605, 506, 408, 507, 413, 415, 414, 510, 500, 509, 513, 515, 508, 505, 511, 514, 501, 600,
)
CUT = 34

def backward_kernel(lens, qk, sq, *refs):
    ni = len(BACK_IN)
    I = dict(zip(BACK_IN, refs[:ni]))
    (o_mx, o_va, o_up, o_wo, o_wd, o_gt, o_tiny, o_red) = refs[ni:ni + 8]
    (WA, WB, L1A, L1B, L2A, L2B, L3A, L3B, L4A, L4B, FA, FB, FSA, FSB, GA, GB_, TOK, PT, U, X0, X1, GT, GG, G1, H, KS, AT, ACC, E, L, Zb,
     T, TL1, TL2, TL4, TG, TP, RR, RL, P6, GMX, Q0, Q1, Q2, SHT, SP, valid, affine, ss, rs, sx, rx, st_, rt_, sr, rr_, li, lo, lw) = refs[ni + 8:]
    p = Pos()
    sem = {name: i for i, name in enumerate(BACK_IN)}
    def load(name, dst): pltpu.make_async_copy(I[name], dst, li.at[sem[name]]).start()
    def ready(*pairs):
        for name, dst in pairs: pltpu.make_async_copy(I[name], dst, li.at[sem[name]]).wait()
    def part_copies(k):
        b, c, w = KINDS[k]
        for h in (0, 1):
            cols = pl.ds((HA, HB)[b] * h + c, w)
            yield pltpu.make_async_copy(I[("wa", "wb")[b]].at[:, cols], (WA, WB)[b].at[:, cols], lw.at[k, h])
    def part(k):
        for cp in part_copies(k): cp.start()
    def part_ready(k):
        for cp in part_copies(k): cp.wait()
    def put(b, half, off, w, get):
        outs = ((o_wo, 0, 384, 384), (o_wd, 384, 768, 384)) if b else ((o_mx, 0, 1536 if half else MXL, MXL), (o_va, VAL, UPL, 768), (o_up, UPL, HA, 768))
        for o, lo_, hi_, step in outs:
            a, e = max(off, lo_), min(off + w, hi_)
            if a < e: o[:, pl.ds(a - lo_ + half * step, e - a)] = get(a - off, e - a)
    g = Scatter(p, (WA, WB), (L1A, L1B), (L2A, L2B), (L3A, L3B), (L4A, L4B), (FA, FB), (FSA, FSB), (GA, GB_), put, ss, rs)
    tot = Total(p, RR, RL, sr, rr_)
    sc = Scan(p, -1, PT, E, L, Zb, sx, rx)
    tiny = Tiny(p, T, TL1, TL2, TL4, o_tiny, TG, st_, rt_)
    v = lambda s, t: pltpu.VMEM(s, t)
    big, mid = v((512, 1536), bf16), v((512, 768), bf16)
    rate, ec, omega = PT.at[0:16, :], PT.at[16:32, :], PT.at[34:35, :]
    gain1, gain2 = PT.at[32:33, :], PT.at[33:34, :]
    def at3(X, i): return X[ds(i, 8), :, :].reshape(64, 768)
    def pair(ref, rows, c, w, step): return jnp.concatenate([ref[rows, c:c + w], ref[rows, c + step:c + step + w]], axis=1)
    def ti2(): tiny.a1(); tiny.zsend()
    def to0():
        for k in range(3):
            t = sub8(sq[pl.ds(k * 8, 8), :]).sum(axis=0, keepdims=True)
            RR[0, 3 + k:4 + k, :] = sum(t[:, j * 128:(j + 1) * 128] for j in range(6))
        RR[0, 6:7, :] = jnp.broadcast_to(jnp.sum(valid[...], axis=0, keepdims=True) * (1.0 / 128.0), (1, 128))
        tot.send(0)
    alone = (sc.sc0, sc.sc1, tiny.st0, tiny.a0, ti2, tiny.fin, tiny.last, to0)
    many = g.steps() + (tot.step,)
    def first(P0, P1, P2, P3, P4, P5, Q3, Q4, PR):
        load("cot", Q4); part(4); load("hs", P0); load("hi", P1)
        def between():
            row_masks(lens, valid, p)
            affine[0:3, :] = qk[...].astype(f32)
            GG[...] = jnp.zeros_like(GG)
            RR[0] = jnp.zeros((8, 128), f32)
            ready(("cot", Q4))
            def rows(i): Q0[ds(i, 64), :] = (Q4[ds(i, 64), :].astype(f32) * valid[ds(i, 64), :]).astype(bf16)
            loop(8, rows)
        full_barrier(p, between=between)
        def lo_():
            part_ready(4); ready(("hs", P0), ("hi", P1))
            part(2); load("n2", Q1); load("mi", X0); load("uc", Q2); load("du", Q3); load("pt", PT)
            load("gt", P3); load("rs", P4); part(3)
        def hi(m):
            c = pl.ds(m * 256, 256)
            ACC[...] = dot_nt(Q0[...], pair(WB, c, DWL, DWL, HB))
            t = dot_tn(P1[:, c], Q0[...]).astype(bf16)
            WB[c, DWL:HB], WB[c, HB + DWL:] = t[:, :DWL], t[:, DWL:]
            def rows(i):
                r = ds(i, 64)
                P2[r, c] = (ACC[r, :] * P0[r, c].astype(f32)).astype(bf16)
            loop(8, rows)
            if m == 5:
                load("at", P0); load("re", P1)
                load("vl", P5); load("vs", P6); load("sp", SP); load("pr", PR); load("tok", TOK); part(1)
        def ub(m):
            if m == 0: part_ready(2); ready(("n2", Q1))
            c = pl.ds(m * 256, 256)
            X1[:, :, c] = (dot_nt(P2[:, 0:768], WA[c, UPL:HA]) + dot_nt(P2[:, 768:], WA[c, HA + UPL:])).reshape(64, 8, 256)
            WA[c, UPL:HA] = dot_tn(Q1[:, c], P2[:, 0:768]).astype(bf16)
            WA[c, HA + UPL:] = dot_tn(Q1[:, c], P2[:, 768:]).astype(bf16)
        def nb():
            load("sh", Q0)
            load("om", Q1)
            ready(("mi", X0), ("uc", Q2), ("du", Q3), ("pt", PT), ("om", Q1))
            def rows(i):
                r = ds(i, 64)
                m_, k = at3(X0, i), at3(X1, i)
                inv = lax.rsqrt(jnp.mean(m_ * m_, axis=-1, keepdims=True) + EPSILON)
                unit = m_ * inv
                GG[0:8, :] += sub8(k * unit)
                k = k * gain2[...]
                gm = Q4[r, :].astype(f32) * valid[r, :] + inv * (k - unit * jnp.mean(k * unit, axis=-1, keepdims=True))
                GMX[r, 0:768] = (gm * Q3[r, :].astype(f32)).astype(bf16)
                GMX[r, 2432:3200] = (gm * Q2[r, :].astype(f32)).astype(bf16)
                GT[r, :] = gm * Q1[r, :].astype(f32)
            loop(8, rows)
            load("bs", Q1)
            part(0)
        def ga(m):
            if m == 0: part_ready(3); ready(("gt", P3), ("at", P0), ("re", P1), ("rs", P4))
            c = pl.ds(m * 256, 256)
            gc = GMX[:, 2432:3200]
            ACC[...] = dot_nt(gc, pair(WB, c, 0, DWL, HB))
            t = dot_tn(P3[:, c], gc).astype(bf16)
            WB[c, 0:DWL], WB[c, HB:HB + DWL] = t[:, :DWL], t[:, DWL:]
            c2 = pl.ds(896 + m * 256, 256)
            def rows(i):
                r = ds(i, 64)
                a = ACC[r, :]
                P2[r, c] = (a * P1[r, c].astype(f32)).astype(bf16)
                GMX[r, c2] = (a * P0[r, c].astype(f32) * P4[r, c].astype(f32)).astype(bf16)
            loop(8, rows)
        def nr():
            ready(("tok", TOK))
            loop(8, lambda i: norm_rows(TOK, PT, U, Q2, i))
        def at_(b):
            if b == 0: ready(("vl", P5), ("vs", P6), ("sp", SP), ("pr", PR))
            r = ds(b, 128)
            pr = PR[r, :]
            gp = dot_nt(P2[r, :], P5[r, :])
            gs = (pr * (gp - jnp.sum(gp * pr, axis=-1, keepdims=True))).astype(bf16)
            el = pr.astype(bf16)
            for m in range(6):
                c = pl.ds(m * 256, 256)
                P6[r, c] = (dot_tn(el, P2[r, c]) * P6[r, c].astype(f32)).astype(bf16)
            s, slope = silu_and_slope(SP[r, :])
            q = (s * affine[0:1, :] + affine[1:2, :]).astype(bf16)
            k = (s * affine[2:3, :]).astype(bf16)
            gq = dot(gs, k) * Z_SCALE
            gk = dot_tn(gs, q) * Z_SCALE
            GMX[r, 768:896] = ((gq * affine[0:1, :] + gk * affine[2:3, :]) * slope).astype(bf16)
            for i, t in enumerate((gq * s, gq, gk * s)):
                RR[0, i:i + 1, :] += jnp.sum(t, axis=0, keepdims=True)
        run_plan(BACKWARD_PLAN[:CUT], (alone + (lo_, nb, nr), many + (hi, ub, ga, at_)))
    pl.run_scoped(first, big, big, big, big, big, big, mid, mid, v((512, 128), f32))
    def second(S, A):
        load("st", S)
        def vb(m):
            if m == 0: part_ready(1)
            c = pl.ds(m * 256, 256)
            X1[:, :, c] = (dot_nt(P6[:, 0:768], WA[c, VAL:UPL]) + dot_nt(P6[:, 768:], WA[c, HA + VAL:HA + UPL])).reshape(64, 8, 256)
        def dv(m):
            c = pl.ds(m * 256, 256)
            WA[c, VAL:UPL] = dot_tn(Q2[:, c], P6[:, 0:768]).astype(bf16)
            WA[c, HA + VAL:HA + UPL] = dot_tn(Q2[:, c], P6[:, 768:]).astype(bf16)
        def bl(m):
            if m == 0: part_ready(0); ready(("bs", Q1), ("sh", Q0))
            c = pl.ds(m * 256, 256)
            ACC[...] = dot_nt(GMX[:, 0:MXL], WA[c, 0:MXL]) + dot_nt(GMX[:, MXL:], WA[c, HA:HA + 1536])
            def rows(i):
                r, k = ds(i, 64), ds(i, 8)
                gb = ACC[r, :] * Q1[r, c].astype(f32)
                X0[k, :, c] = gb.reshape(8, 8, 256)
                GG[8:16, c] += sub8(gb * U[k, :, c].reshape(64, 256))
                X1[k, :, c] += (gb * omega[:, c]).reshape(8, 8, 256)
            loop(8, rows)
        def bk(j):
            if j == 0: ready(("st", S))
            bwd_states(X0, U, S, rate, A, E.at[0], G1, H, KS, j, 2)
        def tr(): SHT[...] = Q0[...].T
        def dm(k):
            off, w = MX_PARTS[k]
            WA[:, off:off + w] = dot(SHT[...], GMX[:, off:off + w]).astype(bf16)
            e = min(off + w, 1536)
            if off < e: WA[:, HA + off:HA + e] = dot(SHT[...], GMX[:, MXL + off:MXL + e]).astype(bf16)
            if off + w > 1536: WA[:, HA + 1536:HA + MXL] = jnp.zeros((768, 128), bf16)
        def gr(j):
            if j == 0: sc.sc2()
            bwd_grad(X0, U, S, A, Zb, rate, ec, H, X1, KS, AT, j, 2)
        def la():
            GG[16:24, :] = jnp.zeros((8, 768), f32)
            def rows(i):
                r = ds(i, 64)
                x = TOK[r, :].astype(f32)
                inv = lax.rsqrt(jnp.mean(x * x, axis=-1, keepdims=True) + EPSILON)
                unit = x * inv
                gn = at3(X1, i)
                GG[16:24, :] += sub8(gn * unit)
                k = gn * gain1[...]
                GT[r, :] += inv * (k - unit * jnp.mean(k * unit, axis=-1, keepdims=True))
            loop(8, rows)
            pltpu.make_async_copy(GT, o_gt, lo.at[0]).start()
            TP[...] = jnp.zeros_like(TP)
            TP[0:16, :] = G1[...]
            TP[16:32, :] = H[...]
            for k, i in ((32, 2), (33, 0), (34, 1)):
                TP[k:k + 1, :] = jnp.sum(GG[pl.ds(i * 8, 8), :], axis=0, keepdims=True)
            for j in range(6): T[j * 128:(j + 1) * 128, :] = TP[:, j * 128:(j + 1) * 128].T
        run_plan(BACKWARD_PLAN[CUT:], (alone + (tr, la), many + (vb, dv, bl, bk, dm, gr)))
    pl.run_scoped(second, v((64, 16, 768), f32), v((64, 16, 768), f32))
    o_red[...] = RR[5]
    g.drain(); tiny.drain(); tot.drain(); sc.drain()
    pltpu.make_async_copy(GT, o_gt, lo.at[0]).wait()

def backward_call(lens, qk, sq, ins):
    n = len(SCATTER_CHUNKS)
    v = pltpu.VMEM
    D_ = pltpu.SemaphoreType.DMA
    sds = jax.ShapeDtypeStruct
    vm_, any_ = pl.BlockSpec(memory_space=pltpu.VMEM), pl.BlockSpec(memory_space=pl.ANY)
    return pl.pallas_call(backward_kernel,
        out_shape=(sds((24, 3200), f32), sds((24, 1536), f32), sds((24, 1536), f32), sds((48, 768), f32), sds((48, 768), f32), sds((512, 768), f32), sds((24, 128), f32), sds((8, 128), f32)),
        in_specs=[pl.BlockSpec(memory_space=pltpu.SMEM)] + [vm_] * 2 + [any_] * len(ins),
        out_specs=[vm_] * 5 + [any_] + [vm_] * 2,
        scratch_shapes=rs_scratch() + [v((512, 768), bf16), v((128, 768), f32), v((64, 8, 768), f32), v((64, 8, 768), f32), v((64, 8, 768), f32), v((512, 768), f32),
            v((24, 768), f32), v((16, 768), f32), v((16, 768), f32), v((8, 128), f32), v((2, 16, 128), f32), v((512, 256), f32),
            v((2, 2, 16, 768), bf16), v((4, 2, 16, 768), bf16), v((2, 16, 768), f32),
            v((768, 128), f32), v((2, 192, 128), f32), v((192, 128), f32), v((3, 48, 128), f32), v((24, 128), f32), v((128, 768), f32),
            v((6, 8, 128), f32), v((5, 8, 128), f32), v((512, 1536), bf16), v((512, 3200), bf16), v((512, 768), bf16), v((512, 768), bf16), v((512, 768), bf16), v((768, 512), bf16), v((512, 128), f32), v((512, 1), f32), v((8, 128), f32),
            D_((n, 11)), D_((n, 11)), D_((4,)), D_((4,)), D_((10,)), D_((10,)), D_((5,)), D_((5,)), D_((len(BACK_IN),)), D_((1,)), D_((len(KINDS), 2))],
        compiler_params=pltpu.CompilerParams(collective_id=1, has_side_effects=True, vmem_limit_bytes=63 * 2**20),
    )(lens, qk, sq, *ins)

def last_kernel(res, gtok, mx, va, wo, wu, wd, tiny, red, rate_t, in_t, out_t, o_res, o_gtok, o_mx, o_va, o_wo, o_wu, o_wd, o_rate, o_in, o_out, o_gain, o_qk, o_rms, *rest):
    mid, ss = rest[:7], rest[7]
    pieces = [(a, m, o, r, a.shape[0] // n) for a, m, o, n in zip((gtok, res, mx, va, wo, wu, wd), mid, (o_gtok, o_res, o_mx, o_va, o_wo, o_wu, o_wd), (4, 2, 1, 1, 1, 1, 1)) for r in range(n)]
    part = lambda ref, r, n: ref.at[pl.ds(r * n, n), :]
    into = [pltpu.make_async_copy(part(a, r, n), part(m, r, n), ss.at[0, k]) for k, (a, m, o, r, n) in enumerate(pieces)]
    big = [pltpu.make_async_copy(part(m, r, n), part(o, r, n), ss.at[1, k]) for k, (a, m, o, r, n) in enumerate(pieces)]
    for cp in into: cp.start()
    for a, b in zip(into, big):
        a.wait()
        b.start()
    t = jnp.concatenate([tiny[...], jnp.zeros((104, 128), f32)], axis=0).T
    g1, h1 = t[0:16, 0:24], t[16:32, 0:24]
    r, a, b = (x[...].astype(f32) for x in (rate_t, in_t, out_t))
    scale = state_scale(r)
    o_out[...] = a * scale * g1
    o_in[...] = b * scale * g1
    o_rate[...] = b * a * (jnp.exp(-2.0 * r) / scale * g1 - scale * h1)
    o_gain[...] = t[32:35, 0:24]
    o_qk[...] = red[0:3, :]
    s = jnp.sum(jnp.concatenate([red[...], jnp.zeros((120, 128), f32)], axis=0).T, axis=0, keepdims=True)
    o_rms[...] = jnp.sqrt(s[:, 3:6] / (s[:, 6:7] * D))
    for cp in big: cp.wait()

def last_call(*args):
    vm_, any_ = pl.BlockSpec(memory_space=pltpu.VMEM), pl.BlockSpec(memory_space=pl.ANY)
    sds = jax.ShapeDtypeStruct
    return pl.pallas_call(last_kernel,
        out_shape=tuple(sds(a.shape, a.dtype) for a in args[:7]) + (sds((16, 24), f32),) * 3 + (sds((3, 24), f32), sds((3, 128), f32), sds((1, 3), f32)),
        in_specs=[any_] * 7 + [vm_] * 5,
        out_specs=[any_] * 7 + [vm_] * 6,
        scratch_shapes=[pltpu.VMEM(args[k].shape, args[k].dtype) for k in (1, 0, 2, 3, 4, 5, 6)] + [pltpu.SemaphoreType.DMA((2, 11))],
        compiler_params=pltpu.CompilerParams(vmem_limit_bytes=63 * 2**20))(*args)


def per_device_tuned(tokens, cotangent, lengths, w_mx, w_value, w_out, w_up, w_down, ema_rate, ema_in, ema_out, gains, qk_affine):
    tok = tokens.reshape(512, D)
    rate_t, in_t, out_t, gain_t = ema_rate.T, ema_in.T, ema_out.T, gains.T
    kept = forward_call(lengths, qk_affine, rate_t, in_t, out_t, gain_t, w_value, w_mx, w_up, w_out, w_down, tok)
    K = {name: t for (name, _, _), t in zip(FORWARD_OUT, kept)}
    K["tok"], K["cot"], K["mi"] = tok, cotangent.reshape(512, D), K["mi"].reshape(64, 8, 768)
    g_mx, g_va, g_up, g_wo, g_wd, g_tok, tiny, red = backward_call(lengths, qk_affine, K["sq"], [K[name] for name in BACK_IN])
    res, g_tok, g_mx, g_va, g_wo, g_up, g_wd, g_rate, g_in, g_out, g_gain, g_qk, rms = last_call(
        K["res"], g_tok, g_mx, g_va, g_wo, g_up, g_wd, tiny, red, rate_t, in_t, out_t)
    return (res.reshape(tokens.shape), g_tok.reshape(tokens.shape), g_mx, g_va, g_wo, g_up, g_wd, g_rate.T, g_in.T, g_out.T, g_gain.T, g_qk, rms.reshape(3))


def solution(mesh):
    placed = (
        P("dp", "seq", None),
        P("dp", "seq", None),
        P("dp"),
        P(("dp", "seq"), None),
        P(("dp", "seq"), None),
        P(("dp", "seq"), None),
        P(("dp", "seq"), None),
        P(("dp", "seq"), None),
        P(("dp", "seq"), None),
        P(("dp", "seq"), None),
        P(("dp", "seq"), None),
        P(("dp", "seq"), None),
        P(),
    )
    step = per_device_tuned if dict(mesh.shape) == {"dp": 4, "seq": 8} else per_device
    return jax.shard_map(
        step,
        mesh=mesh,
        in_specs=placed,
        out_specs=(
            P("dp", "seq", None),
            P("dp", "seq", None),
            P(("dp", "seq"), None),
            P(("dp", "seq"), None),
            P(("dp", "seq"), None),
            P(("dp", "seq"), None),
            P(("dp", "seq"), None),
            P(("dp", "seq"), None),
            P(("dp", "seq"), None),
            P(("dp", "seq"), None),
            P(("dp", "seq"), None),
            P(),
            P(),
        ),
        check_vma=False,
    )
```
